32 devices in a mesh: dp: 16 (over z, y, x), seq: 2 (over core).
Axes of the slice: x: 2, y: 2, z: 4, core: 2. Of those that a mesh axis runs over, the one named last changes fastest.
Arguments:
- block_in: bfloat16 [32, 1024, 768], P('dp', 'seq'), may hold values from -6 to 6
- lengths: int32 [32], P('dp'), may hold values from 128 to 1024, as said below
- out_grad: bfloat16 [32, 1024, 768], P('dp', 'seq'), may hold values from -6 to 6
- w_qkv: float32 [768, 2304], P('dp'), may hold values from -0.21875 to 0.21875
- w_out: float32 [768, 768], P('dp'), may hold values from -1.75 to 1.75
- w_up: float32 [768, 3072], P('dp'), may hold values from -0.21875 to 0.21875
- w_down: float32 [3072, 768], P('dp'), may hold values from -0.109375 to 0.109375
- vectors: float32 [12, 768], P(None, 'dp'), may hold values from -0.4 to 1.4
- first_qkv: float32 [768, 2304], P('dp'), may hold values from -896 to 896
- first_out: float32 [768, 768], P('dp'), may hold values from -64 to 64
- first_up: float32 [768, 3072], P('dp'), may hold values from -224 to 224
- first_down: float32 [3072, 768], P('dp'), may hold values from -512 to 512
- first_vectors: float32 [12, 768], P(None, 'dp'), may hold values from -448 to 448
- second_qkv: float32 [768, 2304], P('dp'), may hold values from 21299.2 to 85196.8
- second_out: float32 [768, 768], P('dp'), may hold values from 104.36608 to 417.46432
- second_up: float32 [768, 3072], P('dp'), may hold values from 1331.2 to 5324.8
- second_down: float32 [3072, 768], P('dp'), may hold values from 7667.712 to 30670.848
- second_vectors: float32 [12, 768], P(None, 'dp'), may hold values from 5324.8 to 21299.2
Outputs:
- block_out: bfloat16 [32, 1024, 768], P('dp', 'seq')
- in_grad: float32 [32, 1024, 768], P('dp', 'seq')
- new_qkv: float32 [768, 2304], P('dp')
- new_out: float32 [768, 768], P('dp')
- new_up: float32 [768, 3072], P('dp')
- new_down: float32 [3072, 768], P('dp')
- new_vectors: float32 [12, 768], P(None, 'dp')
- new_first_qkv: float32 [768, 2304], P('dp')
- new_first_out: float32 [768, 768], P('dp')
- new_first_up: float32 [768, 3072], P('dp')
- new_first_down: float32 [3072, 768], P('dp')
- new_first_vectors: float32 [12, 768], P(None, 'dp')
- new_second_qkv: float32 [768, 2304], P('dp')
- new_second_out: float32 [768, 768], P('dp')
- new_second_up: float32 [768, 3072], P('dp')
- new_second_down: float32 [3072, 768], P('dp')
- new_second_vectors: float32 [12, 768], P(None, 'dp')
The draws below stay inside these ranges and needn't reach their ends.
Inputs may be any that keep to these rules, and one draw needn't show every extreme that they name: `lengths`: among the 2 slots of each index of dp, one has length 1024.
All inputs are finite; a program needn't handle non-finite values.
Results may differ from the reference program's by a relative error of at most 0.0085.
The reference program's roundings to bfloat16 on the way count: a program that leaves them out, or rounds other values in their place, can miss the bound.
Values may be sent and summed in bfloat16 or wider, within the bound.
No kernel may reach another device: no remote copies, remote signals or barrier semaphores. Data moves between devices by JAX's collectives and lax.ppermute only.
A program may use at most 192 MiB of HBM per device.

```python
import math
import jax
import jax.numpy as jnp
from jax import lax

D = 768
HEADS = 12
HEAD_DIM = 64
FF = 3072
SEQ_LEN = 1024
MIN_LEN = 128
STEP = 10
SLOT_DEV = 2
SLOTS = 32
NVEC = 12


def draw_lengths(key, part):
    key = jax.random.fold_in(key, 11)
    key_base, key_pick = jax.random.split(key)
    base_len = jax.random.randint(key_base, (SLOTS,), MIN_LEN, SEQ_LEN + 1)
    picked = jax.random.randint(key_pick, (SLOTS // SLOT_DEV,), 0, SLOT_DEV)
    slot_ids = jnp.arange(SLOTS, dtype=jnp.int32)
    is_full = slot_ids % SLOT_DEV == jnp.repeat(picked, SLOT_DEV)
    return jnp.where(is_full, SEQ_LEN, base_len).astype(jnp.int32)


def draw_vectors(key, part):
    key = jax.random.fold_in(key, 23)
    key_gain, key_bias = jax.random.split(key)
    row_ids = jnp.arange(NVEC, dtype=jnp.int32)[:, None]
    gain_rows = (row_ids == 0) | (row_ids == 5)
    gains = jax.random.uniform(key_gain, (NVEC, D), jnp.float32, 0.6, 1.4)
    biases = jax.random.uniform(key_bias, (NVEC, D), jnp.float32, -0.4, 0.4)
    return jnp.where(gain_rows, gains, biases).astype(jnp.float32)


def level_of(stream_key, extent, cuts, low, largest):
    factor_of, own = 1.0, jax.random.fold_in(stream_key, 6)
    for axis_at, parts in cuts:
        heights = jnp.exp(jax.random.uniform(jax.random.fold_in(own, axis_at), (parts,), jnp.float32, low / len(cuts), largest / len(cuts)))
        factor_of = factor_of * jnp.repeat(heights, extent[axis_at] // parts).reshape([-1 if axis == axis_at else 1 for axis in range(len(extent))])
    return factor_of


def bell_draw(stream_key, extent, spread, limit, pieces=(), held_as=jnp.bfloat16):
    values = jax.random.normal(stream_key, extent, jnp.float32) * spread
    if len(pieces) > 0:
        values = level_of(stream_key, extent, pieces, -0.22, 0.18) * values
    return jnp.clip(values, min=-limit, max=limit).astype(held_as)


def setup_inputs(seed: int = 0) -> dict:
    key_of = jax.random.split(jax.random.key(seed), 19)
    block_in = bell_draw(key_of[0], (SLOTS, SEQ_LEN, D), 1.0, 6.0, ((0, 16), (1, 2)))
    lengths = draw_lengths(jax.random.fold_in(key_of[18], 71), 0)
    out_grad = bell_draw(key_of[2], (SLOTS, SEQ_LEN, D), 1.0, 6.0, ((0, 16), (1, 2)))
    w_qkv = bell_draw(key_of[3], (D, 3 * D), D ** -0.5, 0.21875, ((0, 16),), jnp.float32)
    w_out = bell_draw(key_of[4], (D, D), (D // 64) ** -0.5, 1.75, ((0, 16),), jnp.float32)
    w_up = bell_draw(key_of[5], (D, FF), D ** -0.5, 0.21875, ((0, 16),), jnp.float32)
    w_down = bell_draw(key_of[6], (FF, D), FF ** -0.5, 0.109375, ((0, 16),), jnp.float32)
    vectors = draw_vectors(jax.random.fold_in(key_of[18], 71), 0)
    first_qkv = bell_draw(key_of[8], (D, 3 * D), (1.0 * (SLOTS * SEQ_LEN * 0.65) ** 0.5), 896.0, ((0, 16),), jnp.float32)
    first_out = bell_draw(key_of[9], (D, D), (0.07 * (SLOTS * SEQ_LEN * 0.65) ** 0.5), 64.0, ((0, 16),), jnp.float32)
    first_up = bell_draw(key_of[10], (D, FF), (0.25 * (SLOTS * SEQ_LEN * 0.65) ** 0.5), 224.0, ((0, 16),), jnp.float32)
    first_down = bell_draw(key_of[11], (FF, D), (0.6 * (SLOTS * SEQ_LEN * 0.65) ** 0.5), 512.0, ((0, 16),), jnp.float32)
    first_vectors = bell_draw(key_of[12], (NVEC, D), (0.5 * (SLOTS * SEQ_LEN * 0.65) ** 0.5), 448.0, ((1, 16),), jnp.float32)
    second_qkv = jnp.clip(jnp.exp(math.log(85196.8) - 1.3862944 * jax.random.uniform(key_of[13], (D, 3 * D), jnp.float32) ** level_of(key_of[13], (D, 3 * D), ((0, 16),), -0.2, 0.2)), 21299.2, 85196.8)
    second_out = jnp.clip(jnp.exp(math.log(417.46432) - 1.3862944 * jax.random.uniform(key_of[14], (D, D), jnp.float32) ** level_of(key_of[14], (D, D), ((0, 16),), -0.2, 0.2)), 104.36608, 417.46432)
    second_up = jnp.clip(jnp.exp(math.log(5324.8) - 1.3862944 * jax.random.uniform(key_of[15], (D, FF), jnp.float32) ** level_of(key_of[15], (D, FF), ((0, 16),), -0.2, 0.2)), 1331.2, 5324.8)
    second_down = jnp.clip(jnp.exp(math.log(30670.848) - 1.3862944 * jax.random.uniform(key_of[16], (FF, D), jnp.float32) ** level_of(key_of[16], (FF, D), ((0, 16),), -0.2, 0.2)), 7667.712, 30670.848)
    second_vectors = jnp.clip(jnp.exp(math.log(21299.2) - 1.3862944 * jax.random.uniform(key_of[17], (NVEC, D), jnp.float32) ** level_of(key_of[17], (NVEC, D), ((1, 16),), -0.2, 0.2)), 5324.8, 21299.2)
    return dict(block_in=block_in, lengths=lengths, out_grad=out_grad, w_qkv=w_qkv, w_out=w_out, w_up=w_up, w_down=w_down, vectors=vectors, first_qkv=first_qkv, first_out=first_out, first_up=first_up, first_down=first_down, first_vectors=first_vectors, second_qkv=second_qkv, second_out=second_out, second_up=second_up, second_down=second_down, second_vectors=second_vectors)


@jax.custom_vjp
def low(v):
    return lax.optimization_barrier(v.astype(jnp.bfloat16)).astype(jnp.float32)

@jax.custom_vjp
def low_back(v):
    return v

def low_keep(v):
    return (low(v), None)

def low_pass(kept, grad):
    return (grad,)

def back_keep(v):
    return (v, None)

def back_low(kept, grad):
    return (low(grad),)
low.defvjp(low_keep, low_pass)
low_back.defvjp(back_keep, back_low)
EPS_NORM = 1e-05
EPS_ADAM = 1e-08
BETA_ONE = 0.5
BETA_TWO = 0.5
MATRIX_DECAY = 0.1
VECTOR_RATE = 0.1
NEG_FILL = -1e+30
HIGH = lax.Precision.HIGHEST

def product(left, right):
    return jnp.dot(left, right, precision=HIGH)

def layer_norm(rows, row_gain, row_bias):
    row_mean = lax.optimization_barrier(jnp.mean(rows, axis=-1, keepdims=True))
    centred = rows - row_mean
    variance = lax.optimization_barrier(jnp.mean(centred * centred, axis=-1, keepdims=True))
    return centred * lax.rsqrt(variance + EPS_NORM) * row_gain + row_bias

def slot_forward(stream, length, mat_qkv, mat_out, mat_up, mat_down, vec_all):
    seq_rows = stream.shape[0]
    positions = jnp.arange(seq_rows, dtype=jnp.int32)
    valid_rows = (positions < length).astype(jnp.float32)[:, None]
    normed_one = low(layer_norm(stream, vec_all[0], vec_all[1]))
    qkv_bias = jnp.concatenate([vec_all[2], jnp.zeros_like(vec_all[2]), vec_all[3]])
    qkv_rows = low_back(low(product(normed_one, mat_qkv) + qkv_bias))
    queries = qkv_rows[:, :D].reshape(seq_rows, HEADS, HEAD_DIM)
    key_heads = qkv_rows[:, D:2 * D].reshape(seq_rows, HEADS, HEAD_DIM)
    value_heads = qkv_rows[:, 2 * D:].reshape(seq_rows, HEADS, HEAD_DIM)
    raw_scores = jnp.einsum('qhd,khd->hqk', queries, key_heads, precision=HIGH) * HEAD_DIM ** (-0.5)
    raw_scores = low_back(raw_scores)
    allowed = (positions[None, :] <= positions[:, None]) & (positions[None, :] < length)
    masked = jnp.where(allowed[None], raw_scores, NEG_FILL)
    row_top = lax.optimization_barrier(jnp.max(masked, axis=-1, keepdims=True))
    exp_scores = jnp.exp(masked - row_top)
    attn_probs = low(exp_scores / lax.optimization_barrier(jnp.sum(exp_scores, axis=-1, keepdims=True)))
    attended = jnp.einsum('hqk,khd->qhd', attn_probs, value_heads, precision=HIGH).reshape(seq_rows, D)
    attended = low_back(low(attended))
    projected = low_back(product(attended, mat_out) + vec_all[4])
    mid_rows = stream + projected
    normed_two = low(layer_norm(mid_rows, vec_all[5], vec_all[6]))
    up_rows = low_back(product(normed_two, mat_up) + vec_all[8:].reshape(FF))
    activated = low(jax.nn.gelu(up_rows, approximate=True))
    down_rows = low_back(product(activated, mat_down) + vec_all[7])
    return (mid_rows + down_rows) * valid_rows

def adamw(weight, gradient, first_moment, second_moment, step_rate, weight_decay):
    first_moment = BETA_ONE * first_moment + (1.0 - BETA_ONE) * gradient
    second_moment = BETA_TWO * second_moment + (1.0 - BETA_TWO) * gradient * gradient
    first_fix = 1.0 - BETA_ONE ** STEP
    second_fix = 1.0 - BETA_TWO ** STEP
    direction = first_moment / first_fix / (jnp.sqrt(second_moment / second_fix) + EPS_ADAM)
    return (weight - step_rate * (direction + weight_decay * weight), first_moment, second_moment)

def reference(block_in, lengths, out_grad, w_qkv, w_out, w_up, w_down, vectors, first_qkv, first_out, first_up, first_down, first_vectors, second_qkv, second_out, second_up, second_down, second_vectors):
    stream_all = block_in.astype(jnp.float32)

    def whole(stream_in, raw_qkv, raw_out, raw_up, raw_down, raw_vec):
        mat_qkv = low(raw_qkv)
        mat_out = low(raw_out)
        mat_up = low(raw_up)
        mat_down = low(raw_down)
        vec_all = low(raw_vec)
        checked = jax.checkpoint(slot_forward)

        def one_slot(pair):
            return checked(pair[0], pair[1], mat_qkv, mat_out, mat_up, mat_down, vec_all)
        return lax.map(one_slot, (stream_in, lengths))
    output, pullback = jax.vjp(whole, stream_all, w_qkv, w_out, w_up, w_down, vectors)
    grads = pullback(out_grad.astype(jnp.float32))
    weights = (w_qkv, w_out, w_up, w_down, vectors)
    firsts = (first_qkv, first_out, first_up, first_down, first_vectors)
    seconds = (second_qkv, second_out, second_up, second_down, second_vectors)
    rates = (D ** (-0.5), (D // 64) ** (-0.5), D ** (-0.5), FF ** (-0.5), VECTOR_RATE)
    decays = (MATRIX_DECAY, MATRIX_DECAY, MATRIX_DECAY, MATRIX_DECAY, 0.0)
    results = [adamw(weights[i], grads[i + 1], firsts[i], seconds[i], rates[i], decays[i]) for i in range(5)]
    return (output.astype(jnp.bfloat16), grads[0], results[0][0], results[1][0], results[2][0], results[3][0], results[4][0], results[0][1], results[1][1], results[2][1], results[3][1], results[4][1], results[0][2], results[1][2], results[2][2], results[3][2], results[4][2])
```

```python
import functools

import jax
import jax.numpy as jnp
from jax import lax
from jax.experimental import pallas as pl
from jax.experimental.pallas import tpu as pltpu
from jax.sharding import PartitionSpec as P

D = 768
HEADS = 12
HEAD_DIM = 64
FF = 3072
STEP = 10

EPS_NORM = 1e-05
EPS_ADAM = 1e-08
BETA_ONE = 0.5
BETA_TWO = 0.5
MATRIX_DECAY = 0.1
VECTOR_RATE = 0.1
NEG_FILL = -1e30
GELU_ROOT = 0.7978845608028654
GELU_CUBE = 0.044715
VMEM_LIMIT = 60 * 1024 * 1024

F32 = jnp.float32
BF16 = jnp.bfloat16

NN = (((1,), (0,)), ((), ()))
NT = (((1,), (1,)), ((), ()))
TN = (((0,), (0,)), ((), ()))


def mm(left, right, dims=NN):
    return lax.dot_general(left, right, dims, preferred_element_type=F32)


def cost(flops, nbytes, trans=0):
    return pl.CostEstimate(flops=int(flops), bytes_accessed=int(nbytes), transcendentals=int(trans))


def params():
    return pltpu.CompilerParams(vmem_limit_bytes=VMEM_LIMIT)


def whole_spec(shape):
    return pl.BlockSpec(shape, lambda *idx: (0,) * len(shape), pipeline_mode=pl.Buffered(1))


def norm_parts(rows):
    mean = jnp.mean(rows, axis=-1, keepdims=True)
    centred = rows - mean
    variance = jnp.mean(centred * centred, axis=-1, keepdims=True)
    scale = lax.rsqrt(variance + EPS_NORM)
    return centred * scale, scale


def norm_back(d_normed, normed, scale):
    first = jnp.mean(d_normed, axis=-1, keepdims=True)
    second = jnp.mean(d_normed * normed, axis=-1, keepdims=True)
    return scale * (d_normed - first - normed * second)


def qkv_kernel(x_ref, w_ref, vec_ref, h_ref, qkv_ref):
    normed, _ = norm_parts(x_ref[...].astype(F32))
    h = (normed * vec_ref[0:1, :] + vec_ref[1:2, :]).astype(BF16)
    h_ref[...] = h
    qkv_ref[:, :D] = (mm(h, w_ref[:, :D]) + vec_ref[2:3, :]).astype(BF16)
    qkv_ref[:, D : 2 * D] = mm(h, w_ref[:, D : 2 * D]).astype(BF16)
    qkv_ref[:, 2 * D :] = (mm(h, w_ref[:, 2 * D :]) + vec_ref[3:4, :]).astype(BF16)


def qkv_call(x, w, vec, block=256):
    rows = x.shape[0]
    return pl.pallas_call(
        qkv_kernel,
        name="qkv",
        grid=(rows // block,),
        in_specs=[
            pl.BlockSpec((block, D), lambda i: (i, 0)),
            whole_spec(w.shape),
            whole_spec(vec.shape),
        ],
        out_specs=[
            pl.BlockSpec((block, D), lambda i: (i, 0)),
            pl.BlockSpec((block, 3 * D), lambda i: (i, 0)),
        ],
        out_shape=[
            jax.ShapeDtypeStruct((rows, D), BF16),
            jax.ShapeDtypeStruct((rows, 3 * D), BF16),
        ],
        compiler_params=params(),
        cost_estimate=cost(2 * rows * D * 3 * D, 10e6),
    )(x, w, vec)


def head_parts(length, q_all, k_all, head):
    full_len = q_all.shape[0]
    lane = lax.broadcasted_iota(jnp.int32, (1, 128), 1)
    mine = (lane // HEAD_DIM) == head
    spare = lane == HEAD_DIM * (1 - head)
    pos = lax.broadcasted_iota(jnp.int32, (full_len, 128), 0)
    fill = jnp.where(pos < length, 0.0, NEG_FILL).astype(BF16)
    zero = jnp.zeros((), BF16)
    k_head = jnp.where(mine, k_all, jnp.where(spare, fill, zero))
    q_plain = jnp.where(mine, q_all, zero)
    q_head = jnp.where(spare, jnp.ones((), BF16), q_plain)
    return mine, k_head, q_plain, q_head


def causal_mask(scores, block):
    full = scores.shape[0]
    key_pos = lax.broadcasted_iota(jnp.int32, (block, block), 0)
    query_pos = lax.broadcasted_iota(jnp.int32, (block, block), 1)
    last = jnp.where(key_pos <= query_pos, scores[full - block :], NEG_FILL)
    if full == block:
        return last
    return jnp.concatenate([scores[: full - block], last], axis=0)


def attend_kernel(core_ref, len_ref, q_ref, k_ref, v_ref, a_ref, lse_ref, mixed_ref):
    block = 256
    full_len = q_ref.shape[0]
    length = len_ref[core_ref[0]]
    q_all = q_ref[...] * jnp.asarray(HEAD_DIM ** (-0.5), BF16)
    k_all = k_ref[...]
    v_turned = v_ref[...].T
    for head in range(2):
        _, k_head, _, q_head = head_parts(length, q_all, k_all, head)
        v_head = v_turned[head * HEAD_DIM : (head + 1) * HEAD_DIM]
        for j in range(full_len // block):
            cols = slice(j * block, (j + 1) * block)
            span = (j + 1) * block
            scores = causal_mask(mm(k_head[:span], q_head[cols], NT), block)
            top = jnp.max(scores, axis=0, keepdims=True)
            exped = jnp.exp(scores - top)
            total = jnp.sum(exped, axis=0, keepdims=True)
            mixed = mm(v_head[:, :span], exped.astype(BF16)) / total
            mixed_ref[head * HEAD_DIM : (head + 1) * HEAD_DIM, cols] = mixed
            lse_ref[0, head : head + 1, cols] = top + jnp.log(total)
    a_ref[...] = mixed_ref[...].T.astype(BF16)


def attend_call(core, lengths, qkv):
    rows = qkv.shape[0]
    pairs = HEADS // 2
    return pl.pallas_call(
        attend_kernel,
        name="attend",
        grid_spec=pltpu.PrefetchScalarGridSpec(
            num_scalar_prefetch=2,
            grid=(pairs,),
            in_specs=[
                pl.BlockSpec((rows, 128), lambda i, c, n: (0, i)),
                pl.BlockSpec((rows, 128), lambda i, c, n: (0, i + pairs)),
                pl.BlockSpec((rows, 128), lambda i, c, n: (0, i + 2 * pairs)),
            ],
            out_specs=[
                pl.BlockSpec((rows, 128), lambda i, c, n: (0, i)),
                pl.BlockSpec((1, 8, rows), lambda i, c, n: (i, 0, 0)),
            ],
            scratch_shapes=[pltpu.VMEM((128, rows), F32)],
        ),
        out_shape=[
            jax.ShapeDtypeStruct((rows, D), BF16),
            jax.ShapeDtypeStruct((pairs, 8, rows), F32),
        ],
        compiler_params=params(),
        cost_estimate=cost(1.6e10, 7e6, HEADS * rows * rows * 0.6),
    )(core, lengths, qkv, qkv, qkv)


def attend_back_kernel(
    core_ref, len_ref, q_ref, k_ref, v_ref, a_ref, da_ref, lse_ref, dq_ref, dk_ref, dv_ref, dqt_ref, dk_acc, dv_acc
):
    block = 256
    full_len = q_ref.shape[0]
    length = len_ref[core_ref[0]]
    scale = HEAD_DIM ** (-0.5)
    q_all = q_ref[...] * jnp.asarray(scale, BF16)
    k_all = k_ref[...]
    k_turned = k_all.T
    v_all = v_ref[...]
    da_all = da_ref[...]
    inner = (da_all.astype(F32) * a_ref[...].astype(F32)).T
    first = True
    for head in range(2):
        mine, k_head, q_plain, q_head = head_parts(length, q_all, k_all, head)
        da_head = jnp.where(mine, da_all, jnp.zeros((), BF16))
        lanes = slice(head * HEAD_DIM, (head + 1) * HEAD_DIM)
        centre = jnp.sum(inner[lanes], axis=0, keepdims=True)
        for j in reversed(range(full_len // block)):
            cols = slice(j * block, (j + 1) * block)
            span = (j + 1) * block
            scores = causal_mask(mm(k_head[:span], q_head[cols], NT), block)
            probs = jnp.exp(scores - lse_ref[0, head : head + 1, cols])
            d_probs = mm(v_all[:span], da_head[cols], NT)
            d_scores = (probs * (d_probs - centre[:, cols])).astype(BF16)
            dv_part = mm(probs.astype(BF16), da_head[cols])
            dk_part = mm(d_scores, q_plain[cols])
            if first:
                dv_acc[...] = dv_part
                dk_acc[...] = dk_part
                first = False
            else:
                dv_acc[:span] += dv_part
                dk_acc[:span] += dk_part
            dqt_ref[lanes, cols] = mm(k_turned[lanes, :span], d_scores) * scale
    dq_ref[...] = dqt_ref[...].T.astype(BF16)
    dk_ref[...] = dk_acc[...].astype(BF16)
    dv_ref[...] = dv_acc[...].astype(BF16)


def attend_back_call(core, lengths, qkv, a, da, lse):
    rows = qkv.shape[0]
    pairs = HEADS // 2
    pair_spec = pl.BlockSpec((rows, 128), lambda i, c, n: (0, i))
    return pl.pallas_call(
        attend_back_kernel,
        name="attend_back",
        grid_spec=pltpu.PrefetchScalarGridSpec(
            num_scalar_prefetch=2,
            grid=(pairs,),
            in_specs=[
                pair_spec,
                pl.BlockSpec((rows, 128), lambda i, c, n: (0, i + pairs)),
                pl.BlockSpec((rows, 128), lambda i, c, n: (0, i + 2 * pairs)),
                pair_spec,
                pair_spec,
                pl.BlockSpec((1, 8, rows), lambda i, c, n: (i, 0, 0)),
            ],
            out_specs=[pair_spec, pair_spec, pair_spec],
            scratch_shapes=[
                pltpu.VMEM((128, rows), F32),
                pltpu.VMEM((rows, 128), F32),
                pltpu.VMEM((rows, 128), F32),
            ],
        ),
        out_shape=[jax.ShapeDtypeStruct((rows, D), BF16)] * 3,
        compiler_params=params(),
        cost_estimate=cost(4e10, 13e6, HEADS * rows * rows * 0.6),
    )(core, lengths, qkv, qkv, qkv, a, da, lse)


def valid_rows(core_ref, len_ref, block):
    pos = pl.program_id(0) * block + lax.broadcasted_iota(jnp.int32, (block, 1), 0)
    return pos < len_ref[core_ref[0]]


def add_row(acc_ref, row, value):
    acc_ref[row : row + 1, :] += jnp.sum(value, axis=0, keepdims=True)


def middle_kernel(
    core_ref, len_ref, x_ref, a_ref, og_ref, wo_ref, wu_ref, wd_ref, vec_ref,
    out_ref, dy_ref, e_ref, dz_ref, h_ref, dmb_ref, dm_ref, da_ref, acc_ref, slope_ref,
):
    block = x_ref.shape[0]

    @pl.when(pl.program_id(0) == 0)
    def _():
        acc_ref[...] = jnp.zeros_like(acc_ref)

    valid = valid_rows(core_ref, len_ref, block)
    mid = x_ref[...].astype(F32) + mm(a_ref[...], wo_ref[...]) + vec_ref[4:5, :]
    normed, scale = norm_parts(mid)
    h = (normed * vec_ref[5:6, :] + vec_ref[6:7, :]).astype(BF16)
    h_ref[...] = h
    down = vec_ref[7:8, :] + mid
    for j in range(FF // D):
        cols = slice(j * D, (j + 1) * D)
        z = mm(h, wu_ref[:, cols]) + vec_ref[8 + j : 9 + j, :]
        squared = z * z
        turned = jnp.tanh(GELU_ROOT * z * (1.0 + GELU_CUBE * squared))
        half = 0.5 * (1.0 + turned)
        slope_ref[:, cols] = half + half * (1.0 - turned) * z * (
            GELU_ROOT + (3.0 * GELU_ROOT * GELU_CUBE) * squared
        )
        e = (z * half).astype(BF16)
        e_ref[:, cols] = e
        down += mm(e, wd_ref[cols, :])
    out_ref[...] = jnp.where(valid, down, 0.0).astype(BF16)
    dy = jnp.where(valid, og_ref[...].astype(F32), 0.0)
    dy_low = dy.astype(BF16)
    dy_ref[...] = dy_low
    add_row(acc_ref, 7, dy)
    dh = jnp.zeros((block, D), F32)
    for j in range(FF // D):
        cols = slice(j * D, (j + 1) * D)
        dz = (mm(dy_low, wd_ref[cols, :], NT) * slope_ref[:, cols]).astype(BF16)
        dz_ref[:, cols] = dz
        add_row(acc_ref, 8 + j, dz.astype(F32))
        dh += mm(dz, wu_ref[:, cols], NT)
    add_row(acc_ref, 5, dh * normed)
    add_row(acc_ref, 6, dh)
    dm = dy + norm_back(dh * vec_ref[5:6, :], normed, scale)
    dm_ref[...] = dm
    dm_low = dm.astype(BF16)
    dmb_ref[...] = dm_low
    add_row(acc_ref, 4, dm_low.astype(F32))
    da_ref[...] = mm(dm_low, wo_ref[...], NT).astype(BF16)


def middle_call(core, lengths, x, a, og, wo, wu, wd, vec, block=256):
    rows = x.shape[0]
    row_spec = pl.BlockSpec((block, D), lambda i, c, n: (i, 0))
    wide_spec = pl.BlockSpec((block, FF), lambda i, c, n: (i, 0))
    low = jax.ShapeDtypeStruct((rows, D), BF16)
    wide = jax.ShapeDtypeStruct((rows, FF), BF16)
    return pl.pallas_call(
        middle_kernel,
        name="middle",
        grid_spec=pltpu.PrefetchScalarGridSpec(
            num_scalar_prefetch=2,
            grid=(rows // block,),
            in_specs=[
                row_spec, row_spec, row_spec,
                whole_spec(wo.shape), whole_spec(wu.shape), whole_spec(wd.shape), whole_spec(vec.shape),
            ],
            out_specs=[
                row_spec, row_spec, wide_spec, wide_spec, row_spec, row_spec, row_spec, row_spec,
                pl.BlockSpec((16, D), lambda i, c, n: (0, 0)),
            ],
            scratch_shapes=[pltpu.VMEM((block, FF), F32)],
        ),
        out_shape=[
            low, low, wide, wide, low, low, jax.ShapeDtypeStruct((rows, D), F32), low,
            jax.ShapeDtypeStruct((16, D), F32),
        ],
        compiler_params=params(),
        cost_estimate=cost(2.3e10, 40e6, rows * FF),
    )(core, lengths, x, a, og, wo, wu, wd, vec)


def weight_grad_kernel(count, core_ref, left_ref, *refs):
    rights, own_ref, other_ref = refs[:count], refs[count], refs[count + 1]
    left = left_ref[...]
    parts = [mm(left, right[...], TN) for right in rights]
    whole = parts[0] if count == 1 else jnp.concatenate(parts, axis=1)
    half = whole.shape[1] // 2
    low, high = whole[:, :half], whole[:, half:]

    @pl.when(core_ref[0] == 0)
    def _():
        own_ref[...] = low.astype(own_ref.dtype)
        other_ref[...] = high.astype(BF16)

    @pl.when(core_ref[0] != 0)
    def _():
        own_ref[...] = high.astype(own_ref.dtype)
        other_ref[...] = low.astype(BF16)


def weight_grad_call(core, left, rights, block, name):
    rows, height = left.shape
    width = sum(right.shape[1] for right in rights)
    return pl.pallas_call(
        functools.partial(weight_grad_kernel, len(rights)),
        name=name,
        grid_spec=pltpu.PrefetchScalarGridSpec(
            num_scalar_prefetch=1,
            grid=(height // block,),
            in_specs=[pl.BlockSpec((rows, block), lambda i, c: (0, i))]
            + [whole_spec(right.shape) for right in rights],
            out_specs=[pl.BlockSpec((block, width // 2), lambda i, c: (i, 0))] * 2,
        ),
        out_shape=[
            jax.ShapeDtypeStruct((height, width // 2), BF16),
            jax.ShapeDtypeStruct((height, width // 2), BF16),
        ],
        compiler_params=params(),
        cost_estimate=cost(2 * rows * height * width, rows * (height + width) * 2 + height * width * 2),
    )(core, left, *rights)


def last_kernel(x_ref, dm_ref, dq_ref, dk_ref, dv_ref, w_ref, vec_ref, grad_ref, acc_ref):
    @pl.when(pl.program_id(0) == 0)
    def _():
        acc_ref[...] = jnp.zeros_like(acc_ref)

    normed, scale = norm_parts(x_ref[...].astype(F32))
    dq, dk, dv = dq_ref[...], dk_ref[...], dv_ref[...]
    dh = (
        mm(dq, w_ref[:, :D], NT)
        + mm(dk, w_ref[:, D : 2 * D], NT)
        + mm(dv, w_ref[:, 2 * D :], NT)
    )
    add_row(acc_ref, 0, dh * normed)
    add_row(acc_ref, 1, dh)
    add_row(acc_ref, 2, dq.astype(F32))
    add_row(acc_ref, 3, dv.astype(F32))
    grad_ref[...] = dm_ref[...] + norm_back(dh * vec_ref[0:1, :], normed, scale)


def last_call(x, dm, dq, dk, dv, w, vec, block=256):
    rows = x.shape[0]
    row_spec = pl.BlockSpec((block, D), lambda i: (i, 0))
    return pl.pallas_call(
        last_kernel,
        name="last",
        grid=(rows // block,),
        in_specs=[row_spec] * 5 + [whole_spec(w.shape), whole_spec(vec.shape)],
        out_specs=[row_spec, pl.BlockSpec((16, D), lambda i: (0, 0))],
        out_shape=[jax.ShapeDtypeStruct((rows, D), F32), jax.ShapeDtypeStruct((16, D), F32)],
        compiler_params=params(),
        cost_estimate=cost(2 * rows * D * 3 * D, 16e6),
    )(x, dm, dq, dk, dv, w, vec)


class Grid:
    def __init__(self, chips):
        log = chips.bit_length() - 1
        side = 1 << (log // 3)
        if side * side * (chips // (side * side)) != chips:
            side = 1
        self.chips = chips
        self.nx = self.ny = side
        self.nz = chips // (side * side)
        self.core = lax.axis_index("seq")
        self.chip = lax.axis_index("dp")
        self.x = self.chip % self.nx
        self.y = self.chip // self.nx % self.ny
        self.z = self.chip // (self.nx * self.ny)
        self.first = jnp.where(self.core == 0, self.x, self.y)
        self.second = jnp.where(self.core == 0, self.y, self.x)

    def plane(self, first, second):
        return jnp.where(self.core == 0, second * self.nx + first, first * self.nx + second)

    def permute(self, value, axis, shift):
        pairs = []
        for chip in range(self.chips):
            for core in range(2):
                x, y, z = chip % self.nx, chip // self.nx % self.ny, chip // (self.nx * self.ny)
                to_core = core
                if axis == "z":
                    z = (z + shift) % self.nz
                elif axis == "core":
                    to_core = 1 - core
                elif (axis == "first") == (core == 0):
                    x = (x + shift) % self.nx
                else:
                    y = (y + shift) % self.ny
                pairs.append((chip * 2 + core, ((z * self.ny + y) * self.nx + x) * 2 + to_core))
        return lax.ppermute(value, ("dp", "seq"), pairs)

    def swap(self, value):
        return self.permute(value, "core", 0)

    def join(self, own, other, axis):
        return jnp.where(
            self.core == 0,
            jnp.concatenate([own, other], axis),
            jnp.concatenate([other, own], axis),
        )

    def gather(self, block):
        shape = block.shape
        column = jnp.zeros((self.nz,) + shape, block.dtype)
        column = lax.dynamic_update_slice(column, block[None], (self.z, 0, 0))
        for shift in range(1, self.nz):
            got = self.permute(block, "z", shift)
            column = lax.dynamic_update_slice(column, got[None], ((self.z - shift) % self.nz, 0, 0))
        n = self.nx
        line = [column] + [self.permute(column, "first", s) for s in range(1, n)]
        line_all = jnp.stack(line)
        out = jnp.zeros((self.nz, self.nx * self.ny) + shape, block.dtype)

        def put(out, piece, s1, s2):
            seat = self.plane((self.first - s1) % n, (self.second - s2) % n)
            return lax.dynamic_update_slice(out, piece[:, None], (0, seat, 0, 0))

        for s1 in range(n):
            out = put(out, line[s1], s1, 0)
        for s2 in range(1, n):
            got = self.permute(line_all, "second", s2)
            for s1 in range(n):
                out = put(out, got[s1], s1, s2)
        return out.reshape(self.chips * shape[0], shape[1])

    def gather_whole(self, shard):
        rows, cols = shard.shape
        half = lax.dynamic_slice_in_dim(shard, self.core * (cols // 2), cols // 2, 1)
        mine = self.gather(half.astype(BF16))
        return self.join(mine, self.swap(mine), 1)

    def total_small(self, value, with_cores):
        if with_cores:
            value = value + self.swap(value)
        for axis, count in (("first", self.nx), ("second", self.ny), ("z", self.nz)):
            value = value + sum(self.permute(value, axis, s) for s in range(1, count))
        return value

    def scatter(self, own, other):
        rows, cols = own.shape[0] // self.chips, own.shape[1]
        total = own.astype(F32) + self.swap(other).astype(F32)
        total = total.astype(BF16).reshape(self.nz, self.nx * self.ny, rows, cols)
        n = self.nx

        def seat(s1, s2):
            where = self.plane((self.first + s1) % n, (self.second + s2) % n)
            return lax.dynamic_slice(total, (0, where, 0, 0), (self.nz, 1, rows, cols))

        kept = [seat(0, t).astype(F32) for t in range(n)]
        for s in range(1, n):
            got = self.permute(jnp.stack([seat(s, t) for t in range(n)]), "first", s)
            kept = [kept[t] + got[t].astype(F32) for t in range(n)]
        mine = kept[0]
        for s in range(1, n):
            mine = mine + self.permute(kept[s].astype(BF16), "second", s).astype(F32)
        mine = mine.reshape(self.nz, rows, cols)
        result = lax.dynamic_index_in_dim(mine, self.z, 0, keepdims=False)
        low = mine.astype(BF16)
        for s in range(1, self.nz):
            send = lax.dynamic_index_in_dim(low, (self.z + s) % self.nz, 0, keepdims=False)
            result = result + self.permute(send, "z", s).astype(F32)
        return self.join(result, self.swap(result), 1)


def adamw(weight, gradient, first_moment, second_moment, step_rate, weight_decay):
    first_moment = BETA_ONE * first_moment + (1.0 - BETA_ONE) * gradient
    second_moment = BETA_TWO * second_moment + (1.0 - BETA_TWO) * gradient * gradient
    first_fix = 1.0 - BETA_ONE**STEP
    second_fix = 1.0 - BETA_TWO**STEP
    direction = first_moment / first_fix / (jnp.sqrt(second_moment / second_fix) + EPS_ADAM)
    return (weight - step_rate * (direction + weight_decay * weight), first_moment, second_moment)


def local(
    block_in, lengths, out_grad, w_qkv, w_out, w_up, w_down, vectors,
    first_qkv, first_out, first_up, first_down, first_vectors,
    second_qkv, second_out, second_up, second_down, second_vectors,
):
    grid = Grid(lax.axis_size("dp"))
    core = grid.core
    core_arr = core.reshape(1).astype(jnp.int32)
    half_len = block_in.shape[1]

    def own_slot(halves):
        mine = lax.dynamic_index_in_dim(halves, core, 0, keepdims=False)
        theirs = lax.dynamic_index_in_dim(halves, 1 - core, 0, keepdims=False)
        return grid.join(mine, grid.swap(theirs), 0)

    def both_slots(slot):
        mine = lax.dynamic_slice_in_dim(slot, core * half_len, half_len, 0)
        theirs = lax.dynamic_slice_in_dim(slot, (1 - core) * half_len, half_len, 0)
        return grid.join(mine[None], grid.swap(theirs)[None], 0)

    x = own_slot(block_in)
    vec_here = vectors.shape[1]
    vec_low = jnp.zeros((16, D), BF16)
    vec_low = lax.dynamic_update_slice(vec_low, vectors.astype(BF16), (0, grid.chip * vec_here))
    vec = grid.total_small(vec_low, False).astype(F32)
    mat_qkv = grid.gather_whole(w_qkv)
    mat_out = grid.gather_whole(w_out)
    mat_up = grid.gather_whole(w_up)
    mat_down = grid.gather_whole(w_down)
    og = own_slot(out_grad)

    h1, qkv = qkv_call(x, mat_qkv, vec)
    a, lse = attend_call(core_arr, lengths, qkv)
    out, dy, e, dz, h2, dmb, dm, da, acc_mid = middle_call(
        core_arr, lengths, x, a, og, mat_out, mat_up, mat_down, vec
    )
    block_out = both_slots(out)
    grad_down = grid.scatter(*weight_grad_call(core_arr, e, [dy], 512, "grad_down"))
    grad_up = grid.scatter(*weight_grad_call(core_arr, h2, [dz], 256, "grad_up"))
    grad_out = grid.scatter(*weight_grad_call(core_arr, a, [dmb], 256, "grad_out"))
    dq, dk, dv = attend_back_call(core_arr, lengths, qkv, a, da, lse)
    grad_qkv = grid.scatter(*weight_grad_call(core_arr, h1, [dq, dk, dv], 256, "grad_qkv"))
    in_slot, acc_last = last_call(x, dm, dq, dk, dv, mat_qkv, vec)
    in_grad = both_slots(in_slot)
    vec_total = grid.total_small(acc_mid + acc_last, True)
    grad_vec = lax.dynamic_slice(vec_total, (0, grid.chip * vec_here), (vectors.shape[0], vec_here))

    qkv_new = adamw(w_qkv, grad_qkv, first_qkv, second_qkv, D ** (-0.5), MATRIX_DECAY)
    out_new = adamw(w_out, grad_out, first_out, second_out, (D // 64) ** (-0.5), MATRIX_DECAY)
    up_new = adamw(w_up, grad_up, first_up, second_up, D ** (-0.5), MATRIX_DECAY)
    down_new = adamw(w_down, grad_down, first_down, second_down, FF ** (-0.5), MATRIX_DECAY)
    vec_new = adamw(vectors, grad_vec, first_vectors, second_vectors, VECTOR_RATE, 0.0)
    news = [qkv_new, out_new, up_new, down_new, vec_new]
    return (block_out, in_grad) + tuple(new[kind] for kind in range(3) for new in news)


def solution(mesh):
    weight = P("dp", None)
    vector = P(None, "dp")
    state = (weight, weight, weight, weight, vector)
    tokens = P("dp", "seq", None)
    return jax.shard_map(
        local,
        mesh=mesh,
        in_specs=(tokens, P("dp"), tokens) + state * 3,
        out_specs=(tokens, tokens) + state * 3,
        check_vma=False,
    )
```

```python
import functools

import jax
import jax.numpy as jnp
from jax import lax
from jax.experimental import pallas as pl
from jax.experimental.pallas import tpu as pltpu
from jax.sharding import PartitionSpec as P

D = 768
HEADS = 12
HEAD_DIM = 64
FF = 3072
STEP = 10

EPS_NORM = 1e-05
EPS_ADAM = 1e-08
BETA_ONE = 0.5
BETA_TWO = 0.5
MATRIX_DECAY = 0.1
VECTOR_RATE = 0.1
NEG_FILL = -1e30
GELU_ROOT = 0.7978845608028654
GELU_CUBE = 0.044715
VMEM_LIMIT = 60 * 1024 * 1024
QKV_HALF = 3 * D // 2

F32 = jnp.float32
BF16 = jnp.bfloat16

NN = (((1,), (0,)), ((), ()))
NT = (((1,), (1,)), ((), ()))
TN = (((0,), (0,)), ((), ()))


def mm(left, right, dims=NN):
    return lax.dot_general(left, right, dims, preferred_element_type=F32)


def cost(flops, nbytes, trans=0):
    return pl.CostEstimate(flops=int(flops), bytes_accessed=int(nbytes), transcendentals=int(trans))


def params():
    return pltpu.CompilerParams(vmem_limit_bytes=VMEM_LIMIT)


def whole_spec(shape):
    return pl.BlockSpec(shape, lambda *idx: (0,) * len(shape), pipeline_mode=pl.Buffered(1))


class Pieces:
    def __init__(self, arrays, rows, ordered=False):
        self.arrays = arrays
        self.rows = rows
        self.ordered = ordered
        self.halves = 2
        self.count = len(arrays) // self.halves
        self.lines, self.depth = arrays[0].shape[:2]

    def specs(self):
        return [pl.BlockSpec(memory_space=pl.ANY)] * len(self.arrays)

    def row(self, seat_ref, at):
        return 0 if self.ordered else pl.multiple_of(seat_ref[at] * self.rows, 16)

    def start(self, refs, core_ref, seat_ref, start_col, width, target, sem):
        core = core_ref[0]
        at = 0
        for half in range(self.halves):
            where = core if half == 0 else 1 - core
            for s2 in range(self.count):
                ref = refs[half * self.count + s2]
                for s1 in range(self.lines):
                    for sz in range(self.depth):
                        row = self.row(seat_ref, at)
                        at += 1
                        col = pl.multiple_of(where * width, 128)
                        pltpu.make_async_copy(
                            ref.at[s1, sz, :, pl.ds(start_col, width)],
                            target.at[pl.ds(row, self.rows), pl.ds(col, width)],
                            sem,
                        ).start()

    def start_once(self, refs, seat_ref, start_col, width, target, sem):
        at = 0
        for s2 in range(self.count):
            for s1 in range(self.lines):
                for sz in range(self.depth):
                    row = self.row(seat_ref, at)
                    at += 1
                    pltpu.make_async_copy(
                        refs[s2].at[s1, sz, :, pl.ds(start_col, width)],
                        target.at[pl.ds(row, self.rows), :],
                        sem,
                    ).start()


def wait_all(target, sem):
    pltpu.make_async_copy(target, target, sem).wait()


def norm_parts(rows):
    mean = jnp.mean(rows, axis=-1, keepdims=True)
    centred = rows - mean
    variance = jnp.mean(centred * centred, axis=-1, keepdims=True)
    scale = lax.rsqrt(variance + EPS_NORM)
    return centred * scale, scale


def norm_back(d_normed, normed, scale):
    first = jnp.mean(d_normed, axis=-1, keepdims=True)
    second = jnp.mean(d_normed * normed, axis=-1, keepdims=True)
    return scale * (d_normed - first - normed * second)


def qkv_kernel(group, core_ref, seat_ref, x_ref, *refs):
    refs, (h_ref, qkv_ref, vec_ref, w_ref, turned_ref, sems) = refs[:-6], refs[-6:]

    @pl.when(pl.program_id(0) == 0)
    def _():
        group.start(refs, core_ref, seat_ref, 0, QKV_HALF, w_ref, sems.at[0])
        group.start_once(refs, seat_ref, QKV_HALF, 128, turned_ref, sems.at[1])
        wait_all(turned_ref, sems.at[1])
        vec_ref[...] = turned_ref[...].astype(F32).T[:16]
        wait_all(w_ref, sems.at[0])

    normed, _ = norm_parts(x_ref[...].astype(F32))
    h = (normed * vec_ref[0:1, :] + vec_ref[1:2, :]).astype(BF16)
    h_ref[...] = h
    qkv_ref[:, :D] = (mm(h, w_ref[:, :D]) + vec_ref[2:3, :]).astype(BF16)
    qkv_ref[:, D : 2 * D] = mm(h, w_ref[:, D : 2 * D]).astype(BF16)
    qkv_ref[:, 2 * D :] = (mm(h, w_ref[:, 2 * D :]) + vec_ref[3:4, :]).astype(BF16)


def qkv_call(core, seats, x, group, block=256):
    rows = x.shape[0]
    return pl.pallas_call(
        functools.partial(qkv_kernel, group),
        name="qkv",
        grid_spec=pltpu.PrefetchScalarGridSpec(
            num_scalar_prefetch=2,
            grid=(rows // block,),
            in_specs=[pl.BlockSpec((block, D), lambda i, *s: (i, 0))] + group.specs(),
            out_specs=[
                pl.BlockSpec((block, D), lambda i, *s: (i, 0)),
                pl.BlockSpec((block, 3 * D), lambda i, *s: (i, 0)),
                pl.BlockSpec((16, D), lambda i, *s: (0, 0)),
            ],
            scratch_shapes=[
                pltpu.VMEM((D, 3 * D), BF16),
                pltpu.VMEM((D, 128), BF16),
                pltpu.SemaphoreType.DMA((2,)),
            ],
        ),
        out_shape=[
            jax.ShapeDtypeStruct((rows, D), BF16),
            jax.ShapeDtypeStruct((rows, 3 * D), BF16),
            jax.ShapeDtypeStruct((16, D), F32),
        ],
        compiler_params=params(),
        cost_estimate=cost(2 * rows * D * 3 * D, 10e6),
    )(core, seats, x, *group.arrays)


def head_parts(length, q_all, k_all, head):
    full_len = q_all.shape[0]
    lane = lax.broadcasted_iota(jnp.int32, (1, 128), 1)
    mine = (lane // HEAD_DIM) == head
    spare = lane == HEAD_DIM * (1 - head)
    pos = lax.broadcasted_iota(jnp.int32, (full_len, 128), 0)
    fill = jnp.where(pos < length, 0.0, NEG_FILL).astype(BF16)
    zero = jnp.zeros((), BF16)
    k_head = jnp.where(mine, k_all, jnp.where(spare, fill, zero))
    q_plain = jnp.where(mine, q_all, zero)
    q_head = jnp.where(spare, jnp.ones((), BF16), q_plain)
    return mine, k_head, q_plain, q_head


def causal_mask(scores, block):
    full = scores.shape[0]
    key_pos = lax.broadcasted_iota(jnp.int32, (block, block), 0)
    query_pos = lax.broadcasted_iota(jnp.int32, (block, block), 1)
    last = jnp.where(key_pos <= query_pos, scores[full - block :], NEG_FILL)
    if full == block:
        return last
    return jnp.concatenate([scores[: full - block], last], axis=0)


def attend_kernel(core_ref, len_ref, q_ref, k_ref, v_ref, *refs):
    a_ref, lse_ref, mixed_ref = refs[-3:]
    block = 256
    full_len = q_ref.shape[0]
    length = len_ref[core_ref[0]]
    q_all = q_ref[...] * jnp.asarray(HEAD_DIM ** (-0.5), BF16)
    k_all = k_ref[...]
    v_turned = v_ref[...].T
    for head in range(2):
        _, k_head, _, q_head = head_parts(length, q_all, k_all, head)
        v_head = v_turned[head * HEAD_DIM : (head + 1) * HEAD_DIM]
        for j in range(full_len // block):
            cols = slice(j * block, (j + 1) * block)
            span = (j + 1) * block
            scores = causal_mask(mm(k_head[:span], q_head[cols], NT), block)
            top = jnp.max(scores, axis=0, keepdims=True)
            exped = jnp.exp(scores - top)
            total = jnp.sum(exped, axis=0, keepdims=True)
            mixed = mm(v_head[:, :span], exped.astype(BF16)) / total
            mixed_ref[head * HEAD_DIM : (head + 1) * HEAD_DIM, cols] = mixed
            lse_ref[0, head : head + 1, cols] = top + jnp.log(total)
    a_ref[...] = mixed_ref[...].T.astype(BF16)


def attend_call(core, lengths, qkv, first, count, before):
    rows = qkv.shape[0]
    pairs = HEADS // 2
    before = list(before)
    return pl.pallas_call(
        attend_kernel,
        name="attend",
        grid_spec=pltpu.PrefetchScalarGridSpec(
            num_scalar_prefetch=2,
            grid=(count,),
            in_specs=[
                pl.BlockSpec((rows, 128), lambda i, c, n: (0, i + first)),
                pl.BlockSpec((rows, 128), lambda i, c, n: (0, i + first + pairs)),
                pl.BlockSpec((rows, 128), lambda i, c, n: (0, i + first + 2 * pairs)),
            ]
            + [pl.BlockSpec(memory_space=pl.ANY)] * len(before),
            out_specs=[
                pl.BlockSpec((rows, 128), lambda i, c, n: (0, i + first)),
                pl.BlockSpec((1, 8, rows), lambda i, c, n: (i + first, 0, 0)),
            ],
            scratch_shapes=[pltpu.VMEM((128, rows), F32)],
        ),
        out_shape=[
            jax.ShapeDtypeStruct((rows, D), BF16),
            jax.ShapeDtypeStruct((pairs, 8, rows), F32),
        ],
        input_output_aliases={5 + i: i for i in range(len(before))},
        compiler_params=params(),
        cost_estimate=cost(3e9 * count, 1.2e6 * count, 2 * rows * rows * 0.6 * count),
    )(core, lengths, qkv, qkv, qkv, *before)


def attend_back_kernel(core_ref, len_ref, q_ref, k_ref, v_ref, a_ref, da_ref, lse_ref, *refs):
    dq_ref, dk_ref, dv_ref, dqt_ref, dk_acc, dv_acc = refs[-6:]
    block = 256
    full_len = q_ref.shape[0]
    length = len_ref[core_ref[0]]
    scale = HEAD_DIM ** (-0.5)
    q_all = q_ref[...] * jnp.asarray(scale, BF16)
    k_all = k_ref[...]
    k_turned = k_all.T
    v_all = v_ref[...]
    da_all = da_ref[...]
    inner = (da_all.astype(F32) * a_ref[...].astype(F32)).T
    first = True
    for head in range(2):
        mine, k_head, q_plain, q_head = head_parts(length, q_all, k_all, head)
        da_head = jnp.where(mine, da_all, jnp.zeros((), BF16))
        lanes = slice(head * HEAD_DIM, (head + 1) * HEAD_DIM)
        centre = jnp.sum(inner[lanes], axis=0, keepdims=True)
        for j in reversed(range(full_len // block)):
            cols = slice(j * block, (j + 1) * block)
            span = (j + 1) * block
            scores = causal_mask(mm(k_head[:span], q_head[cols], NT), block)
            probs = jnp.exp(scores - lse_ref[0, head : head + 1, cols])
            d_probs = mm(v_all[:span], da_head[cols], NT)
            d_scores = (probs * (d_probs - centre[:, cols])).astype(BF16)
            dv_part = mm(probs.astype(BF16), da_head[cols])
            dk_part = mm(d_scores, q_plain[cols])
            if first:
                dv_acc[...] = dv_part
                dk_acc[...] = dk_part
                first = False
            else:
                dv_acc[:span] += dv_part
                dk_acc[:span] += dk_part
            dqt_ref[lanes, cols] = mm(k_turned[lanes, :span], d_scores) * scale
    dq_ref[...] = dqt_ref[...].T.astype(BF16)
    dk_ref[...] = dk_acc[...].astype(BF16)
    dv_ref[...] = dv_acc[...].astype(BF16)


def attend_back_call(core, lengths, qkv, a, da, lse, start, count, before):
    rows = qkv.shape[0]
    pairs = HEADS // 2
    before = list(before)
    pair_spec = pl.BlockSpec((rows, 128), lambda i, c, n: (0, i + start))
    return pl.pallas_call(
        attend_back_kernel,
        name="attend_back",
        grid_spec=pltpu.PrefetchScalarGridSpec(
            num_scalar_prefetch=2,
            grid=(count,),
            in_specs=[
                pair_spec,
                pl.BlockSpec((rows, 128), lambda i, c, n: (0, i + start + pairs)),
                pl.BlockSpec((rows, 128), lambda i, c, n: (0, i + start + 2 * pairs)),
                pair_spec,
                pair_spec,
                pl.BlockSpec((1, 8, rows), lambda i, c, n: (i + start, 0, 0)),
            ]
            + [pl.BlockSpec(memory_space=pl.ANY)] * len(before),
            out_specs=[pair_spec, pair_spec, pair_spec],
            scratch_shapes=[
                pltpu.VMEM((128, rows), F32),
                pltpu.VMEM((rows, 128), F32),
                pltpu.VMEM((rows, 128), F32),
            ],
        ),
        out_shape=[jax.ShapeDtypeStruct((rows, D), BF16)] * 3,
        input_output_aliases={8 + i: i for i in range(len(before))},
        compiler_params=params(),
        cost_estimate=cost(6e9 * count, 2e6 * count, 2 * rows * rows * 0.6 * count),
    )(core, lengths, qkv, qkv, qkv, a, da, lse, *before)


def valid_rows(core_ref, len_ref, block):
    pos = pl.program_id(0) * block + lax.broadcasted_iota(jnp.int32, (block, 1), 0)
    return pos < len_ref[core_ref[0]]


def add_row(acc_ref, row, value):
    acc_ref[row : row + 1, :] += jnp.sum(value, axis=0, keepdims=True)


def up_kernel(group, core_ref, len_ref, seat_ref, x_ref, a_ref, og_ref, vec_ref, *refs):
    refs, (mid_ref, h_ref, e_ref, slope_ref, dy_ref, wo_ref, wu_ref, sems) = refs[:-8], refs[-8:]
    block = x_ref.shape[0]

    @pl.when(pl.program_id(0) == 0)
    def _():
        group.start(refs, core_ref, seat_ref, 0, D // 2, wo_ref, sems.at[0])
        group.start(refs, core_ref, seat_ref, D // 2, FF // 2, wu_ref, sems.at[1])
        wait_all(wo_ref, sems.at[0])
        wait_all(wu_ref, sems.at[1])

    valid = valid_rows(core_ref, len_ref, block)
    dy_ref[...] = jnp.where(valid, og_ref[...].astype(F32), 0.0).astype(BF16)
    mid = x_ref[...].astype(F32) + mm(a_ref[...], wo_ref[...]) + vec_ref[4:5, :]
    mid_ref[...] = mid
    normed, _ = norm_parts(mid)
    h = (normed * vec_ref[5:6, :] + vec_ref[6:7, :]).astype(BF16)
    h_ref[...] = h
    for j in range(FF // D):
        cols = slice(j * D, (j + 1) * D)
        z = mm(h, wu_ref[:, cols]) + vec_ref[8 + j : 9 + j, :]
        squared = z * z
        turned = jnp.tanh(GELU_ROOT * z * (1.0 + GELU_CUBE * squared))
        half = 0.5 * (1.0 + turned)
        slope_ref[:, cols] = half + half * (1.0 - turned) * z * (
            GELU_ROOT + (3.0 * GELU_ROOT * GELU_CUBE) * squared
        )
        e_ref[:, cols] = (z * half).astype(BF16)


def up_call(core, lengths, seats, x, a, og, vec, group, block=256):
    rows = x.shape[0]
    row_spec = pl.BlockSpec((block, D), lambda i, *s: (i, 0))
    wide_spec = pl.BlockSpec((block, FF), lambda i, *s: (i, 0))
    low = jax.ShapeDtypeStruct((rows, D), BF16)
    return pl.pallas_call(
        functools.partial(up_kernel, group),
        name="up",
        grid_spec=pltpu.PrefetchScalarGridSpec(
            num_scalar_prefetch=3,
            grid=(rows // block,),
            in_specs=[row_spec, row_spec, row_spec, whole_spec(vec.shape)] + group.specs(),
            out_specs=[row_spec, row_spec, wide_spec, wide_spec, row_spec],
            scratch_shapes=[
                pltpu.VMEM((D, D), BF16),
                pltpu.VMEM((D, FF), BF16),
                pltpu.SemaphoreType.DMA((2,)),
            ],
        ),
        out_shape=[
            jax.ShapeDtypeStruct((rows, D), F32),
            low,
            jax.ShapeDtypeStruct((rows, FF), BF16),
            jax.ShapeDtypeStruct((rows, FF), F32),
            low,
        ],
        compiler_params=params(),
        cost_estimate=cost(6e9, 30e6, rows * FF),
    )(core, lengths, seats, x, a, og, vec, *group.arrays)


def down_kernel(up_group, down_group, core_ref, len_ref, seat_ref, mid_ref, e_ref, slope_ref, dy_ref, vec_ref, *refs):
    count = len(up_group.arrays)
    up_refs, down_refs = refs[:count], refs[count : count + len(down_group.arrays)]
    out_ref, dz_ref, dmb_ref, dm_ref, da_ref, acc_ref, wo_ref, wu_ref, wd_ref, sems = refs[-10:]
    block = mid_ref.shape[0]

    @pl.when(pl.program_id(0) == 0)
    def _():
        down_group.start(down_refs, core_ref, seat_ref, 0, D // 2, wd_ref, sems.at[2])
        up_group.start(up_refs, core_ref, seat_ref, D // 2, FF // 2, wu_ref, sems.at[1])
        up_group.start(up_refs, core_ref, seat_ref, 0, D // 2, wo_ref, sems.at[0])
        acc_ref[...] = jnp.zeros_like(acc_ref)
        wait_all(wd_ref, sems.at[2])
        wait_all(wu_ref, sems.at[1])
        wait_all(wo_ref, sems.at[0])

    valid = valid_rows(core_ref, len_ref, block)
    mid = mid_ref[...]
    normed, scale = norm_parts(mid)
    down = vec_ref[7:8, :] + mid + mm(e_ref[...], wd_ref[...])
    out_ref[...] = jnp.where(valid, down, 0.0).astype(BF16)
    dy_low = dy_ref[...]
    dy = dy_low.astype(F32)
    add_row(acc_ref, 7, dy)
    dh = jnp.zeros((block, D), F32)
    for j in range(FF // D):
        cols = slice(j * D, (j + 1) * D)
        dz = (mm(dy_low, wd_ref[cols, :], NT) * slope_ref[:, cols]).astype(BF16)
        dz_ref[:, cols] = dz
        add_row(acc_ref, 8 + j, dz.astype(F32))
        dh += mm(dz, wu_ref[:, cols], NT)
    add_row(acc_ref, 5, dh * normed)
    add_row(acc_ref, 6, dh)
    dm = dy + norm_back(dh * vec_ref[5:6, :], normed, scale)
    dm_ref[...] = dm
    dm_low = dm.astype(BF16)
    dmb_ref[...] = dm_low
    add_row(acc_ref, 4, dm_low.astype(F32))
    da_ref[...] = mm(dm_low, wo_ref[...], NT).astype(BF16)


def down_call(core, lengths, seats, mid, e, slope, dy, vec, up_group, down_group, block=256):
    rows = mid.shape[0]
    row_spec = pl.BlockSpec((block, D), lambda i, *s: (i, 0))
    wide_spec = pl.BlockSpec((block, FF), lambda i, *s: (i, 0))
    low = jax.ShapeDtypeStruct((rows, D), BF16)
    return pl.pallas_call(
        functools.partial(down_kernel, up_group, down_group),
        name="down",
        grid_spec=pltpu.PrefetchScalarGridSpec(
            num_scalar_prefetch=3,
            grid=(rows // block,),
            in_specs=[row_spec, wide_spec, wide_spec, row_spec, whole_spec(vec.shape)]
            + up_group.specs()
            + down_group.specs(),
            out_specs=[
                row_spec, wide_spec, row_spec, row_spec, row_spec,
                pl.BlockSpec((16, D), lambda i, *s: (0, 0)),
            ],
            scratch_shapes=[
                pltpu.VMEM((D, D), BF16),
                pltpu.VMEM((D, FF), BF16),
                pltpu.VMEM((FF, D), BF16),
                pltpu.SemaphoreType.DMA((3,)),
            ],
        ),
        out_shape=[
            low, jax.ShapeDtypeStruct((rows, FF), BF16), low, jax.ShapeDtypeStruct((rows, D), F32), low,
            jax.ShapeDtypeStruct((16, D), F32),
        ],
        compiler_params=params(),
        cost_estimate=cost(1.6e10, 40e6),
    )(core, lengths, seats, mid, e, slope, dy, vec, *up_group.arrays, *down_group.arrays)


def weight_grad_kernel(lefts, rights, core_ref, *refs):
    left_refs, right_refs = refs[:lefts], refs[lefts : lefts + sum(rights)]
    own_ref, other_ref = refs[-2:]
    lows, highs = [], []
    at = 0
    for left_ref, count in zip(left_refs, rights):
        left = left_ref[...]
        parts = [mm(left, right_refs[at + i][...], TN).astype(BF16) for i in range(count)]
        at += count
        whole = parts[0] if count == 1 else jnp.concatenate(parts, axis=1)
        half = whole.shape[1] // 2
        lows.append(whole[:, :half])
        highs.append(whole[:, half:])
    low = lows[0] if lefts == 1 else jnp.concatenate(lows, axis=1)
    high = highs[0] if lefts == 1 else jnp.concatenate(highs, axis=1)

    @pl.when(core_ref[0] == 0)
    def _():
        own_ref[...] = low
        other_ref[...] = high

    @pl.when(core_ref[0] != 0)
    def _():
        own_ref[...] = high
        other_ref[...] = low


def weight_grad_call(core, products, block, name):
    rows, height = products[0][0].shape
    lefts = [left for left, _ in products]
    rights = [right for _, group in products for right in group]
    width = sum(right.shape[1] for right in rights)
    return pl.pallas_call(
        functools.partial(weight_grad_kernel, len(lefts), [len(group) for _, group in products]),
        name=name,
        grid_spec=pltpu.PrefetchScalarGridSpec(
            num_scalar_prefetch=1,
            grid=(height // block,),
            in_specs=[pl.BlockSpec((rows, block), lambda i, c: (0, i))] * len(lefts)
            + [whole_spec(right.shape) for right in rights],
            out_specs=[pl.BlockSpec((block, width // 2), lambda i, c: (i, 0))] * 2,
        ),
        out_shape=[jax.ShapeDtypeStruct((height, width // 2), BF16)] * 2,
        compiler_params=params(),
        cost_estimate=cost(2 * rows * height * width, rows * (height + width) * 2 + height * width * 2),
    )(core, *lefts, *rights)


def last_kernel(group, core_ref, seat_ref, x_ref, dm_ref, dq_ref, dk_ref, dv_ref, vec_ref, mid_acc_ref, *refs):
    refs, (grad_ref, turned_ref, w_ref, acc_ref, sems) = refs[:-5], refs[-5:]

    @pl.when(pl.program_id(0) == 0)
    def _():
        group.start(refs, core_ref, seat_ref, 0, QKV_HALF, w_ref, sems.at[0])
        acc_ref[...] = jnp.zeros_like(acc_ref)
        acc_ref[:16] = mid_acc_ref[...]
        wait_all(w_ref, sems.at[0])

    normed, scale = norm_parts(x_ref[...].astype(F32))
    dq, dk, dv = dq_ref[...], dk_ref[...], dv_ref[...]
    dh = (
        mm(dq, w_ref[:, :D], NT)
        + mm(dk, w_ref[:, D : 2 * D], NT)
        + mm(dv, w_ref[:, 2 * D :], NT)
    )
    add_row(acc_ref, 0, dh * normed)
    add_row(acc_ref, 1, dh)
    add_row(acc_ref, 2, dq.astype(F32))
    add_row(acc_ref, 3, dv.astype(F32))
    grad_ref[...] = dm_ref[...] + norm_back(dh * vec_ref[0:1, :], normed, scale)

    @pl.when(pl.program_id(0) == pl.num_programs(0) - 1)
    def _():
        turned_ref[...] = acc_ref[...].T


def last_call(core, seats, x, dm, dq, dk, dv, vec, mid_acc, group, block=256):
    rows = x.shape[0]
    row_spec = pl.BlockSpec((block, D), lambda i, *s: (i, 0))
    return pl.pallas_call(
        functools.partial(last_kernel, group),
        name="last",
        grid_spec=pltpu.PrefetchScalarGridSpec(
            num_scalar_prefetch=2,
            grid=(rows // block,),
            in_specs=[row_spec] * 5 + [whole_spec(vec.shape), whole_spec(mid_acc.shape)] + group.specs(),
            out_specs=[row_spec, pl.BlockSpec((D, 128), lambda i, *s: (0, 0))],
            scratch_shapes=[
                pltpu.VMEM((D, 3 * D), BF16),
                pltpu.VMEM((128, D), F32),
                pltpu.SemaphoreType.DMA((1,)),
            ],
        ),
        out_shape=[jax.ShapeDtypeStruct((rows, D), F32), jax.ShapeDtypeStruct((D, 128), F32)],
        compiler_params=params(),
        cost_estimate=cost(2 * rows * D * 3 * D, 16e6),
    )(core, seats, x, dm, dq, dk, dv, vec, mid_acc, *group.arrays)


def after(value, *others):
    if not others:
        return value
    return lax.optimization_barrier((value,) + others)[0]


class Grid:
    def __init__(self, chips):
        log = chips.bit_length() - 1
        side = 1 << (log // 3)
        if side * side * (chips // (side * side)) != chips:
            side = 1
        self.chips = chips
        self.n = side
        self.nz = chips // (side * side)
        self.core = lax.axis_index("seq")
        self.chip = lax.axis_index("dp")
        self.x = self.chip % side
        self.y = self.chip // side % side
        self.z = self.chip // (side * side)

    def plane(self, first, second, core):
        return jnp.where(core == 0, second * self.n + first, first * self.n + second)

    def coords(self, core):
        return jnp.where(core == 0, self.x, self.y), jnp.where(core == 0, self.y, self.x)

    def permute(self, value, axis, shift=0):
        pairs = []
        for chip in range(self.chips):
            for core in range(2):
                x, y, z = chip % self.n, chip // self.n % self.n, chip // (self.n * self.n)
                to_core = core
                if axis == "z":
                    z = (z + shift) % self.nz
                elif axis == "core":
                    to_core = 1 - core
                elif (axis == "first") == (core == 0):
                    x = (x + shift) % self.n
                else:
                    y = (y + shift) % self.n
                pairs.append((chip * 2 + core, ((z * self.n + y) * self.n + x) * 2 + to_core))
        return lax.ppermute(value, ("dp", "seq"), pairs)

    def swap(self, value):
        return self.permute(value, "core")

    def join(self, own, other, axis):
        return jnp.where(
            self.core == 0,
            jnp.concatenate([own, other], axis),
            jnp.concatenate([other, own], axis),
        )

    def seats(self):
        found = []
        for half in range(2):
            core = self.core if half == 0 else 1 - self.core
            first, second = self.coords(core)
            for s2 in range(self.n):
                for s1 in range(self.n):
                    flat = self.plane((first - s1) % self.n, (second - s2) % self.n, core)
                    for sz in range(self.nz):
                        found.append(((self.z - sz) % self.nz) * self.n * self.n + flat)
        return jnp.stack(found).astype(jnp.int32)

    def gather_z(self, block, *until):
        return jnp.stack([block] + [after(self.permute(block, "z", s), *until) for s in range(1, self.nz)])

    def gather_first(self, column, *until):
        return jnp.stack([column] + [after(self.permute(column, "first", s), *until) for s in range(1, self.n)])

    def gather_second(self, line, *until):
        return [after(self.permute(line, "second", s), *until) for s in range(1, self.n)]

    def scatter_first(self, total, *until):
        rows, cols = total.shape[0] // self.chips, total.shape[1]
        total = total.reshape(self.nz, self.n * self.n, rows, cols)
        first, second = self.coords(self.core)
        n = self.n

        def seat(s1, s2):
            where = self.plane((first + s1) % n, (second + s2) % n, self.core)
            return lax.dynamic_slice(total, (0, where, 0, 0), (self.nz, 1, rows, cols))

        kept = [seat(0, t).astype(F32) for t in range(n)]
        for s in range(1, n):
            got = after(self.permute(jnp.stack([seat(s, t) for t in range(n)]), "first", s), *until)
            kept = [kept[t] + got[t].astype(F32) for t in range(n)]
        return kept[0], [part.astype(BF16) for part in kept[1:]]

    def scatter_second(self, kept, *until):
        mine, rest = kept
        got = [after(self.permute(rest[s - 1], "second", s), *until) for s in range(1, self.n)]
        for part in got:
            mine = mine + part.astype(F32)
        return mine.reshape((self.nz,) + mine.shape[2:]), got

    def scatter_z(self, mine, *until):
        result = lax.dynamic_index_in_dim(mine, self.z, 0, keepdims=False)
        low = mine.astype(BF16)
        for s in range(1, self.nz):
            send = lax.dynamic_index_in_dim(low, (self.z + s) % self.nz, 0, keepdims=False)
            result = result + after(self.permute(send, "z", s), *until).astype(F32)
        return result


def adamw(weight, gradient, first_moment, second_moment, step_rate, weight_decay):
    first_moment = BETA_ONE * first_moment + (1.0 - BETA_ONE) * gradient
    second_moment = BETA_TWO * second_moment + (1.0 - BETA_TWO) * gradient * gradient
    first_fix = 1.0 - BETA_ONE**STEP
    second_fix = 1.0 - BETA_TWO**STEP
    direction = first_moment / first_fix / (jnp.sqrt(second_moment / second_fix) + EPS_ADAM)
    return (weight - step_rate * (direction + weight_decay * weight), first_moment, second_moment)


def local(
    block_in, lengths, out_grad, w_qkv, w_out, w_up, w_down, vectors,
    first_qkv, first_out, first_up, first_down, first_vectors,
    second_qkv, second_out, second_up, second_down, second_vectors,
):
    grid = Grid(lax.axis_size("dp"))
    core = grid.core
    core_arr = core.reshape(1).astype(jnp.int32)
    half_len = block_in.shape[1]
    vec_count, vec_here = vectors.shape

    def own_slot(halves):
        mine = lax.dynamic_index_in_dim(halves, core, 0, keepdims=False)
        theirs = lax.dynamic_index_in_dim(halves, 1 - core, 0, keepdims=False)
        return grid.join(mine, grid.swap(theirs), 0)

    def both_slots(slot):
        mine = lax.dynamic_slice_in_dim(slot, core * half_len, half_len, 0)
        theirs = lax.dynamic_slice_in_dim(slot, (1 - core) * half_len, half_len, 0)
        return grid.join(mine[None], grid.swap(theirs)[None], 0)

    def half_of(shard):
        width = shard.shape[1] // 2
        return lax.dynamic_slice_in_dim(shard, core * width, width, 1).astype(BF16)

    seats = grid.seats()

    turned = jnp.pad(vectors.T.astype(BF16), ((0, 0), (0, 128 - vec_count)))
    q_block = jnp.concatenate([half_of(w_qkv), turned], axis=1)
    u_block = jnp.concatenate([half_of(w_out), half_of(w_up)], axis=1)
    d_block = half_of(w_down)
    q_col = grid.gather_z(q_block)
    x = own_slot(block_in)
    q_line = grid.gather_first(q_col, x)
    q_rest = grid.gather_second(q_line)
    q_line_swap = grid.swap(q_line)
    q_rest_swap = [grid.swap(part) for part in q_rest]
    q_group = finish_group(grid, seats, [q_line] + q_rest, [q_line_swap] + q_rest_swap)
    u_col = grid.gather_z(after(u_block, q_line_swap), *q_rest)
    og = own_slot(after(out_grad, *q_rest_swap))

    h1, qkv, vec = qkv_call(core_arr, seats, after(x, u_col, og), q_group)
    u_line = grid.gather_first(u_col, qkv)
    att = attend_call(core_arr, lengths, after(qkv, u_line), 0, 2, ())
    d_col = grid.gather_z(after(d_block, u_line), *att)
    u_line_swap = after(grid.swap(u_line), *att)
    att = attend_call(core_arr, lengths, after(qkv, u_line_swap, d_col), 2, 2, att)
    u_rest = grid.gather_second(u_line, *att)
    d_col = after(d_col, *u_rest)
    att_in = after(qkv, d_col)
    att = attend_call(core_arr, lengths, att_in, 4, 2, att)
    u_rest_swap = [after(grid.swap(part), *att) for part in u_rest]
    d_line = grid.gather_first(d_col, *att)
    u_group = finish_group(grid, seats, [u_line] + u_rest, [u_line_swap] + u_rest_swap)
    a, lse = att
    mid, h2, e, slope, dy = up_call(core_arr, lengths, seats, x, after(a, d_line), og, vec, u_group)
    d_line_swap = after(grid.swap(d_line), mid)
    d_rest = grid.gather_second(d_line, mid)
    down_own, down_other = weight_grad_call(core_arr, [(after(e, *d_rest), [dy])], 512, "grad_down")
    d_rest_swap = [after(grid.swap(part), down_own) for part in d_rest]
    d_group = finish_group(grid, seats, [d_line] + d_rest, [d_line_swap] + d_rest_swap)
    out, dz, dmb, dm, da, acc_mid = down_call(
        core_arr, lengths, seats, mid, e, slope, dy, vec, u_group, d_group
    )
    down_total = after(grid.swap(down_other), dz) + down_own
    up_own, up_other = weight_grad_call(
        core_arr, [(a, [dmb]), (h2, [after(dz, down_total)])], 256, "grad_up"
    )
    down_kept = grid.scatter_first(down_total, up_own)
    back = attend_back_call(core_arr, lengths, qkv, a, after(da, up_own, *down_kept[1]), lse, 0, 2, ())
    down_sum, down_here = grid.scatter_second(down_kept, *back)
    up_total = after(grid.swap(up_other), *back) + up_own
    back = attend_back_call(core_arr, lengths, qkv, a, after(da, up_total, *down_here), lse, 2, 2, back)
    down_mine = grid.scatter_z(down_sum, *back)
    block_out = both_slots(after(out, back[0]))
    back = attend_back_call(core_arr, lengths, qkv, a, after(da, down_mine), lse, 4, 2, back)
    up_kept = grid.scatter_first(up_total, *back)
    down_grad = grid.join(down_mine, grid.swap(down_mine), 1)
    dq, dk, dv = back
    q_own, q_other = weight_grad_call(core_arr, [(h1, [after(dq, *up_kept[1]), dk, dv])], 256, "grad_qkv")
    up_sum, up_here = grid.scatter_second(up_kept, q_own)
    in_slot, vec_part = last_call(
        core_arr, seats, x, dm, after(dq, q_own, *up_here), dk, dv, vec, acc_mid, q_group
    )
    q_got = after(grid.swap(q_other), in_slot)
    up_mine = grid.scatter_z(up_sum, in_slot)
    vec_total = vec_part + grid.swap(vec_part.astype(BF16)).astype(F32)
    q_total = jnp.concatenate([q_got + q_own, vec_total.astype(BF16)], axis=1)
    in_grad = both_slots(after(in_slot, q_total))
    up_grad = grid.join(up_mine, grid.swap(up_mine), 0)
    q_kept = grid.scatter_first(q_total, up_grad)
    q_sum, _ = grid.scatter_second(q_kept)
    q_mine = grid.scatter_z(q_sum)
    q_half = q_mine[:, :QKV_HALF]
    q_grad = grid.join(q_half, grid.swap(q_half), 1)
    vec_grad = q_mine[:, QKV_HALF : QKV_HALF + vec_count].T

    here = w_out.shape[0]
    out_grads = jnp.concatenate([up_grad[:here, : D // 2], up_grad[here:, : D // 2]], axis=1)
    up_grads = jnp.concatenate([up_grad[:here, D // 2 :], up_grad[here:, D // 2 :]], axis=1)
    qkv_new = adamw(w_qkv, q_grad, first_qkv, second_qkv, D ** (-0.5), MATRIX_DECAY)
    out_new = adamw(w_out, out_grads, first_out, second_out, (D // 64) ** (-0.5), MATRIX_DECAY)
    up_new = adamw(w_up, up_grads, first_up, second_up, D ** (-0.5), MATRIX_DECAY)
    down_new = adamw(w_down, down_grad, first_down, second_down, FF ** (-0.5), MATRIX_DECAY)
    vec_new = adamw(vectors, vec_grad, first_vectors, second_vectors, VECTOR_RATE, 0.0)
    news = [qkv_new, out_new, up_new, down_new, vec_new]
    return (block_out, in_grad) + tuple(new[kind] for kind in range(3) for new in news)


def finish_group(grid, seats, own, other):
    rows, cols = own[0].shape[-2:]
    if rows % 16 == 0:
        return Pieces(own + other, rows)
    found = []
    for half, parts in enumerate((own, other)):
        here = seats[half * grid.chips : (half + 1) * grid.chips]
        order = jnp.zeros((grid.chips,), jnp.int32).at[here].set(jnp.arange(grid.chips, dtype=jnp.int32))
        blocks = jnp.concatenate(parts).reshape(grid.chips, rows, cols)
        found.append(jnp.take(blocks, order, axis=0).reshape(1, 1, grid.chips * rows, cols))
    return Pieces(found, grid.chips * rows, True)


def solution(mesh):
    weight = P("dp", None)
    vector = P(None, "dp")
    state = (weight, weight, weight, weight, vector)
    tokens = P("dp", "seq", None)
    return jax.shard_map(
        local,
        mesh=mesh,
        in_specs=(tokens, P("dp"), tokens) + state * 3,
        out_specs=(tokens, tokens) + state * 3,
        check_vma=False,
    )
```

```python
import functools

import jax
import jax.numpy as jnp
from jax import lax
from jax.experimental import pallas as pl
from jax.experimental.pallas import tpu as pltpu
from jax.sharding import PartitionSpec as P

D = 768
HEADS = 12
HEAD_DIM = 64
FF = 3072
STEP = 10

EPS_NORM = 1e-05
EPS_ADAM = 1e-08
BETA_ONE = 0.5
BETA_TWO = 0.5
MATRIX_DECAY = 0.1
VECTOR_RATE = 0.1
NEG_FILL = -1e30
GELU_ROOT = 0.7978845608028654
GELU_CUBE = 0.044715
QKV_HALF = 3 * D // 2

F32 = jnp.float32
BF16 = jnp.bfloat16

NN = (((1,), (0,)), ((), ()))
NT = (((1,), (1,)), ((), ()))
TN = (((0,), (0,)), ((), ()))


def mm(left, right, dims=NN):
    return lax.dot_general(left, right, dims, preferred_element_type=F32)


def cost(flops, nbytes, trans=0):
    return pl.CostEstimate(flops=int(flops), bytes_accessed=int(nbytes), transcendentals=int(trans))


def params(mib):
    return pltpu.CompilerParams(vmem_limit_bytes=mib * 1024 * 1024)


def whole_spec(shape):
    return pl.BlockSpec(shape, lambda *idx: (0,) * len(shape), pipeline_mode=pl.Buffered(1))


class Pieces:
    def __init__(self, arrays, rows, ordered=False):
        self.arrays = arrays
        self.rows = rows
        self.ordered = ordered
        self.halves = 2
        self.count = len(arrays) // self.halves
        self.lines, self.depth = arrays[0].shape[:2]

    def specs(self):
        return [pl.BlockSpec(memory_space=pl.ANY)] * len(self.arrays)

    def row(self, seat_ref, at):
        return 0 if self.ordered else pl.multiple_of(seat_ref[at] * self.rows, 16)

    def start(self, refs, core_ref, seat_ref, start_col, width, target, sem):
        core = core_ref[0]
        at = 0
        for half in range(self.halves):
            where = core if half == 0 else 1 - core
            for s2 in range(self.count):
                ref = refs[half * self.count + s2]
                for s1 in range(self.lines):
                    for sz in range(self.depth):
                        row = self.row(seat_ref, at)
                        at += 1
                        col = pl.multiple_of(where * width, 128)
                        pltpu.make_async_copy(
                            ref.at[s1, sz, :, pl.ds(start_col, width)],
                            target.at[pl.ds(row, self.rows), pl.ds(col, width)],
                            sem,
                        ).start()

    def start_once(self, refs, seat_ref, start_col, width, target, sem):
        at = 0
        for s2 in range(self.count):
            for s1 in range(self.lines):
                for sz in range(self.depth):
                    row = self.row(seat_ref, at)
                    at += 1
                    pltpu.make_async_copy(
                        refs[s2].at[s1, sz, :, pl.ds(start_col, width)],
                        target.at[pl.ds(row, self.rows), :],
                        sem,
                    ).start()


def wait_all(target, sem):
    pltpu.make_async_copy(target, target, sem).wait()


def norm_parts(rows):
    mean = jnp.mean(rows, axis=-1, keepdims=True)
    centred = rows - mean
    variance = jnp.mean(centred * centred, axis=-1, keepdims=True)
    scale = lax.rsqrt(variance + EPS_NORM)
    return centred * scale, scale


def norm_back(d_normed, normed, scale):
    first = jnp.mean(d_normed, axis=-1, keepdims=True)
    second = jnp.mean(d_normed * normed, axis=-1, keepdims=True)
    return scale * (d_normed - first - normed * second)


def qkv_kernel(group, core_ref, seat_ref, x_ref, *refs):
    refs, (h_ref, qkv_ref, vec_ref, w_ref, turned_ref, sems) = refs[:-6], refs[-6:]

    @pl.when(pl.program_id(0) == 0)
    def _():
        group.start(refs, core_ref, seat_ref, 0, QKV_HALF, w_ref, sems.at[0])
        group.start_once(refs, seat_ref, QKV_HALF, 128, turned_ref, sems.at[1])
        wait_all(turned_ref, sems.at[1])
        vec_ref[...] = turned_ref[...].astype(F32).T[:16]
        wait_all(w_ref, sems.at[0])

    normed, _ = norm_parts(x_ref[...].astype(F32))
    h = (normed * vec_ref[0:1, :] + vec_ref[1:2, :]).astype(BF16)
    h_ref[...] = h
    qkv_ref[:, :D] = (mm(h, w_ref[:, :D]) + vec_ref[2:3, :]).astype(BF16)
    qkv_ref[:, D : 2 * D] = mm(h, w_ref[:, D : 2 * D]).astype(BF16)
    qkv_ref[:, 2 * D :] = (mm(h, w_ref[:, 2 * D :]) + vec_ref[3:4, :]).astype(BF16)


def qkv_call(core, seats, x, group, block=256):
    rows = x.shape[0]
    return pl.pallas_call(
        functools.partial(qkv_kernel, group),
        name="qkv",
        grid_spec=pltpu.PrefetchScalarGridSpec(
            num_scalar_prefetch=2,
            grid=(rows // block,),
            in_specs=[pl.BlockSpec((block, D), lambda i, *s: (i, 0))] + group.specs(),
            out_specs=[
                pl.BlockSpec((block, D), lambda i, *s: (i, 0)),
                pl.BlockSpec((block, 3 * D), lambda i, *s: (i, 0)),
                pl.BlockSpec((16, D), lambda i, *s: (0, 0)),
            ],
            scratch_shapes=[
                pltpu.VMEM((D, 3 * D), BF16),
                pltpu.VMEM((D, 128), BF16),
                pltpu.SemaphoreType.DMA((2,)),
            ],
        ),
        out_shape=[
            jax.ShapeDtypeStruct((rows, D), BF16),
            jax.ShapeDtypeStruct((rows, 3 * D), BF16),
            jax.ShapeDtypeStruct((16, D), F32),
        ],
        compiler_params=params(20),
        cost_estimate=cost(2 * rows * D * 3 * D, 10e6),
    )(core, seats, x, *group.arrays)


def head_parts(length, q_all, k_all, head):
    full_len = q_all.shape[0]
    lane = lax.broadcasted_iota(jnp.int32, (1, 128), 1)
    mine = (lane // HEAD_DIM) == head
    spare = lane == HEAD_DIM * (1 - head)
    pos = lax.broadcasted_iota(jnp.int32, (full_len, 128), 0)
    fill = jnp.where(pos < length, 0.0, NEG_FILL).astype(BF16)
    zero = jnp.zeros((), BF16)
    k_head = jnp.where(mine, k_all, jnp.where(spare, fill, zero))
    q_plain = jnp.where(mine, q_all, zero)
    q_head = jnp.where(spare, jnp.ones((), BF16), q_plain)
    return mine, k_head, q_plain, q_head


def causal_mask(scores, block):
    full = scores.shape[0]
    key_pos = lax.broadcasted_iota(jnp.int32, (block, block), 0)
    query_pos = lax.broadcasted_iota(jnp.int32, (block, block), 1)
    last = jnp.where(key_pos <= query_pos, scores[full - block :], NEG_FILL)
    if full == block:
        return last
    return jnp.concatenate([scores[: full - block], last], axis=0)


def attend_kernel(core_ref, len_ref, q_ref, k_ref, v_ref, *refs):
    a_ref, lse_ref, mixed_ref = refs[-3:]
    block = 256
    full_len = q_ref.shape[0]
    length = len_ref[core_ref[0]]
    q_all = q_ref[...] * jnp.asarray(HEAD_DIM ** (-0.5), BF16)
    k_all = k_ref[...]
    v_turned = v_ref[...].T
    for head in range(2):
        _, k_head, _, q_head = head_parts(length, q_all, k_all, head)
        v_head = v_turned[head * HEAD_DIM : (head + 1) * HEAD_DIM]
        for j in range(full_len // block):
            cols = slice(j * block, (j + 1) * block)
            span = (j + 1) * block
            scores = causal_mask(mm(k_head[:span], q_head[cols], NT), block)
            top = jnp.max(scores, axis=0, keepdims=True)
            exped = jnp.exp(scores - top)
            total = jnp.sum(exped, axis=0, keepdims=True)
            mixed = mm(v_head[:, :span], exped.astype(BF16)) / total
            mixed_ref[head * HEAD_DIM : (head + 1) * HEAD_DIM, cols] = mixed
            lse_ref[0, head : head + 1, cols] = top + jnp.log(total)
    a_ref[...] = mixed_ref[...].T.astype(BF16)


def attend_call(core, lengths, qkv, first, count, before):
    rows = qkv.shape[0]
    pairs = HEADS // 2
    before = list(before)
    return pl.pallas_call(
        attend_kernel,
        name="attend",
        grid_spec=pltpu.PrefetchScalarGridSpec(
            num_scalar_prefetch=2,
            grid=(count,),
            in_specs=[
                pl.BlockSpec((rows, 128), lambda i, c, n: (0, i + first)),
                pl.BlockSpec((rows, 128), lambda i, c, n: (0, i + first + pairs)),
                pl.BlockSpec((rows, 128), lambda i, c, n: (0, i + first + 2 * pairs)),
            ]
            + [pl.BlockSpec(memory_space=pl.ANY)] * len(before),
            out_specs=[
                pl.BlockSpec((rows, 128), lambda i, c, n: (0, i + first)),
                pl.BlockSpec((1, 8, rows), lambda i, c, n: (i + first, 0, 0)),
            ],
            scratch_shapes=[pltpu.VMEM((128, rows), F32)],
        ),
        out_shape=[
            jax.ShapeDtypeStruct((rows, D), BF16),
            jax.ShapeDtypeStruct((pairs, 8, rows), F32),
        ],
        input_output_aliases={5 + i: i for i in range(len(before))},
        compiler_params=params(20),
        cost_estimate=cost(3e9 * count, 1.2e6 * count, 2 * rows * rows * 0.6 * count),
    )(core, lengths, qkv, qkv, qkv, *before)


def attend_back_kernel(core_ref, len_ref, q_ref, k_ref, v_ref, a_ref, da_ref, lse_ref, *refs):
    dq_ref, dk_ref, dv_ref, dqt_ref, dk_acc, dv_acc = refs[-6:]
    block = 256
    full_len = q_ref.shape[0]
    length = len_ref[core_ref[0]]
    scale = HEAD_DIM ** (-0.5)
    q_all = q_ref[...] * jnp.asarray(scale, BF16)
    k_all = k_ref[...]
    k_turned = k_all.T
    v_all = v_ref[...]
    da_all = da_ref[...]
    inner = (da_all.astype(F32) * a_ref[...].astype(F32)).T
    first = True
    for head in range(2):
        mine, k_head, q_plain, q_head = head_parts(length, q_all, k_all, head)
        da_head = jnp.where(mine, da_all, jnp.zeros((), BF16))
        lanes = slice(head * HEAD_DIM, (head + 1) * HEAD_DIM)
        centre = jnp.sum(inner[lanes], axis=0, keepdims=True)
        for j in reversed(range(full_len // block)):
            cols = slice(j * block, (j + 1) * block)
            span = (j + 1) * block
            scores = causal_mask(mm(k_head[:span], q_head[cols], NT), block)
            probs = jnp.exp(scores - lse_ref[0, head : head + 1, cols])
            d_probs = mm(v_all[:span], da_head[cols], NT)
            d_scores = (probs * (d_probs - centre[:, cols])).astype(BF16)
            dv_part = mm(probs.astype(BF16), da_head[cols])
            dk_part = mm(d_scores, q_plain[cols])
            if first:
                dv_acc[...] = dv_part
                dk_acc[...] = dk_part
                first = False
            else:
                dv_acc[:span] += dv_part
                dk_acc[:span] += dk_part
            dqt_ref[lanes, cols] = mm(k_turned[lanes, :span], d_scores) * scale
    dq_ref[...] = dqt_ref[...].T.astype(BF16)
    dk_ref[...] = dk_acc[...].astype(BF16)
    dv_ref[...] = dv_acc[...].astype(BF16)


def attend_back_call(core, lengths, qkv, a, da, lse, start, count, before):
    rows = qkv.shape[0]
    pairs = HEADS // 2
    before = list(before)
    pair_spec = pl.BlockSpec((rows, 128), lambda i, c, n: (0, i + start))
    return pl.pallas_call(
        attend_back_kernel,
        name="attend_back",
        grid_spec=pltpu.PrefetchScalarGridSpec(
            num_scalar_prefetch=2,
            grid=(count,),
            in_specs=[
                pair_spec,
                pl.BlockSpec((rows, 128), lambda i, c, n: (0, i + start + pairs)),
                pl.BlockSpec((rows, 128), lambda i, c, n: (0, i + start + 2 * pairs)),
                pair_spec,
                pair_spec,
                pl.BlockSpec((1, 8, rows), lambda i, c, n: (i + start, 0, 0)),
            ]
            + [pl.BlockSpec(memory_space=pl.ANY)] * len(before),
            out_specs=[pair_spec, pair_spec, pair_spec],
            scratch_shapes=[
                pltpu.VMEM((128, rows), F32),
                pltpu.VMEM((rows, 128), F32),
                pltpu.VMEM((rows, 128), F32),
            ],
        ),
        out_shape=[jax.ShapeDtypeStruct((rows, D), BF16)] * 3,
        input_output_aliases={8 + i: i for i in range(len(before))},
        compiler_params=params(24),
        cost_estimate=cost(6e9 * count, 2e6 * count, 2 * rows * rows * 0.6 * count),
    )(core, lengths, qkv, qkv, qkv, a, da, lse, *before)


def valid_rows(core_ref, len_ref, block):
    pos = pl.program_id(0) * block + lax.broadcasted_iota(jnp.int32, (block, 1), 0)
    return pos < len_ref[core_ref[0]]


def add_row(acc_ref, row, value):
    acc_ref[row : row + 1, :] += jnp.sum(value, axis=0, keepdims=True)


def up_kernel(group, core_ref, len_ref, seat_ref, x_ref, a_ref, og_ref, vec_ref, *refs):
    refs, (mid_ref, h_ref, e_ref, slope_ref, dy_ref, wo_ref, wu_ref, sems) = refs[:-8], refs[-8:]
    block = x_ref.shape[0]

    @pl.when(pl.program_id(0) == 0)
    def _():
        group.start(refs, core_ref, seat_ref, 0, D // 2, wo_ref, sems.at[0])
        group.start(refs, core_ref, seat_ref, D // 2, FF // 2, wu_ref, sems.at[1])
        wait_all(wo_ref, sems.at[0])
        wait_all(wu_ref, sems.at[1])

    valid = valid_rows(core_ref, len_ref, block)
    dy_ref[...] = jnp.where(valid, og_ref[...].astype(F32), 0.0).astype(BF16)
    mid = x_ref[...].astype(F32) + mm(a_ref[...], wo_ref[...]) + vec_ref[4:5, :]
    mid_ref[...] = mid
    normed, _ = norm_parts(mid)
    h = (normed * vec_ref[5:6, :] + vec_ref[6:7, :]).astype(BF16)
    h_ref[...] = h
    for j in range(FF // D):
        cols = slice(j * D, (j + 1) * D)
        z = mm(h, wu_ref[:, cols]) + vec_ref[8 + j : 9 + j, :]
        squared = z * z
        turned = jnp.tanh(z * (GELU_ROOT + (GELU_ROOT * GELU_CUBE) * squared))
        half = 0.5 * turned + 0.5
        act = z * half
        e_ref[:, cols] = act.astype(BF16)
        slope = half + act * (1.0 - turned) * (GELU_ROOT + (3.0 * GELU_ROOT * GELU_CUBE) * squared)
        slope_ref[:, cols] = slope.astype(BF16)


def up_call(core, lengths, seats, x, a, og, vec, group, block=256):
    rows = x.shape[0]
    row_spec = pl.BlockSpec((block, D), lambda i, *s: (i, 0))
    wide_spec = pl.BlockSpec((block, FF), lambda i, *s: (i, 0))
    low = jax.ShapeDtypeStruct((rows, D), BF16)
    return pl.pallas_call(
        functools.partial(up_kernel, group),
        name="up",
        grid_spec=pltpu.PrefetchScalarGridSpec(
            num_scalar_prefetch=3,
            grid=(rows // block,),
            in_specs=[row_spec, row_spec, row_spec, whole_spec(vec.shape)] + group.specs(),
            out_specs=[row_spec, row_spec, wide_spec, wide_spec, row_spec],
            scratch_shapes=[
                pltpu.VMEM((D, D), BF16),
                pltpu.VMEM((D, FF), BF16),
                pltpu.SemaphoreType.DMA((2,)),
            ],
        ),
        out_shape=[
            jax.ShapeDtypeStruct((rows, D), F32),
            low,
            jax.ShapeDtypeStruct((rows, FF), BF16),
            jax.ShapeDtypeStruct((rows, FF), BF16),
            low,
        ],
        compiler_params=params(32),
        cost_estimate=cost(6e9, 30e6, rows * FF),
    )(core, lengths, seats, x, a, og, vec, *group.arrays)


def down_kernel(up_group, down_group, core_ref, seat_ref, mid_ref, slope_ref, dy_ref, vec_ref, *refs):
    count = len(up_group.arrays)
    up_refs, down_refs = refs[:count], refs[count : count + len(down_group.arrays)]
    dz_ref, dmb_ref, dm_ref, da_ref, acc_ref, wo_ref, wu_ref, wd_ref, sems = refs[-9:]
    block = mid_ref.shape[0]

    @pl.when(pl.program_id(0) == 0)
    def _():
        down_group.start(down_refs, core_ref, seat_ref, 0, D // 2, wd_ref, sems.at[2])
        up_group.start(up_refs, core_ref, seat_ref, D // 2, FF // 2, wu_ref, sems.at[1])
        up_group.start(up_refs, core_ref, seat_ref, 0, D // 2, wo_ref, sems.at[0])
        acc_ref[...] = jnp.zeros_like(acc_ref)
        wait_all(wd_ref, sems.at[2])
        wait_all(wu_ref, sems.at[1])
        wait_all(wo_ref, sems.at[0])

    mid = mid_ref[...]
    normed, scale = norm_parts(mid)
    dy_low = dy_ref[...]
    dy = dy_low.astype(F32)
    add_row(acc_ref, 7, dy)
    dh = jnp.zeros((block, D), F32)
    for j in range(FF // D):
        cols = slice(j * D, (j + 1) * D)
        dz = (mm(dy_low, wd_ref[cols, :], NT) * slope_ref[:, cols].astype(F32)).astype(BF16)
        dz_ref[:, cols] = dz
        add_row(acc_ref, 8 + j, dz.astype(F32))
        dh += mm(dz, wu_ref[:, cols], NT)
    add_row(acc_ref, 5, dh * normed)
    add_row(acc_ref, 6, dh)
    dm = dy + norm_back(dh * vec_ref[5:6, :], normed, scale)
    dm_ref[...] = dm
    dm_low = dm.astype(BF16)
    dmb_ref[...] = dm_low
    add_row(acc_ref, 4, dm_low.astype(F32))
    da_ref[...] = mm(dm_low, wo_ref[...], NT).astype(BF16)


def down_call(core, seats, mid, slope, dy, vec, up_group, down_group, block=256):
    rows = mid.shape[0]
    row_spec = pl.BlockSpec((block, D), lambda i, *s: (i, 0))
    wide_spec = pl.BlockSpec((block, FF), lambda i, *s: (i, 0))
    low = jax.ShapeDtypeStruct((rows, D), BF16)
    return pl.pallas_call(
        functools.partial(down_kernel, up_group, down_group),
        name="down",
        grid_spec=pltpu.PrefetchScalarGridSpec(
            num_scalar_prefetch=2,
            grid=(rows // block,),
            in_specs=[row_spec, wide_spec, row_spec, whole_spec(vec.shape)]
            + up_group.specs()
            + down_group.specs(),
            out_specs=[
                wide_spec, row_spec, row_spec, row_spec,
                pl.BlockSpec((16, D), lambda i, *s: (0, 0)),
            ],
            scratch_shapes=[
                pltpu.VMEM((D, D), BF16),
                pltpu.VMEM((D, FF), BF16),
                pltpu.VMEM((FF, D), BF16),
                pltpu.SemaphoreType.DMA((3,)),
            ],
        ),
        out_shape=[
            jax.ShapeDtypeStruct((rows, FF), BF16), low, jax.ShapeDtypeStruct((rows, D), F32), low,
            jax.ShapeDtypeStruct((16, D), F32),
        ],
        compiler_params=params(44),
        cost_estimate=cost(1.1e10, 30e6),
    )(core, seats, mid, slope, dy, vec, *up_group.arrays, *down_group.arrays)


def out_kernel(group, first, core_ref, len_ref, seat_ref, mid_ref, e_ref, vec_ref, *refs):
    refs, (out_ref, wd_ref, sems) = refs[:-3], refs[-3:]
    block = mid_ref.shape[0]

    @pl.when(pl.program_id(0) == 0)
    def _():
        group.start(refs, core_ref, seat_ref, 0, D // 2, wd_ref, sems.at[0])
        wait_all(wd_ref, sems.at[0])

    half = core_ref[0] if first is None else 1 - core_ref[0]
    pos = (half * pl.num_programs(0) + pl.program_id(0)) * block
    valid = pos + lax.broadcasted_iota(jnp.int32, (block, 1), 0) < len_ref[core_ref[0]]
    down = vec_ref[7:8, :] + mid_ref[...] + mm(e_ref[...], wd_ref[...])
    down = jnp.where(valid, down, 0.0).astype(BF16)
    if first is None:
        out_ref[0] = down
    else:
        out_ref[...] = down


def half_specs(first, steps, block):
    def half(core):
        return core[0] if first is None else 1 - core[0]

    def rows(width):
        return pl.BlockSpec((block, width), lambda i, c, *s: (half(c) * steps + i, 0))

    if first is None:
        out = pl.BlockSpec((1, block, D), lambda i, c, *s: (c[0], i, 0))
    else:
        out = pl.BlockSpec((block, D), lambda i, c, *s: (i, 0))
    return rows, out


def out_call(core, lengths, seats, mid, e, vec, group, first, block=256):
    half_len = mid.shape[0] // 2
    steps = half_len // block
    rows, out_spec = half_specs(first, steps, block)
    shape = (2, half_len, D) if first is None else (half_len, D)
    return pl.pallas_call(
        functools.partial(out_kernel, group, first),
        name="out",
        grid_spec=pltpu.PrefetchScalarGridSpec(
            num_scalar_prefetch=3,
            grid=(steps,),
            in_specs=[rows(D), rows(FF), whole_spec(vec.shape)] + group.specs(),
            out_specs=out_spec,
            scratch_shapes=[pltpu.VMEM((FF, D), BF16), pltpu.SemaphoreType.DMA((1,))],
        ),
        out_shape=jax.ShapeDtypeStruct(shape, BF16),
        compiler_params=params(24),
        cost_estimate=cost(2.4e9, 9e6),
    )(core, lengths, seats, mid, e, vec, *group.arrays)


def pick(values, half, mode):
    if mode == "split":
        width = values.shape[1] // 2
        return [values[:, half * width : (half + 1) * width]]
    return [values[:, at : at + 128] for at in range(half * 128, values.shape[1], 256)]


def weight_grad_kernel(lefts, rights, mode, core_ref, *refs):
    left_refs, right_refs = refs[:lefts], refs[lefts : lefts + sum(rights)]
    own_ref, other_ref = refs[-2:]
    halves = ([], [])
    at = 0
    for left_ref, count in zip(left_refs, rights):
        left = left_ref[...]
        for right_ref in right_refs[at : at + count]:
            whole = mm(left, right_ref[...], TN).astype(BF16)
            for half in range(2):
                halves[half].extend(pick(whole, half, mode))
        at += count
    low, high = [part[0] if len(part) == 1 else jnp.concatenate(part, axis=1) for part in halves]

    @pl.when(core_ref[0] == 0)
    def _():
        own_ref[...] = low
        other_ref[...] = high

    @pl.when(core_ref[0] != 0)
    def _():
        own_ref[...] = high
        other_ref[...] = low


def weight_grad_call(core, products, block, name, mode="split", cols=None):
    rows, height = products[0][0].shape
    lefts = [left for left, _ in products]
    rights = [right for _, group in products for right in group]
    widths = [right.shape[1] if cols is None else cols[0] for right in rights]
    width = sum(widths)
    seat = 0 if cols is None else cols[1]
    return pl.pallas_call(
        functools.partial(weight_grad_kernel, len(lefts), [len(group) for _, group in products], mode),
        name=name,
        grid_spec=pltpu.PrefetchScalarGridSpec(
            num_scalar_prefetch=1,
            grid=(height // block,),
            in_specs=[pl.BlockSpec((rows, block), lambda i, c: (0, i))] * len(lefts)
            + [
                pl.BlockSpec((rows, w), lambda i, c: (0, seat), pipeline_mode=pl.Buffered(1)) for w in widths
            ],
            out_specs=[pl.BlockSpec((block, width // 2), lambda i, c: (i, 0))] * 2,
        ),
        out_shape=[jax.ShapeDtypeStruct((height, width // 2), BF16)] * 2,
        compiler_params=params(40),
        cost_estimate=cost(2 * rows * height * width, rows * (height + width) * 2 + height * width * 2),
    )(core, *lefts, *rights)


def last_kernel(group, first, core_ref, seat_ref, x_ref, dm_ref, dq_ref, dk_ref, dv_ref, vec_ref, before_ref, *refs):
    refs, (grad_ref, acc_ref, w_ref, sems) = refs[:-4], refs[-4:]

    @pl.when(pl.program_id(0) == 0)
    def _():
        group.start(refs, core_ref, seat_ref, 0, QKV_HALF, w_ref, sems.at[0])
        acc_ref[...] = before_ref[...]
        wait_all(w_ref, sems.at[0])

    normed, scale = norm_parts(x_ref[...].astype(F32))
    dq, dk, dv = dq_ref[...], dk_ref[...], dv_ref[...]
    dh = (
        mm(dq, w_ref[:, :D], NT)
        + mm(dk, w_ref[:, D : 2 * D], NT)
        + mm(dv, w_ref[:, 2 * D :], NT)
    )
    add_row(acc_ref, 0, dh * normed)
    add_row(acc_ref, 1, dh)
    add_row(acc_ref, 2, dq.astype(F32))
    add_row(acc_ref, 3, dv.astype(F32))
    grad = dm_ref[...] + norm_back(dh * vec_ref[0:1, :], normed, scale)
    if first is None:
        grad_ref[0] = grad
    else:
        grad_ref[...] = grad


def last_call(core, seats, x, dm, dq, dk, dv, vec, before, group, first, block=256):
    half_len = x.shape[0] // 2
    steps = half_len // block
    rows, out_spec = half_specs(first, steps, block)
    shape = (2, half_len, D) if first is None else (half_len, D)
    return pl.pallas_call(
        functools.partial(last_kernel, group, first),
        name="last",
        grid_spec=pltpu.PrefetchScalarGridSpec(
            num_scalar_prefetch=2,
            grid=(steps,),
            in_specs=[rows(D)] * 5 + [whole_spec(vec.shape), whole_spec(before.shape)] + group.specs(),
            out_specs=[out_spec, pl.BlockSpec((16, D), lambda i, *s: (0, 0))],
            scratch_shapes=[pltpu.VMEM((D, 3 * D), BF16), pltpu.SemaphoreType.DMA((1,))],
        ),
        out_shape=[jax.ShapeDtypeStruct(shape, F32), jax.ShapeDtypeStruct((16, D), F32)],
        compiler_params=params(24),
        cost_estimate=cost(half_len * 6 * D * D, 10e6),
    )(core, seats, x, dm, dq, dk, dv, vec, before, *group.arrays)


def adam_kernel(plans, sources, core_ref, *refs):
    halves = [refs[2 * i : 2 * i + 2] for i in range(sources)]
    count = len(plans)
    states = refs[2 * sources : 2 * sources + 3 * count]
    outs = refs[2 * sources + 3 * count : 2 * sources + 6 * count]
    grads = refs[2 * sources + 6 * count :]
    for core in range(2):

        @pl.when(core_ref[0] == core)
        def _():
            for (_, _, moves), grad_ref in zip(plans, grads):
                for source, start, width, place0, place1 in moves:
                    for half, place in ((0, place0), (1, place1)):
                        ref = halves[source][0 if half == core else 1]
                        grad_ref[:, place : place + width] = ref[:, start : start + width]

    for i, (rate, decay, _) in enumerate(plans):
        weight, first, second = states[3 * i : 3 * i + 3]
        new = adamw(weight[...], grads[i][...], first[...], second[...], rate, decay)
        for out, value in zip(outs[3 * i : 3 * i + 3], new):
            out[...] = value


def adam_call(core, halves, states, plans):
    flat = [part for pair in halves for part in pair]
    held = [part for state in states for part in state]
    spec = pl.BlockSpec(memory_space=pltpu.VMEM)
    news = pl.pallas_call(
        functools.partial(adam_kernel, plans, len(halves)),
        name="adam",
        in_specs=[pl.BlockSpec(memory_space=pltpu.SMEM)] + [spec] * (len(flat) + len(held)),
        out_specs=[spec] * len(held),
        out_shape=[jax.ShapeDtypeStruct(part.shape, F32) for part in held],
        scratch_shapes=[pltpu.VMEM(state[0].shape, F32) for state in states],
        compiler_params=params(24),
        cost_estimate=cost(1e6, 24 * sum(state[0].size for state in states)),
    )(core, *flat, *held)
    return [news[3 * i : 3 * i + 3] for i in range(len(states))]


def after(value, *others):
    if not others:
        return value
    return lax.optimization_barrier((value,) + others)[0]


class Grid:
    def __init__(self, chips):
        log = chips.bit_length() - 1
        side = 1 << (log // 3)
        if side * side * (chips // (side * side)) != chips:
            side = 1
        self.chips = chips
        self.n = side
        self.nz = chips // (side * side)
        self.core = lax.axis_index("seq")
        self.chip = lax.axis_index("dp")
        self.x = self.chip % side
        self.y = self.chip // side % side
        self.z = self.chip // (side * side)

    def plane(self, first, second, core):
        return jnp.where(core == 0, second * self.n + first, first * self.n + second)

    def coords(self, core):
        return jnp.where(core == 0, self.x, self.y), jnp.where(core == 0, self.y, self.x)

    def permute(self, value, axis, shift=0):
        pairs = []
        for chip in range(self.chips):
            for core in range(2):
                x, y, z = chip % self.n, chip // self.n % self.n, chip // (self.n * self.n)
                to_core = core
                if axis == "z":
                    z = (z + shift) % self.nz
                elif axis == "core":
                    to_core = 1 - core
                elif (axis == "first") == (core == 0):
                    x = (x + shift) % self.n
                else:
                    y = (y + shift) % self.n
                pairs.append((chip * 2 + core, ((z * self.n + y) * self.n + x) * 2 + to_core))
        return lax.ppermute(value, ("dp", "seq"), pairs)

    def swap(self, value):
        return self.permute(value, "core")

    def join(self, own, other, axis):
        return jnp.where(
            self.core == 0,
            jnp.concatenate([own, other], axis),
            jnp.concatenate([other, own], axis),
        )

    def seats(self):
        found = []
        for half in range(2):
            core = self.core if half == 0 else 1 - self.core
            first, second = self.coords(core)
            for s2 in range(self.n):
                for s1 in range(self.n):
                    flat = self.plane((first - s1) % self.n, (second - s2) % self.n, core)
                    for sz in range(self.nz):
                        found.append(((self.z - sz) % self.nz) * self.n * self.n + flat)
        return jnp.stack(found).astype(jnp.int32)

    def total_small(self, value, *untils):
        for (axis, count), until in zip((("core", 2), ("first", self.n), ("second", self.n), ("z", self.nz)), untils):
            value = value + sum(after(self.permute(value, axis, s), *until) for s in range(1, count))
        return value

    def gather_z(self, block, *until):
        return jnp.stack([block] + [after(self.permute(block, "z", s), *until) for s in range(1, self.nz)])

    def gather_first(self, column, *until):
        return jnp.stack([column] + [after(self.permute(column, "first", s), *until) for s in range(1, self.n)])

    def gather_second(self, line, *until):
        return [after(self.permute(line, "second", s), *until) for s in range(1, self.n)]

    def scatter_first(self, total, *until):
        rows, cols = total.shape[0] // self.chips, total.shape[1]
        total = total.reshape(self.nz, self.n * self.n, rows, cols)
        first, second = self.coords(self.core)
        n = self.n

        def seat(s1, s2):
            where = self.plane((first + s1) % n, (second + s2) % n, self.core)
            return lax.dynamic_slice(total, (0, where, 0, 0), (self.nz, 1, rows, cols))

        kept = [seat(0, t).astype(F32) for t in range(n)]
        for s in range(1, n):
            got = after(self.permute(jnp.stack([seat(s, t) for t in range(n)]), "first", s), *until)
            kept = [kept[t] + got[t].astype(F32) for t in range(n)]
        return kept[0], [part.astype(BF16) for part in kept[1:]]

    def scatter_second(self, kept, *until):
        mine, rest = kept
        got = [after(self.permute(rest[s - 1], "second", s), *until) for s in range(1, self.n)]
        for part in got:
            mine = mine + part.astype(F32)
        return mine.reshape((self.nz,) + mine.shape[2:]), got

    def scatter_z(self, mine, *until):
        result = lax.dynamic_index_in_dim(mine, self.z, 0, keepdims=False)
        low = mine.astype(BF16)
        for s in range(1, self.nz):
            send = lax.dynamic_index_in_dim(low, (self.z + s) % self.nz, 0, keepdims=False)
            result = result + after(self.permute(send, "z", s), *until).astype(F32)
        return result


def adamw(weight, gradient, first_moment, second_moment, step_rate, weight_decay):
    first_moment = BETA_ONE * first_moment + (1.0 - BETA_ONE) * gradient
    second_moment = BETA_TWO * second_moment + (1.0 - BETA_TWO) * gradient * gradient
    first_fix = 1.0 - BETA_ONE**STEP
    second_fix = 1.0 - BETA_TWO**STEP
    direction = first_moment / first_fix / (jnp.sqrt(second_moment / second_fix) + EPS_ADAM)
    return (weight - step_rate * (direction + weight_decay * weight), first_moment, second_moment)


def local(
    block_in, lengths, out_grad, w_qkv, w_out, w_up, w_down, vectors,
    first_qkv, first_out, first_up, first_down, first_vectors,
    second_qkv, second_out, second_up, second_down, second_vectors,
):
    grid = Grid(lax.axis_size("dp"))
    core = grid.core
    core_arr = core.reshape(1).astype(jnp.int32)
    half_len = block_in.shape[1]
    vec_count, vec_here = vectors.shape

    def own_slot(halves):
        mine = lax.dynamic_index_in_dim(halves, core, 0, keepdims=False)
        theirs = lax.dynamic_index_in_dim(halves, 1 - core, 0, keepdims=False)
        return grid.join(mine, grid.swap(theirs), 0)

    def both_slots(mine, got):
        return lax.dynamic_update_slice(mine, got[None], (1 - core, 0, 0))

    def half_of(shard):
        width = shard.shape[1] // 2
        return lax.dynamic_slice_in_dim(shard, core * width, width, 1).astype(BF16)

    seats = grid.seats()

    turned = jnp.pad(vectors.T.astype(BF16), ((0, 0), (0, 128 - vec_count)))
    q_block = jnp.concatenate([half_of(w_qkv), turned], axis=1)
    u_block = jnp.concatenate([half_of(w_out), half_of(w_up)], axis=1)
    d_block = half_of(w_down)
    q_col = grid.gather_z(q_block)
    x = own_slot(block_in)
    q_line = grid.gather_first(q_col, x)
    q_rest = grid.gather_second(q_line)
    q_line_swap = grid.swap(q_line)
    q_rest_swap = [grid.swap(part) for part in q_rest]
    q_group = finish_group(grid, seats, [q_line] + q_rest, [q_line_swap] + q_rest_swap)

    h1, qkv, vec = qkv_call(core_arr, seats, x, q_group)
    u_col = grid.gather_z(after(u_block, *q_rest), qkv)
    og = own_slot(after(out_grad, qkv))
    att = attend_call(core_arr, lengths, after(qkv, u_col), 0, 2, ())
    u_line = grid.gather_first(u_col, *att)
    att = attend_call(core_arr, lengths, after(qkv, u_line), 2, 3, att)
    d_col = grid.gather_z(after(d_block, u_line), *att)
    u_line_swap = after(grid.swap(u_line), *att)
    u_rest = grid.gather_second(u_line, *att)
    d_col = after(d_col, *u_rest)
    att = attend_call(core_arr, lengths, after(qkv, d_col), 5, 1, att)
    u_rest_swap = [after(grid.swap(part), *att) for part in u_rest]
    d_line = grid.gather_first(d_col, *att)
    u_group = finish_group(grid, seats, [u_line] + u_rest, [u_line_swap] + u_rest_swap)
    a, lse = att
    mid, h2, e, slope, dy = up_call(core_arr, lengths, seats, x, after(a, d_line), og, vec, u_group)
    d_line_swap = after(grid.swap(d_line), mid)
    d_rest = grid.gather_second(d_line, mid)
    d_own, d_other = weight_grad_call(core_arr, [(after(e, *d_rest), [dy])], 512, "grad_down")
    d_rest_swap = [after(grid.swap(part), d_own) for part in d_rest]
    d_group = finish_group(grid, seats, [d_line] + d_rest, [d_line_swap] + d_rest_swap)
    dz, dmb, dm, da, acc_mid = down_call(core_arr, seats, mid, slope, dy, vec, u_group, d_group)

    d_total = after(grid.swap(d_other), dz) + d_own
    u_own, u_other = weight_grad_call(core_arr, [(a, [dmb]), (h2, [after(dz, d_total)])], 256, "grad_up")
    d_kept = grid.scatter_first(d_total, u_own)

    def back_call(ready, start, before, *needs):
        return attend_back_call(core_arr, lengths, qkv, a, after(ready, *needs), lse, start, 2, before)

    def grad_qkv_call(ready, start, count, name):
        cols = (128 * count, start // count)
        return weight_grad_call(core_arr, [(h1, ready)], 256, name, "turns", cols)

    back = back_call(da, 0, (), u_own, *d_kept[1])
    d_sum, d_here = grid.scatter_second(d_kept, *back)
    u_total = after(grid.swap(u_other), *back) + u_own
    back = back_call(da, 2, back, u_total, *d_here)
    d_mine = grid.scatter_z(d_sum, *back)
    p_own, p_other = grad_qkv_call([after(back[0], d_mine), back[1], back[2]], 0, 4, "grad_qkv")
    u_kept = grid.scatter_first(u_total, p_own)
    back = back_call(da, 4, back, p_own, *u_kept[1])
    d_other_mine = after(grid.swap(d_mine), *back)
    p_total = after(grid.swap(p_other), *back) + p_own
    u_sum, u_here = grid.scatter_second(u_kept, *back)
    dq, dk, dv = back
    r_own, r_other = grad_qkv_call([after(dq, p_total, *u_here), dk, dv], 4, 2, "grad_qkv")
    p_kept = grid.scatter_first(p_total, r_own)
    in_theirs, acc = last_call(
        core_arr, seats, x, dm, after(dq, r_own, *p_kept[1]), dk, dv, vec, acc_mid, q_group, True
    )
    u_mine = grid.scatter_z(u_sum, in_theirs)
    r_total = after(grid.swap(r_other), in_theirs) + r_own
    p_sum, p_here = grid.scatter_second(p_kept, in_theirs)
    in_mine, acc = last_call(
        core_arr, seats, x, dm, after(dq, r_total, *p_here), dk, dv, vec, acc, q_group, None
    )
    in_got = after(grid.swap(in_theirs), in_mine)
    r_kept = grid.scatter_first(r_total, in_mine)
    out_theirs = out_call(
        core_arr, lengths, seats, after(mid, in_mine, *r_kept[1]), e, vec, d_group, True
    )
    u_other_mine = after(grid.swap(u_mine), out_theirs)
    p_mine = grid.scatter_z(p_sum, out_theirs)
    r_sum, r_here = grid.scatter_second(r_kept, out_theirs)
    out_mine = out_call(core_arr, lengths, seats, after(mid, *r_here), e, vec, d_group, None)
    out_got = after(grid.swap(out_theirs), out_mine)
    p_other_mine = grid.swap(p_mine)
    r_mine = grid.scatter_z(r_sum)
    r_other_mine = grid.swap(r_mine)
    vec_total = grid.total_small(acc, (out_theirs,), (out_mine,), (), ())
    block_out = both_slots(out_mine, out_got)
    in_grad = both_slots(in_mine, in_got)

    half, wide = D // 2, FF // 2
    down_new, = adam_call(
        core_arr,
        [(d_mine, d_other_mine)],
        [(after(w_down, out_theirs), first_down, second_down)],
        [(FF ** (-0.5), MATRIX_DECAY, [(0, 0, half, 0, half)])],
    )
    out_new, up_new = adam_call(
        core_arr,
        [(u_mine, u_other_mine)],
        [(after(w_out, in_grad, block_out), first_out, second_out), (w_up, first_up, second_up)],
        [
            ((D // 64) ** (-0.5), MATRIX_DECAY, [(0, 0, half, 0, half)]),
            (D ** (-0.5), MATRIX_DECAY, [(0, half, wide, 0, wide)]),
        ],
    )
    moves = []
    for part in range(3):
        for turn in range(2):
            at = part * D + turn * 256
            moves.append((0, (part * 2 + turn) * 128, 128, at, at + 128))
        moves.append((1, part * 128, 128, part * D + 512, part * D + 640))
    qkv_new, = adam_call(
        core_arr,
        [(p_mine, p_other_mine), (r_mine, r_other_mine)],
        [(w_qkv, first_qkv, second_qkv)],
        [(D ** (-0.5), MATRIX_DECAY, moves)],
    )
    vec_grad = lax.dynamic_slice(vec_total, (0, grid.chip * vec_here), (vec_count, vec_here))
    vec_new = adamw(vectors, vec_grad, first_vectors, second_vectors, VECTOR_RATE, 0.0)
    news = [qkv_new, out_new, up_new, down_new, vec_new]
    return (block_out, in_grad) + tuple(new[kind] for kind in range(3) for new in news)


def finish_group(grid, seats, own, other):
    rows, cols = own[0].shape[-2:]
    if rows % 16 == 0:
        return Pieces(own + other, rows)
    found = []
    for half, parts in enumerate((own, other)):
        here = seats[half * grid.chips : (half + 1) * grid.chips]
        order = jnp.zeros((grid.chips,), jnp.int32).at[here].set(jnp.arange(grid.chips, dtype=jnp.int32))
        blocks = jnp.concatenate(parts).reshape(grid.chips, rows, cols)
        found.append(jnp.take(blocks, order, axis=0).reshape(1, 1, grid.chips * rows, cols))
    return Pieces(found, grid.chips * rows, True)


def solution(mesh):
    weight = P("dp", None)
    vector = P(None, "dp")
    state = (weight, weight, weight, weight, vector)
    tokens = P("dp", "seq", None)
    return jax.shard_map(
        local,
        mesh=mesh,
        in_specs=(tokens, P("dp"), tokens) + state * 3,
        out_specs=(tokens, tokens) + state * 3,
        check_vma=False,
    )
```

```python
import functools

import jax
import jax.numpy as jnp
from jax import lax
from jax.experimental import pallas as pl
from jax.experimental.pallas import tpu as pltpu
from jax.sharding import PartitionSpec as P

D = 768
HEADS = 12
HEAD_DIM = 64
FF = 3072
STEP = 10

EPS_NORM = 1e-05
EPS_ADAM = 1e-08
BETA_ONE = 0.5
BETA_TWO = 0.5
MATRIX_DECAY = 0.1
VECTOR_RATE = 0.1
NEG_FILL = -1e30
GELU_ROOT = 0.7978845608028654
GELU_CUBE = 0.044715
QKV_HALF = 3 * D // 2

F32 = jnp.float32
BF16 = jnp.bfloat16

NN = (((1,), (0,)), ((), ()))
NT = (((1,), (1,)), ((), ()))
TN = (((0,), (0,)), ((), ()))


def mm(left, right, dims=NN):
    return lax.dot_general(left, right, dims, preferred_element_type=F32)


def cost(flops, nbytes, trans=0):
    return pl.CostEstimate(flops=int(flops), bytes_accessed=int(nbytes), transcendentals=int(trans))


def params(mib):
    return pltpu.CompilerParams(vmem_limit_bytes=mib * 1024 * 1024)


def whole_spec(shape):
    return pl.BlockSpec(shape, lambda *idx: (0,) * len(shape), pipeline_mode=pl.Buffered(1))


class Pieces:
    def __init__(self, arrays, rows, ordered=False):
        self.arrays = arrays
        self.rows = rows
        self.ordered = ordered
        self.halves = 2
        self.count = len(arrays) // self.halves
        self.lines, self.depth = arrays[0].shape[:2]

    def specs(self):
        return [pl.BlockSpec(memory_space=pltpu.HBM)] * len(self.arrays)

    def row(self, seat_ref, at):
        return 0 if self.ordered else pl.multiple_of(seat_ref[at] * self.rows, 16)

    def start(self, refs, core_ref, seat_ref, start_col, width, target, sem):
        core = core_ref[0]
        at = 0
        for half in range(self.halves):
            where = core if half == 0 else 1 - core
            for s2 in range(self.count):
                ref = refs[half * self.count + s2]
                for s1 in range(self.lines):
                    for sz in range(self.depth):
                        row = self.row(seat_ref, at)
                        at += 1
                        col = pl.multiple_of(where * width, 128)
                        pltpu.make_async_copy(
                            ref.at[s1, sz, :, pl.ds(start_col, width)],
                            target.at[pl.ds(row, self.rows), pl.ds(col, width)],
                            sem,
                        ).start()

    def start_once(self, refs, seat_ref, start_col, width, target, sem):
        at = 0
        for s2 in range(self.count):
            for s1 in range(self.lines):
                for sz in range(self.depth):
                    row = self.row(seat_ref, at)
                    at += 1
                    pltpu.make_async_copy(
                        refs[s2].at[s1, sz, :, pl.ds(start_col, width)],
                        target.at[pl.ds(row, self.rows), :],
                        sem,
                    ).start()


def wait_all(target, sem):
    pltpu.make_async_copy(target, target, sem).wait()


def norm_parts(rows):
    mean = jnp.mean(rows, axis=-1, keepdims=True)
    centred = rows - mean
    variance = jnp.mean(centred * centred, axis=-1, keepdims=True)
    scale = lax.rsqrt(variance + EPS_NORM)
    return centred * scale, scale


def norm_back(d_normed, normed, scale):
    first = jnp.mean(d_normed, axis=-1, keepdims=True)
    second = jnp.mean(d_normed * normed, axis=-1, keepdims=True)
    return scale * (d_normed - first - normed * second)


def qkv_kernel(group, core_ref, seat_ref, x_ref, *refs):
    refs, (h_ref, qkv_ref, vec_ref, w_ref, turned_ref, sems) = refs[:-6], refs[-6:]

    @pl.when(pl.program_id(0) == 0)
    def _():
        group.start(refs, core_ref, seat_ref, 0, QKV_HALF, w_ref, sems.at[0])
        group.start_once(refs, seat_ref, QKV_HALF, 128, turned_ref, sems.at[1])
        wait_all(turned_ref, sems.at[1])
        vec_ref[...] = turned_ref[...].astype(F32).T[:16]
        wait_all(w_ref, sems.at[0])

    normed, _ = norm_parts(x_ref[...].astype(F32))
    h = (normed * vec_ref[0:1, :] + vec_ref[1:2, :]).astype(BF16)
    h_ref[...] = h
    qkv_ref[:, :D] = (mm(h, w_ref[:, :D]) + vec_ref[2:3, :]).astype(BF16)
    qkv_ref[:, D : 2 * D] = mm(h, w_ref[:, D : 2 * D]).astype(BF16)
    qkv_ref[:, 2 * D :] = (mm(h, w_ref[:, 2 * D :]) + vec_ref[3:4, :]).astype(BF16)


def qkv_call(core, seats, x, group, block=256):
    rows = x.shape[0]
    return pl.pallas_call(
        functools.partial(qkv_kernel, group),
        name="qkv",
        grid_spec=pltpu.PrefetchScalarGridSpec(
            num_scalar_prefetch=2,
            grid=(rows // block,),
            in_specs=[pl.BlockSpec((block, D), lambda i, *s: (i, 0))] + group.specs(),
            out_specs=[
                pl.BlockSpec((block, D), lambda i, *s: (i, 0)),
                pl.BlockSpec((block, 3 * D), lambda i, *s: (i, 0)),
                pl.BlockSpec((16, D), lambda i, *s: (0, 0)),
            ],
            scratch_shapes=[
                pltpu.VMEM((D, 3 * D), BF16),
                pltpu.VMEM((D, 128), BF16),
                pltpu.SemaphoreType.DMA((2,)),
            ],
        ),
        out_shape=[
            jax.ShapeDtypeStruct((rows, D), BF16),
            jax.ShapeDtypeStruct((rows, 3 * D), BF16),
            jax.ShapeDtypeStruct((16, D), F32),
        ],
        compiler_params=params(20),
        cost_estimate=cost(2 * rows * D * 3 * D, 10e6),
    )(core, seats, x, *group.arrays)


def head_parts(length, q_all, k_all, head):
    full_len = q_all.shape[0]
    lane = lax.broadcasted_iota(jnp.int32, (1, 128), 1)
    mine = (lane // HEAD_DIM) == head
    spare = lane == HEAD_DIM * (1 - head)
    pos = lax.broadcasted_iota(jnp.int32, (full_len, 128), 0)
    fill = jnp.where(pos < length, 0.0, NEG_FILL).astype(BF16)
    zero = jnp.zeros((), BF16)
    k_head = jnp.where(mine, k_all, jnp.where(spare, fill, zero))
    q_plain = jnp.where(mine, q_all, zero)
    q_head = jnp.where(spare, jnp.ones((), BF16), q_plain)
    return mine, k_head, q_plain, q_head


def causal_mask(scores, block):
    full = scores.shape[0]
    key_pos = lax.broadcasted_iota(jnp.int32, (block, block), 0)
    query_pos = lax.broadcasted_iota(jnp.int32, (block, block), 1)
    last = jnp.where(key_pos <= query_pos, scores[full - block :], NEG_FILL)
    if full == block:
        return last
    return jnp.concatenate([scores[: full - block], last], axis=0)


def attend_kernel(core_ref, len_ref, q_ref, k_ref, v_ref, *refs):
    a_ref, lse_ref, mixed_ref = refs[-3:]
    block = 256
    full_len = q_ref.shape[0]
    length = len_ref[core_ref[0]]
    q_all = q_ref[...] * jnp.asarray(HEAD_DIM ** (-0.5), BF16)
    k_all = k_ref[...]
    v_turned = v_ref[...].T
    for head in range(2):
        _, k_head, _, q_head = head_parts(length, q_all, k_all, head)
        v_head = v_turned[head * HEAD_DIM : (head + 1) * HEAD_DIM]
        for j in range(full_len // block):
            cols = slice(j * block, (j + 1) * block)
            span = (j + 1) * block
            scores = causal_mask(mm(k_head[:span], q_head[cols], NT), block)
            top = jnp.max(scores, axis=0, keepdims=True)
            exped = jnp.exp(scores - top)
            total = jnp.sum(exped, axis=0, keepdims=True)
            mixed = mm(v_head[:, :span], exped.astype(BF16)) / total
            mixed_ref[head * HEAD_DIM : (head + 1) * HEAD_DIM, cols] = mixed
            lse_ref[0, head : head + 1, cols] = top + jnp.log(total)
    a_ref[...] = mixed_ref[...].T.astype(BF16)


def attend_call(core, lengths, qkv, first, count, before):
    rows = qkv.shape[0]
    pairs = HEADS // 2
    before = list(before)
    return pl.pallas_call(
        attend_kernel,
        name="attend",
        grid_spec=pltpu.PrefetchScalarGridSpec(
            num_scalar_prefetch=2,
            grid=(count,),
            in_specs=[
                pl.BlockSpec((rows, 128), lambda i, c, n: (0, i + first)),
                pl.BlockSpec((rows, 128), lambda i, c, n: (0, i + first + pairs)),
                pl.BlockSpec((rows, 128), lambda i, c, n: (0, i + first + 2 * pairs)),
            ]
            + [pl.BlockSpec(memory_space=pl.ANY)] * len(before),
            out_specs=[
                pl.BlockSpec((rows, 128), lambda i, c, n: (0, i + first)),
                pl.BlockSpec((1, 8, rows), lambda i, c, n: (i + first, 0, 0)),
            ],
            scratch_shapes=[pltpu.VMEM((128, rows), F32)],
        ),
        out_shape=[
            jax.ShapeDtypeStruct((rows, D), BF16),
            jax.ShapeDtypeStruct((pairs, 8, rows), F32),
        ],
        input_output_aliases={5 + i: i for i in range(len(before))},
        compiler_params=params(20),
        cost_estimate=cost(3e9 * count, 1.2e6 * count, 2 * rows * rows * 0.6 * count),
    )(core, lengths, qkv, qkv, qkv, *before)


def attend_back_kernel(core_ref, len_ref, q_ref, k_ref, v_ref, a_ref, da_ref, lse_ref, *refs):
    dq_ref, dk_ref, dv_ref, dqt_ref, dk_acc, dv_acc = refs[-6:]
    block = 256
    full_len = q_ref.shape[0]
    length = len_ref[core_ref[0]]
    scale = HEAD_DIM ** (-0.5)
    q_all = q_ref[...] * jnp.asarray(scale, BF16)
    k_all = k_ref[...]
    k_turned = k_all.T
    v_all = v_ref[...]
    da_all = da_ref[...]
    inner = (da_all.astype(F32) * a_ref[...].astype(F32)).T
    first = True
    for head in range(2):
        mine, k_head, q_plain, q_head = head_parts(length, q_all, k_all, head)
        da_head = jnp.where(mine, da_all, jnp.zeros((), BF16))
        lanes = slice(head * HEAD_DIM, (head + 1) * HEAD_DIM)
        centre = jnp.sum(inner[lanes], axis=0, keepdims=True)
        for j in reversed(range(full_len // block)):
            cols = slice(j * block, (j + 1) * block)
            span = (j + 1) * block
            scores = causal_mask(mm(k_head[:span], q_head[cols], NT), block)
            probs = jnp.exp(scores - lse_ref[0, head : head + 1, cols])
            d_probs = mm(v_all[:span], da_head[cols], NT)
            d_scores = (probs * (d_probs - centre[:, cols])).astype(BF16)
            dv_part = mm(probs.astype(BF16), da_head[cols])
            dk_part = mm(d_scores, q_plain[cols])
            if first:
                dv_acc[...] = dv_part
                dk_acc[...] = dk_part
                first = False
            else:
                dv_acc[:span] += dv_part
                dk_acc[:span] += dk_part
            dqt_ref[lanes, cols] = mm(k_turned[lanes, :span], d_scores) * scale
    dq_ref[...] = dqt_ref[...].T.astype(BF16)
    dk_ref[...] = dk_acc[...].astype(BF16)
    dv_ref[...] = dv_acc[...].astype(BF16)


def attend_back_call(core, lengths, qkv, a, da, lse, start, count, before):
    rows = qkv.shape[0]
    pairs = HEADS // 2
    before = list(before)
    pair_spec = pl.BlockSpec((rows, 128), lambda i, c, n: (0, i + start))
    return pl.pallas_call(
        attend_back_kernel,
        name="attend_back",
        grid_spec=pltpu.PrefetchScalarGridSpec(
            num_scalar_prefetch=2,
            grid=(count,),
            in_specs=[
                pair_spec,
                pl.BlockSpec((rows, 128), lambda i, c, n: (0, i + start + pairs)),
                pl.BlockSpec((rows, 128), lambda i, c, n: (0, i + start + 2 * pairs)),
                pair_spec,
                pair_spec,
                pl.BlockSpec((1, 8, rows), lambda i, c, n: (i + start, 0, 0)),
            ]
            + [pl.BlockSpec(memory_space=pl.ANY)] * len(before),
            out_specs=[pair_spec, pair_spec, pair_spec],
            scratch_shapes=[
                pltpu.VMEM((128, rows), F32),
                pltpu.VMEM((rows, 128), F32),
                pltpu.VMEM((rows, 128), F32),
            ],
        ),
        out_shape=[jax.ShapeDtypeStruct((rows, D), BF16)] * 3,
        input_output_aliases={8 + i: i for i in range(len(before))},
        compiler_params=params(24),
        cost_estimate=cost(6e9 * count, 2e6 * count, 2 * rows * rows * 0.6 * count),
    )(core, lengths, qkv, qkv, qkv, a, da, lse, *before)


def valid_rows(core_ref, len_ref, block):
    pos = pl.program_id(0) * block + lax.broadcasted_iota(jnp.int32, (block, 1), 0)
    return pos < len_ref[core_ref[0]]


def add_row(acc_ref, row, value):
    acc_ref[row : row + 1, :] += jnp.sum(value, axis=0, keepdims=True)


def up_kernel(group, core_ref, len_ref, seat_ref, x_ref, a_ref, og_ref, vec_ref, *refs):
    refs, (mid_ref, h_ref, e_ref, slope_ref, dy_ref, wo_ref, wu_ref, sems) = refs[:-8], refs[-8:]
    block = x_ref.shape[0]

    @pl.when(pl.program_id(0) == 0)
    def _():
        group.start(refs, core_ref, seat_ref, 0, D // 2, wo_ref, sems.at[0])
        group.start(refs, core_ref, seat_ref, D // 2, FF // 2, wu_ref, sems.at[1])
        wait_all(wo_ref, sems.at[0])
        wait_all(wu_ref, sems.at[1])

    valid = valid_rows(core_ref, len_ref, block)
    dy_ref[...] = jnp.where(valid, og_ref[...].astype(F32), 0.0).astype(BF16)
    mid = x_ref[...].astype(F32) + mm(a_ref[...], wo_ref[...]) + vec_ref[4:5, :]
    mid_ref[...] = mid
    normed, _ = norm_parts(mid)
    h = (normed * vec_ref[5:6, :] + vec_ref[6:7, :]).astype(BF16)
    h_ref[...] = h
    for j in range(FF // D):
        cols = slice(j * D, (j + 1) * D)
        z = mm(h, wu_ref[:, cols]) + vec_ref[8 + j : 9 + j, :]
        squared = z * z
        turned = jnp.tanh(z * (GELU_ROOT + (GELU_ROOT * GELU_CUBE) * squared))
        half = 0.5 * turned + 0.5
        act = z * half
        e_ref[:, cols] = act.astype(BF16)
        slope = half + act * (1.0 - turned) * (GELU_ROOT + (3.0 * GELU_ROOT * GELU_CUBE) * squared)
        slope_ref[:, cols] = slope.astype(BF16)


def up_call(core, lengths, seats, x, a, og, vec, group, block=256):
    rows = x.shape[0]
    row_spec = pl.BlockSpec((block, D), lambda i, *s: (i, 0))
    wide_spec = pl.BlockSpec((block, FF), lambda i, *s: (i, 0))
    low = jax.ShapeDtypeStruct((rows, D), BF16)
    return pl.pallas_call(
        functools.partial(up_kernel, group),
        name="up",
        grid_spec=pltpu.PrefetchScalarGridSpec(
            num_scalar_prefetch=3,
            grid=(rows // block,),
            in_specs=[row_spec, row_spec, row_spec, whole_spec(vec.shape)] + group.specs(),
            out_specs=[row_spec, row_spec, wide_spec, wide_spec, row_spec],
            scratch_shapes=[
                pltpu.VMEM((D, D), BF16),
                pltpu.VMEM((D, FF), BF16),
                pltpu.SemaphoreType.DMA((2,)),
            ],
        ),
        out_shape=[
            jax.ShapeDtypeStruct((rows, D), F32),
            low,
            jax.ShapeDtypeStruct((rows, FF), BF16),
            jax.ShapeDtypeStruct((rows, FF), BF16),
            low,
        ],
        compiler_params=params(32),
        cost_estimate=cost(6e9, 30e6, rows * FF),
    )(core, lengths, seats, x, a, og, vec, *group.arrays)


def down_kernel(up_group, down_group, core_ref, seat_ref, mid_ref, slope_ref, dy_ref, vec_ref, *refs):
    count = len(up_group.arrays)
    up_refs, down_refs = refs[:count], refs[count : count + len(down_group.arrays)]
    dz_ref, dmb_ref, dm_ref, da_ref, acc_ref, wo_ref, wu_ref, wd_ref, sems = refs[-9:]
    block = mid_ref.shape[0]

    @pl.when(pl.program_id(0) == 0)
    def _():
        down_group.start(down_refs, core_ref, seat_ref, 0, D // 2, wd_ref, sems.at[2])
        up_group.start(up_refs, core_ref, seat_ref, D // 2, FF // 2, wu_ref, sems.at[1])
        up_group.start(up_refs, core_ref, seat_ref, 0, D // 2, wo_ref, sems.at[0])
        acc_ref[...] = jnp.zeros_like(acc_ref)
        wait_all(wd_ref, sems.at[2])
        wait_all(wu_ref, sems.at[1])
        wait_all(wo_ref, sems.at[0])

    mid = mid_ref[...]
    normed, scale = norm_parts(mid)
    dy_low = dy_ref[...]
    dy = dy_low.astype(F32)
    add_row(acc_ref, 7, dy)
    dh = jnp.zeros((block, D), F32)
    for j in range(FF // D):
        cols = slice(j * D, (j + 1) * D)
        dz = (mm(dy_low, wd_ref[cols, :], NT) * slope_ref[:, cols].astype(F32)).astype(BF16)
        dz_ref[:, cols] = dz
        add_row(acc_ref, 8 + j, dz.astype(F32))
        dh += mm(dz, wu_ref[:, cols], NT)
    add_row(acc_ref, 5, dh * normed)
    add_row(acc_ref, 6, dh)
    dm = dy + norm_back(dh * vec_ref[5:6, :], normed, scale)
    dm_ref[...] = dm
    dm_low = dm.astype(BF16)
    dmb_ref[...] = dm_low
    add_row(acc_ref, 4, dm_low.astype(F32))
    da_ref[...] = mm(dm_low, wo_ref[...], NT).astype(BF16)


def down_call(core, seats, mid, slope, dy, vec, up_group, down_group, block=256):
    rows = mid.shape[0]
    row_spec = pl.BlockSpec((block, D), lambda i, *s: (i, 0))
    wide_spec = pl.BlockSpec((block, FF), lambda i, *s: (i, 0))
    low = jax.ShapeDtypeStruct((rows, D), BF16)
    return pl.pallas_call(
        functools.partial(down_kernel, up_group, down_group),
        name="down",
        grid_spec=pltpu.PrefetchScalarGridSpec(
            num_scalar_prefetch=2,
            grid=(rows // block,),
            in_specs=[row_spec, wide_spec, row_spec, whole_spec(vec.shape)]
            + up_group.specs()
            + down_group.specs(),
            out_specs=[
                wide_spec, row_spec, row_spec, row_spec,
                pl.BlockSpec((16, D), lambda i, *s: (0, 0)),
            ],
            scratch_shapes=[
                pltpu.VMEM((D, D), BF16),
                pltpu.VMEM((D, FF), BF16),
                pltpu.VMEM((FF, D), BF16),
                pltpu.SemaphoreType.DMA((3,)),
            ],
        ),
        out_shape=[
            jax.ShapeDtypeStruct((rows, FF), BF16), low, jax.ShapeDtypeStruct((rows, D), F32), low,
            jax.ShapeDtypeStruct((16, D), F32),
        ],
        compiler_params=params(44),
        cost_estimate=cost(1.1e10, 30e6),
    )(core, seats, mid, slope, dy, vec, *up_group.arrays, *down_group.arrays)


def out_kernel(group, first, core_ref, len_ref, seat_ref, mid_ref, e_ref, vec_ref, *refs):
    refs, (out_ref, wd_ref, sems) = refs[:-3], refs[-3:]
    block = mid_ref.shape[0]

    @pl.when(pl.program_id(0) == 0)
    def _():
        group.start(refs, core_ref, seat_ref, 0, D // 2, wd_ref, sems.at[0])
        wait_all(wd_ref, sems.at[0])

    half = core_ref[0] if first is None else 1 - core_ref[0]
    pos = (half * pl.num_programs(0) + pl.program_id(0)) * block
    valid = pos + lax.broadcasted_iota(jnp.int32, (block, 1), 0) < len_ref[core_ref[0]]
    down = vec_ref[7:8, :] + mid_ref[...] + mm(e_ref[...], wd_ref[...])
    down = jnp.where(valid, down, 0.0).astype(BF16)
    if first is None:
        out_ref[0] = down
    else:
        out_ref[...] = down


def half_specs(first, steps, block):
    def half(core):
        return core[0] if first is None else 1 - core[0]

    def rows(width):
        return pl.BlockSpec((block, width), lambda i, c, *s: (half(c) * steps + i, 0))

    if first is None:
        out = pl.BlockSpec((1, block, D), lambda i, c, *s: (c[0], i, 0))
    else:
        out = pl.BlockSpec((block, D), lambda i, c, *s: (i, 0))
    return rows, out


def out_call(core, lengths, seats, mid, e, vec, group, first, block=256):
    half_len = mid.shape[0] // 2
    steps = half_len // block
    rows, out_spec = half_specs(first, steps, block)
    shape = (2, half_len, D) if first is None else (half_len, D)
    return pl.pallas_call(
        functools.partial(out_kernel, group, first),
        name="out",
        grid_spec=pltpu.PrefetchScalarGridSpec(
            num_scalar_prefetch=3,
            grid=(steps,),
            in_specs=[rows(D), rows(FF), whole_spec(vec.shape)] + group.specs(),
            out_specs=out_spec,
            scratch_shapes=[pltpu.VMEM((FF, D), BF16), pltpu.SemaphoreType.DMA((1,))],
        ),
        out_shape=jax.ShapeDtypeStruct(shape, BF16),
        compiler_params=params(24),
        cost_estimate=cost(2.4e9, 9e6),
    )(core, lengths, seats, mid, e, vec, *group.arrays)


def pick(values, half, mode):
    if mode == "split":
        width = values.shape[1] // 2
        return [values[:, half * width : (half + 1) * width]]
    return [values[:, at : at + 128] for at in range(half * 128, values.shape[1], 256)]


def weight_grad_kernel(lefts, rights, mode, core_ref, *refs):
    left_refs, right_refs = refs[:lefts], refs[lefts : lefts + sum(rights)]
    own_ref, other_ref = refs[-2:]
    halves = ([], [])
    at = 0
    for left_ref, count in zip(left_refs, rights):
        left = left_ref[...]
        for right_ref in right_refs[at : at + count]:
            whole = mm(left, right_ref[...], TN).astype(BF16)
            for half in range(2):
                halves[half].extend(pick(whole, half, mode))
        at += count
    low, high = [part[0] if len(part) == 1 else jnp.concatenate(part, axis=1) for part in halves]

    @pl.when(core_ref[0] == 0)
    def _():
        own_ref[...] = low
        other_ref[...] = high

    @pl.when(core_ref[0] != 0)
    def _():
        own_ref[...] = high
        other_ref[...] = low


def weight_grad_call(core, products, block, name, mode="split", cols=None):
    rows, height = products[0][0].shape
    lefts = [left for left, _ in products]
    rights = [right for _, group in products for right in group]
    widths = [right.shape[1] if cols is None else cols[0] for right in rights]
    width = sum(widths)
    seat = 0 if cols is None else cols[1]
    return pl.pallas_call(
        functools.partial(weight_grad_kernel, len(lefts), [len(group) for _, group in products], mode),
        name=name,
        grid_spec=pltpu.PrefetchScalarGridSpec(
            num_scalar_prefetch=1,
            grid=(height // block,),
            in_specs=[pl.BlockSpec((rows, block), lambda i, c: (0, i))] * len(lefts)
            + [
                pl.BlockSpec((rows, w), lambda i, c: (0, seat), pipeline_mode=pl.Buffered(1)) for w in widths
            ],
            out_specs=[pl.BlockSpec((block, width // 2), lambda i, c: (i, 0))] * 2,
        ),
        out_shape=[jax.ShapeDtypeStruct((height, width // 2), BF16)] * 2,
        compiler_params=params(40),
        cost_estimate=cost(2 * rows * height * width, rows * (height + width) * 2 + height * width * 2),
    )(core, *lefts, *rights)


def last_kernel(group, first, core_ref, seat_ref, x_ref, dm_ref, dq_ref, dk_ref, dv_ref, vec_ref, before_ref, *refs):
    refs, (grad_ref, acc_ref, w_ref, sems) = refs[:-4], refs[-4:]

    @pl.when(pl.program_id(0) == 0)
    def _():
        group.start(refs, core_ref, seat_ref, 0, QKV_HALF, w_ref, sems.at[0])
        acc_ref[...] = before_ref[...]
        wait_all(w_ref, sems.at[0])

    normed, scale = norm_parts(x_ref[...].astype(F32))
    dq, dk, dv = dq_ref[...], dk_ref[...], dv_ref[...]
    dh = (
        mm(dq, w_ref[:, :D], NT)
        + mm(dk, w_ref[:, D : 2 * D], NT)
        + mm(dv, w_ref[:, 2 * D :], NT)
    )
    add_row(acc_ref, 0, dh * normed)
    add_row(acc_ref, 1, dh)
    add_row(acc_ref, 2, dq.astype(F32))
    add_row(acc_ref, 3, dv.astype(F32))
    grad = dm_ref[...] + norm_back(dh * vec_ref[0:1, :], normed, scale)
    if first is None:
        grad_ref[0] = grad
    else:
        grad_ref[...] = grad


def last_call(core, seats, x, dm, dq, dk, dv, vec, before, group, first, block=256):
    half_len = x.shape[0] // 2
    steps = half_len // block
    rows, out_spec = half_specs(first, steps, block)
    shape = (2, half_len, D) if first is None else (half_len, D)
    return pl.pallas_call(
        functools.partial(last_kernel, group, first),
        name="last",
        grid_spec=pltpu.PrefetchScalarGridSpec(
            num_scalar_prefetch=2,
            grid=(steps,),
            in_specs=[rows(D)] * 5 + [whole_spec(vec.shape), whole_spec(before.shape)] + group.specs(),
            out_specs=[out_spec, pl.BlockSpec((16, D), lambda i, *s: (0, 0))],
            scratch_shapes=[pltpu.VMEM((D, 3 * D), BF16), pltpu.SemaphoreType.DMA((1,))],
        ),
        out_shape=[jax.ShapeDtypeStruct(shape, F32), jax.ShapeDtypeStruct((16, D), F32)],
        compiler_params=params(24),
        cost_estimate=cost(half_len * 6 * D * D, 10e6),
    )(core, seats, x, dm, dq, dk, dv, vec, before, *group.arrays)


def adam_kernel(plans, sources, core_ref, *refs):
    halves = [refs[2 * i : 2 * i + 2] for i in range(sources)]
    count = len(plans)
    states = refs[2 * sources : 2 * sources + 3 * count]
    outs = refs[2 * sources + 3 * count : 2 * sources + 6 * count]
    grads = refs[2 * sources + 6 * count :]
    for core in range(2):

        @pl.when(core_ref[0] == core)
        def _():
            for (_, _, moves), grad_ref in zip(plans, grads):
                for source, start, width, place0, place1 in moves:
                    for half, place in ((0, place0), (1, place1)):
                        ref = halves[source][0 if half == core else 1]
                        grad_ref[:, place : place + width] = ref[:, start : start + width].astype(F32)

    for i, (rate, decay, _) in enumerate(plans):
        weight, first, second = states[3 * i : 3 * i + 3]
        new = adamw(weight[...], grads[i][...], first[...], second[...], rate, decay)
        for out, value in zip(outs[3 * i : 3 * i + 3], new):
            out[...] = value


def adam_call(core, halves, states, plans):
    flat = [part for pair in halves for part in pair]
    held = [part for state in states for part in state]
    spec = pl.BlockSpec(memory_space=pltpu.VMEM)
    news = pl.pallas_call(
        functools.partial(adam_kernel, plans, len(halves)),
        name="adam",
        in_specs=[pl.BlockSpec(memory_space=pltpu.SMEM)] + [spec] * (len(flat) + len(held)),
        out_specs=[spec] * len(held),
        out_shape=[jax.ShapeDtypeStruct(part.shape, F32) for part in held],
        scratch_shapes=[pltpu.VMEM(state[0].shape, F32) for state in states],
        compiler_params=params(24),
        cost_estimate=cost(1e6, 24 * sum(state[0].size for state in states)),
    )(core, *flat, *held)
    return [news[3 * i : 3 * i + 3] for i in range(len(states))]


def after(value, *others):
    if not others:
        return value
    return lax.optimization_barrier((value,) + others)[0]


class Grid:
    def __init__(self, chips):
        log = chips.bit_length() - 1
        side = 1 << (log // 3)
        if side * side * (chips // (side * side)) != chips:
            side = 1
        self.chips = chips
        self.n = side
        self.nz = chips // (side * side)
        self.core = lax.axis_index("seq")
        self.chip = lax.axis_index("dp")
        self.x = self.chip % side
        self.y = self.chip // side % side
        self.z = self.chip // (side * side)

    def plane(self, first, second, core):
        return jnp.where(core == 0, second * self.n + first, first * self.n + second)

    def coords(self, core):
        return jnp.where(core == 0, self.x, self.y), jnp.where(core == 0, self.y, self.x)

    def permute(self, value, axis, shift=0):
        pairs = []
        for chip in range(self.chips):
            for core in range(2):
                x, y, z = chip % self.n, chip // self.n % self.n, chip // (self.n * self.n)
                to_core = core
                if axis == "z":
                    z = (z + shift) % self.nz
                elif axis == "core":
                    to_core = 1 - core
                elif (axis == "first") == (core == 0):
                    x = (x + shift) % self.n
                else:
                    y = (y + shift) % self.n
                pairs.append((chip * 2 + core, ((z * self.n + y) * self.n + x) * 2 + to_core))
        return lax.ppermute(value, ("dp", "seq"), pairs)

    def swap(self, value):
        return self.permute(value, "core")

    def join(self, own, other, axis):
        return jnp.where(
            self.core == 0,
            jnp.concatenate([own, other], axis),
            jnp.concatenate([other, own], axis),
        )

    def seats(self):
        found = []
        for half in range(2):
            core = self.core if half == 0 else 1 - self.core
            first, second = self.coords(core)
            for s2 in range(self.n):
                for s1 in range(self.n):
                    flat = self.plane((first - s1) % self.n, (second - s2) % self.n, core)
                    for sz in range(self.nz):
                        found.append(((self.z - sz) % self.nz) * self.n * self.n + flat)
        return jnp.stack(found).astype(jnp.int32)

    def total_small(self, value, *untils):
        for (axis, count), until in zip((("core", 2), ("first", self.n), ("second", self.n), ("z", self.nz)), untils):
            value = value + sum(after(self.permute(value, axis, s), *until) for s in range(1, count))
        return value

    def gather_z(self, block, *until):
        return jnp.stack([block] + [after(self.permute(block, "z", s), *until) for s in range(1, self.nz)])

    def gather_first(self, column, *until):
        return jnp.stack([column] + [after(self.permute(column, "first", s), *until) for s in range(1, self.n)])

    def gather_second(self, line, *until):
        return [after(self.permute(line, "second", s), *until) for s in range(1, self.n)]

    def scatter_first(self, total, *until):
        rows, cols = total.shape[0] // self.chips, total.shape[1]
        total = total.reshape(self.nz, self.n * self.n, rows, cols)
        first, second = self.coords(self.core)
        n = self.n

        def seat(s1, s2):
            where = self.plane((first + s1) % n, (second + s2) % n, self.core)
            return lax.dynamic_slice(total, (0, where, 0, 0), (self.nz, 1, rows, cols))

        kept = [seat(0, t).astype(F32) for t in range(n)]
        for s in range(1, n):
            got = after(self.permute(jnp.stack([seat(s, t) for t in range(n)]), "first", s), *until)
            kept = [kept[t] + got[t].astype(F32) for t in range(n)]
        return kept[0], [part.astype(BF16) for part in kept[1:]]

    def scatter_second(self, kept, *until):
        mine, rest = kept
        got = [after(self.permute(rest[s - 1], "second", s), *until) for s in range(1, self.n)]
        for part in got:
            mine = mine + part.astype(F32)
        return mine.reshape((self.nz,) + mine.shape[2:]), got

    def scatter_z(self, mine, *until):
        result = lax.dynamic_index_in_dim(mine, self.z, 0, keepdims=False)
        low = mine.astype(BF16)
        for s in range(1, self.nz):
            send = lax.dynamic_index_in_dim(low, (self.z + s) % self.nz, 0, keepdims=False)
            result = result + after(self.permute(send, "z", s), *until).astype(F32)
        return result


def adamw(weight, gradient, first_moment, second_moment, step_rate, weight_decay):
    first_moment = BETA_ONE * first_moment + (1.0 - BETA_ONE) * gradient
    second_moment = BETA_TWO * second_moment + (1.0 - BETA_TWO) * gradient * gradient
    first_fix = 1.0 - BETA_ONE**STEP
    second_fix = 1.0 - BETA_TWO**STEP
    direction = first_moment / first_fix / (jnp.sqrt(second_moment / second_fix) + EPS_ADAM)
    return (weight - step_rate * (direction + weight_decay * weight), first_moment, second_moment)


def local(
    block_in, lengths, out_grad, w_qkv, w_out, w_up, w_down, vectors,
    first_qkv, first_out, first_up, first_down, first_vectors,
    second_qkv, second_out, second_up, second_down, second_vectors,
):
    grid = Grid(lax.axis_size("dp"))
    core = grid.core
    core_arr = core.reshape(1).astype(jnp.int32)
    half_len = block_in.shape[1]
    vec_count, vec_here = vectors.shape

    def own_slot(halves):
        mine = lax.dynamic_index_in_dim(halves, core, 0, keepdims=False)
        theirs = lax.dynamic_index_in_dim(halves, 1 - core, 0, keepdims=False)
        return grid.join(mine, grid.swap(theirs), 0)

    def both_slots(mine, got):
        return lax.dynamic_update_slice(mine, got[None], (1 - core, 0, 0))

    def half_of(shard):
        width = shard.shape[1] // 2
        return lax.dynamic_slice_in_dim(shard, core * width, width, 1).astype(BF16)

    seats = grid.seats()

    turned = jnp.pad(vectors.T.astype(BF16), ((0, 0), (0, 128 - vec_count)))
    q_block = jnp.concatenate([half_of(w_qkv), turned], axis=1)
    u_block = jnp.concatenate([half_of(w_out), half_of(w_up)], axis=1)
    u_half = lax.all_gather(u_block, "dp", axis=0, tiled=True)
    d_half = lax.all_gather(half_of(w_down), "dp", axis=0, tiled=True)
    q_col = grid.gather_z(q_block)
    x = own_slot(block_in)
    q_line = grid.gather_first(q_col, x)
    q_rest = grid.gather_second(q_line)
    q_line_swap = grid.swap(q_line)
    q_rest_swap = [grid.swap(part) for part in q_rest]
    q_group = finish_group(grid, seats, [q_line] + q_rest, [q_line_swap] + q_rest_swap)

    h1, qkv, vec = qkv_call(core_arr, seats, x, q_group)
    og = own_slot(after(out_grad, qkv))
    att = attend_call(core_arr, lengths, qkv, 0, 4, ())
    u_half = after(u_half, *att)
    a, lse = attend_call(core_arr, lengths, after(qkv, u_half), 4, 2, att)
    u_group = Pieces([part[None, None] for part in (u_half, grid.swap(u_half))], u_half.shape[0], True)
    d_half = after(d_half, a)
    mid, h2, e, slope, dy = up_call(core_arr, lengths, seats, x, a, og, vec, u_group)
    d_group = Pieces([part[None, None] for part in (d_half, grid.swap(d_half))], d_half.shape[0], True)
    d_own, d_other = weight_grad_call(core_arr, [(e, [dy])], 512, "grad_down")
    dz, dmb, dm, da, acc_mid = down_call(core_arr, seats, mid, slope, dy, vec, u_group, d_group)

    d_total = after(grid.swap(d_other), dz) + d_own
    u_own, u_other = weight_grad_call(core_arr, [(a, [dmb]), (h2, [after(dz, d_total)])], 256, "grad_up")
    d_mine = lax.psum_scatter(d_total, "dp", scatter_dimension=0, tiled=True)

    def back_call(ready, start, before, *needs):
        return attend_back_call(core_arr, lengths, qkv, a, after(ready, *needs), lse, start, 2, before)

    def grad_qkv_call(ready, start, count, name):
        cols = (128 * count, start // count)
        return weight_grad_call(core_arr, [(h1, ready)], 256, name, "turns", cols)

    back = back_call(da, 0, (), u_own)
    u_total = after(grid.swap(u_other), *back) + u_own
    u_mine = lax.psum_scatter(u_total, "dp", scatter_dimension=0, tiled=True)
    back = back_call(da, 2, back, u_total)
    p_own, p_other = grad_qkv_call(back, 0, 4, "grad_qkv")
    back = back_call(da, 4, back, p_own)
    p_total = after(grid.swap(p_other), *back) + p_own
    dq, dk, dv = back
    r_own, r_other = grad_qkv_call([after(dq, p_total), dk, dv], 4, 2, "grad_qkv")
    p_kept = grid.scatter_first(p_total, r_own)
    in_theirs, acc = last_call(
        core_arr, seats, x, dm, after(dq, r_own, *p_kept[1]), dk, dv, vec, acc_mid, q_group, True
    )
    r_total = after(grid.swap(r_other), in_theirs) + r_own
    p_sum, p_here = grid.scatter_second(p_kept, in_theirs)
    in_mine, acc = last_call(
        core_arr, seats, x, dm, after(dq, r_total, *p_here), dk, dv, vec, acc, q_group, None
    )
    in_got = after(grid.swap(in_theirs), in_mine)
    r_kept = grid.scatter_first(r_total, in_mine)
    out_theirs = out_call(
        core_arr, lengths, seats, after(mid, in_mine, *r_kept[1]), e, vec, d_group, True
    )
    d_other_mine = grid.swap(after(d_mine, in_mine))
    u_other_mine = grid.swap(after(u_mine, out_theirs))
    p_mine = grid.scatter_z(p_sum, out_theirs)
    r_sum, r_here = grid.scatter_second(r_kept, out_theirs)
    out_mine = out_call(core_arr, lengths, seats, after(mid, *r_here), e, vec, d_group, None)
    out_got = after(grid.swap(out_theirs), out_mine)
    p_other_mine = grid.swap(p_mine)
    r_mine = grid.scatter_z(r_sum)
    r_other_mine = grid.swap(r_mine)
    vec_total = grid.total_small(acc, (out_theirs,), (out_mine,), (), ())
    block_out = both_slots(out_mine, out_got)
    in_grad = both_slots(in_mine, in_got)

    half, wide = D // 2, FF // 2
    down_new, = adam_call(
        core_arr,
        [(d_mine, d_other_mine)],
        [(after(w_down, out_theirs), first_down, second_down)],
        [(FF ** (-0.5), MATRIX_DECAY, [(0, 0, half, 0, half)])],
    )
    out_new, up_new = adam_call(
        core_arr,
        [(u_mine, u_other_mine)],
        [(after(w_out, in_grad, block_out), first_out, second_out), (w_up, first_up, second_up)],
        [
            ((D // 64) ** (-0.5), MATRIX_DECAY, [(0, 0, half, 0, half)]),
            (D ** (-0.5), MATRIX_DECAY, [(0, half, wide, 0, wide)]),
        ],
    )
    moves = []
    for part in range(3):
        for turn in range(2):
            at = part * D + turn * 256
            moves.append((0, (part * 2 + turn) * 128, 128, at, at + 128))
        moves.append((1, part * 128, 128, part * D + 512, part * D + 640))
    qkv_new, = adam_call(
        core_arr,
        [(p_mine, p_other_mine), (r_mine, r_other_mine)],
        [(w_qkv, first_qkv, second_qkv)],
        [(D ** (-0.5), MATRIX_DECAY, moves)],
    )
    vec_grad = lax.dynamic_slice(vec_total, (0, grid.chip * vec_here), (vec_count, vec_here))
    vec_new = adamw(vectors, vec_grad, first_vectors, second_vectors, VECTOR_RATE, 0.0)
    news = [qkv_new, out_new, up_new, down_new, vec_new]
    return (block_out, in_grad) + tuple(new[kind] for kind in range(3) for new in news)


def finish_group(grid, seats, own, other):
    rows, cols = own[0].shape[-2:]
    if rows % 16 == 0:
        return Pieces(own + other, rows)
    found = []
    for half, parts in enumerate((own, other)):
        here = seats[half * grid.chips : (half + 1) * grid.chips]
        order = jnp.zeros((grid.chips,), jnp.int32).at[here].set(jnp.arange(grid.chips, dtype=jnp.int32))
        blocks = jnp.concatenate(parts).reshape(grid.chips, rows, cols)
        found.append(jnp.take(blocks, order, axis=0).reshape(1, 1, grid.chips * rows, cols))
    return Pieces(found, grid.chips * rows, True)


def solution(mesh):
    weight = P("dp", None)
    vector = P(None, "dp")
    state = (weight, weight, weight, weight, vector)
    tokens = P("dp", "seq", None)
    return jax.shard_map(
        local,
        mesh=mesh,
        in_specs=(tokens, P("dp"), tokens) + state * 3,
        out_specs=(tokens, tokens) + state * 3,
        check_vma=False,
    )
```

```python
import functools

import jax
import jax.numpy as jnp
from jax import lax
from jax.experimental import pallas as pl
from jax.experimental.pallas import tpu as pltpu
from jax.sharding import PartitionSpec as P

D = 768
HEADS = 12
HEAD_DIM = 64
FF = 3072
STEP = 10

EPS_NORM = 1e-05
EPS_ADAM = 1e-08
BETA_ONE = 0.5
BETA_TWO = 0.5
MATRIX_DECAY = 0.1
VECTOR_RATE = 0.1
NEG_FILL = -1e30
GELU_ROOT = 0.7978845608028654
GELU_CUBE = 0.044715
QKV_HALF = 3 * D // 2

F32 = jnp.float32
BF16 = jnp.bfloat16

NN = (((1,), (0,)), ((), ()))
NT = (((1,), (1,)), ((), ()))
TN = (((0,), (0,)), ((), ()))


def mm(left, right, dims=NN):
    return lax.dot_general(left, right, dims, preferred_element_type=F32)


def cost(flops, nbytes, trans=0):
    return pl.CostEstimate(flops=int(flops), bytes_accessed=int(nbytes), transcendentals=int(trans))


def params():
    return pltpu.CompilerParams(vmem_limit_bytes=60 * 1024 * 1024)


def whole_spec(shape):
    return pl.BlockSpec(shape, lambda *idx: (0,) * len(shape), pipeline_mode=pl.Buffered(1))


class Pieces:
    def __init__(self, arrays, rows, ordered=False):
        self.arrays = arrays
        self.rows = rows
        self.ordered = ordered
        self.halves = 2
        self.count = len(arrays) // self.halves
        self.lines, self.depth = arrays[0].shape[:2]

    def specs(self):
        return [pl.BlockSpec(memory_space=pltpu.HBM)] * len(self.arrays)

    def row(self, seat_ref, at):
        return 0 if self.ordered else pl.multiple_of(seat_ref[at] * self.rows, 16)

    def start(self, refs, core_ref, seat_ref, start_col, width, target, sem):
        core = core_ref[0]
        at = 0
        for half in range(self.halves):
            where = core if half == 0 else 1 - core
            for s2 in range(self.count):
                ref = refs[half * self.count + s2]
                for s1 in range(self.lines):
                    for sz in range(self.depth):
                        row = self.row(seat_ref, at)
                        at += 1
                        col = pl.multiple_of(where * width, 128)
                        pltpu.make_async_copy(
                            ref.at[s1, sz, :, pl.ds(start_col, width)],
                            target.at[pl.ds(row, self.rows), pl.ds(col, width)],
                            sem,
                        ).start()

    def start_once(self, refs, seat_ref, start_col, width, target, sem):
        at = 0
        for s2 in range(self.count):
            for s1 in range(self.lines):
                for sz in range(self.depth):
                    row = self.row(seat_ref, at)
                    at += 1
                    pltpu.make_async_copy(
                        refs[s2].at[s1, sz, :, pl.ds(start_col, width)],
                        target.at[pl.ds(row, self.rows), :],
                        sem,
                    ).start()


def wait_all(target, sem):
    pltpu.make_async_copy(target, target, sem).wait()


def norm_parts(rows):
    mean = jnp.mean(rows, axis=-1, keepdims=True)
    centred = rows - mean
    variance = jnp.mean(centred * centred, axis=-1, keepdims=True)
    scale = lax.rsqrt(variance + EPS_NORM)
    return centred * scale, scale


def norm_back(d_normed, normed, scale):
    first = jnp.mean(d_normed, axis=-1, keepdims=True)
    second = jnp.mean(d_normed * normed, axis=-1, keepdims=True)
    return scale * (d_normed - first - normed * second)


def qkv_kernel(group, core_ref, seat_ref, x_ref, *refs):
    refs, (h_ref, qkv_ref, vec_ref, w_ref, turned_ref, sems) = refs[:-6], refs[-6:]

    @pl.when(pl.program_id(0) == 0)
    def _():
        group.start(refs, core_ref, seat_ref, 0, QKV_HALF, w_ref, sems.at[0])
        group.start_once(refs, seat_ref, QKV_HALF, 128, turned_ref, sems.at[1])
        wait_all(turned_ref, sems.at[1])
        vec_ref[...] = turned_ref[...].astype(F32).T[:16]
        wait_all(w_ref, sems.at[0])

    normed, _ = norm_parts(x_ref[...].astype(F32))
    h = (normed * vec_ref[0:1, :] + vec_ref[1:2, :]).astype(BF16)
    h_ref[...] = h
    qkv_ref[:, :D] = (mm(h, w_ref[:, :D]) + vec_ref[2:3, :]).astype(BF16)
    qkv_ref[:, D : 2 * D] = mm(h, w_ref[:, D : 2 * D]).astype(BF16)
    qkv_ref[:, 2 * D :] = (mm(h, w_ref[:, 2 * D :]) + vec_ref[3:4, :]).astype(BF16)


def qkv_call(core, seats, x, group, block=256):
    rows = x.shape[0]
    return pl.pallas_call(
        functools.partial(qkv_kernel, group),
        name="qkv",
        grid_spec=pltpu.PrefetchScalarGridSpec(
            num_scalar_prefetch=2,
            grid=(rows // block,),
            in_specs=[pl.BlockSpec((block, D), lambda i, *s: (i, 0))] + group.specs(),
            out_specs=[
                pl.BlockSpec((block, D), lambda i, *s: (i, 0)),
                pl.BlockSpec((block, 3 * D), lambda i, *s: (i, 0)),
                pl.BlockSpec((16, D), lambda i, *s: (0, 0)),
            ],
            scratch_shapes=[
                pltpu.VMEM((D, 3 * D), BF16),
                pltpu.VMEM((D, 128), BF16),
                pltpu.SemaphoreType.DMA((2,)),
            ],
        ),
        out_shape=[
            jax.ShapeDtypeStruct((rows, D), BF16),
            jax.ShapeDtypeStruct((rows, 3 * D), BF16),
            jax.ShapeDtypeStruct((16, D), F32),
        ],
        compiler_params=params(),
        cost_estimate=cost(2 * rows * D * 3 * D, 10e6),
    )(core, seats, x, *group.arrays)


def head_parts(length, q_all, k_all, head):
    full_len = q_all.shape[0]
    lane = lax.broadcasted_iota(jnp.int32, (1, 128), 1)
    mine = (lane // HEAD_DIM) == head
    spare = lane == HEAD_DIM * (1 - head)
    pos = lax.broadcasted_iota(jnp.int32, (full_len, 128), 0)
    fill = jnp.where(pos < length, 0.0, NEG_FILL).astype(BF16)
    zero = jnp.zeros((), BF16)
    k_head = jnp.where(mine, k_all, jnp.where(spare, fill, zero))
    q_plain = jnp.where(mine, q_all, zero)
    q_head = jnp.where(spare, jnp.ones((), BF16), q_plain)
    return mine, k_head, q_plain, q_head


def causal_mask(scores, block):
    full = scores.shape[0]
    key_pos = lax.broadcasted_iota(jnp.int32, (block, block), 0)
    query_pos = lax.broadcasted_iota(jnp.int32, (block, block), 1)
    last = jnp.where(key_pos <= query_pos, scores[full - block :], NEG_FILL)
    if full == block:
        return last
    return jnp.concatenate([scores[: full - block], last], axis=0)


def attend_kernel(core_ref, len_ref, q_ref, k_ref, v_ref, *refs):
    a_ref, lse_ref, mixed_ref = refs[-3:]
    block = 256
    full_len = q_ref.shape[0]
    length = len_ref[core_ref[0]]
    q_all = q_ref[...] * jnp.asarray(HEAD_DIM ** (-0.5), BF16)
    k_all = k_ref[...]
    v_turned = v_ref[...].T
    for head in range(2):
        _, k_head, _, q_head = head_parts(length, q_all, k_all, head)
        v_head = v_turned[head * HEAD_DIM : (head + 1) * HEAD_DIM]
        for j in range(full_len // block):
            cols = slice(j * block, (j + 1) * block)
            span = (j + 1) * block
            scores = causal_mask(mm(k_head[:span], q_head[cols], NT), block)
            top = jnp.max(scores, axis=0, keepdims=True)
            exped = jnp.exp(scores - top)
            total = jnp.sum(exped, axis=0, keepdims=True)
            mixed = mm(v_head[:, :span], exped.astype(BF16)) / total
            mixed_ref[head * HEAD_DIM : (head + 1) * HEAD_DIM, cols] = mixed
            lse_ref[0, head : head + 1, cols] = top + jnp.log(total)
    a_ref[...] = mixed_ref[...].T.astype(BF16)


def attend_call(core, lengths, qkv, first, count, before):
    rows = qkv.shape[0]
    pairs = HEADS // 2
    before = list(before)
    return pl.pallas_call(
        attend_kernel,
        name="attend",
        grid_spec=pltpu.PrefetchScalarGridSpec(
            num_scalar_prefetch=2,
            grid=(count,),
            in_specs=[
                pl.BlockSpec((rows, 128), lambda i, c, n: (0, i + first)),
                pl.BlockSpec((rows, 128), lambda i, c, n: (0, i + first + pairs)),
                pl.BlockSpec((rows, 128), lambda i, c, n: (0, i + first + 2 * pairs)),
            ]
            + [pl.BlockSpec(memory_space=pl.ANY)] * len(before),
            out_specs=[
                pl.BlockSpec((rows, 128), lambda i, c, n: (0, i + first)),
                pl.BlockSpec((1, 8, rows), lambda i, c, n: (i + first, 0, 0)),
            ],
            scratch_shapes=[pltpu.VMEM((128, rows), F32)],
        ),
        out_shape=[
            jax.ShapeDtypeStruct((rows, D), BF16),
            jax.ShapeDtypeStruct((pairs, 8, rows), F32),
        ],
        input_output_aliases={5 + i: i for i in range(len(before))},
        compiler_params=params(),
        cost_estimate=cost(3e9 * count, 1.2e6 * count, 2 * rows * rows * 0.6 * count),
    )(core, lengths, qkv, qkv, qkv, *before)


def attend_back_kernel(core_ref, len_ref, q_ref, k_ref, v_ref, a_ref, da_ref, lse_ref, *refs):
    dq_ref, dk_ref, dv_ref, dqt_ref, dk_acc, dv_acc = refs[-6:]
    block = 256
    full_len = q_ref.shape[0]
    length = len_ref[core_ref[0]]
    scale = HEAD_DIM ** (-0.5)
    q_all = q_ref[...] * jnp.asarray(scale, BF16)
    k_all = k_ref[...]
    k_turned = k_all.T
    v_all = v_ref[...]
    da_all = da_ref[...]
    inner = (da_all.astype(F32) * a_ref[...].astype(F32)).T
    first = True
    for head in range(2):
        mine, k_head, q_plain, q_head = head_parts(length, q_all, k_all, head)
        da_head = jnp.where(mine, da_all, jnp.zeros((), BF16))
        lanes = slice(head * HEAD_DIM, (head + 1) * HEAD_DIM)
        centre = jnp.sum(inner[lanes], axis=0, keepdims=True)
        for j in reversed(range(full_len // block)):
            cols = slice(j * block, (j + 1) * block)
            span = (j + 1) * block
            scores = causal_mask(mm(k_head[:span], q_head[cols], NT), block)
            probs = jnp.exp(scores - lse_ref[0, head : head + 1, cols])
            d_probs = mm(v_all[:span], da_head[cols], NT)
            d_scores = (probs * (d_probs - centre[:, cols])).astype(BF16)
            dv_part = mm(probs.astype(BF16), da_head[cols])
            dk_part = mm(d_scores, q_plain[cols])
            if first:
                dv_acc[...] = dv_part
                dk_acc[...] = dk_part
                first = False
            else:
                dv_acc[:span] += dv_part
                dk_acc[:span] += dk_part
            dqt_ref[lanes, cols] = mm(k_turned[lanes, :span], d_scores) * scale
    dq_ref[...] = dqt_ref[...].T.astype(BF16)
    dk_ref[...] = dk_acc[...].astype(BF16)
    dv_ref[...] = dv_acc[...].astype(BF16)


def attend_back_call(core, lengths, qkv, a, da, lse, start, count, before):
    rows = qkv.shape[0]
    pairs = HEADS // 2
    before = list(before)
    pair_spec = pl.BlockSpec((rows, 128), lambda i, c, n: (0, i + start))
    return pl.pallas_call(
        attend_back_kernel,
        name="attend_back",
        grid_spec=pltpu.PrefetchScalarGridSpec(
            num_scalar_prefetch=2,
            grid=(count,),
            in_specs=[
                pair_spec,
                pl.BlockSpec((rows, 128), lambda i, c, n: (0, i + start + pairs)),
                pl.BlockSpec((rows, 128), lambda i, c, n: (0, i + start + 2 * pairs)),
                pair_spec,
                pair_spec,
                pl.BlockSpec((1, 8, rows), lambda i, c, n: (i + start, 0, 0)),
            ]
            + [pl.BlockSpec(memory_space=pl.ANY)] * len(before),
            out_specs=[pair_spec, pair_spec, pair_spec],
            scratch_shapes=[
                pltpu.VMEM((128, rows), F32),
                pltpu.VMEM((rows, 128), F32),
                pltpu.VMEM((rows, 128), F32),
            ],
        ),
        out_shape=[jax.ShapeDtypeStruct((rows, D), BF16)] * 3,
        input_output_aliases={8 + i: i for i in range(len(before))},
        compiler_params=params(),
        cost_estimate=cost(6e9 * count, 2e6 * count, 2 * rows * rows * 0.6 * count),
    )(core, lengths, qkv, qkv, qkv, a, da, lse, *before)


def valid_rows(core_ref, len_ref, block):
    pos = pl.program_id(0) * block + lax.broadcasted_iota(jnp.int32, (block, 1), 0)
    return pos < len_ref[core_ref[0]]


def add_row(acc_ref, row, value):
    acc_ref[row : row + 1, :] += jnp.sum(value, axis=0, keepdims=True)


def row_block(core, i, steps):
    half = steps // 2
    return jnp.where(i < half, (1 - core) * half + i, core * half + i - half)


def up_kernel(group, core_ref, len_ref, seat_ref, x_ref, a_ref, og_ref, vec_ref, *refs):
    refs, (mid_ref, h_ref, e_ref, slope_ref, dy_ref, wo_ref, wu_ref, sems) = refs[:-8], refs[-8:]
    block = x_ref.shape[0]

    @pl.when(pl.program_id(0) == 0)
    def _():
        group.start(refs, core_ref, seat_ref, 0, D // 2, wo_ref, sems.at[0])
        group.start(refs, core_ref, seat_ref, D // 2, FF // 2, wu_ref, sems.at[1])
        wait_all(wo_ref, sems.at[0])
        wait_all(wu_ref, sems.at[1])

    valid = valid_rows(core_ref, len_ref, block)
    dy_ref[...] = jnp.where(valid, og_ref[...].astype(F32), 0.0).astype(BF16)
    mid = x_ref[...].astype(F32) + mm(a_ref[...], wo_ref[...]) + vec_ref[4:5, :]
    mid_ref[...] = mid
    normed, _ = norm_parts(mid)
    h = (normed * vec_ref[5:6, :] + vec_ref[6:7, :]).astype(BF16)
    h_ref[...] = h
    for j in range(FF // D):
        cols = slice(j * D, (j + 1) * D)
        z = mm(h, wu_ref[:, cols]) + vec_ref[8 + j : 9 + j, :]
        squared = z * z
        turned = jnp.tanh(z * (GELU_ROOT + (GELU_ROOT * GELU_CUBE) * squared))
        half = 0.5 * turned + 0.5
        act = z * half
        e_ref[:, cols] = act.astype(BF16)
        slope = half + act * (1.0 - turned) * (GELU_ROOT + (3.0 * GELU_ROOT * GELU_CUBE) * squared)
        slope_ref[:, cols] = slope.astype(BF16)


def up_call(core, lengths, seats, x, a, og, vec, group, block=256):
    rows = x.shape[0]
    row_spec = pl.BlockSpec((block, D), lambda i, *s: (i, 0))
    wide_spec = pl.BlockSpec((block, FF), lambda i, *s: (i, 0))
    low = jax.ShapeDtypeStruct((rows, D), BF16)
    return pl.pallas_call(
        functools.partial(up_kernel, group),
        name="up",
        grid_spec=pltpu.PrefetchScalarGridSpec(
            num_scalar_prefetch=3,
            grid=(rows // block,),
            in_specs=[row_spec, row_spec, row_spec, whole_spec(vec.shape)] + group.specs(),
            out_specs=[row_spec, row_spec, wide_spec, wide_spec, row_spec],
            scratch_shapes=[
                pltpu.VMEM((D, D), BF16),
                pltpu.VMEM((D, FF), BF16),
                pltpu.SemaphoreType.DMA((2,)),
            ],
        ),
        out_shape=[
            jax.ShapeDtypeStruct((rows, D), F32),
            low,
            jax.ShapeDtypeStruct((rows, FF), BF16),
            jax.ShapeDtypeStruct((rows, FF), BF16),
            low,
        ],
        compiler_params=params(),
        cost_estimate=cost(6e9, 30e6, rows * FF),
    )(core, lengths, seats, x, a, og, vec, *group.arrays)


def down_kernel(up_group, down_group, core_ref, len_ref, seat_ref, mid_ref, e_ref, slope_ref, dy_ref, vec_ref, *refs):
    count = len(up_group.arrays)
    up_refs, down_refs = refs[:count], refs[count : count + len(down_group.arrays)]
    (
        theirs_ref, mine_ref, dz_ref, dmb_ref, dm_ref, da_ref, acc_ref, wo_ref, wu_ref, wd_ref, sems,
    ) = refs[-11:]
    block = mid_ref.shape[0]
    step, steps = pl.program_id(0), pl.num_programs(0)

    @pl.when(pl.program_id(0) == 0)
    def _():
        down_group.start(down_refs, core_ref, seat_ref, 0, D // 2, wd_ref, sems.at[2])
        up_group.start(up_refs, core_ref, seat_ref, D // 2, FF // 2, wu_ref, sems.at[1])
        up_group.start(up_refs, core_ref, seat_ref, 0, D // 2, wo_ref, sems.at[0])
        acc_ref[...] = jnp.zeros_like(acc_ref)
        wait_all(wd_ref, sems.at[2])

    mid = mid_ref[...]
    normed, scale = norm_parts(mid)
    pos = row_block(core_ref[0], step, steps) * block + lax.broadcasted_iota(jnp.int32, (block, 1), 0)
    down = vec_ref[7:8, :] + mid + mm(e_ref[...], wd_ref[...])
    down = jnp.where(pos < len_ref[core_ref[0]], down, 0.0).astype(BF16)

    @pl.when(step < steps // 2)
    def _():
        theirs_ref[...] = down

    @pl.when(step >= steps // 2)
    def _():
        mine_ref[0] = down

    @pl.when(step == 0)
    def _():
        wait_all(wu_ref, sems.at[1])
        wait_all(wo_ref, sems.at[0])

    dy_low = dy_ref[...]
    dy = dy_low.astype(F32)
    add_row(acc_ref, 7, dy)
    dh = jnp.zeros((block, D), F32)
    for j in range(FF // D):
        cols = slice(j * D, (j + 1) * D)
        dz = (mm(dy_low, wd_ref[cols, :], NT) * slope_ref[:, cols].astype(F32)).astype(BF16)
        dz_ref[:, cols] = dz
        add_row(acc_ref, 8 + j, dz.astype(F32))
        dh += mm(dz, wu_ref[:, cols], NT)
    add_row(acc_ref, 5, dh * normed)
    add_row(acc_ref, 6, dh)
    dm = dy + norm_back(dh * vec_ref[5:6, :], normed, scale)
    dm_ref[...] = dm
    dm_low = dm.astype(BF16)
    dmb_ref[...] = dm_low
    add_row(acc_ref, 4, dm_low.astype(F32))
    da_ref[...] = mm(dm_low, wo_ref[...], NT).astype(BF16)


def down_call(core, lengths, seats, mid, e, slope, dy, vec, up_group, down_group, block=256):
    rows = mid.shape[0]
    steps = rows // block
    half = steps // 2
    row_spec = pl.BlockSpec((block, D), lambda i, c, *s: (row_block(c[0], i, steps), 0))
    wide_spec = pl.BlockSpec((block, FF), lambda i, c, *s: (row_block(c[0], i, steps), 0))
    low = jax.ShapeDtypeStruct((rows, D), BF16)
    return pl.pallas_call(
        functools.partial(down_kernel, up_group, down_group),
        name="down",
        grid_spec=pltpu.PrefetchScalarGridSpec(
            num_scalar_prefetch=3,
            grid=(steps,),
            in_specs=[row_spec, wide_spec, wide_spec, row_spec, whole_spec(vec.shape)]
            + up_group.specs()
            + down_group.specs(),
            out_specs=[
                pl.BlockSpec((block, D), lambda i, *s: (jnp.minimum(i, half - 1), 0)),
                pl.BlockSpec((1, block, D), lambda i, c, *s: (c[0], jnp.maximum(i - half, 0), 0)),
                wide_spec, row_spec, row_spec, row_spec,
                pl.BlockSpec((16, D), lambda i, *s: (0, 0)),
            ],
            scratch_shapes=[
                pltpu.VMEM((D, D), BF16),
                pltpu.VMEM((D, FF), BF16),
                pltpu.VMEM((FF, D), BF16),
                pltpu.SemaphoreType.DMA((3,)),
            ],
        ),
        out_shape=[
            jax.ShapeDtypeStruct((rows // 2, D), BF16),
            jax.ShapeDtypeStruct((2, rows // 2, D), BF16),
            jax.ShapeDtypeStruct((rows, FF), BF16), low, jax.ShapeDtypeStruct((rows, D), F32), low,
            jax.ShapeDtypeStruct((16, D), F32),
        ],
        compiler_params=params(),
        cost_estimate=cost(1.6e10, 35e6),
    )(core, lengths, seats, mid, e, slope, dy, vec, *up_group.arrays, *down_group.arrays)


def half_specs(first, steps, block):
    def half(core):
        return core[0] if first is None else 1 - core[0]

    def rows(width):
        return pl.BlockSpec((block, width), lambda i, c, *s: (half(c) * steps + i, 0))

    if first is None:
        out = pl.BlockSpec((1, block, D), lambda i, c, *s: (c[0], i, 0))
    else:
        out = pl.BlockSpec((block, D), lambda i, c, *s: (i, 0))
    return rows, out


def pick(values, half, mode):
    if mode == "split":
        width = values.shape[1] // 2
        return [values[:, half * width : (half + 1) * width]]
    return [values[:, at : at + 128] for at in range(half * 128, values.shape[1], 256)]


def weight_grad_kernel(lefts, rights, mode, core_ref, *refs):
    left_refs, right_refs = refs[:lefts], refs[lefts : lefts + sum(rights)]
    own_ref, other_ref = refs[-2:]
    halves = ([], [])
    at = 0
    for left_ref, count in zip(left_refs, rights):
        left = left_ref[...]
        for right_ref in right_refs[at : at + count]:
            whole = mm(left, right_ref[...], TN).astype(BF16)
            for half in range(2):
                halves[half].extend(pick(whole, half, mode))
        at += count
    low, high = [part[0] if len(part) == 1 else jnp.concatenate(part, axis=1) for part in halves]

    @pl.when(core_ref[0] == 0)
    def _():
        own_ref[...] = low
        other_ref[...] = high

    @pl.when(core_ref[0] != 0)
    def _():
        own_ref[...] = high
        other_ref[...] = low


def weight_grad_call(core, products, block, name, mode="split", cols=None):
    rows, height = products[0][0].shape
    lefts = [left for left, _ in products]
    rights = [right for _, group in products for right in group]
    widths = [right.shape[1] if cols is None else cols[0] for right in rights]
    width = sum(widths)
    seat = 0 if cols is None else cols[1]
    return pl.pallas_call(
        functools.partial(weight_grad_kernel, len(lefts), [len(group) for _, group in products], mode),
        name=name,
        grid_spec=pltpu.PrefetchScalarGridSpec(
            num_scalar_prefetch=1,
            grid=(height // block,),
            in_specs=[pl.BlockSpec((rows, block), lambda i, c: (0, i))] * len(lefts)
            + [
                pl.BlockSpec((rows, w), lambda i, c: (0, seat), pipeline_mode=pl.Buffered(1)) for w in widths
            ],
            out_specs=[pl.BlockSpec((block, width // 2), lambda i, c: (i, 0))] * 2,
        ),
        out_shape=[jax.ShapeDtypeStruct((height, width // 2), BF16)] * 2,
        compiler_params=params(),
        cost_estimate=cost(2 * rows * height * width, rows * (height + width) * 2 + height * width * 2),
    )(core, *lefts, *rights)


def last_kernel(group, first, core_ref, seat_ref, x_ref, dm_ref, dq_ref, dk_ref, dv_ref, vec_ref, before_ref, *refs):
    refs, (grad_ref, acc_ref, w_ref, sems) = refs[:-4], refs[-4:]

    @pl.when(pl.program_id(0) == 0)
    def _():
        group.start(refs, core_ref, seat_ref, 0, QKV_HALF, w_ref, sems.at[0])
        acc_ref[...] = before_ref[...]
        wait_all(w_ref, sems.at[0])

    normed, scale = norm_parts(x_ref[...].astype(F32))
    dq, dk, dv = dq_ref[...], dk_ref[...], dv_ref[...]
    dh = (
        mm(dq, w_ref[:, :D], NT)
        + mm(dk, w_ref[:, D : 2 * D], NT)
        + mm(dv, w_ref[:, 2 * D :], NT)
    )
    add_row(acc_ref, 0, dh * normed)
    add_row(acc_ref, 1, dh)
    add_row(acc_ref, 2, dq.astype(F32))
    add_row(acc_ref, 3, dv.astype(F32))
    grad = dm_ref[...] + norm_back(dh * vec_ref[0:1, :], normed, scale)
    if first is None:
        grad_ref[0] = grad
    else:
        grad_ref[...] = grad


def last_call(core, seats, x, dm, dq, dk, dv, vec, before, group, first, block=256):
    half_len = x.shape[0] // 2
    steps = half_len // block
    rows, out_spec = half_specs(first, steps, block)
    shape = (2, half_len, D) if first is None else (half_len, D)
    return pl.pallas_call(
        functools.partial(last_kernel, group, first),
        name="last",
        grid_spec=pltpu.PrefetchScalarGridSpec(
            num_scalar_prefetch=2,
            grid=(steps,),
            in_specs=[rows(D)] * 5 + [whole_spec(vec.shape), whole_spec(before.shape)] + group.specs(),
            out_specs=[out_spec, pl.BlockSpec((16, D), lambda i, *s: (0, 0))],
            scratch_shapes=[pltpu.VMEM((D, 3 * D), BF16), pltpu.SemaphoreType.DMA((1,))],
        ),
        out_shape=[jax.ShapeDtypeStruct(shape, F32), jax.ShapeDtypeStruct((16, D), F32)],
        compiler_params=params(),
        cost_estimate=cost(half_len * 6 * D * D, 10e6),
    )(core, seats, x, dm, dq, dk, dv, vec, before, *group.arrays)


def adam_kernel(plans, sources, core_ref, *refs):
    halves = [refs[2 * i : 2 * i + 2] for i in range(sources)]
    count = len(plans)
    states = refs[2 * sources : 2 * sources + 3 * count]
    outs = refs[2 * sources + 3 * count : 2 * sources + 6 * count]
    grads = refs[2 * sources + 6 * count :]
    for core in range(2):

        @pl.when(core_ref[0] == core)
        def _():
            for (_, _, moves), grad_ref in zip(plans, grads):
                for source, start, width, place0, place1 in moves:
                    for half, place in ((0, place0), (1, place1)):
                        ref = halves[source][0 if half == core else 1]
                        grad_ref[:, place : place + width] = ref[:, start : start + width].astype(F32)

    for i, (rate, decay, _) in enumerate(plans):
        weight, first, second = states[3 * i : 3 * i + 3]
        new = adamw(weight[...], grads[i][...], first[...], second[...], rate, decay)
        for out, value in zip(outs[3 * i : 3 * i + 3], new):
            out[...] = value


def adam_call(core, halves, states, plans):
    flat = [part for pair in halves for part in pair]
    held = [part for state in states for part in state]
    spec = pl.BlockSpec(memory_space=pltpu.VMEM)
    news = pl.pallas_call(
        functools.partial(adam_kernel, plans, len(halves)),
        name="adam",
        in_specs=[pl.BlockSpec(memory_space=pltpu.SMEM)] + [spec] * (len(flat) + len(held)),
        out_specs=[spec] * len(held),
        out_shape=[jax.ShapeDtypeStruct(part.shape, F32) for part in held],
        scratch_shapes=[pltpu.VMEM(state[0].shape, F32) for state in states],
        compiler_params=params(),
        cost_estimate=cost(1e6, 24 * sum(state[0].size for state in states)),
    )(core, *flat, *held)
    return [news[3 * i : 3 * i + 3] for i in range(len(states))]


def after(value, *others):
    if not others:
        return value
    return lax.optimization_barrier((value,) + others)[0]


class Grid:
    def __init__(self, chips):
        log = chips.bit_length() - 1
        side = 1 << (log // 3)
        if side * side * (chips // (side * side)) != chips:
            side = 1
        self.chips = chips
        self.n = side
        self.nz = chips // (side * side)
        self.core = lax.axis_index("seq")
        self.chip = lax.axis_index("dp")
        self.x = self.chip % side
        self.y = self.chip // side % side
        self.z = self.chip // (side * side)

    def plane(self, first, second, core):
        return jnp.where(core == 0, second * self.n + first, first * self.n + second)

    def coords(self, core):
        return jnp.where(core == 0, self.x, self.y), jnp.where(core == 0, self.y, self.x)

    def permute(self, value, axis, shift=0):
        pairs = []
        for chip in range(self.chips):
            for core in range(2):
                x, y, z = chip % self.n, chip // self.n % self.n, chip // (self.n * self.n)
                to_core = core
                if axis == "z":
                    z = (z + shift) % self.nz
                elif axis == "zx":
                    z = z ^ shift
                elif axis == "core":
                    to_core = 1 - core
                elif (axis == "first") == (core == 0):
                    x = (x + shift) % self.n
                else:
                    y = (y + shift) % self.n
                pairs.append((chip * 2 + core, ((z * self.n + y) * self.n + x) * 2 + to_core))
        return lax.ppermute(value, ("dp", "seq"), pairs)

    def swap(self, value):
        return self.permute(value, "core")

    def join(self, own, other, axis):
        return jnp.where(
            self.core == 0,
            jnp.concatenate([own, other], axis),
            jnp.concatenate([other, own], axis),
        )

    def seats(self, halving):
        found = []
        for half in range(2):
            core = self.core if half == 0 else 1 - self.core
            first, second = self.coords(core)
            for s2 in range(self.n):
                for s1 in range(self.n):
                    flat = self.plane((first - s1) % self.n, (second - s2) % self.n, core)
                    for sz in range(self.nz):
                        z = self.z ^ sz if halving else (self.z - sz) % self.nz
                        found.append(z * self.n * self.n + flat)
        return jnp.stack(found).astype(jnp.int32)

    def total_small(self, value, *untils):
        steps = [("core", 0), ("first", 1), ("second", 1)] if self.n == 2 else [("core", 0)]
        if self.n != 2:
            for axis in ("first", "second"):
                value = value + sum(self.permute(value, axis, s) for s in range(1, self.n))
        bit = 1
        while bit < self.nz:
            steps.append(("zx", bit))
            bit *= 2
        for at, (axis, shift) in enumerate(steps):
            until = untils[at] if at < len(untils) else ()
            value = value + after(self.permute(value, axis, shift), *until)
        return value

    def gather_z(self, block, *until):
        return jnp.stack([block] + [after(self.permute(block, "z", s), *until) for s in range(1, self.nz)])

    def gather_bit(self, held, bit, *until):
        return jnp.concatenate([held, after(self.permute(held, "zx", bit), *until)])

    def gather_first(self, column, *until):
        return jnp.stack([column] + [after(self.permute(column, "first", s), *until) for s in range(1, self.n)])

    def gather_second(self, line, *until):
        return [after(self.permute(line, "second", s), *until) for s in range(1, self.n)]

    def scatter_first(self, own, pair, *until):
        rows, cols = own.shape[0] // self.chips, own.shape[1]
        first, second = self.coords(self.core)
        n = self.n

        def seat(s1, s2):
            where = self.plane((first + s1) % n, (second + s2) % n, self.core)
            own_part, pair_part = [
                lax.dynamic_slice(
                    part.reshape(self.nz, n * n, rows, cols), (0, where, 0, 0), (self.nz, 1, rows, cols)
                ).astype(F32)
                for part in (own, pair)
            ]
            return own_part + pair_part

        kept = [seat(0, t) for t in range(n)]
        for s in range(1, n):
            send = jnp.stack([seat(s, t).astype(BF16) for t in range(n)])
            got = after(self.permute(send, "first", s), *until)
            kept = [kept[t] + got[t].astype(F32) for t in range(n)]
        return kept[0], [part.astype(BF16) for part in kept[1:]]

    def scatter_second(self, kept, *until):
        mine, rest = kept
        got = [after(self.permute(rest[s - 1], "second", s), *until) for s in range(1, self.n)]
        for part in got:
            mine = mine + part.astype(F32)
        return mine.reshape((self.nz,) + mine.shape[2:]), got

    def order_z(self, mine):
        return [lax.dynamic_index_in_dim(mine, self.z ^ at, 0, keepdims=False) for at in range(self.nz)]

    def scatter_bit(self, parts, *until):
        half = len(parts) // 2
        send = parts[half] if half == 1 else jnp.stack([part.astype(BF16) for part in parts[half:]])
        got = after(self.permute(send.astype(BF16), "zx", half), *until)
        if half == 1:
            return [parts[0] + got.astype(F32)], got
        return [part + got[at].astype(F32) for at, part in enumerate(parts[:half])], got

    def scatter_z(self, parts):
        while len(parts) > 1:
            parts, _ = self.scatter_bit(parts)
        return parts[0]


def adamw(weight, gradient, first_moment, second_moment, step_rate, weight_decay):
    first_moment = BETA_ONE * first_moment + (1.0 - BETA_ONE) * gradient
    second_moment = BETA_TWO * second_moment + (1.0 - BETA_TWO) * gradient * gradient
    first_fix = 1.0 - BETA_ONE**STEP
    second_fix = 1.0 - BETA_TWO**STEP
    direction = first_moment / first_fix / (jnp.sqrt(second_moment / second_fix) + EPS_ADAM)
    return (weight - step_rate * (direction + weight_decay * weight), first_moment, second_moment)


def local(
    block_in, lengths, out_grad, w_qkv, w_out, w_up, w_down, vectors,
    first_qkv, first_out, first_up, first_down, first_vectors,
    second_qkv, second_out, second_up, second_down, second_vectors,
):
    grid = Grid(lax.axis_size("dp"))
    core = grid.core
    core_arr = core.reshape(1).astype(jnp.int32)
    half_len = block_in.shape[1]
    vec_count, vec_here = vectors.shape

    def own_slot(halves):
        mine = lax.dynamic_index_in_dim(halves, core, 0, keepdims=False)
        theirs = lax.dynamic_index_in_dim(halves, 1 - core, 0, keepdims=False)
        return grid.join(mine, grid.swap(theirs), 0)

    def both_slots(mine, got):
        return lax.dynamic_update_slice(mine, got[None], (1 - core, 0, 0))

    def half_of(shard):
        width = shard.shape[1] // 2
        return lax.dynamic_slice_in_dim(shard, core * width, width, 1).astype(BF16)

    seats, q_seats = grid.seats(True), grid.seats(False)

    turned = jnp.pad(vectors.T.astype(BF16), ((0, 0), (0, 128 - vec_count)))
    q_block = jnp.concatenate([half_of(w_qkv), turned], axis=1)
    u_block = jnp.concatenate([half_of(w_out), half_of(w_up)], axis=1)
    d_col = half_of(w_down)[None]
    q_col = grid.gather_z(q_block)
    x = own_slot(block_in)
    q_line = grid.gather_first(q_col, x)
    u_col = u_block[None]
    bits = [1 << at for at in range((grid.nz - 1).bit_length())]
    for bit in bits[:-1]:
        u_col = grid.gather_bit(u_col, bit)
        d_col = grid.gather_bit(d_col, bit)
    q_rest = grid.gather_second(q_line)
    q_line_swap = grid.swap(q_line)
    q_rest_swap = [grid.swap(after(part, u_col, d_col)) for part in q_rest]
    q_group = finish_group(grid, q_seats, [q_line] + q_rest, [q_line_swap] + q_rest_swap)

    h1, qkv, vec = qkv_call(core_arr, q_seats, x, q_group)
    u_col = grid.gather_bit(after(u_col, *q_rest), bits[-1], qkv)
    og = own_slot(after(out_grad, qkv))
    att = attend_call(core_arr, lengths, after(qkv, u_col), 0, 2, ())
    u_line = grid.gather_first(u_col, *att)
    att = attend_call(core_arr, lengths, after(qkv, u_line), 2, 3, att)
    u_line_swap = after(grid.swap(u_line), *att)
    u_rest = grid.gather_second(u_line, *att)
    d_col = after(grid.gather_bit(after(d_col, u_col), bits[-1], *att), *u_rest)
    a, lse = attend_call(core_arr, lengths, after(qkv, d_col), 5, 1, att)
    u_rest_swap = [after(grid.swap(part), a) for part in u_rest]
    d_line = grid.gather_first(d_col, a)
    u_group = finish_group(grid, seats, [u_line] + u_rest, [u_line_swap] + u_rest_swap)
    mid, h2, e, slope, dy = up_call(core_arr, lengths, seats, x, after(a, d_line), og, vec, u_group)
    d_line_swap = after(grid.swap(d_line), mid)
    d_rest = grid.gather_second(d_line, mid)
    d_own, d_other = weight_grad_call(core_arr, [(after(e, *d_rest), [dy])], 512, "grad_down")
    d_rest_swap = [after(grid.swap(part), d_own) for part in d_rest]
    d_group = finish_group(grid, seats, [d_line] + d_rest, [d_line_swap] + d_rest_swap)
    out_theirs, out_mine, dz, dmb, dm, da, acc_mid = down_call(
        core_arr, lengths, seats, mid, e, slope, dy, vec, u_group, d_group
    )

    d_pair = after(grid.swap(d_other), dz)
    u_own, u_other = weight_grad_call(
        core_arr, [(a, [dmb]), (h2, [after(dz, d_pair)])], 256, "grad_up"
    )
    d_kept = grid.scatter_first(d_own, d_pair, u_own)

    def back_call(start, count, before, *needs):
        return attend_back_call(core_arr, lengths, qkv, a, after(da, *needs), lse, start, count, before)

    back = back_call(0, 2, (), u_own, *d_kept[1])
    d_sum, d_here = grid.scatter_second(d_kept, *back)
    u_pair = after(grid.swap(u_other), *back)
    back = back_call(2, 2, back, u_pair, *d_here)
    d_parts, d_got = grid.scatter_bit(grid.order_z(d_sum), *back)
    back = back_call(4, 2, back, d_got)
    u_kept = grid.scatter_first(u_own, u_pair, *back)
    dq, dk, dv = back
    block_out = both_slots(out_mine, after(grid.swap(after(out_theirs, back[0])), dq))
    q_own, q_other = weight_grad_call(
        core_arr, [(h1, [after(dq, *u_kept[1]), dk, dv])], 256, "grad_qkv", "turns"
    )
    u_sum, u_here = grid.scatter_second(u_kept, q_own)
    d_mine = grid.scatter_z(d_parts)
    in_theirs, acc = last_call(
        core_arr, q_seats, x, dm, after(dq, q_own, *u_here), dk, dv, vec, acc_mid, q_group, True
    )
    q_pair = after(grid.swap(q_other), in_theirs)
    u_parts, u_got = grid.scatter_bit(grid.order_z(u_sum), in_theirs)
    d_other_mine = grid.swap(after(d_mine, in_theirs))
    in_mine, acc = last_call(
        core_arr, q_seats, x, dm, after(dq, q_pair, u_got), dk, dv, vec, acc, q_group, None
    )
    in_got = after(grid.swap(in_theirs), in_mine)
    q_kept = grid.scatter_first(q_own, q_pair, in_mine)
    u_mine = grid.scatter_z(u_parts)
    q_sum, q_here = grid.scatter_second(q_kept)
    u_other_mine = grid.swap(u_mine)
    in_grad = both_slots(in_mine, in_got)
    vec_total = grid.total_small(acc, q_kept[1], q_here)
    q_parts = grid.order_z(q_sum)
    q_mine = grid.scatter_z(q_parts)
    q_other_mine = grid.swap(q_mine)

    half, wide = D // 2, FF // 2
    down_new, = adam_call(
        core_arr,
        [(d_mine, d_other_mine)],
        [(after(w_down, in_mine), first_down, second_down)],
        [(FF ** (-0.5), MATRIX_DECAY, [(0, 0, half, 0, half)])],
    )
    out_new, up_new = adam_call(
        core_arr,
        [(u_mine, u_other_mine)],
        [(w_out, first_out, second_out), (w_up, first_up, second_up)],
        [
            ((D // 64) ** (-0.5), MATRIX_DECAY, [(0, 0, half, 0, half)]),
            (D ** (-0.5), MATRIX_DECAY, [(0, half, wide, 0, wide)]),
        ],
    )
    moves = []
    for turn in range(3 * D // 256):
        moves.append((0, turn * 128, 128, turn * 256, turn * 256 + 128))
    qkv_new, = adam_call(
        core_arr,
        [(q_mine, q_other_mine)],
        [(w_qkv, first_qkv, second_qkv)],
        [(D ** (-0.5), MATRIX_DECAY, moves)],
    )
    vec_grad = lax.dynamic_slice(vec_total, (0, grid.chip * vec_here), (vec_count, vec_here))
    vec_new = adamw(vectors, vec_grad, first_vectors, second_vectors, VECTOR_RATE, 0.0)
    news = [qkv_new, out_new, up_new, down_new, vec_new]
    return (block_out, in_grad) + tuple(new[kind] for kind in range(3) for new in news)


def finish_group(grid, seats, own, other):
    rows, cols = own[0].shape[-2:]
    if rows % 16 == 0:
        return Pieces(own + other, rows)
    found = []
    for half, parts in enumerate((own, other)):
        here = seats[half * grid.chips : (half + 1) * grid.chips]
        order = jnp.zeros((grid.chips,), jnp.int32).at[here].set(jnp.arange(grid.chips, dtype=jnp.int32))
        blocks = jnp.concatenate(parts).reshape(grid.chips, rows, cols)
        found.append(jnp.take(blocks, order, axis=0).reshape(1, 1, grid.chips * rows, cols))
    return Pieces(found, grid.chips * rows, True)


def solution(mesh):
    weight = P("dp", None)
    vector = P(None, "dp")
    state = (weight, weight, weight, weight, vector)
    tokens = P("dp", "seq", None)
    return jax.shard_map(
        local,
        mesh=mesh,
        in_specs=(tokens, P("dp"), tokens) + state * 3,
        out_specs=(tokens, tokens) + state * 3,
        check_vma=False,
    )
```

```python
import functools

import jax
import jax.numpy as jnp
from jax import lax
from jax.experimental import pallas as pl
from jax.experimental.pallas import tpu as pltpu
from jax.sharding import PartitionSpec as P

D = 768
HEADS = 12
HEAD_DIM = 64
FF = 3072
STEP = 10

EPS_NORM = 1e-05
EPS_ADAM = 1e-08
BETA_ONE = 0.5
BETA_TWO = 0.5
MATRIX_DECAY = 0.1
VECTOR_RATE = 0.1
NEG_FILL = -1e30
GELU_ROOT = 0.7978845608028654
GELU_CUBE = 0.044715
QKV_HALF = 3 * D // 2

F32 = jnp.float32
BF16 = jnp.bfloat16

NN = (((1,), (0,)), ((), ()))
NT = (((1,), (1,)), ((), ()))
TN = (((0,), (0,)), ((), ()))


def mm(left, right, dims=NN):
    return lax.dot_general(left, right, dims, preferred_element_type=F32)


def cost(flops, nbytes, trans=0):
    return pl.CostEstimate(flops=int(flops), bytes_accessed=int(nbytes), transcendentals=int(trans))


def params():
    return pltpu.CompilerParams(vmem_limit_bytes=60 * 1024 * 1024)


def whole_spec(shape):
    return pl.BlockSpec(shape, lambda *idx: (0,) * len(shape), pipeline_mode=pl.Buffered(1))


class Pieces:
    def __init__(self, arrays, rows, ordered=False):
        self.arrays = arrays
        self.rows = rows
        self.ordered = ordered
        self.halves = 2
        self.count = len(arrays) // self.halves
        self.lines, self.depth = arrays[0].shape[:2]

    def specs(self):
        return [pl.BlockSpec(memory_space=pltpu.HBM)] * len(self.arrays)

    def row(self, seat_ref, at):
        return 0 if self.ordered else pl.multiple_of(seat_ref[at] * self.rows, 16)

    def start(self, refs, core_ref, seat_ref, start_col, width, target, sem):
        core = core_ref[0]
        at = 0
        for half in range(self.halves):
            where = core if half == 0 else 1 - core
            for s2 in range(self.count):
                ref = refs[half * self.count + s2]
                for s1 in range(self.lines):
                    for sz in range(self.depth):
                        row = self.row(seat_ref, at)
                        at += 1
                        col = pl.multiple_of(where * width, 128)
                        pltpu.make_async_copy(
                            ref.at[s1, sz, :, pl.ds(start_col, width)],
                            target.at[pl.ds(row, self.rows), pl.ds(col, width)],
                            sem,
                        ).start()

    def start_once(self, refs, seat_ref, start_col, width, target, sem):
        at = 0
        for s2 in range(self.count):
            for s1 in range(self.lines):
                for sz in range(self.depth):
                    row = self.row(seat_ref, at)
                    at += 1
                    pltpu.make_async_copy(
                        refs[s2].at[s1, sz, :, pl.ds(start_col, width)],
                        target.at[pl.ds(row, self.rows), :],
                        sem,
                    ).start()


def wait_all(target, sem):
    pltpu.make_async_copy(target, target, sem).wait()


def norm_parts(rows):
    mean = jnp.mean(rows, axis=-1, keepdims=True)
    centred = rows - mean
    variance = jnp.mean(centred * centred, axis=-1, keepdims=True)
    scale = lax.rsqrt(variance + EPS_NORM)
    return centred * scale, scale


def norm_back(d_normed, normed, scale):
    first = jnp.mean(d_normed, axis=-1, keepdims=True)
    second = jnp.mean(d_normed * normed, axis=-1, keepdims=True)
    return scale * (d_normed - first - normed * second)


def qkv_kernel(group, core_ref, seat_ref, x_ref, *refs):
    refs, (h_ref, qkv_ref, vec_ref, w_ref, turned_ref, sems) = refs[:-6], refs[-6:]

    @pl.when(pl.program_id(0) == 0)
    def _():
        group.start(refs, core_ref, seat_ref, 0, QKV_HALF, w_ref, sems.at[0])
        group.start_once(refs, seat_ref, QKV_HALF, 128, turned_ref, sems.at[1])
        wait_all(turned_ref, sems.at[1])
        vec_ref[...] = turned_ref[...].astype(F32).T[:16]
        wait_all(w_ref, sems.at[0])

    def norm(rows):
        normed, _ = norm_parts(x_ref[rows, :].astype(F32))
        h = (normed * vec_ref[0:1, :] + vec_ref[1:2, :]).astype(BF16)
        h_ref[rows, :] = h
        return h

    subs = sub_blocks(x_ref.shape[0])
    h = norm(subs[0])
    for at, rows in enumerate(subs):
        queries = mm(h, w_ref[:, :D])
        after_h = norm(subs[at + 1]) if at + 1 < len(subs) else None
        qkv_ref[rows, :D] = (queries + vec_ref[2:3, :]).astype(BF16)
        qkv_ref[rows, D : 2 * D] = mm(h, w_ref[:, D : 2 * D]).astype(BF16)
        qkv_ref[rows, 2 * D :] = (mm(h, w_ref[:, 2 * D :]) + vec_ref[3:4, :]).astype(BF16)
        h = after_h


def sub_blocks(rows):
    return [slice(at, at + 256) for at in range(0, rows, 256)]


def qkv_call(core, seats, x, group, block=512):
    rows = x.shape[0]
    return pl.pallas_call(
        functools.partial(qkv_kernel, group),
        name="qkv",
        grid_spec=pltpu.PrefetchScalarGridSpec(
            num_scalar_prefetch=2,
            grid=(rows // block,),
            in_specs=[pl.BlockSpec((block, D), lambda i, *s: (i, 0))] + group.specs(),
            out_specs=[
                pl.BlockSpec((block, D), lambda i, *s: (i, 0)),
                pl.BlockSpec((block, 3 * D), lambda i, *s: (i, 0)),
                pl.BlockSpec((16, D), lambda i, *s: (0, 0)),
            ],
            scratch_shapes=[
                pltpu.VMEM((D, 3 * D), BF16),
                pltpu.VMEM((D, 128), BF16),
                pltpu.SemaphoreType.DMA((2,)),
            ],
        ),
        out_shape=[
            jax.ShapeDtypeStruct((rows, D), BF16),
            jax.ShapeDtypeStruct((rows, 3 * D), BF16),
            jax.ShapeDtypeStruct((16, D), F32),
        ],
        compiler_params=params(),
        cost_estimate=cost(2 * rows * D * 3 * D, 10e6),
    )(core, seats, x, *group.arrays)


def head_parts(length, q_all, k_all, head):
    full_len = q_all.shape[0]
    lane = lax.broadcasted_iota(jnp.int32, (1, 128), 1)
    mine = (lane // HEAD_DIM) == head
    spare = lane == HEAD_DIM * (1 - head)
    pos = lax.broadcasted_iota(jnp.int32, (full_len, 128), 0)
    fill = jnp.where(pos < length, 0.0, NEG_FILL).astype(BF16)
    zero = jnp.zeros((), BF16)
    k_head = jnp.where(mine, k_all, jnp.where(spare, fill, zero))
    q_plain = jnp.where(mine, q_all, zero)
    q_head = jnp.where(spare, jnp.ones((), BF16), q_plain)
    return mine, k_head, q_plain, q_head


def causal_mask(scores, block):
    full = scores.shape[0]
    key_pos = lax.broadcasted_iota(jnp.int32, (block, block), 0)
    query_pos = lax.broadcasted_iota(jnp.int32, (block, block), 1)
    last = jnp.where(key_pos <= query_pos, scores[full - block :], NEG_FILL)
    if full == block:
        return last
    return jnp.concatenate([scores[: full - block], last], axis=0)


def attend_kernel(core_ref, len_ref, q_ref, k_ref, v_ref, *refs):
    a_ref, lse_ref, mixed_ref, scores_ref = refs[-4:]
    block = 256
    full_len = q_ref.shape[0]
    length = len_ref[core_ref[0]]
    q_all = q_ref[...] * jnp.asarray(HEAD_DIM ** (-0.5), BF16)
    k_all = k_ref[...]
    v_turned = v_ref[...].T
    ones = jnp.ones((16, full_len), BF16)
    parts = []
    for head in range(2):
        _, k_head, _, q_head = head_parts(length, q_all, k_all, head)
        v_head = jnp.concatenate([v_turned[head * HEAD_DIM : (head + 1) * HEAD_DIM], ones], axis=0)
        parts.append((k_head, q_head, v_head))
    units = [(head, j) for j in reversed(range(full_len // block)) for head in range(2)]

    def score(at):
        head, j = units[at]
        k_head, q_head, _ = parts[head]
        top = None
        for i in range(j + 1):
            rows = slice(i * block, (i + 1) * block)
            tile = mm(k_head[rows], q_head[j * block : (j + 1) * block], NT)
            if i == j:
                tile = causal_mask(tile, block)
            scores_ref[at % 2, rows, :] = tile
            part = jnp.max(tile.reshape(block // 8, 8, block), axis=0)
            top = part if top is None else jnp.maximum(top, part)
        return jnp.max(top, axis=0, keepdims=True)

    def finish(at, top):
        head, j = units[at]
        v_head = parts[head][2]
        cols = slice(j * block, (j + 1) * block)
        mixed = None
        for i in range(j + 1):
            rows = slice(i * block, (i + 1) * block)
            exped = jnp.exp(scores_ref[at % 2, rows, :] - top).astype(BF16)
            part = mm(v_head[:, rows], exped)
            mixed = part if mixed is None else mixed + part
        total = mixed[HEAD_DIM : HEAD_DIM + 1]
        mixed_ref[head * HEAD_DIM : (head + 1) * HEAD_DIM, cols] = mixed[:HEAD_DIM] / total
        lse_ref[0, head : head + 1, cols] = top + jnp.log(total)

    top = score(0)
    for at in range(len(units)):
        later = score(at + 1) if at + 1 < len(units) else None
        finish(at, top)
        top = later
    a_ref[...] = mixed_ref[...].T.astype(BF16)


def attend_call(core, lengths, qkv, first, count, before):
    rows = qkv.shape[0]
    pairs = HEADS // 2
    before = list(before)
    return pl.pallas_call(
        attend_kernel,
        name="attend",
        grid_spec=pltpu.PrefetchScalarGridSpec(
            num_scalar_prefetch=2,
            grid=(count,),
            in_specs=[
                pl.BlockSpec((rows, 128), lambda i, c, n: (0, i + first)),
                pl.BlockSpec((rows, 128), lambda i, c, n: (0, i + first + pairs)),
                pl.BlockSpec((rows, 128), lambda i, c, n: (0, i + first + 2 * pairs)),
            ]
            + [pl.BlockSpec(memory_space=pl.ANY)] * len(before),
            out_specs=[
                pl.BlockSpec((rows, 128), lambda i, c, n: (0, i + first)),
                pl.BlockSpec((1, 8, rows), lambda i, c, n: (i + first, 0, 0)),
            ],
            scratch_shapes=[pltpu.VMEM((128, rows), F32), pltpu.VMEM((2, rows, 256), F32)],
        ),
        out_shape=[
            jax.ShapeDtypeStruct((rows, D), BF16),
            jax.ShapeDtypeStruct((pairs, 8, rows), F32),
        ],
        input_output_aliases={5 + i: i for i in range(len(before))},
        compiler_params=params(),
        cost_estimate=cost(3e9 * count, 1.2e6 * count, 2 * rows * rows * 0.6 * count),
    )(core, lengths, qkv, qkv, qkv, *before)


def attend_back_kernel(core_ref, len_ref, q_ref, k_ref, v_ref, a_ref, da_ref, lse_ref, *refs):
    dq_ref, dk_ref, dv_ref, dqt_ref, dk_acc, dv_acc = refs[-6:]
    block = 256
    full_len = q_ref.shape[0]
    length = len_ref[core_ref[0]]
    scale = HEAD_DIM ** (-0.5)
    q_all = q_ref[...] * jnp.asarray(scale, BF16)
    k_all = k_ref[...]
    k_turned = k_all.T
    v_all = v_ref[...]
    da_all = da_ref[...]
    inner = (da_all.astype(F32) * a_ref[...].astype(F32)).T
    parts = []
    for head in range(2):
        mine, k_head, q_plain, q_head = head_parts(length, q_all, k_all, head)
        da_head = jnp.where(mine, da_all, jnp.zeros((), BF16))
        lanes = slice(head * HEAD_DIM, (head + 1) * HEAD_DIM)
        centre = jnp.sum(inner[lanes], axis=0, keepdims=True)
        parts.append((k_head, q_plain, q_head, da_head, lanes, centre))
    units = [
        (head, j, i)
        for j in reversed(range(full_len // block))
        for head in range(2)
        for i in range(j + 1)
    ]

    def score(at):
        head, j, i = units[at]
        k_head, _, q_head, da_head, _, _ = parts[head]
        rows, cols = slice(i * block, (i + 1) * block), slice(j * block, (j + 1) * block)
        tile = mm(k_head[rows], q_head[cols], NT)
        if i == j:
            tile = causal_mask(tile, block)
        return tile, mm(v_all[rows], da_head[cols], NT)

    seen = set()
    ready = score(0)
    dq_part = None
    for at, (head, j, i) in enumerate(units):
        later = score(at + 1) if at + 1 < len(units) else None
        scores, d_probs = ready
        _, q_plain, _, da_head, lanes, centre = parts[head]
        rows, cols = slice(i * block, (i + 1) * block), slice(j * block, (j + 1) * block)
        probs = jnp.exp(scores - lse_ref[0, head : head + 1, cols])
        d_scores = (probs * (d_probs - centre[:, cols])).astype(BF16)
        dv_part = mm(probs.astype(BF16), da_head[cols])
        dk_part = mm(d_scores, q_plain[cols])
        if i in seen:
            dv_acc[rows] += dv_part
            dk_acc[rows] += dk_part
        else:
            seen.add(i)
            dv_acc[rows] = dv_part
            dk_acc[rows] = dk_part
        part = mm(k_turned[lanes, rows], d_scores)
        dq_part = part if i == 0 else dq_part + part
        if i == j:
            dqt_ref[lanes, cols] = dq_part * scale
        ready = later
    dq_ref[...] = dqt_ref[...].T.astype(BF16)
    dk_ref[...] = dk_acc[...].astype(BF16)
    dv_ref[...] = dv_acc[...].astype(BF16)


def attend_back_call(core, lengths, qkv, a, da, lse, start, count, before):
    rows = qkv.shape[0]
    pairs = HEADS // 2
    before = list(before)
    pair_spec = pl.BlockSpec((rows, 128), lambda i, c, n: (0, i + start))
    return pl.pallas_call(
        attend_back_kernel,
        name="attend_back",
        grid_spec=pltpu.PrefetchScalarGridSpec(
            num_scalar_prefetch=2,
            grid=(count,),
            in_specs=[
                pair_spec,
                pl.BlockSpec((rows, 128), lambda i, c, n: (0, i + start + pairs)),
                pl.BlockSpec((rows, 128), lambda i, c, n: (0, i + start + 2 * pairs)),
                pair_spec,
                pair_spec,
                pl.BlockSpec((1, 8, rows), lambda i, c, n: (i + start, 0, 0)),
            ]
            + [pl.BlockSpec(memory_space=pl.ANY)] * len(before),
            out_specs=[pair_spec, pair_spec, pair_spec],
            scratch_shapes=[
                pltpu.VMEM((128, rows), F32),
                pltpu.VMEM((rows, 128), F32),
                pltpu.VMEM((rows, 128), F32),
            ],
        ),
        out_shape=[jax.ShapeDtypeStruct((rows, D), BF16)] * 3,
        input_output_aliases={8 + i: i for i in range(len(before))},
        compiler_params=params(),
        cost_estimate=cost(6e9 * count, 2e6 * count, 2 * rows * rows * 0.6 * count),
    )(core, lengths, qkv, qkv, qkv, a, da, lse, *before)


def valid_rows(core_ref, len_ref, block):
    pos = pl.program_id(0) * block + lax.broadcasted_iota(jnp.int32, (block, 1), 0)
    return pos < len_ref[core_ref[0]]


def add_row(acc_ref, row, value):
    acc_ref[row : row + 1, :] += jnp.sum(value, axis=0, keepdims=True)


def row_block(core, i, steps):
    half = steps // 2
    return jnp.where(i < half, (1 - core) * half + i, core * half + i - half)


def up_kernel(group, core_ref, len_ref, seat_ref, x_ref, a_ref, og_ref, vec_ref, *refs):
    refs, (mid_ref, h_ref, e_ref, slope_ref, dy_ref, wo_ref, wu_ref, sems) = refs[:-8], refs[-8:]
    block = x_ref.shape[0]

    @pl.when(pl.program_id(0) == 0)
    def _():
        group.start(refs, core_ref, seat_ref, 0, D // 2, wo_ref, sems.at[0])
        group.start(refs, core_ref, seat_ref, D // 2, FF // 2, wu_ref, sems.at[1])
        wait_all(wo_ref, sems.at[0])
        wait_all(wu_ref, sems.at[1])

    valid = valid_rows(core_ref, len_ref, block)
    dy_ref[...] = jnp.where(valid, og_ref[...].astype(F32), 0.0).astype(BF16)
    subs = sub_blocks(block)

    def open_up(rows):
        return x_ref[rows, :].astype(F32) + mm(a_ref[rows, :], wo_ref[...]) + vec_ref[4:5, :]

    def norm(rows, mid):
        mid_ref[rows, :] = mid
        normed, _ = norm_parts(mid)
        h = (normed * vec_ref[5:6, :] + vec_ref[6:7, :]).astype(BF16)
        h_ref[rows, :] = h
        return h

    def act(rows, j, z):
        cols = slice(j * D, (j + 1) * D)
        z = z + vec_ref[8 + j : 9 + j, :]
        squared = z * z
        turned = jnp.tanh(z * (GELU_ROOT + (GELU_ROOT * GELU_CUBE) * squared))
        half = 0.5 * turned + 0.5
        act = z * half
        e_ref[rows, cols] = act.astype(BF16)
        slope = half + act * (1.0 - turned) * (GELU_ROOT + (3.0 * GELU_ROOT * GELU_CUBE) * squared)
        slope_ref[rows, cols] = slope.astype(BF16)

    hs = {0: norm(subs[0], open_up(subs[0]))}
    waiting = None
    for at, rows in enumerate(subs):
        later = open_up(subs[at + 1]) if at + 1 < len(subs) else None
        for j in range(FF // D):
            z = mm(hs[at], wu_ref[:, j * D : (j + 1) * D])
            if waiting is not None:
                act(*waiting)
            waiting = (rows, j, z)
            if j == 1 and later is not None:
                hs[at + 1] = norm(subs[at + 1], later)
    act(*waiting)


def up_call(core, lengths, seats, x, a, og, vec, group, block=512):
    rows = x.shape[0]
    row_spec = pl.BlockSpec((block, D), lambda i, *s: (i, 0))
    wide_spec = pl.BlockSpec((block, FF), lambda i, *s: (i, 0))
    low = jax.ShapeDtypeStruct((rows, D), BF16)
    return pl.pallas_call(
        functools.partial(up_kernel, group),
        name="up",
        grid_spec=pltpu.PrefetchScalarGridSpec(
            num_scalar_prefetch=3,
            grid=(rows // block,),
            in_specs=[row_spec, row_spec, row_spec, whole_spec(vec.shape)] + group.specs(),
            out_specs=[row_spec, row_spec, wide_spec, wide_spec, row_spec],
            scratch_shapes=[
                pltpu.VMEM((D, D), BF16),
                pltpu.VMEM((D, FF), BF16),
                pltpu.SemaphoreType.DMA((2,)),
            ],
        ),
        out_shape=[
            jax.ShapeDtypeStruct((rows, D), F32),
            low,
            jax.ShapeDtypeStruct((rows, FF), BF16),
            jax.ShapeDtypeStruct((rows, FF), BF16),
            low,
        ],
        compiler_params=params(),
        cost_estimate=cost(6e9, 30e6, rows * FF),
    )(core, lengths, seats, x, a, og, vec, *group.arrays)


def down_kernel(up_group, down_group, core_ref, len_ref, seat_ref, mid_ref, e_ref, slope_ref, dy_ref, vec_ref, *refs):
    count = len(up_group.arrays)
    up_refs, down_refs = refs[:count], refs[count : count + len(down_group.arrays)]
    (
        theirs_ref, mine_ref, dz_ref, dmb_ref, dm_ref, da_ref, acc_ref, wo_ref, wu_ref, wd_ref, sems,
    ) = refs[-11:]
    block = mid_ref.shape[0]
    step, steps = pl.program_id(0), pl.num_programs(0)

    @pl.when(pl.program_id(0) == 0)
    def _():
        down_group.start(down_refs, core_ref, seat_ref, 0, D // 2, wd_ref, sems.at[2])
        up_group.start(up_refs, core_ref, seat_ref, D // 2, FF // 2, wu_ref, sems.at[1])
        up_group.start(up_refs, core_ref, seat_ref, 0, D // 2, wo_ref, sems.at[0])
        acc_ref[...] = jnp.zeros_like(acc_ref)
        wait_all(wd_ref, sems.at[2])

    pos = row_block(core_ref[0], step, steps) * block + lax.broadcasted_iota(jnp.int32, (block, 1), 0)
    down = vec_ref[7:8, :] + mid_ref[...] + mm(e_ref[...], wd_ref[...])
    down = jnp.where(pos < len_ref[core_ref[0]], down, 0.0).astype(BF16)

    @pl.when(step < steps // 2)
    def _():
        theirs_ref[...] = down

    @pl.when(step >= steps // 2)
    def _():
        mine_ref[0] = down

    @pl.when(step == 0)
    def _():
        wait_all(wu_ref, sems.at[1])
        wait_all(wo_ref, sems.at[0])

    subs = sub_blocks(block)
    add_row(acc_ref, 7, dy_ref[...].astype(F32))
    dhs = [None] * len(subs)
    normals = [None] * len(subs)

    def turn(at, j, de):
        rows, cols = subs[at], slice(j * D, (j + 1) * D)
        dz = (de * slope_ref[rows, cols].astype(F32)).astype(BF16)
        dz_ref[rows, cols] = dz
        add_row(acc_ref, 8 + j, dz.astype(F32))
        part = mm(dz, wu_ref[:, cols], NT)
        dhs[at] = part if dhs[at] is None else dhs[at] + part

    def close(at):
        rows = subs[at]
        normed, scale = norm_parts(mid_ref[rows, :])
        dh = dhs[at]
        add_row(acc_ref, 5, dh * normed)
        add_row(acc_ref, 6, dh)
        dm = dy_ref[rows, :].astype(F32) + norm_back(dh * vec_ref[5:6, :], normed, scale)
        dm_ref[rows, :] = dm
        dm_low = dm.astype(BF16)
        dmb_ref[rows, :] = dm_low
        add_row(acc_ref, 4, dm_low.astype(F32))
        da_ref[rows, :] = mm(dm_low, wo_ref[...], NT).astype(BF16)

    waiting = None
    for at, rows in enumerate(subs):
        for j in range(FF // D):
            de = mm(dy_ref[rows, :], wd_ref[j * D : (j + 1) * D, :], NT)
            if waiting is not None:
                turn(*waiting)
            waiting = (at, j, de)
            if j == 1 and at > 0:
                close(at - 1)
    turn(*waiting)
    close(len(subs) - 1)


def down_call(core, lengths, seats, mid, e, slope, dy, vec, up_group, down_group, block=512):
    rows = mid.shape[0]
    steps = rows // block
    half = steps // 2
    row_spec = pl.BlockSpec((block, D), lambda i, c, *s: (row_block(c[0], i, steps), 0))
    wide_spec = pl.BlockSpec((block, FF), lambda i, c, *s: (row_block(c[0], i, steps), 0))
    low = jax.ShapeDtypeStruct((rows, D), BF16)
    return pl.pallas_call(
        functools.partial(down_kernel, up_group, down_group),
        name="down",
        grid_spec=pltpu.PrefetchScalarGridSpec(
            num_scalar_prefetch=3,
            grid=(steps,),
            in_specs=[row_spec, wide_spec, wide_spec, row_spec, whole_spec(vec.shape)]
            + up_group.specs()
            + down_group.specs(),
            out_specs=[
                pl.BlockSpec((block, D), lambda i, *s: (jnp.minimum(i, half - 1), 0)),
                pl.BlockSpec((1, block, D), lambda i, c, *s: (c[0], jnp.maximum(i - half, 0), 0)),
                wide_spec, row_spec, row_spec, row_spec,
                pl.BlockSpec((16, D), lambda i, *s: (0, 0)),
            ],
            scratch_shapes=[
                pltpu.VMEM((D, D), BF16),
                pltpu.VMEM((D, FF), BF16),
                pltpu.VMEM((FF, D), BF16),
                pltpu.SemaphoreType.DMA((3,)),
            ],
        ),
        out_shape=[
            jax.ShapeDtypeStruct((rows // 2, D), BF16),
            jax.ShapeDtypeStruct((2, rows // 2, D), BF16),
            jax.ShapeDtypeStruct((rows, FF), BF16), low, jax.ShapeDtypeStruct((rows, D), F32), low,
            jax.ShapeDtypeStruct((16, D), F32),
        ],
        compiler_params=params(),
        cost_estimate=cost(1.6e10, 35e6),
    )(core, lengths, seats, mid, e, slope, dy, vec, *up_group.arrays, *down_group.arrays)


def pick(values, half, mode):
    if mode == "split":
        width = values.shape[1] // 2
        return [values[:, half * width : (half + 1) * width]]
    return [values[:, at : at + 128] for at in range(half * 128, values.shape[1], 256)]


def weight_grad_kernel(lefts, rights, mode, core_ref, *refs):
    left_refs, right_refs = refs[:lefts], refs[lefts : lefts + sum(rights)]
    own_ref, other_ref = refs[-2:]
    halves = ([], [])
    at = 0
    for left_ref, count in zip(left_refs, rights):
        left = left_ref[...]
        for right_ref in right_refs[at : at + count]:
            whole = mm(left, right_ref[...], TN).astype(BF16)
            for half in range(2):
                halves[half].extend(pick(whole, half, mode))
        at += count
    low, high = [part[0] if len(part) == 1 else jnp.concatenate(part, axis=1) for part in halves]

    @pl.when(core_ref[0] == 0)
    def _():
        own_ref[...] = low
        other_ref[...] = high

    @pl.when(core_ref[0] != 0)
    def _():
        own_ref[...] = high
        other_ref[...] = low


def weight_grad_call(core, products, block, name, mode="split", cols=None):
    rows, height = products[0][0].shape
    lefts = [left for left, _ in products]
    rights = [right for _, group in products for right in group]
    widths = [right.shape[1] if cols is None else cols[0] for right in rights]
    width = sum(widths)
    seat = 0 if cols is None else cols[1]
    return pl.pallas_call(
        functools.partial(weight_grad_kernel, len(lefts), [len(group) for _, group in products], mode),
        name=name,
        grid_spec=pltpu.PrefetchScalarGridSpec(
            num_scalar_prefetch=1,
            grid=(height // block,),
            in_specs=[pl.BlockSpec((rows, block), lambda i, c: (0, i))] * len(lefts)
            + [
                pl.BlockSpec((rows, w), lambda i, c: (0, seat), pipeline_mode=pl.Buffered(1)) for w in widths
            ],
            out_specs=[pl.BlockSpec((block, width // 2), lambda i, c: (i, 0))] * 2,
        ),
        out_shape=[jax.ShapeDtypeStruct((height, width // 2), BF16)] * 2,
        compiler_params=params(),
        cost_estimate=cost(2 * rows * height * width, rows * (height + width) * 2 + height * width * 2),
    )(core, *lefts, *rights)


def last_kernel(group, core_ref, seat_ref, x_ref, dm_ref, dq_ref, dk_ref, dv_ref, vec_ref, before_ref, *refs):
    refs, (theirs_ref, mine_ref, acc_ref, w_ref, sems) = refs[:-5], refs[-5:]
    step, steps = pl.program_id(0), pl.num_programs(0)

    @pl.when(step == 0)
    def _():
        group.start(refs, core_ref, seat_ref, 0, QKV_HALF, w_ref, sems.at[0])
        acc_ref[...] = before_ref[...]
        wait_all(w_ref, sems.at[0])

    subs = sub_blocks(x_ref.shape[0])

    def product(rows):
        return (
            mm(dq_ref[rows, :], w_ref[:, :D], NT)
            + mm(dk_ref[rows, :], w_ref[:, D : 2 * D], NT)
            + mm(dv_ref[rows, :], w_ref[:, 2 * D :], NT)
        )

    grads = []
    dh = product(subs[0])
    add_row(acc_ref, 2, dq_ref[...].astype(F32))
    add_row(acc_ref, 3, dv_ref[...].astype(F32))
    for at, rows in enumerate(subs):
        later = product(subs[at + 1]) if at + 1 < len(subs) else None
        normed, scale = norm_parts(x_ref[rows, :].astype(F32))
        add_row(acc_ref, 0, dh * normed)
        add_row(acc_ref, 1, dh)
        grads.append(dm_ref[rows, :] + norm_back(dh * vec_ref[0:1, :], normed, scale))
        dh = later

    @pl.when(step < steps // 2)
    def _():
        for rows, grad in zip(subs, grads):
            theirs_ref[rows, :] = grad

    @pl.when(step >= steps // 2)
    def _():
        for rows, grad in zip(subs, grads):
            mine_ref[0, rows, :] = grad


def last_call(core, seats, x, dm, dq, dk, dv, vec, before, group, block=512):
    rows = x.shape[0]
    steps = rows // block
    half = steps // 2
    row_spec = pl.BlockSpec((block, D), lambda i, c, *s: (row_block(c[0], i, steps), 0))
    return pl.pallas_call(
        functools.partial(last_kernel, group),
        name="last",
        grid_spec=pltpu.PrefetchScalarGridSpec(
            num_scalar_prefetch=2,
            grid=(steps,),
            in_specs=[row_spec] * 5 + [whole_spec(vec.shape), whole_spec(before.shape)] + group.specs(),
            out_specs=[
                pl.BlockSpec((block, D), lambda i, *s: (jnp.minimum(i, half - 1), 0)),
                pl.BlockSpec((1, block, D), lambda i, c, *s: (c[0], jnp.maximum(i - half, 0), 0)),
                pl.BlockSpec((16, D), lambda i, *s: (0, 0)),
            ],
            scratch_shapes=[pltpu.VMEM((D, 3 * D), BF16), pltpu.SemaphoreType.DMA((1,))],
        ),
        out_shape=[
            jax.ShapeDtypeStruct((rows // 2, D), F32),
            jax.ShapeDtypeStruct((2, rows // 2, D), F32),
            jax.ShapeDtypeStruct((16, D), F32),
        ],
        compiler_params=params(),
        cost_estimate=cost(rows * 6 * D * D, 16e6),
    )(core, seats, x, dm, dq, dk, dv, vec, before, *group.arrays)


def adam_kernel(plans, sources, core_ref, *refs):
    halves = [refs[2 * i : 2 * i + 2] for i in range(sources)]
    count = len(plans)
    states = refs[2 * sources : 2 * sources + 3 * count]
    outs = refs[2 * sources + 3 * count : 2 * sources + 6 * count]
    grads = refs[2 * sources + 6 * count :]
    for core in range(2):

        @pl.when(core_ref[0] == core)
        def _():
            for (_, _, moves), grad_ref in zip(plans, grads):
                for source, start, width, place0, place1 in moves:
                    for half, place in ((0, place0), (1, place1)):
                        ref = halves[source][0 if half == core else 1]
                        grad_ref[:, place : place + width] = ref[:, start : start + width].astype(F32)

    for i, (rate, decay, _) in enumerate(plans):
        weight, first, second = states[3 * i : 3 * i + 3]
        new = adamw(weight[...], grads[i][...], first[...], second[...], rate, decay)
        for out, value in zip(outs[3 * i : 3 * i + 3], new):
            out[...] = value


def adam_call(core, halves, states, plans):
    flat = [part for pair in halves for part in pair]
    held = [part for state in states for part in state]
    spec = pl.BlockSpec(memory_space=pltpu.VMEM)
    news = pl.pallas_call(
        functools.partial(adam_kernel, plans, len(halves)),
        name="adam",
        in_specs=[pl.BlockSpec(memory_space=pltpu.SMEM)] + [spec] * (len(flat) + len(held)),
        out_specs=[spec] * len(held),
        out_shape=[jax.ShapeDtypeStruct(part.shape, F32) for part in held],
        scratch_shapes=[pltpu.VMEM(state[0].shape, F32) for state in states],
        compiler_params=params(),
        cost_estimate=cost(1e6, 24 * sum(state[0].size for state in states)),
    )(core, *flat, *held)
    return [news[3 * i : 3 * i + 3] for i in range(len(states))]


def after(value, *others):
    if not others:
        return value
    return lax.optimization_barrier((value,) + others)[0]


class Grid:
    def __init__(self, chips):
        log = chips.bit_length() - 1
        side = 1 << (log // 3)
        if side * side * (chips // (side * side)) != chips:
            side = 1
        self.chips = chips
        self.n = side
        self.nz = chips // (side * side)
        self.core = lax.axis_index("seq")
        self.chip = lax.axis_index("dp")
        self.x = self.chip % side
        self.y = self.chip // side % side
        self.z = self.chip // (side * side)

    def plane(self, first, second, core):
        return jnp.where(core == 0, second * self.n + first, first * self.n + second)

    def coords(self, core):
        return jnp.where(core == 0, self.x, self.y), jnp.where(core == 0, self.y, self.x)

    def permute(self, value, axis, shift=0):
        pairs = []
        for chip in range(self.chips):
            for core in range(2):
                x, y, z = chip % self.n, chip // self.n % self.n, chip // (self.n * self.n)
                to_core = core
                if axis == "z":
                    z = (z + shift) % self.nz
                elif axis == "zx":
                    z = z ^ shift
                elif axis == "core":
                    to_core = 1 - core
                elif (axis == "first") == (core == 0):
                    x = (x + shift) % self.n
                else:
                    y = (y + shift) % self.n
                pairs.append((chip * 2 + core, ((z * self.n + y) * self.n + x) * 2 + to_core))
        return lax.ppermute(value, ("dp", "seq"), pairs)

    def swap(self, value):
        return self.permute(value, "core")

    def join(self, own, other, axis):
        return jnp.where(
            self.core == 0,
            jnp.concatenate([own, other], axis),
            jnp.concatenate([other, own], axis),
        )

    def seats(self, halving):
        found = []
        for half in range(2):
            core = self.core if half == 0 else 1 - self.core
            first, second = self.coords(core)
            for s2 in range(self.n):
                for s1 in range(self.n):
                    flat = self.plane((first - s1) % self.n, (second - s2) % self.n, core)
                    for sz in range(self.nz):
                        z = self.z ^ sz if halving else (self.z - sz) % self.nz
                        found.append(z * self.n * self.n + flat)
        return jnp.stack(found).astype(jnp.int32)

    def total_small(self, value, *untils):
        steps = [("core", 0), ("first", 1), ("second", 1)] if self.n == 2 else [("core", 0)]
        if self.n != 2:
            for axis in ("first", "second"):
                value = value + sum(self.permute(value, axis, s) for s in range(1, self.n))
        bit = 1
        while bit < self.nz:
            steps.append(("zx", bit))
            bit *= 2
        for at, (axis, shift) in enumerate(steps):
            until = untils[at] if at < len(untils) else ()
            value = value + after(self.permute(value, axis, shift), *until)
        return value

    def gather_z(self, block, *until):
        return jnp.stack([block] + [after(self.permute(block, "z", s), *until) for s in range(1, self.nz)])

    def gather_bit(self, held, bit, *until):
        return jnp.concatenate([held, after(self.permute(held, "zx", bit), *until)])

    def gather_first(self, column, *until):
        return jnp.stack([column] + [after(self.permute(column, "first", s), *until) for s in range(1, self.n)])

    def gather_second(self, line, *until):
        return [after(self.permute(line, "second", s), *until) for s in range(1, self.n)]

    def scatter_first(self, own, pair, *until):
        rows, cols = own.shape[0] // self.chips, own.shape[1]
        first, second = self.coords(self.core)
        n = self.n

        def seat(s1, s2):
            where = self.plane((first + s1) % n, (second + s2) % n, self.core)
            own_part, pair_part = [
                lax.dynamic_slice(
                    part.reshape(self.nz, n * n, rows, cols), (0, where, 0, 0), (self.nz, 1, rows, cols)
                ).astype(F32)
                for part in (own, pair)
            ]
            return own_part + pair_part

        kept = [seat(0, t) for t in range(n)]
        for s in range(1, n):
            send = jnp.stack([seat(s, t).astype(BF16) for t in range(n)])
            got = after(self.permute(send, "first", s), *until)
            kept = [kept[t] + got[t].astype(F32) for t in range(n)]
        return kept[0], [part.astype(BF16) for part in kept[1:]]

    def scatter_second(self, kept, *until):
        mine, rest = kept
        got = [after(self.permute(rest[s - 1], "second", s), *until) for s in range(1, self.n)]
        for part in got:
            mine = mine + part.astype(F32)
        return mine.reshape((self.nz,) + mine.shape[2:]), got

    def order_z(self, mine):
        return [lax.dynamic_index_in_dim(mine, self.z ^ at, 0, keepdims=False) for at in range(self.nz)]

    def scatter_bit(self, parts, *until):
        half = len(parts) // 2
        send = parts[half] if half == 1 else jnp.stack([part.astype(BF16) for part in parts[half:]])
        got = after(self.permute(send.astype(BF16), "zx", half), *until)
        if half == 1:
            return [parts[0] + got.astype(F32)], got
        return [part + got[at].astype(F32) for at, part in enumerate(parts[:half])], got

    def scatter_z(self, parts):
        while len(parts) > 1:
            parts, _ = self.scatter_bit(parts)
        return parts[0]


def adamw(weight, gradient, first_moment, second_moment, step_rate, weight_decay):
    first_moment = BETA_ONE * first_moment + (1.0 - BETA_ONE) * gradient
    second_moment = BETA_TWO * second_moment + (1.0 - BETA_TWO) * gradient * gradient
    first_fix = 1.0 - BETA_ONE**STEP
    second_fix = 1.0 - BETA_TWO**STEP
    direction = first_moment / first_fix / (jnp.sqrt(second_moment / second_fix) + EPS_ADAM)
    return (weight - step_rate * (direction + weight_decay * weight), first_moment, second_moment)


def local(
    block_in, lengths, out_grad, w_qkv, w_out, w_up, w_down, vectors,
    first_qkv, first_out, first_up, first_down, first_vectors,
    second_qkv, second_out, second_up, second_down, second_vectors,
):
    grid = Grid(lax.axis_size("dp"))
    core = grid.core
    core_arr = core.reshape(1).astype(jnp.int32)
    half_len = block_in.shape[1]
    vec_count, vec_here = vectors.shape

    def own_slot(halves):
        mine = lax.dynamic_index_in_dim(halves, core, 0, keepdims=False)
        theirs = lax.dynamic_index_in_dim(halves, 1 - core, 0, keepdims=False)
        return grid.join(mine, grid.swap(theirs), 0)

    def both_slots(mine, got):
        return lax.dynamic_update_slice(mine, got[None], (1 - core, 0, 0))

    def half_of(shard):
        width = shard.shape[1] // 2
        return lax.dynamic_slice_in_dim(shard, core * width, width, 1).astype(BF16)

    seats, q_seats = grid.seats(True), grid.seats(False)

    turned = jnp.pad(vectors.T.astype(BF16), ((0, 0), (0, 128 - vec_count)))
    q_block = jnp.concatenate([half_of(w_qkv), turned], axis=1)
    u_block = jnp.concatenate([half_of(w_out), half_of(w_up)], axis=1)
    d_col = half_of(w_down)[None]
    q_col = grid.gather_z(q_block)
    x = own_slot(block_in)
    q_line = grid.gather_first(q_col, x)
    u_col = u_block[None]
    bits = [1 << at for at in range((grid.nz - 1).bit_length())]
    for bit in bits[:-1]:
        u_col = grid.gather_bit(u_col, bit)
        d_col = grid.gather_bit(d_col, bit)
    q_rest = grid.gather_second(q_line)
    q_line_swap = grid.swap(q_line)
    q_rest_swap = [grid.swap(after(part, u_col, d_col)) for part in q_rest]
    q_group = finish_group(grid, q_seats, [q_line] + q_rest, [q_line_swap] + q_rest_swap)

    h1, qkv, vec = qkv_call(core_arr, q_seats, x, q_group)
    u_col = grid.gather_bit(after(u_col, *q_rest), bits[-1], qkv)
    og = own_slot(after(out_grad, qkv))
    att = attend_call(core_arr, lengths, after(qkv, u_col), 0, 2, ())
    u_line = grid.gather_first(u_col, *att)
    att = attend_call(core_arr, lengths, after(qkv, u_line), 2, 3, att)
    u_line_swap = after(grid.swap(u_line), *att)
    u_rest = grid.gather_second(u_line, *att)
    d_col = after(grid.gather_bit(after(d_col, u_col), bits[-1], *att), *u_rest)
    a, lse = attend_call(core_arr, lengths, after(qkv, d_col), 5, 1, att)
    u_rest_swap = [after(grid.swap(part), a) for part in u_rest]
    d_line = grid.gather_first(d_col, a)
    u_group = finish_group(grid, seats, [u_line] + u_rest, [u_line_swap] + u_rest_swap)
    mid, h2, e, slope, dy = up_call(core_arr, lengths, seats, x, after(a, d_line), og, vec, u_group)
    d_line_swap = after(grid.swap(d_line), mid)
    d_rest = grid.gather_second(d_line, mid)
    d_own, d_other = weight_grad_call(core_arr, [(after(e, *d_rest), [dy])], 512, "grad_down")
    d_rest_swap = [after(grid.swap(part), d_own) for part in d_rest]
    d_group = finish_group(grid, seats, [d_line] + d_rest, [d_line_swap] + d_rest_swap)
    out_theirs, out_mine, dz, dmb, dm, da, acc_mid = down_call(
        core_arr, lengths, seats, mid, e, slope, dy, vec, u_group, d_group
    )

    d_pair = after(grid.swap(d_other), dz)
    u_own, u_other = weight_grad_call(
        core_arr, [(a, [dmb]), (h2, [after(dz, d_pair)])], 256, "grad_up"
    )
    d_kept = grid.scatter_first(d_own, d_pair, u_own)

    def back_call(start, count, before, *needs):
        return attend_back_call(core_arr, lengths, qkv, a, after(da, *needs), lse, start, count, before)

    back = back_call(0, 2, (), u_own, *d_kept[1])
    d_sum, d_here = grid.scatter_second(d_kept, *back)
    u_pair = after(grid.swap(u_other), *back)
    back = back_call(2, 2, back, u_pair, *d_here)
    d_parts, d_got = grid.scatter_bit(grid.order_z(d_sum), *back)
    back = back_call(4, 2, back, d_got)
    u_kept = grid.scatter_first(u_own, u_pair, *back)
    dq, dk, dv = back
    block_out = both_slots(out_mine, after(grid.swap(after(out_theirs, back[0])), dq))
    q_own, q_other = weight_grad_call(
        core_arr, [(h1, [after(dq, *u_kept[1]), dk, dv])], 256, "grad_qkv", "turns"
    )
    u_sum, u_here = grid.scatter_second(u_kept, q_own)
    d_mine = grid.scatter_z(d_parts)
    in_theirs, in_mine, acc = last_call(
        core_arr, q_seats, x, dm, after(dq, q_own, *u_here), dk, dv, vec, acc_mid, q_group
    )
    q_pair = after(grid.swap(q_other), in_theirs)
    u_parts, u_got = grid.scatter_bit(grid.order_z(u_sum), in_theirs)
    d_other_mine = after(grid.swap(d_mine), in_theirs)
    q_kept = grid.scatter_first(q_own, q_pair)
    in_got = grid.swap(after(in_theirs, q_pair))
    down_new, = adam_call(
        core_arr,
        [(d_mine, d_other_mine)],
        [(after(w_down, in_theirs), first_down, second_down)],
        [(FF ** (-0.5), MATRIX_DECAY, [(0, 0, D // 2, 0, D // 2)])],
    )
    u_mine = grid.scatter_z(u_parts)
    q_sum, q_here = grid.scatter_second(q_kept)
    u_other_mine = grid.swap(u_mine)
    in_grad = both_slots(in_mine, in_got)
    vec_total = grid.total_small(acc, q_kept[1], q_here)
    q_mine = grid.scatter_z(grid.order_z(q_sum))
    q_other_mine = grid.swap(q_mine)

    half, wide = D // 2, FF // 2
    out_new, up_new = adam_call(
        core_arr,
        [(u_mine, u_other_mine)],
        [(w_out, first_out, second_out), (w_up, first_up, second_up)],
        [
            ((D // 64) ** (-0.5), MATRIX_DECAY, [(0, 0, half, 0, half)]),
            (D ** (-0.5), MATRIX_DECAY, [(0, half, wide, 0, wide)]),
        ],
    )
    moves = []
    for turn in range(3 * D // 256):
        moves.append((0, turn * 128, 128, turn * 256, turn * 256 + 128))
    qkv_new, = adam_call(
        core_arr,
        [(q_mine, q_other_mine)],
        [(w_qkv, first_qkv, second_qkv)],
        [(D ** (-0.5), MATRIX_DECAY, moves)],
    )
    vec_grad = lax.dynamic_slice(vec_total, (0, grid.chip * vec_here), (vec_count, vec_here))
    vec_new = adamw(vectors, vec_grad, first_vectors, second_vectors, VECTOR_RATE, 0.0)
    news = [qkv_new, out_new, up_new, down_new, vec_new]
    return (block_out, in_grad) + tuple(new[kind] for kind in range(3) for new in news)


def finish_group(grid, seats, own, other):
    rows, cols = own[0].shape[-2:]
    if rows % 16 == 0:
        return Pieces(own + other, rows)
    found = []
    for half, parts in enumerate((own, other)):
        here = seats[half * grid.chips : (half + 1) * grid.chips]
        order = jnp.zeros((grid.chips,), jnp.int32).at[here].set(jnp.arange(grid.chips, dtype=jnp.int32))
        blocks = jnp.concatenate(parts).reshape(grid.chips, rows, cols)
        found.append(jnp.take(blocks, order, axis=0).reshape(1, 1, grid.chips * rows, cols))
    return Pieces(found, grid.chips * rows, True)


def solution(mesh):
    weight = P("dp", None)
    vector = P(None, "dp")
    state = (weight, weight, weight, weight, vector)
    tokens = P("dp", "seq", None)
    return jax.shard_map(
        local,
        mesh=mesh,
        in_specs=(tokens, P("dp"), tokens) + state * 3,
        out_specs=(tokens, tokens) + state * 3,
        check_vma=False,
    )
```

```python
import functools

import jax
import jax.numpy as jnp
from jax import lax
from jax.experimental import pallas as pl
from jax.experimental.pallas import tpu as pltpu
from jax.sharding import PartitionSpec as P

D = 768
HEADS = 12
HEAD_DIM = 64
FF = 3072
STEP = 10

EPS_NORM = 1e-05
EPS_ADAM = 1e-08
BETA_ONE = 0.5
BETA_TWO = 0.5
MATRIX_DECAY = 0.1
VECTOR_RATE = 0.1
NEG_FILL = -1e30
GELU_ROOT = 0.7978845608028654
GELU_CUBE = 0.044715
QKV_HALF = 3 * D // 2

F32 = jnp.float32
BF16 = jnp.bfloat16

NN = (((1,), (0,)), ((), ()))
NT = (((1,), (1,)), ((), ()))
TN = (((0,), (0,)), ((), ()))


def mm(left, right, dims=NN):
    return lax.dot_general(left, right, dims, preferred_element_type=F32)


def cost(flops, nbytes, trans=0):
    return pl.CostEstimate(flops=int(flops), bytes_accessed=int(nbytes), transcendentals=int(trans))


def params():
    return pltpu.CompilerParams(vmem_limit_bytes=60 * 1024 * 1024)


def whole_spec(shape):
    return pl.BlockSpec(shape, lambda *idx: (0,) * len(shape), pipeline_mode=pl.Buffered(1))


class Pieces:
    def __init__(self, arrays, rows, ordered=False):
        self.arrays = arrays
        self.rows = rows
        self.ordered = ordered
        self.halves = 2
        self.count = len(arrays) // self.halves
        self.lines, self.depth = arrays[0].shape[:2]

    def specs(self):
        return [pl.BlockSpec(memory_space=pltpu.HBM)] * len(self.arrays)

    def row(self, seat_ref, at):
        return 0 if self.ordered else pl.multiple_of(seat_ref[at] * self.rows, 16)

    def start(self, refs, core_ref, seat_ref, start_col, width, target, sem):
        core = core_ref[0]
        at = 0
        for half in range(self.halves):
            where = core if half == 0 else 1 - core
            for s2 in range(self.count):
                ref = refs[half * self.count + s2]
                for s1 in range(self.lines):
                    for sz in range(self.depth):
                        row = self.row(seat_ref, at)
                        at += 1
                        col = pl.multiple_of(where * width, 128)
                        pltpu.make_async_copy(
                            ref.at[s1, sz, :, pl.ds(start_col, width)],
                            target.at[pl.ds(row, self.rows), pl.ds(col, width)],
                            sem,
                        ).start()

    def start_once(self, refs, seat_ref, start_col, width, target, sem):
        at = 0
        for s2 in range(self.count):
            for s1 in range(self.lines):
                for sz in range(self.depth):
                    row = self.row(seat_ref, at)
                    at += 1
                    pltpu.make_async_copy(
                        refs[s2].at[s1, sz, :, pl.ds(start_col, width)],
                        target.at[pl.ds(row, self.rows), :],
                        sem,
                    ).start()


def wait_all(target, sem):
    pltpu.make_async_copy(target, target, sem).wait()


def norm_parts(rows):
    mean = jnp.mean(rows, axis=-1, keepdims=True)
    centred = rows - mean
    variance = jnp.mean(centred * centred, axis=-1, keepdims=True)
    scale = lax.rsqrt(variance + EPS_NORM)
    return centred * scale, scale


def norm_back(d_normed, normed, scale):
    first = jnp.mean(d_normed, axis=-1, keepdims=True)
    second = jnp.mean(d_normed * normed, axis=-1, keepdims=True)
    return scale * (d_normed - first - normed * second)


def qkv_kernel(group, core_ref, seat_ref, x_ref, *refs):
    refs, (h_ref, qkv_ref, vec_ref, w_ref, turned_ref, sems) = refs[:-6], refs[-6:]

    @pl.when(pl.program_id(0) == 0)
    def _():
        group.start(refs, core_ref, seat_ref, 0, QKV_HALF, w_ref, sems.at[0])
        group.start_once(refs, seat_ref, QKV_HALF, 128, turned_ref, sems.at[1])
        wait_all(turned_ref, sems.at[1])
        vec_ref[...] = turned_ref[...].astype(F32).T[:16]
        wait_all(w_ref, sems.at[0])

    def norm(rows):
        normed, _ = norm_parts(x_ref[rows, :].astype(F32))
        h = (normed * vec_ref[0:1, :] + vec_ref[1:2, :]).astype(BF16)
        h_ref[rows, :] = h
        return h

    subs = sub_blocks(x_ref.shape[0])
    h = norm(subs[0])
    for at, rows in enumerate(subs):
        queries = mm(h, w_ref[:, :D])
        after_h = norm(subs[at + 1]) if at + 1 < len(subs) else None
        qkv_ref[rows, :D] = (queries + vec_ref[2:3, :]).astype(BF16)
        qkv_ref[rows, D : 2 * D] = mm(h, w_ref[:, D : 2 * D]).astype(BF16)
        qkv_ref[rows, 2 * D :] = (mm(h, w_ref[:, 2 * D :]) + vec_ref[3:4, :]).astype(BF16)
        h = after_h


def sub_blocks(rows):
    return [slice(at, at + 512) for at in range(0, rows, 512)]


def qkv_call(core, seats, x, group, block=512):
    rows = x.shape[0]
    return pl.pallas_call(
        functools.partial(qkv_kernel, group),
        name="qkv",
        grid_spec=pltpu.PrefetchScalarGridSpec(
            num_scalar_prefetch=2,
            grid=(rows // block,),
            in_specs=[pl.BlockSpec((block, D), lambda i, *s: (i, 0))] + group.specs(),
            out_specs=[
                pl.BlockSpec((block, D), lambda i, *s: (i, 0)),
                pl.BlockSpec((block, 3 * D), lambda i, *s: (i, 0)),
                pl.BlockSpec((16, D), lambda i, *s: (0, 0)),
            ],
            scratch_shapes=[
                pltpu.VMEM((D, 3 * D), BF16),
                pltpu.VMEM((D, 128), BF16),
                pltpu.SemaphoreType.DMA((2,)),
            ],
        ),
        out_shape=[
            jax.ShapeDtypeStruct((rows, D), BF16),
            jax.ShapeDtypeStruct((rows, 3 * D), BF16),
            jax.ShapeDtypeStruct((16, D), F32),
        ],
        compiler_params=params(),
        cost_estimate=cost(2 * rows * D * 3 * D, 10e6),
    )(core, seats, x, *group.arrays)


def head_parts(length, q_all, k_all, head):
    full_len = q_all.shape[0]
    lane = lax.broadcasted_iota(jnp.int32, (1, 128), 1)
    mine = (lane // HEAD_DIM) == head
    spare = lane == HEAD_DIM * (1 - head)
    pos = lax.broadcasted_iota(jnp.int32, (full_len, 128), 0)
    fill = jnp.where(pos < length, 0.0, NEG_FILL).astype(BF16)
    zero = jnp.zeros((), BF16)
    k_head = jnp.where(mine, k_all, jnp.where(spare, fill, zero))
    q_plain = jnp.where(mine, q_all, zero)
    q_head = jnp.where(spare, jnp.ones((), BF16), q_plain)
    return mine, k_head, q_plain, q_head


def causal_mask(scores, block):
    full = scores.shape[0]
    key_pos = lax.broadcasted_iota(jnp.int32, (block, block), 0)
    query_pos = lax.broadcasted_iota(jnp.int32, (block, block), 1)
    last = jnp.where(key_pos <= query_pos, scores[full - block :], NEG_FILL)
    if full == block:
        return last
    return jnp.concatenate([scores[: full - block], last], axis=0)


def attend_kernel(core_ref, len_ref, q_ref, k_ref, v_ref, *refs):
    a_ref, lse_ref, mixed_ref, scores_ref = refs[-4:]
    block = 256
    full_len = q_ref.shape[0]
    length = len_ref[core_ref[0]]
    q_all = q_ref[...] * jnp.asarray(HEAD_DIM ** (-0.5), BF16)
    k_all = k_ref[...]
    v_turned = v_ref[...].T
    ones = jnp.ones((16, full_len), BF16)
    parts = []
    for head in range(2):
        _, k_head, _, q_head = head_parts(length, q_all, k_all, head)
        v_head = jnp.concatenate([v_turned[head * HEAD_DIM : (head + 1) * HEAD_DIM], ones], axis=0)
        parts.append((k_head, q_head, v_head))
    units = [(head, j) for j in reversed(range(full_len // block)) for head in range(2)]

    def score(at):
        head, j = units[at]
        k_head, q_head, _ = parts[head]
        top = None
        for i in range(j + 1):
            rows = slice(i * block, (i + 1) * block)
            tile = mm(k_head[rows], q_head[j * block : (j + 1) * block], NT)
            if i == j:
                tile = causal_mask(tile, block)
            scores_ref[at % 2, rows, :] = tile
            part = jnp.max(tile.reshape(block // 8, 8, block), axis=0)
            top = part if top is None else jnp.maximum(top, part)
        return jnp.max(top, axis=0, keepdims=True)

    def finish(at, top):
        head, j = units[at]
        v_head = parts[head][2]
        cols = slice(j * block, (j + 1) * block)
        mixed = None
        for i in range(j + 1):
            rows = slice(i * block, (i + 1) * block)
            exped = jnp.exp(scores_ref[at % 2, rows, :] - top).astype(BF16)
            part = mm(v_head[:, rows], exped)
            mixed = part if mixed is None else mixed + part
        total = mixed[HEAD_DIM : HEAD_DIM + 1]
        mixed_ref[head * HEAD_DIM : (head + 1) * HEAD_DIM, cols] = mixed[:HEAD_DIM] / total
        lse_ref[0, head : head + 1, cols] = top + jnp.log(total)

    top = score(0)
    for at in range(len(units)):
        later = score(at + 1) if at + 1 < len(units) else None
        finish(at, top)
        top = later
    a_ref[...] = mixed_ref[...].T.astype(BF16)


def attend_call(core, lengths, qkv, first, count, before):
    rows = qkv.shape[0]
    pairs = HEADS // 2
    before = list(before)
    return pl.pallas_call(
        attend_kernel,
        name="attend",
        grid_spec=pltpu.PrefetchScalarGridSpec(
            num_scalar_prefetch=2,
            grid=(count,),
            in_specs=[
                pl.BlockSpec((rows, 128), lambda i, c, n: (0, i + first)),
                pl.BlockSpec((rows, 128), lambda i, c, n: (0, i + first + pairs)),
                pl.BlockSpec((rows, 128), lambda i, c, n: (0, i + first + 2 * pairs)),
            ]
            + [pl.BlockSpec(memory_space=pl.ANY)] * len(before),
            out_specs=[
                pl.BlockSpec((rows, 128), lambda i, c, n: (0, i + first)),
                pl.BlockSpec((1, 8, rows), lambda i, c, n: (i + first, 0, 0)),
            ],
            scratch_shapes=[pltpu.VMEM((128, rows), F32), pltpu.VMEM((2, rows, 256), F32)],
        ),
        out_shape=[
            jax.ShapeDtypeStruct((rows, D), BF16),
            jax.ShapeDtypeStruct((pairs, 8, rows), F32),
        ],
        input_output_aliases={5 + i: i for i in range(len(before))},
        compiler_params=params(),
        cost_estimate=cost(3e9 * count, 1.2e6 * count, 2 * rows * rows * 0.6 * count),
    )(core, lengths, qkv, qkv, qkv, *before)


def attend_back_kernel(core_ref, len_ref, q_ref, k_ref, v_ref, a_ref, da_ref, lse_ref, *refs):
    dq_ref, dk_ref, dv_ref, dqt_ref, dk_acc, dv_acc = refs[-6:]
    block = 256
    full_len = q_ref.shape[0]
    length = len_ref[core_ref[0]]
    scale = HEAD_DIM ** (-0.5)
    q_all = q_ref[...] * jnp.asarray(scale, BF16)
    k_all = k_ref[...]
    k_turned = k_all.T
    v_all = v_ref[...]
    da_all = da_ref[...]
    inner = (da_all.astype(F32) * a_ref[...].astype(F32)).T
    parts = []
    for head in range(2):
        mine, k_head, q_plain, q_head = head_parts(length, q_all, k_all, head)
        da_head = jnp.where(mine, da_all, jnp.zeros((), BF16))
        lanes = slice(head * HEAD_DIM, (head + 1) * HEAD_DIM)
        centre = jnp.sum(inner[lanes], axis=0, keepdims=True)
        parts.append((k_head, q_plain, q_head, da_head, lanes, centre))
    units = [
        (head, j, i)
        for j in reversed(range(full_len // block))
        for head in range(2)
        for i in range(j + 1)
    ]

    def score(at):
        head, j, i = units[at]
        k_head, _, q_head, da_head, _, _ = parts[head]
        rows, cols = slice(i * block, (i + 1) * block), slice(j * block, (j + 1) * block)
        tile = mm(k_head[rows], q_head[cols], NT)
        if i == j:
            tile = causal_mask(tile, block)
        return tile, mm(v_all[rows], da_head[cols], NT)

    seen = set()
    ready = score(0)
    dq_part = None
    for at, (head, j, i) in enumerate(units):
        later = score(at + 1) if at + 1 < len(units) else None
        scores, d_probs = ready
        _, q_plain, _, da_head, lanes, centre = parts[head]
        rows, cols = slice(i * block, (i + 1) * block), slice(j * block, (j + 1) * block)
        probs = jnp.exp(scores - lse_ref[0, head : head + 1, cols])
        d_scores = (probs * (d_probs - centre[:, cols])).astype(BF16)
        dv_part = mm(probs.astype(BF16), da_head[cols])
        dk_part = mm(d_scores, q_plain[cols])
        if i in seen:
            dv_acc[rows] += dv_part
            dk_acc[rows] += dk_part
        else:
            seen.add(i)
            dv_acc[rows] = dv_part
            dk_acc[rows] = dk_part
        part = mm(k_turned[lanes, rows], d_scores)
        dq_part = part if i == 0 else dq_part + part
        if i == j:
            dqt_ref[lanes, cols] = dq_part * scale
        ready = later
    dq_ref[...] = dqt_ref[...].T.astype(BF16)
    dk_ref[...] = dk_acc[...].astype(BF16)
    dv_ref[...] = dv_acc[...].astype(BF16)


def attend_back_call(core, lengths, qkv, a, da, lse, start, count, before):
    rows = qkv.shape[0]
    pairs = HEADS // 2
    before = list(before)
    pair_spec = pl.BlockSpec((rows, 128), lambda i, c, n: (0, i + start))
    return pl.pallas_call(
        attend_back_kernel,
        name="attend_back",
        grid_spec=pltpu.PrefetchScalarGridSpec(
            num_scalar_prefetch=2,
            grid=(count,),
            in_specs=[
                pair_spec,
                pl.BlockSpec((rows, 128), lambda i, c, n: (0, i + start + pairs)),
                pl.BlockSpec((rows, 128), lambda i, c, n: (0, i + start + 2 * pairs)),
                pair_spec,
                pair_spec,
                pl.BlockSpec((1, 8, rows), lambda i, c, n: (i + start, 0, 0)),
            ]
            + [pl.BlockSpec(memory_space=pl.ANY)] * len(before),
            out_specs=[pair_spec, pair_spec, pair_spec],
            scratch_shapes=[
                pltpu.VMEM((128, rows), F32),
                pltpu.VMEM((rows, 128), F32),
                pltpu.VMEM((rows, 128), F32),
            ],
        ),
        out_shape=[jax.ShapeDtypeStruct((rows, D), BF16)] * 3,
        input_output_aliases={8 + i: i for i in range(len(before))},
        compiler_params=params(),
        cost_estimate=cost(6e9 * count, 2e6 * count, 2 * rows * rows * 0.6 * count),
    )(core, lengths, qkv, qkv, qkv, a, da, lse, *before)


def valid_rows(core_ref, len_ref, block):
    pos = pl.program_id(0) * block + lax.broadcasted_iota(jnp.int32, (block, 1), 0)
    return pos < len_ref[core_ref[0]]


def add_row(acc_ref, row, value):
    acc_ref[row : row + 1, :] += jnp.sum(value, axis=0, keepdims=True)


def row_block(core, i, steps):
    half = steps // 2
    return jnp.where(i < half, (1 - core) * half + i, core * half + i - half)


def up_kernel(group, core_ref, len_ref, seat_ref, x_ref, a_ref, og_ref, vec_ref, *refs):
    refs, (mid_ref, h_ref, e_ref, slope_ref, dy_ref, wo_ref, wu_ref, sems) = refs[:-8], refs[-8:]
    block = x_ref.shape[0]

    @pl.when(pl.program_id(0) == 0)
    def _():
        group.start(refs, core_ref, seat_ref, 0, D // 2, wo_ref, sems.at[0])
        group.start(refs, core_ref, seat_ref, D // 2, FF // 2, wu_ref, sems.at[1])
        wait_all(wo_ref, sems.at[0])
        wait_all(wu_ref, sems.at[1])

    valid = valid_rows(core_ref, len_ref, block)
    dy_ref[...] = jnp.where(valid, og_ref[...].astype(F32), 0.0).astype(BF16)
    subs = sub_blocks(block)

    def open_up(rows):
        return x_ref[rows, :].astype(F32) + mm(a_ref[rows, :], wo_ref[...]) + vec_ref[4:5, :]

    def norm(rows, mid):
        mid_ref[rows, :] = mid
        normed, _ = norm_parts(mid)
        h = (normed * vec_ref[5:6, :] + vec_ref[6:7, :]).astype(BF16)
        h_ref[rows, :] = h
        return h

    def act(rows, j, z):
        cols = slice(j * D, (j + 1) * D)
        z = z + vec_ref[8 + j : 9 + j, :]
        squared = z * z
        turned = jnp.tanh(z * (GELU_ROOT + (GELU_ROOT * GELU_CUBE) * squared))
        half = 0.5 * turned + 0.5
        act = z * half
        e_ref[rows, cols] = act.astype(BF16)
        slope = half + act * (1.0 - turned) * (GELU_ROOT + (3.0 * GELU_ROOT * GELU_CUBE) * squared)
        slope_ref[rows, cols] = slope.astype(BF16)

    hs = {0: norm(subs[0], open_up(subs[0]))}
    waiting = None
    for at, rows in enumerate(subs):
        later = open_up(subs[at + 1]) if at + 1 < len(subs) else None
        for j in range(FF // D):
            z = mm(hs[at], wu_ref[:, j * D : (j + 1) * D])
            if waiting is not None:
                act(*waiting)
            waiting = (rows, j, z)
            if j == 1 and later is not None:
                hs[at + 1] = norm(subs[at + 1], later)
    act(*waiting)


def up_call(core, lengths, seats, x, a, og, vec, group, block=512):
    rows = x.shape[0]
    row_spec = pl.BlockSpec((block, D), lambda i, *s: (i, 0))
    wide_spec = pl.BlockSpec((block, FF), lambda i, *s: (i, 0))
    low = jax.ShapeDtypeStruct((rows, D), BF16)
    return pl.pallas_call(
        functools.partial(up_kernel, group),
        name="up",
        grid_spec=pltpu.PrefetchScalarGridSpec(
            num_scalar_prefetch=3,
            grid=(rows // block,),
            in_specs=[row_spec, row_spec, row_spec, whole_spec(vec.shape)] + group.specs(),
            out_specs=[row_spec, row_spec, wide_spec, wide_spec, row_spec],
            scratch_shapes=[
                pltpu.VMEM((D, D), BF16),
                pltpu.VMEM((D, FF), BF16),
                pltpu.SemaphoreType.DMA((2,)),
            ],
        ),
        out_shape=[
            jax.ShapeDtypeStruct((rows, D), F32),
            low,
            jax.ShapeDtypeStruct((rows, FF), BF16),
            jax.ShapeDtypeStruct((rows, FF), BF16),
            low,
        ],
        compiler_params=params(),
        cost_estimate=cost(6e9, 30e6, rows * FF),
    )(core, lengths, seats, x, a, og, vec, *group.arrays)


def down_kernel(up_group, down_group, core_ref, len_ref, seat_ref, mid_ref, e_ref, slope_ref, dy_ref, vec_ref, *refs):
    count = len(up_group.arrays)
    up_refs, down_refs = refs[:count], refs[count : count + len(down_group.arrays)]
    (
        theirs_ref, mine_ref, dz_ref, dmb_ref, dm_ref, da_ref, acc_ref, wo_ref, wu_ref, wd_ref, sems,
    ) = refs[-11:]
    block = mid_ref.shape[0]
    step, steps = pl.program_id(0), pl.num_programs(0)

    @pl.when(pl.program_id(0) == 0)
    def _():
        down_group.start(down_refs, core_ref, seat_ref, 0, D // 2, wd_ref, sems.at[2])
        up_group.start(up_refs, core_ref, seat_ref, D // 2, FF // 2, wu_ref, sems.at[1])
        up_group.start(up_refs, core_ref, seat_ref, 0, D // 2, wo_ref, sems.at[0])
        acc_ref[...] = jnp.zeros_like(acc_ref)
        wait_all(wd_ref, sems.at[2])

    pos = row_block(core_ref[0], step, steps) * block + lax.broadcasted_iota(jnp.int32, (block, 1), 0)
    down = vec_ref[7:8, :] + mid_ref[...] + mm(e_ref[...], wd_ref[...])
    down = jnp.where(pos < len_ref[core_ref[0]], down, 0.0).astype(BF16)

    @pl.when(step < steps // 2)
    def _():
        theirs_ref[...] = down

    @pl.when(step >= steps // 2)
    def _():
        mine_ref[0] = down

    @pl.when(step == 0)
    def _():
        wait_all(wu_ref, sems.at[1])
        wait_all(wo_ref, sems.at[0])

    subs = sub_blocks(block)
    add_row(acc_ref, 7, dy_ref[...].astype(F32))
    dhs = [None] * len(subs)
    normals = [None] * len(subs)

    def turn(at, j, de):
        rows, cols = subs[at], slice(j * D, (j + 1) * D)
        dz = (de * slope_ref[rows, cols].astype(F32)).astype(BF16)
        dz_ref[rows, cols] = dz
        add_row(acc_ref, 8 + j, dz.astype(F32))
        part = mm(dz, wu_ref[:, cols], NT)
        dhs[at] = part if dhs[at] is None else dhs[at] + part

    def close(at):
        rows = subs[at]
        normed, scale = norm_parts(mid_ref[rows, :])
        dh = dhs[at]
        add_row(acc_ref, 5, dh * normed)
        add_row(acc_ref, 6, dh)
        dm = dy_ref[rows, :].astype(F32) + norm_back(dh * vec_ref[5:6, :], normed, scale)
        dm_ref[rows, :] = dm
        dm_low = dm.astype(BF16)
        dmb_ref[rows, :] = dm_low
        add_row(acc_ref, 4, dm_low.astype(F32))
        da_ref[rows, :] = mm(dm_low, wo_ref[...], NT).astype(BF16)

    waiting = None
    for at, rows in enumerate(subs):
        for j in range(FF // D):
            de = mm(dy_ref[rows, :], wd_ref[j * D : (j + 1) * D, :], NT)
            if waiting is not None:
                turn(*waiting)
            waiting = (at, j, de)
            if j == 1 and at > 0:
                close(at - 1)
    turn(*waiting)
    close(len(subs) - 1)


def down_call(core, lengths, seats, mid, e, slope, dy, vec, up_group, down_group, block=512):
    rows = mid.shape[0]
    steps = rows // block
    half = steps // 2
    row_spec = pl.BlockSpec((block, D), lambda i, c, *s: (row_block(c[0], i, steps), 0))
    wide_spec = pl.BlockSpec((block, FF), lambda i, c, *s: (row_block(c[0], i, steps), 0))
    low = jax.ShapeDtypeStruct((rows, D), BF16)
    return pl.pallas_call(
        functools.partial(down_kernel, up_group, down_group),
        name="down",
        grid_spec=pltpu.PrefetchScalarGridSpec(
            num_scalar_prefetch=3,
            grid=(steps,),
            in_specs=[row_spec, wide_spec, wide_spec, row_spec, whole_spec(vec.shape)]
            + up_group.specs()
            + down_group.specs(),
            out_specs=[
                pl.BlockSpec((block, D), lambda i, *s: (jnp.minimum(i, half - 1), 0)),
                pl.BlockSpec((1, block, D), lambda i, c, *s: (c[0], jnp.maximum(i - half, 0), 0)),
                wide_spec, row_spec, row_spec, row_spec,
                pl.BlockSpec((16, D), lambda i, *s: (0, 0)),
            ],
            scratch_shapes=[
                pltpu.VMEM((D, D), BF16),
                pltpu.VMEM((D, FF), BF16),
                pltpu.VMEM((FF, D), BF16),
                pltpu.SemaphoreType.DMA((3,)),
            ],
        ),
        out_shape=[
            jax.ShapeDtypeStruct((rows // 2, D), BF16),
            jax.ShapeDtypeStruct((2, rows // 2, D), BF16),
            jax.ShapeDtypeStruct((rows, FF), BF16), low, jax.ShapeDtypeStruct((rows, D), F32), low,
            jax.ShapeDtypeStruct((16, D), F32),
        ],
        compiler_params=params(),
        cost_estimate=cost(1.6e10, 35e6),
    )(core, lengths, seats, mid, e, slope, dy, vec, *up_group.arrays, *down_group.arrays)


def pick(values, half, mode):
    if mode == "split":
        width = values.shape[1] // 2
        return [values[:, half * width : (half + 1) * width]]
    return [values[:, at : at + 128] for at in range(half * 128, values.shape[1], 256)]


def weight_grad_kernel(lefts, rights, mode, core_ref, *refs):
    left_refs, right_refs = refs[:lefts], refs[lefts : lefts + sum(rights)]
    own_ref, other_ref = refs[-2:]
    halves = ([], [])
    at = 0
    for left_ref, count in zip(left_refs, rights):
        left = left_ref[...]
        for right_ref in right_refs[at : at + count]:
            whole = mm(left, right_ref[...], TN).astype(BF16)
            for half in range(2):
                halves[half].extend(pick(whole, half, mode))
        at += count
    low, high = [part[0] if len(part) == 1 else jnp.concatenate(part, axis=1) for part in halves]

    @pl.when(core_ref[0] == 0)
    def _():
        own_ref[...] = low
        other_ref[...] = high

    @pl.when(core_ref[0] != 0)
    def _():
        own_ref[...] = high
        other_ref[...] = low


def weight_grad_call(core, products, block, name, mode="split", cols=None):
    rows, height = products[0][0].shape
    lefts = [left for left, _ in products]
    rights = [right for _, group in products for right in group]
    widths = [right.shape[1] if cols is None else cols[0] for right in rights]
    width = sum(widths)
    seat = 0 if cols is None else cols[1]
    return pl.pallas_call(
        functools.partial(weight_grad_kernel, len(lefts), [len(group) for _, group in products], mode),
        name=name,
        grid_spec=pltpu.PrefetchScalarGridSpec(
            num_scalar_prefetch=1,
            grid=(height // block,),
            in_specs=[pl.BlockSpec((rows, block), lambda i, c: (0, i))] * len(lefts)
            + [
                pl.BlockSpec((rows, w), lambda i, c: (0, seat), pipeline_mode=pl.Buffered(1)) for w in widths
            ],
            out_specs=[pl.BlockSpec((block, width // 2), lambda i, c: (i, 0))] * 2,
        ),
        out_shape=[jax.ShapeDtypeStruct((height, width // 2), BF16)] * 2,
        compiler_params=params(),
        cost_estimate=cost(2 * rows * height * width, rows * (height + width) * 2 + height * width * 2),
    )(core, *lefts, *rights)


def last_kernel(group, core_ref, seat_ref, x_ref, dm_ref, dq_ref, dk_ref, dv_ref, vec_ref, before_ref, *refs):
    refs, (theirs_ref, mine_ref, acc_ref, w_ref, sems) = refs[:-5], refs[-5:]
    step, steps = pl.program_id(0), pl.num_programs(0)

    @pl.when(step == 0)
    def _():
        group.start(refs, core_ref, seat_ref, 0, QKV_HALF, w_ref, sems.at[0])
        acc_ref[...] = before_ref[...]
        wait_all(w_ref, sems.at[0])

    subs = sub_blocks(x_ref.shape[0])

    def product(rows):
        return (
            mm(dq_ref[rows, :], w_ref[:, :D], NT)
            + mm(dk_ref[rows, :], w_ref[:, D : 2 * D], NT)
            + mm(dv_ref[rows, :], w_ref[:, 2 * D :], NT)
        )

    grads = []
    dh = product(subs[0])
    add_row(acc_ref, 2, dq_ref[...].astype(F32))
    add_row(acc_ref, 3, dv_ref[...].astype(F32))
    for at, rows in enumerate(subs):
        later = product(subs[at + 1]) if at + 1 < len(subs) else None
        normed, scale = norm_parts(x_ref[rows, :].astype(F32))
        add_row(acc_ref, 0, dh * normed)
        add_row(acc_ref, 1, dh)
        grads.append(dm_ref[rows, :] + norm_back(dh * vec_ref[0:1, :], normed, scale))
        dh = later

    @pl.when(step < steps // 2)
    def _():
        for rows, grad in zip(subs, grads):
            theirs_ref[rows, :] = grad

    @pl.when(step >= steps // 2)
    def _():
        for rows, grad in zip(subs, grads):
            mine_ref[0, rows, :] = grad


def last_call(core, seats, x, dm, dq, dk, dv, vec, before, group, block=512):
    rows = x.shape[0]
    steps = rows // block
    half = steps // 2
    row_spec = pl.BlockSpec((block, D), lambda i, c, *s: (row_block(c[0], i, steps), 0))
    return pl.pallas_call(
        functools.partial(last_kernel, group),
        name="last",
        grid_spec=pltpu.PrefetchScalarGridSpec(
            num_scalar_prefetch=2,
            grid=(steps,),
            in_specs=[row_spec] * 5 + [whole_spec(vec.shape), whole_spec(before.shape)] + group.specs(),
            out_specs=[
                pl.BlockSpec((block, D), lambda i, *s: (jnp.minimum(i, half - 1), 0)),
                pl.BlockSpec((1, block, D), lambda i, c, *s: (c[0], jnp.maximum(i - half, 0), 0)),
                pl.BlockSpec((16, D), lambda i, *s: (0, 0)),
            ],
            scratch_shapes=[pltpu.VMEM((D, 3 * D), BF16), pltpu.SemaphoreType.DMA((1,))],
        ),
        out_shape=[
            jax.ShapeDtypeStruct((rows // 2, D), F32),
            jax.ShapeDtypeStruct((2, rows // 2, D), F32),
            jax.ShapeDtypeStruct((16, D), F32),
        ],
        compiler_params=params(),
        cost_estimate=cost(rows * 6 * D * D, 16e6),
    )(core, seats, x, dm, dq, dk, dv, vec, before, *group.arrays)


def adam_kernel(plans, sources, core_ref, *refs):
    halves = [refs[2 * i : 2 * i + 2] for i in range(sources)]
    count = len(plans)
    states = refs[2 * sources : 2 * sources + 3 * count]
    outs = refs[2 * sources + 3 * count : 2 * sources + 6 * count]
    grads = refs[2 * sources + 6 * count :]
    for core in range(2):

        @pl.when(core_ref[0] == core)
        def _():
            for (_, _, moves), grad_ref in zip(plans, grads):
                for source, start, width, place0, place1 in moves:
                    for half, place in ((0, place0), (1, place1)):
                        ref = halves[source][0 if half == core else 1]
                        grad_ref[:, place : place + width] = ref[:, start : start + width].astype(F32)

    for i, (rate, decay, _) in enumerate(plans):
        weight, first, second = states[3 * i : 3 * i + 3]
        new = adamw(weight[...], grads[i][...], first[...], second[...], rate, decay)
        for out, value in zip(outs[3 * i : 3 * i + 3], new):
            out[...] = value


def adam_call(core, halves, states, plans):
    flat = [part for pair in halves for part in pair]
    held = [part for state in states for part in state]
    spec = pl.BlockSpec(memory_space=pltpu.VMEM)
    news = pl.pallas_call(
        functools.partial(adam_kernel, plans, len(halves)),
        name="adam",
        in_specs=[pl.BlockSpec(memory_space=pltpu.SMEM)] + [spec] * (len(flat) + len(held)),
        out_specs=[spec] * len(held),
        out_shape=[jax.ShapeDtypeStruct(part.shape, F32) for part in held],
        scratch_shapes=[pltpu.VMEM(state[0].shape, F32) for state in states],
        compiler_params=params(),
        cost_estimate=cost(1e6, 24 * sum(state[0].size for state in states)),
    )(core, *flat, *held)
    return [news[3 * i : 3 * i + 3] for i in range(len(states))]


def after(value, *others):
    if not others:
        return value
    return lax.optimization_barrier((value,) + others)[0]


class Grid:
    def __init__(self, chips):
        log = chips.bit_length() - 1
        side = 1 << (log // 3)
        if side * side * (chips // (side * side)) != chips:
            side = 1
        self.chips = chips
        self.n = side
        self.nz = chips // (side * side)
        self.core = lax.axis_index("seq")
        self.chip = lax.axis_index("dp")
        self.x = self.chip % side
        self.y = self.chip // side % side
        self.z = self.chip // (side * side)

    def plane(self, first, second, core):
        return jnp.where(core == 0, second * self.n + first, first * self.n + second)

    def coords(self, core):
        return jnp.where(core == 0, self.x, self.y), jnp.where(core == 0, self.y, self.x)

    def permute(self, value, axis, shift=0):
        pairs = []
        for chip in range(self.chips):
            for core in range(2):
                x, y, z = chip % self.n, chip // self.n % self.n, chip // (self.n * self.n)
                to_core = core
                if axis == "z":
                    z = (z + shift) % self.nz
                elif axis == "zx":
                    z = z ^ shift
                elif axis == "core":
                    to_core = 1 - core
                elif (axis == "first") == (core == 0):
                    x = (x + shift) % self.n
                else:
                    y = (y + shift) % self.n
                pairs.append((chip * 2 + core, ((z * self.n + y) * self.n + x) * 2 + to_core))
        return lax.ppermute(value, ("dp", "seq"), pairs)

    def swap(self, value):
        return self.permute(value, "core")

    def join(self, own, other, axis):
        return jnp.where(
            self.core == 0,
            jnp.concatenate([own, other], axis),
            jnp.concatenate([other, own], axis),
        )

    def seats(self, halving):
        found = []
        for half in range(2):
            core = self.core if half == 0 else 1 - self.core
            first, second = self.coords(core)
            for s2 in range(self.n):
                for s1 in range(self.n):
                    flat = self.plane((first - s1) % self.n, (second - s2) % self.n, core)
                    for sz in range(self.nz):
                        z = self.z ^ sz if halving else (self.z - sz) % self.nz
                        found.append(z * self.n * self.n + flat)
        return jnp.stack(found).astype(jnp.int32)

    def total_small(self, value, *untils):
        steps = [("core", 0), ("first", 1), ("second", 1)] if self.n == 2 else [("core", 0)]
        if self.n != 2:
            for axis in ("first", "second"):
                value = value + sum(self.permute(value, axis, s) for s in range(1, self.n))
        bit = 1
        while bit < self.nz:
            steps.append(("zx", bit))
            bit *= 2
        for at, (axis, shift) in enumerate(steps):
            until = untils[at] if at < len(untils) else ()
            value = value + after(self.permute(value, axis, shift), *until)
        return value

    def gather_z(self, block, *until):
        return jnp.stack([block] + [after(self.permute(block, "z", s), *until) for s in range(1, self.nz)])

    def gather_bit(self, held, bit, *until):
        return jnp.concatenate([held, after(self.permute(held, "zx", bit), *until)])

    def gather_first(self, column, *until):
        return jnp.stack([column] + [after(self.permute(column, "first", s), *until) for s in range(1, self.n)])

    def gather_second(self, line, *until):
        return [after(self.permute(line, "second", s), *until) for s in range(1, self.n)]

    def scatter_first(self, own, pair, *until):
        rows, cols = own.shape[0] // self.chips, own.shape[1]
        first, second = self.coords(self.core)
        n = self.n

        def seat(s1, s2):
            where = self.plane((first + s1) % n, (second + s2) % n, self.core)
            own_part, pair_part = [
                lax.dynamic_slice(
                    part.reshape(self.nz, n * n, rows, cols), (0, where, 0, 0), (self.nz, 1, rows, cols)
                ).astype(F32)
                for part in (own, pair)
            ]
            return own_part + pair_part

        kept = [seat(0, t) for t in range(n)]
        for s in range(1, n):
            send = jnp.stack([seat(s, t).astype(BF16) for t in range(n)])
            got = after(self.permute(send, "first", s), *until)
            kept = [kept[t] + got[t].astype(F32) for t in range(n)]
        return kept[0], [part.astype(BF16) for part in kept[1:]]

    def scatter_second(self, kept, *until):
        mine, rest = kept
        got = [after(self.permute(rest[s - 1], "second", s), *until) for s in range(1, self.n)]
        for part in got:
            mine = mine + part.astype(F32)
        return mine.reshape((self.nz,) + mine.shape[2:]), got

    def order_z(self, mine):
        return [lax.dynamic_index_in_dim(mine, self.z ^ at, 0, keepdims=False) for at in range(self.nz)]

    def scatter_bit(self, parts, *until):
        half = len(parts) // 2
        send = parts[half] if half == 1 else jnp.stack([part.astype(BF16) for part in parts[half:]])
        got = after(self.permute(send.astype(BF16), "zx", half), *until)
        if half == 1:
            return [parts[0] + got.astype(F32)], got
        return [part + got[at].astype(F32) for at, part in enumerate(parts[:half])], got

    def scatter_z(self, parts):
        while len(parts) > 1:
            parts, _ = self.scatter_bit(parts)
        return parts[0]


def adamw(weight, gradient, first_moment, second_moment, step_rate, weight_decay):
    first_moment = BETA_ONE * first_moment + (1.0 - BETA_ONE) * gradient
    second_moment = BETA_TWO * second_moment + (1.0 - BETA_TWO) * gradient * gradient
    first_fix = 1.0 - BETA_ONE**STEP
    second_fix = 1.0 - BETA_TWO**STEP
    direction = first_moment / first_fix / (jnp.sqrt(second_moment / second_fix) + EPS_ADAM)
    return (weight - step_rate * (direction + weight_decay * weight), first_moment, second_moment)


def local(
    block_in, lengths, out_grad, w_qkv, w_out, w_up, w_down, vectors,
    first_qkv, first_out, first_up, first_down, first_vectors,
    second_qkv, second_out, second_up, second_down, second_vectors,
):
    grid = Grid(lax.axis_size("dp"))
    core = grid.core
    core_arr = core.reshape(1).astype(jnp.int32)
    half_len = block_in.shape[1]
    vec_count, vec_here = vectors.shape

    def own_slot(halves):
        mine = lax.dynamic_index_in_dim(halves, core, 0, keepdims=False)
        theirs = lax.dynamic_index_in_dim(halves, 1 - core, 0, keepdims=False)
        return grid.join(mine, grid.swap(theirs), 0)

    def both_slots(mine, got):
        return lax.dynamic_update_slice(mine, got[None], (1 - core, 0, 0))

    def half_of(shard):
        width = shard.shape[1] // 2
        return lax.dynamic_slice_in_dim(shard, core * width, width, 1).astype(BF16)

    seats, q_seats = grid.seats(True), grid.seats(False)

    turned = jnp.pad(vectors.T.astype(BF16), ((0, 0), (0, 128 - vec_count)))
    q_block = jnp.concatenate([half_of(w_qkv), turned], axis=1)
    u_block = jnp.concatenate([half_of(w_out), half_of(w_up)], axis=1)
    d_block = half_of(w_down)
    q_col = grid.gather_z(q_block)
    x = own_slot(block_in)
    bits = [1 << at for at in range((grid.nz - 1).bit_length())]
    u_col, d_col = u_block[None], d_block[None]
    for bit in bits[:-1]:
        u_col = grid.gather_bit(u_col, bit)
        d_col = grid.gather_bit(d_col, bit)
    q_line = after(grid.gather_first(q_col, x), u_col, d_col)
    q_rest = grid.gather_second(q_line)
    u_col = grid.gather_bit(after(u_col, q_line), bits[-1])
    q_line_swap = grid.swap(q_line)
    q_rest_swap = [grid.swap(after(part, u_col)) for part in q_rest]
    q_group = finish_group(grid, q_seats, [q_line] + q_rest, [q_line_swap] + q_rest_swap)

    h1, qkv, vec = qkv_call(core_arr, q_seats, x, q_group)
    u_line = grid.gather_first(u_col, qkv)
    d_col = grid.gather_bit(after(d_col, u_col), bits[-1], qkv)
    og = own_slot(after(out_grad, qkv))
    att = attend_call(core_arr, lengths, after(qkv, u_line, d_col), 0, 4, ())
    u_line_swap = after(grid.swap(u_line), *att)
    u_rest = grid.gather_second(u_line, *att)
    d_col = after(d_col, *u_rest)
    a, lse = attend_call(core_arr, lengths, after(qkv, d_col), 4, 2, att)
    u_rest_swap = [after(grid.swap(part), a) for part in u_rest]
    d_line = grid.gather_first(d_col, a)
    u_group = finish_group(grid, seats, [u_line] + u_rest, [u_line_swap] + u_rest_swap)
    mid, h2, e, slope, dy = up_call(core_arr, lengths, seats, x, after(a, d_line), og, vec, u_group)
    d_line_swap = after(grid.swap(d_line), mid)
    d_rest = grid.gather_second(d_line, mid)
    d_own, d_other = weight_grad_call(core_arr, [(after(e, *d_rest), [dy])], 512, "grad_down")
    d_rest_swap = [after(grid.swap(part), d_own) for part in d_rest]
    d_group = finish_group(grid, seats, [d_line] + d_rest, [d_line_swap] + d_rest_swap)
    out_theirs, out_mine, dz, dmb, dm, da, acc_mid = down_call(
        core_arr, lengths, seats, mid, e, slope, dy, vec, u_group, d_group
    )

    d_pair = after(grid.swap(d_other), dz)
    u_own, u_other = weight_grad_call(
        core_arr, [(a, [dmb]), (h2, [after(dz, d_pair)])], 384, "grad_up"
    )
    d_kept = grid.scatter_first(d_own, d_pair, u_own)

    def back_call(start, count, before, *needs):
        return attend_back_call(core_arr, lengths, qkv, a, after(da, *needs), lse, start, count, before)

    back = back_call(0, 2, (), u_own, *d_kept[1])
    d_sum, d_here = grid.scatter_second(d_kept, *back)
    u_pair = after(grid.swap(u_other), *back)
    back = back_call(2, 2, back, u_pair, *d_here)
    d_parts, d_got = grid.scatter_bit(grid.order_z(d_sum), *back)
    back = back_call(4, 2, back, d_got)
    u_kept = grid.scatter_first(u_own, u_pair, *back)
    dq, dk, dv = back
    block_out = both_slots(out_mine, after(grid.swap(after(out_theirs, back[0])), dq))
    q_own, q_other = weight_grad_call(
        core_arr, [(h1, [after(dq, *u_kept[1]), dk, dv])], 384, "grad_qkv", "turns"
    )
    u_sum, u_here = grid.scatter_second(u_kept, q_own)
    d_mine = grid.scatter_z(d_parts)
    in_theirs, in_mine, acc = last_call(
        core_arr, q_seats, x, dm, after(dq, q_own, *u_here), dk, dv, vec, acc_mid, q_group
    )
    q_pair = after(grid.swap(q_other), in_theirs)
    u_parts, u_got = grid.scatter_bit(grid.order_z(u_sum), in_theirs)
    d_other_mine = after(grid.swap(d_mine), in_theirs)
    q_kept = grid.scatter_first(q_own, after(q_pair, u_got))
    in_got = grid.swap(after(in_theirs, q_pair))
    down_new, = adam_call(
        core_arr,
        [(d_mine, d_other_mine)],
        [(after(w_down, in_theirs), first_down, second_down)],
        [(FF ** (-0.5), MATRIX_DECAY, [(0, 0, D // 2, 0, D // 2)])],
    )
    u_mine = grid.scatter_z(u_parts)
    q_sum, q_here = grid.scatter_second(q_kept)
    u_other_mine = grid.swap(u_mine)
    in_grad = both_slots(in_mine, in_got)
    vec_total = grid.total_small(acc, q_kept[1], q_here)
    q_mine = grid.scatter_z(grid.order_z(q_sum))
    q_other_mine = grid.swap(q_mine)

    half, wide = D // 2, FF // 2
    out_new, up_new = adam_call(
        core_arr,
        [(u_mine, u_other_mine)],
        [(w_out, first_out, second_out), (w_up, first_up, second_up)],
        [
            ((D // 64) ** (-0.5), MATRIX_DECAY, [(0, 0, half, 0, half)]),
            (D ** (-0.5), MATRIX_DECAY, [(0, half, wide, 0, wide)]),
        ],
    )
    moves = []
    for turn in range(3 * D // 256):
        moves.append((0, turn * 128, 128, turn * 256, turn * 256 + 128))
    qkv_new, = adam_call(
        core_arr,
        [(q_mine, q_other_mine)],
        [(w_qkv, first_qkv, second_qkv)],
        [(D ** (-0.5), MATRIX_DECAY, moves)],
    )
    vec_grad = lax.dynamic_slice(vec_total, (0, grid.chip * vec_here), (vec_count, vec_here))
    vec_new = adamw(vectors, vec_grad, first_vectors, second_vectors, VECTOR_RATE, 0.0)
    news = [qkv_new, out_new, up_new, down_new, vec_new]
    return (block_out, in_grad) + tuple(new[kind] for kind in range(3) for new in news)


def finish_group(grid, seats, own, other):
    rows, cols = own[0].shape[-2:]
    if rows % 16 == 0:
        return Pieces(own + other, rows)
    found = []
    for half, parts in enumerate((own, other)):
        here = seats[half * grid.chips : (half + 1) * grid.chips]
        order = jnp.zeros((grid.chips,), jnp.int32).at[here].set(jnp.arange(grid.chips, dtype=jnp.int32))
        blocks = jnp.concatenate(parts).reshape(grid.chips, rows, cols)
        found.append(jnp.take(blocks, order, axis=0).reshape(1, 1, grid.chips * rows, cols))
    return Pieces(found, grid.chips * rows, True)


def solution(mesh):
    weight = P("dp", None)
    vector = P(None, "dp")
    state = (weight, weight, weight, weight, vector)
    tokens = P("dp", "seq", None)
    return jax.shard_map(
        local,
        mesh=mesh,
        in_specs=(tokens, P("dp"), tokens) + state * 3,
        out_specs=(tokens, tokens) + state * 3,
        check_vma=False,
    )
```

```python
import functools

import jax
import jax.numpy as jnp
from jax import lax
from jax.experimental import pallas as pl
from jax.experimental.pallas import tpu as pltpu
from jax.sharding import PartitionSpec as P

D = 768
HEADS = 12
HEAD_DIM = 64
FF = 3072
STEP = 10

EPS_NORM = 1e-05
EPS_ADAM = 1e-08
BETA_ONE = 0.5
BETA_TWO = 0.5
MATRIX_DECAY = 0.1
VECTOR_RATE = 0.1
NEG_FILL = -1e30
GELU_ROOT = 0.7978845608028654
GELU_CUBE = 0.044715
QKV_HALF = 3 * D // 2

F32 = jnp.float32
BF16 = jnp.bfloat16

NN = (((1,), (0,)), ((), ()))
NT = (((1,), (1,)), ((), ()))
TN = (((0,), (0,)), ((), ()))


def mm(left, right, dims=NN):
    return lax.dot_general(left, right, dims, preferred_element_type=F32)


def cost(flops, nbytes, trans=0):
    return pl.CostEstimate(flops=int(4 * flops), bytes_accessed=int(4 * nbytes), transcendentals=int(trans))


def params(mib=60):
    return pltpu.CompilerParams(vmem_limit_bytes=mib * 1024 * 1024)


def held_spec():
    return pl.BlockSpec(memory_space=pltpu.VMEM)


def at_rows(block):
    return pl.ds(pl.multiple_of(pl.program_id(0) * block, block), block)


def whole_spec(shape):
    return pl.BlockSpec(shape, lambda *idx: (0,) * len(shape), pipeline_mode=pl.Buffered(1))


class Pieces:
    def __init__(self, arrays, rows, ordered=False):
        self.arrays = arrays
        self.rows = rows
        self.ordered = ordered
        self.halves = 2
        self.count = len(arrays) // self.halves
        self.lines, self.depth = arrays[0].shape[:2]

    def specs(self):
        return [pl.BlockSpec(memory_space=pltpu.HBM)] * len(self.arrays)

    def row(self, seat_ref, at):
        return 0 if self.ordered else pl.multiple_of(seat_ref[at] * self.rows, 16)

    def start(self, refs, core_ref, seat_ref, start_col, width, target, sem):
        core = core_ref[0]
        at = 0
        for half in range(self.halves):
            where = core if half == 0 else 1 - core
            for s2 in range(self.count):
                ref = refs[half * self.count + s2]
                for s1 in range(self.lines):
                    for sz in range(self.depth):
                        row = self.row(seat_ref, at)
                        at += 1
                        col = pl.multiple_of(where * width, 128)
                        pltpu.make_async_copy(
                            ref.at[s1, sz, :, pl.ds(start_col, width)],
                            target.at[pl.ds(row, self.rows), pl.ds(col, width)],
                            sem,
                        ).start()

    def start_once(self, refs, seat_ref, start_col, width, target, sem):
        at = 0
        for s2 in range(self.count):
            for s1 in range(self.lines):
                for sz in range(self.depth):
                    row = self.row(seat_ref, at)
                    at += 1
                    pltpu.make_async_copy(
                        refs[s2].at[s1, sz, :, pl.ds(start_col, width)],
                        target.at[pl.ds(row, self.rows), :],
                        sem,
                    ).start()


def wait_all(target, sem):
    pltpu.make_async_copy(target, target, sem).wait()


def norm_parts(rows):
    mean = jnp.mean(rows, axis=-1, keepdims=True)
    centred = rows - mean
    variance = jnp.mean(centred * centred, axis=-1, keepdims=True)
    scale = lax.rsqrt(variance + EPS_NORM)
    return centred * scale, scale


def norm_back(d_normed, normed, scale):
    first = jnp.mean(d_normed, axis=-1, keepdims=True)
    second = jnp.mean(d_normed * normed, axis=-1, keepdims=True)
    return scale * (d_normed - first - normed * second)


def qkv_kernel(group, core_ref, seat_ref, x_ref, *refs):
    refs, (h_ref, qkv_ref, held_ref, vec_ref, w_ref, turned_ref, sems) = refs[:-7], refs[-7:]

    @pl.when(pl.program_id(0) == 0)
    def _():
        group.start(refs, core_ref, seat_ref, 0, QKV_HALF, w_ref, sems.at[0])
        group.start_once(refs, seat_ref, QKV_HALF, 128, turned_ref, sems.at[1])
        wait_all(turned_ref, sems.at[1])
        vec_ref[...] = turned_ref[...].astype(F32).T[:16]
        wait_all(w_ref, sems.at[0])

    def norm(rows):
        normed, _ = norm_parts(x_ref[rows, :].astype(F32))
        h = (normed * vec_ref[0:1, :] + vec_ref[1:2, :]).astype(BF16)
        h_ref[rows, :] = h
        return h

    block = x_ref.shape[0]
    h = norm(slice(0, block))
    for part, bias in enumerate((2, None, 3)):
        cols = slice(part * D, (part + 1) * D)
        product = mm(h, w_ref[:, cols])
        if bias is not None:
            product = product + vec_ref[bias : bias + 1, :]
        product = product.astype(BF16)
        qkv_ref[:, cols] = product
        held_ref[at_rows(block), cols] = product


def sub_blocks(rows):
    return [slice(at, at + 256) for at in range(0, rows, 256)]


def qkv_call(core, seats, x, group, block=256):
    rows = x.shape[0]
    return pl.pallas_call(
        functools.partial(qkv_kernel, group),
        name="qkv",
        grid_spec=pltpu.PrefetchScalarGridSpec(
            num_scalar_prefetch=2,
            grid=(rows // block,),
            in_specs=[pl.BlockSpec((block, D), lambda i, *s: (i, 0))] + group.specs(),
            out_specs=[
                pl.BlockSpec((block, D), lambda i, *s: (i, 0)),
                pl.BlockSpec((block, 3 * D), lambda i, *s: (i, 0)),
                held_spec(),
                pl.BlockSpec((16, D), lambda i, *s: (0, 0)),
            ],
            scratch_shapes=[
                pltpu.VMEM((D, 3 * D), BF16),
                pltpu.VMEM((D, 128), BF16),
                pltpu.SemaphoreType.DMA((2,)),
            ],
        ),
        out_shape=[
            jax.ShapeDtypeStruct((rows, D), BF16),
            jax.ShapeDtypeStruct((rows, 3 * D), BF16),
            pltpu.VMEM((rows, 3 * D), BF16),
            jax.ShapeDtypeStruct((16, D), F32),
        ],
        compiler_params=params(24),
        cost_estimate=cost(2 * rows * D * 3 * D, 10e6),
    )(core, seats, x, *group.arrays)


def head_parts(length, q_all, k_all, head):
    full_len = q_all.shape[0]
    lane = lax.broadcasted_iota(jnp.int32, (1, 128), 1)
    mine = (lane // HEAD_DIM) == head
    spare = lane == HEAD_DIM * (1 - head)
    pos = lax.broadcasted_iota(jnp.int32, (full_len, 128), 0)
    fill = jnp.where(pos < length, 0.0, NEG_FILL).astype(BF16)
    zero = jnp.zeros((), BF16)
    k_head = jnp.where(mine, k_all, jnp.where(spare, fill, zero))
    q_plain = jnp.where(mine, q_all, zero)
    q_head = jnp.where(spare, jnp.ones((), BF16), q_plain)
    return mine, k_head, q_plain, q_head


def causal_mask(scores, block):
    full = scores.shape[0]
    key_pos = lax.broadcasted_iota(jnp.int32, (block, block), 0)
    query_pos = lax.broadcasted_iota(jnp.int32, (block, block), 1)
    last = jnp.where(key_pos <= query_pos, scores[full - block :], NEG_FILL)
    if full == block:
        return last
    return jnp.concatenate([scores[: full - block], last], axis=0)


def attend_kernel(start, core_ref, len_ref, qkv_ref, *refs):
    a_ref, lse_ref, mixed_ref, scores_ref = refs[-4:]
    block = 256
    full_len = qkv_ref.shape[0]
    length = len_ref[core_ref[0]]
    q_all, k_all, v_all = [
        qkv_ref[:, pl.ds(pl.multiple_of((pl.program_id(0) + start) * 128 + part * D, 128), 128)] for part in range(3)
    ]
    q_all = q_all * jnp.asarray(HEAD_DIM ** (-0.5), BF16)
    v_turned = v_all.T
    ones = jnp.ones((16, full_len), BF16)
    parts = []
    for head in range(2):
        _, k_head, _, q_head = head_parts(length, q_all, k_all, head)
        v_head = jnp.concatenate([v_turned[head * HEAD_DIM : (head + 1) * HEAD_DIM], ones], axis=0)
        parts.append((k_head, q_head, v_head))
    units = [(head, j) for j in reversed(range(full_len // block)) for head in range(2)]

    def score(at):
        head, j = units[at]
        k_head, q_head, _ = parts[head]
        top = None
        for i in range(j + 1):
            rows = slice(i * block, (i + 1) * block)
            tile = mm(k_head[rows], q_head[j * block : (j + 1) * block], NT)
            if i == j:
                tile = causal_mask(tile, block)
            scores_ref[at % 2, rows, :] = tile
            part = jnp.max(tile.reshape(block // 8, 8, block), axis=0)
            top = part if top is None else jnp.maximum(top, part)
        return jnp.max(top, axis=0, keepdims=True)

    def finish(at, top):
        head, j = units[at]
        v_head = parts[head][2]
        cols = slice(j * block, (j + 1) * block)
        mixed = None
        for i in range(j + 1):
            rows = slice(i * block, (i + 1) * block)
            exped = jnp.exp(scores_ref[at % 2, rows, :] - top).astype(BF16)
            part = mm(v_head[:, rows], exped)
            mixed = part if mixed is None else mixed + part
        total = mixed[HEAD_DIM : HEAD_DIM + 1]
        mixed_ref[head * HEAD_DIM : (head + 1) * HEAD_DIM, cols] = mixed[:HEAD_DIM] / total
        lse_ref[0, head : head + 1, cols] = top + jnp.log(total)

    top = score(0)
    for at in range(len(units)):
        later = score(at + 1) if at + 1 < len(units) else None
        finish(at, top)
        top = later
    a_ref[...] = mixed_ref[...].T.astype(BF16)


def attend_call(core, lengths, qkv, first, count, before):
    rows = qkv.shape[0]
    pairs = HEADS // 2
    before = list(before)
    return pl.pallas_call(
        functools.partial(attend_kernel, first),
        name="attend",
        grid_spec=pltpu.PrefetchScalarGridSpec(
            num_scalar_prefetch=2,
            grid=(count,),
            in_specs=[held_spec()] + [pl.BlockSpec(memory_space=pl.ANY)] * len(before),
            out_specs=[
                pl.BlockSpec((rows, 128), lambda i, c, n: (0, i + first)),
                pl.BlockSpec((1, 8, rows), lambda i, c, n: (i + first, 0, 0)),
            ],
            scratch_shapes=[pltpu.VMEM((128, rows), F32), pltpu.VMEM((2, rows, 256), F32)],
        ),
        out_shape=[
            jax.ShapeDtypeStruct((rows, D), BF16),
            jax.ShapeDtypeStruct((pairs, 8, rows), F32),
        ],
        input_output_aliases={3 + i: i for i in range(len(before))},
        compiler_params=params(40),
        cost_estimate=cost(3e9 * count, 1.2e6 * count, 2 * rows * rows * 0.6 * count),
    )(core, lengths, qkv, *before)


def attend_back_kernel(core_ref, len_ref, q_ref, k_ref, v_ref, a_ref, da_ref, lse_ref, *refs):
    dq_ref, dk_ref, dv_ref, dqt_ref, dk_acc, dv_acc = refs[-6:]
    block = 256
    full_len = q_ref.shape[0]
    length = len_ref[core_ref[0]]
    scale = HEAD_DIM ** (-0.5)
    q_all = q_ref[...] * jnp.asarray(scale, BF16)
    k_all = k_ref[...]
    k_turned = k_all.T
    v_all = v_ref[...]
    da_all = da_ref[...]
    inner = (da_all.astype(F32) * a_ref[...].astype(F32)).T
    parts = []
    for head in range(2):
        mine, k_head, q_plain, q_head = head_parts(length, q_all, k_all, head)
        da_head = jnp.where(mine, da_all, jnp.zeros((), BF16))
        lanes = slice(head * HEAD_DIM, (head + 1) * HEAD_DIM)
        centre = jnp.sum(inner[lanes], axis=0, keepdims=True)
        parts.append((k_head, q_plain, q_head, da_head, lanes, centre))
    units = [
        (head, j, i)
        for j in reversed(range(full_len // block))
        for head in range(2)
        for i in range(j + 1)
    ]

    def score(at):
        head, j, i = units[at]
        k_head, _, q_head, da_head, _, _ = parts[head]
        rows, cols = slice(i * block, (i + 1) * block), slice(j * block, (j + 1) * block)
        tile = mm(k_head[rows], q_head[cols], NT)
        if i == j:
            tile = causal_mask(tile, block)
        return tile, mm(v_all[rows], da_head[cols], NT)

    seen = set()
    ready = score(0)
    dq_part = None
    for at, (head, j, i) in enumerate(units):
        later = score(at + 1) if at + 1 < len(units) else None
        scores, d_probs = ready
        _, q_plain, _, da_head, lanes, centre = parts[head]
        rows, cols = slice(i * block, (i + 1) * block), slice(j * block, (j + 1) * block)
        probs = jnp.exp(scores - lse_ref[0, head : head + 1, cols])
        d_scores = (probs * (d_probs - centre[:, cols])).astype(BF16)
        dv_part = mm(probs.astype(BF16), da_head[cols])
        dk_part = mm(d_scores, q_plain[cols])
        if i in seen:
            dv_acc[rows] += dv_part
            dk_acc[rows] += dk_part
        else:
            seen.add(i)
            dv_acc[rows] = dv_part
            dk_acc[rows] = dk_part
        part = mm(k_turned[lanes, rows], d_scores)
        dq_part = part if i == 0 else dq_part + part
        if i == j:
            dqt_ref[lanes, cols] = dq_part * scale
        ready = later
    dq_ref[...] = dqt_ref[...].T.astype(BF16)
    dk_ref[...] = dk_acc[...].astype(BF16)
    dv_ref[...] = dv_acc[...].astype(BF16)


def attend_back_call(core, lengths, qkv, a, da, lse, start, count, before):
    rows = qkv.shape[0]
    pairs = HEADS // 2
    before = list(before)
    pair_spec = pl.BlockSpec((rows, 128), lambda i, c, n: (0, i + start))
    return pl.pallas_call(
        attend_back_kernel,
        name="attend_back",
        grid_spec=pltpu.PrefetchScalarGridSpec(
            num_scalar_prefetch=2,
            grid=(count,),
            in_specs=[
                pair_spec,
                pl.BlockSpec((rows, 128), lambda i, c, n: (0, i + start + pairs)),
                pl.BlockSpec((rows, 128), lambda i, c, n: (0, i + start + 2 * pairs)),
                pair_spec,
                pair_spec,
                pl.BlockSpec((1, 8, rows), lambda i, c, n: (i + start, 0, 0)),
            ]
            + [pl.BlockSpec(memory_space=pl.ANY)] * len(before),
            out_specs=[pair_spec, pair_spec, pair_spec],
            scratch_shapes=[
                pltpu.VMEM((128, rows), F32),
                pltpu.VMEM((rows, 128), F32),
                pltpu.VMEM((rows, 128), F32),
            ],
        ),
        out_shape=[jax.ShapeDtypeStruct((rows, D), BF16)] * 3,
        input_output_aliases={8 + i: i for i in range(len(before))},
        compiler_params=params(),
        cost_estimate=cost(6e9 * count, 2e6 * count, 2 * rows * rows * 0.6 * count),
    )(core, lengths, qkv, qkv, qkv, a, da, lse, *before)


def valid_rows(core_ref, len_ref, block):
    pos = pl.program_id(0) * block + lax.broadcasted_iota(jnp.int32, (block, 1), 0)
    return pos < len_ref[core_ref[0]]


def add_row(acc_ref, row, value):
    acc_ref[row : row + 1, :] += jnp.sum(value, axis=0, keepdims=True)


def row_block(core, i, steps):
    half = steps // 2
    return jnp.where(i < half, (1 - core) * half + i, core * half + i - half)


def up_kernel(group, core_ref, len_ref, seat_ref, x_ref, a_ref, og_ref, vec_ref, *refs):
    refs, (mid_ref, h_ref, e_ref, slope_ref, dy_ref, wo_ref, wu_ref, sems) = refs[:-8], refs[-8:]
    block = x_ref.shape[0]

    @pl.when(pl.program_id(0) == 0)
    def _():
        group.start(refs, core_ref, seat_ref, 0, D // 2, wo_ref, sems.at[0])
        group.start(refs, core_ref, seat_ref, D // 2, FF // 2, wu_ref, sems.at[1])
        wait_all(wo_ref, sems.at[0])
        wait_all(wu_ref, sems.at[1])

    rows = at_rows(block)
    valid = valid_rows(core_ref, len_ref, block)
    dy_ref[rows, :] = jnp.where(valid, og_ref[...].astype(F32), 0.0).astype(BF16)
    mid = x_ref[...].astype(F32) + mm(a_ref[...], wo_ref[...]) + vec_ref[4:5, :]
    mid_ref[rows, :] = mid
    normed, _ = norm_parts(mid)
    h = (normed * vec_ref[5:6, :] + vec_ref[6:7, :]).astype(BF16)
    h_ref[rows, :] = h

    def act(rows, j, z):
        cols = slice(j * D, (j + 1) * D)
        z = z + vec_ref[8 + j : 9 + j, :]
        squared = z * z
        turned = jnp.tanh(z * (GELU_ROOT + (GELU_ROOT * GELU_CUBE) * squared))
        half = 0.5 * turned + 0.5
        act = z * half
        e_ref[rows, cols] = act.astype(BF16)
        slope = half + act * (1.0 - turned) * (GELU_ROOT + (3.0 * GELU_ROOT * GELU_CUBE) * squared)
        slope_ref[rows, cols] = slope.astype(BF16)

    waiting = None
    for j in range(FF // D):
        z = mm(h, wu_ref[:, j * D : (j + 1) * D])
        if waiting is not None:
            act(rows, *waiting)
        waiting = (j, z)
    act(rows, *waiting)


def up_call(core, lengths, seats, x, a, og, vec, group, block=256):
    rows = x.shape[0]
    row_spec = pl.BlockSpec((block, D), lambda i, *s: (i, 0))
    return pl.pallas_call(
        functools.partial(up_kernel, group),
        name="up",
        grid_spec=pltpu.PrefetchScalarGridSpec(
            num_scalar_prefetch=3,
            grid=(rows // block,),
            in_specs=[row_spec, row_spec, row_spec, whole_spec(vec.shape)] + group.specs(),
            out_specs=[held_spec()] * 7,
            scratch_shapes=[pltpu.SemaphoreType.DMA((2,))],
        ),
        out_shape=[
            pltpu.VMEM((rows, D), F32),
            pltpu.VMEM((rows, D), BF16),
            pltpu.VMEM((rows, FF), BF16),
            pltpu.VMEM((rows, FF), BF16),
            pltpu.VMEM((rows, D), BF16),
            pltpu.VMEM((D, D), BF16),
            pltpu.VMEM((D, FF), BF16),
        ],
        compiler_params=params(24),
        cost_estimate=cost(6e9, 30e6, rows * FF),
    )(core, lengths, seats, x, a, og, vec, *group.arrays)


def down_kernel(
    group, core_ref, len_ref, seat_ref, mid_ref, e_ref, slope_ref, dy_ref, wo_ref, wu_ref, vec_ref, *refs
):
    refs, (theirs_ref, mine_ref, dz_ref, dmb_ref, dm_ref, da_ref, acc_ref, wd_ref, sems) = refs[:-9], refs[-9:]
    block = da_ref.shape[0]
    step, steps = pl.program_id(0), pl.num_programs(0)

    @pl.when(step == 0)
    def _():
        group.start(refs, core_ref, seat_ref, 0, D // 2, wd_ref, sems.at[0])
        acc_ref[...] = jnp.zeros_like(acc_ref)
        wait_all(wd_ref, sems.at[0])

    first = row_block(core_ref[0], step, steps) * block
    rows = pl.ds(pl.multiple_of(first, block), block)
    mid = mid_ref[rows, :]
    down = vec_ref[7:8, :] + mid + mm(e_ref[rows, :], wd_ref[...])
    pos = first + lax.broadcasted_iota(jnp.int32, (block, 1), 0)
    down = jnp.where(pos < len_ref[core_ref[0]], down, 0.0).astype(BF16)

    @pl.when(step < steps // 2)
    def _():
        theirs_ref[...] = down

    @pl.when(step >= steps // 2)
    def _():
        mine_ref[0] = down

    dy = dy_ref[rows, :]
    add_row(acc_ref, 7, dy.astype(F32))
    dh = None
    waiting = None
    for j in range(FF // D + 1):
        later = None
        if j < FF // D:
            later = (j, mm(dy, wd_ref[j * D : (j + 1) * D, :], NT))
        if waiting is not None:
            at, de = waiting
            cols = slice(at * D, (at + 1) * D)
            dz = (de * slope_ref[rows, cols].astype(F32)).astype(BF16)
            dz_ref[rows, cols] = dz
            add_row(acc_ref, 8 + at, dz.astype(F32))
            part = mm(dz, wu_ref[:, cols], NT)
            dh = part if dh is None else dh + part
        waiting = later
    normed, scale = norm_parts(mid)
    add_row(acc_ref, 5, dh * normed)
    add_row(acc_ref, 6, dh)
    dm = dy.astype(F32) + norm_back(dh * vec_ref[5:6, :], normed, scale)
    dm_ref[...] = dm
    dm_low = dm.astype(BF16)
    dmb_ref[rows, :] = dm_low
    add_row(acc_ref, 4, dm_low.astype(F32))
    da_ref[...] = mm(dm_low, wo_ref[...], NT).astype(BF16)


def down_call(core, lengths, seats, mid, e, slope, dy, wo, wu, vec, group, block=256):
    rows = mid.shape[0]
    steps = rows // block
    half = steps // 2
    row_spec = pl.BlockSpec((block, D), lambda i, c, *s: (row_block(c[0], i, steps), 0))
    return pl.pallas_call(
        functools.partial(down_kernel, group),
        name="down",
        grid_spec=pltpu.PrefetchScalarGridSpec(
            num_scalar_prefetch=3,
            grid=(steps,),
            in_specs=[held_spec()] * 6 + [whole_spec(vec.shape)] + group.specs(),
            out_specs=[
                pl.BlockSpec((block, D), lambda i, *s: (jnp.minimum(i, half - 1), 0)),
                pl.BlockSpec((1, block, D), lambda i, c, *s: (c[0], jnp.maximum(i - half, 0), 0)),
                held_spec(), held_spec(), row_spec, row_spec,
                pl.BlockSpec((16, D), lambda i, *s: (0, 0)),
            ],
            scratch_shapes=[pltpu.VMEM((FF, D), BF16), pltpu.SemaphoreType.DMA((1,))],
        ),
        out_shape=[
            jax.ShapeDtypeStruct((rows // 2, D), BF16),
            jax.ShapeDtypeStruct((2, rows // 2, D), BF16),
            pltpu.VMEM((rows, FF), BF16),
            pltpu.VMEM((rows, D), BF16),
            jax.ShapeDtypeStruct((rows, D), F32),
            jax.ShapeDtypeStruct((rows, D), BF16),
            jax.ShapeDtypeStruct((16, D), F32),
        ],
        compiler_params=params(24),
        cost_estimate=cost(1.6e10, 35e6),
    )(core, lengths, seats, mid, e, slope, dy, wo, wu, vec, *group.arrays)


def pick(values, half, mode):
    if mode == "split":
        width = values.shape[1] // 2
        return [values[:, half * width : (half + 1) * width]]
    return [values[:, at : at + 128] for at in range(half * 128, values.shape[1], 256)]


def weight_grad_kernel(lefts, rights, mode, block, held, core_ref, *refs):
    left_refs, right_refs = refs[:lefts], refs[lefts : lefts + sum(rights)]
    own_ref, other_ref = refs[-2:]
    halves = ([], [])
    at = 0
    for left_ref, count in zip(left_refs, rights):
        left = left_ref[:, at_rows(block)] if held else left_ref[...]
        for right_ref in right_refs[at : at + count]:
            whole = mm(left, right_ref[...], TN).astype(BF16)
            for half in range(2):
                halves[half].extend(pick(whole, half, mode))
        at += count
    low, high = [part[0] if len(part) == 1 else jnp.concatenate(part, axis=1) for part in halves]

    @pl.when(core_ref[0] == 0)
    def _():
        own_ref[...] = low
        other_ref[...] = high

    @pl.when(core_ref[0] != 0)
    def _():
        own_ref[...] = high
        other_ref[...] = low


def weight_grad_call(core, products, block, name, mode="split", cols=None, held=False):
    rows, height = products[0][0].shape
    lefts = [left for left, _ in products]
    rights = [right for _, group in products for right in group]
    widths = [right.shape[1] if cols is None else cols[0] for right in rights]
    width = sum(widths)
    seat = 0 if cols is None else cols[1]
    return pl.pallas_call(
        functools.partial(weight_grad_kernel, len(lefts), [len(group) for _, group in products], mode, block, held),
        name=name,
        grid_spec=pltpu.PrefetchScalarGridSpec(
            num_scalar_prefetch=1,
            grid=(height // block,),
            in_specs=[held_spec()] * (len(lefts) + len(rights))
            if held
            else [pl.BlockSpec((rows, block), lambda i, c: (0, i))] * len(lefts)
            + [
                pl.BlockSpec((rows, w), lambda i, c: (0, seat), pipeline_mode=pl.Buffered(1)) for w in widths
            ],
            out_specs=[pl.BlockSpec((block, width // 2), lambda i, c: (i, 0))] * 2,
        ),
        out_shape=[jax.ShapeDtypeStruct((height, width // 2), BF16)] * 2,
        compiler_params=params(24 if held else 60),
        cost_estimate=cost(2 * rows * height * width, rows * (height + width) * 2 + height * width * 2),
    )(core, *lefts, *rights)


def last_kernel(group, core_ref, seat_ref, x_ref, dm_ref, dq_ref, dk_ref, dv_ref, vec_ref, before_ref, *refs):
    refs, (theirs_ref, mine_ref, acc_ref, w_ref, sems) = refs[:-5], refs[-5:]
    step, steps = pl.program_id(0), pl.num_programs(0)

    @pl.when(step == 0)
    def _():
        group.start(refs, core_ref, seat_ref, 0, QKV_HALF, w_ref, sems.at[0])
        acc_ref[...] = before_ref[...]
        wait_all(w_ref, sems.at[0])

    subs = sub_blocks(x_ref.shape[0])

    def product(rows):
        return (
            mm(dq_ref[rows, :], w_ref[:, :D], NT)
            + mm(dk_ref[rows, :], w_ref[:, D : 2 * D], NT)
            + mm(dv_ref[rows, :], w_ref[:, 2 * D :], NT)
        )

    grads = []
    dh = product(subs[0])
    add_row(acc_ref, 2, dq_ref[...].astype(F32))
    add_row(acc_ref, 3, dv_ref[...].astype(F32))
    for at, rows in enumerate(subs):
        later = product(subs[at + 1]) if at + 1 < len(subs) else None
        normed, scale = norm_parts(x_ref[rows, :].astype(F32))
        add_row(acc_ref, 0, dh * normed)
        add_row(acc_ref, 1, dh)
        grads.append(dm_ref[rows, :] + norm_back(dh * vec_ref[0:1, :], normed, scale))
        dh = later

    @pl.when(step < steps // 2)
    def _():
        for rows, grad in zip(subs, grads):
            theirs_ref[rows, :] = grad

    @pl.when(step >= steps // 2)
    def _():
        for rows, grad in zip(subs, grads):
            mine_ref[0, rows, :] = grad


def last_call(core, seats, x, dm, dq, dk, dv, vec, before, group, block=256):
    rows = x.shape[0]
    steps = rows // block
    half = steps // 2
    row_spec = pl.BlockSpec((block, D), lambda i, c, *s: (row_block(c[0], i, steps), 0))
    return pl.pallas_call(
        functools.partial(last_kernel, group),
        name="last",
        grid_spec=pltpu.PrefetchScalarGridSpec(
            num_scalar_prefetch=2,
            grid=(steps,),
            in_specs=[row_spec] * 5 + [whole_spec(vec.shape), whole_spec(before.shape)] + group.specs(),
            out_specs=[
                pl.BlockSpec((block, D), lambda i, *s: (jnp.minimum(i, half - 1), 0)),
                pl.BlockSpec((1, block, D), lambda i, c, *s: (c[0], jnp.maximum(i - half, 0), 0)),
                pl.BlockSpec((16, D), lambda i, *s: (0, 0)),
            ],
            scratch_shapes=[pltpu.VMEM((D, 3 * D), BF16), pltpu.SemaphoreType.DMA((1,))],
        ),
        out_shape=[
            jax.ShapeDtypeStruct((rows // 2, D), F32),
            jax.ShapeDtypeStruct((2, rows // 2, D), F32),
            jax.ShapeDtypeStruct((16, D), F32),
        ],
        compiler_params=params(),
        cost_estimate=cost(rows * 6 * D * D, 16e6),
    )(core, seats, x, dm, dq, dk, dv, vec, before, *group.arrays)


def adam_kernel(plans, sources, core_ref, *refs):
    halves = [refs[2 * i : 2 * i + 2] for i in range(sources)]
    count = len(plans)
    states = refs[2 * sources : 2 * sources + 3 * count]
    outs = refs[2 * sources + 3 * count : 2 * sources + 6 * count]
    grads = refs[2 * sources + 6 * count :]
    for core in range(2):

        @pl.when(core_ref[0] == core)
        def _():
            for (_, _, moves), grad_ref in zip(plans, grads):
                for source, start, width, place0, place1 in moves:
                    for half, place in ((0, place0), (1, place1)):
                        ref = halves[source][0 if half == core else 1]
                        grad_ref[:, place : place + width] = ref[:, start : start + width].astype(F32)

    for i, (rate, decay, _) in enumerate(plans):
        weight, first, second = states[3 * i : 3 * i + 3]
        new = adamw(weight[...], grads[i][...], first[...], second[...], rate, decay)
        for out, value in zip(outs[3 * i : 3 * i + 3], new):
            out[...] = value


def adam_call(core, halves, states, plans):
    flat = [part for pair in halves for part in pair]
    held = [part for state in states for part in state]
    spec = pl.BlockSpec(memory_space=pltpu.VMEM)
    news = pl.pallas_call(
        functools.partial(adam_kernel, plans, len(halves)),
        name="adam",
        in_specs=[pl.BlockSpec(memory_space=pltpu.SMEM)] + [spec] * (len(flat) + len(held)),
        out_specs=[spec] * len(held),
        out_shape=[jax.ShapeDtypeStruct(part.shape, F32) for part in held],
        scratch_shapes=[pltpu.VMEM(state[0].shape, F32) for state in states],
        compiler_params=params(16),
        cost_estimate=cost(1e6, 24 * sum(state[0].size for state in states)),
    )(core, *flat, *held)
    return [news[3 * i : 3 * i + 3] for i in range(len(states))]


def after(value, *others):
    if not others:
        return value
    return lax.optimization_barrier((value,) + others)[0]


class Grid:
    def __init__(self, chips):
        log = chips.bit_length() - 1
        side = 1 << (log // 3)
        if side * side * (chips // (side * side)) != chips:
            side = 1
        self.chips = chips
        self.n = side
        self.nz = chips // (side * side)
        self.core = lax.axis_index("seq")
        self.chip = lax.axis_index("dp")
        self.x = self.chip % side
        self.y = self.chip // side % side
        self.z = self.chip // (side * side)

    def plane(self, first, second, core):
        return jnp.where(core == 0, second * self.n + first, first * self.n + second)

    def coords(self, core):
        return jnp.where(core == 0, self.x, self.y), jnp.where(core == 0, self.y, self.x)

    def permute(self, value, axis, shift=0):
        pairs = []
        for chip in range(self.chips):
            for core in range(2):
                x, y, z = chip % self.n, chip // self.n % self.n, chip // (self.n * self.n)
                to_core = core
                if axis == "z":
                    z = (z + shift) % self.nz
                elif axis == "zx":
                    z = z ^ shift
                elif axis == "core":
                    to_core = 1 - core
                elif (axis == "first") == (core == 0):
                    x = (x + shift) % self.n
                else:
                    y = (y + shift) % self.n
                pairs.append((chip * 2 + core, ((z * self.n + y) * self.n + x) * 2 + to_core))
        return lax.ppermute(value, ("dp", "seq"), pairs)

    def swap(self, value):
        return self.permute(value, "core")

    def join(self, own, other, axis):
        return jnp.where(
            self.core == 0,
            jnp.concatenate([own, other], axis),
            jnp.concatenate([other, own], axis),
        )

    def seats(self, halving):
        found = []
        for half in range(2):
            core = self.core if half == 0 else 1 - self.core
            first, second = self.coords(core)
            for s2 in range(self.n):
                for s1 in range(self.n):
                    flat = self.plane((first - s1) % self.n, (second - s2) % self.n, core)
                    for sz in range(self.nz):
                        z = self.z ^ sz if halving else (self.z - sz) % self.nz
                        found.append(z * self.n * self.n + flat)
        return jnp.stack(found).astype(jnp.int32)

    def total_small(self, value, *untils):
        steps = [("core", 0), ("first", 1), ("second", 1)] if self.n == 2 else [("core", 0)]
        if self.n != 2:
            for axis in ("first", "second"):
                value = value + sum(self.permute(value, axis, s) for s in range(1, self.n))
        bit = 1
        while bit < self.nz:
            steps.append(("zx", bit))
            bit *= 2
        for at, (axis, shift) in enumerate(steps):
            until = untils[at] if at < len(untils) else ()
            value = value + after(self.permute(value, axis, shift), *until)
        return value

    def gather_z(self, block, *until):
        return jnp.stack([block] + [after(self.permute(block, "z", s), *until) for s in range(1, self.nz)])

    def gather_bit(self, held, bit, *until):
        return jnp.concatenate([held, after(self.permute(held, "zx", bit), *until)])

    def gather_first(self, column, *until):
        return jnp.stack([column] + [after(self.permute(column, "first", s), *until) for s in range(1, self.n)])

    def gather_second(self, line, *until):
        return [after(self.permute(line, "second", s), *until) for s in range(1, self.n)]

    def scatter_first(self, own, pair, *until):
        rows, cols = own.shape[0] // self.chips, own.shape[1]
        first, second = self.coords(self.core)
        n = self.n

        def seat(s1, s2):
            where = self.plane((first + s1) % n, (second + s2) % n, self.core)
            own_part, pair_part = [
                lax.dynamic_slice(
                    part.reshape(self.nz, n * n, rows, cols), (0, where, 0, 0), (self.nz, 1, rows, cols)
                ).astype(F32)
                for part in (own, pair)
            ]
            return own_part + pair_part

        kept = [seat(0, t) for t in range(n)]
        for s in range(1, n):
            send = jnp.stack([seat(s, t).astype(BF16) for t in range(n)])
            got = after(self.permute(send, "first", s), *until)
            kept = [kept[t] + got[t].astype(F32) for t in range(n)]
        return kept[0], [part.astype(BF16) for part in kept[1:]]

    def scatter_second(self, kept, *until):
        mine, rest = kept
        got = [after(self.permute(rest[s - 1], "second", s), *until) for s in range(1, self.n)]
        for part in got:
            mine = mine + part.astype(F32)
        return mine.reshape((self.nz,) + mine.shape[2:]), got

    def order_z(self, mine):
        return [lax.dynamic_index_in_dim(mine, self.z ^ at, 0, keepdims=False) for at in range(self.nz)]

    def scatter_bit(self, parts, *until):
        half = len(parts) // 2
        send = parts[half] if half == 1 else jnp.stack([part.astype(BF16) for part in parts[half:]])
        got = after(self.permute(send.astype(BF16), "zx", half), *until)
        if half == 1:
            return [parts[0] + got.astype(F32)], got
        return [part + got[at].astype(F32) for at, part in enumerate(parts[:half])], got

    def scatter_z(self, parts):
        while len(parts) > 1:
            parts, _ = self.scatter_bit(parts)
        return parts[0]


def adamw(weight, gradient, first_moment, second_moment, step_rate, weight_decay):
    first_moment = BETA_ONE * first_moment + (1.0 - BETA_ONE) * gradient
    second_moment = BETA_TWO * second_moment + (1.0 - BETA_TWO) * gradient * gradient
    first_fix = 1.0 - BETA_ONE**STEP
    second_fix = 1.0 - BETA_TWO**STEP
    direction = first_moment / first_fix / (jnp.sqrt(second_moment / second_fix) + EPS_ADAM)
    return (weight - step_rate * (direction + weight_decay * weight), first_moment, second_moment)


def local(
    block_in, lengths, out_grad, w_qkv, w_out, w_up, w_down, vectors,
    first_qkv, first_out, first_up, first_down, first_vectors,
    second_qkv, second_out, second_up, second_down, second_vectors,
):
    grid = Grid(lax.axis_size("dp"))
    core = grid.core
    core_arr = core.reshape(1).astype(jnp.int32)
    half_len = block_in.shape[1]
    vec_count, vec_here = vectors.shape

    def own_slot(halves):
        mine = lax.dynamic_index_in_dim(halves, core, 0, keepdims=False)
        theirs = lax.dynamic_index_in_dim(halves, 1 - core, 0, keepdims=False)
        return grid.join(mine, grid.swap(theirs), 0)

    def both_slots(mine, got):
        return lax.dynamic_update_slice(mine, got[None], (1 - core, 0, 0))

    def half_of(shard):
        width = shard.shape[1] // 2
        return lax.dynamic_slice_in_dim(shard, core * width, width, 1).astype(BF16)

    seats, q_seats = grid.seats(True), grid.seats(False)

    turned = jnp.pad(vectors.T.astype(BF16), ((0, 0), (0, 128 - vec_count)))
    q_block = jnp.concatenate([half_of(w_qkv), turned], axis=1)
    u_block = jnp.concatenate([half_of(w_out), half_of(w_up)], axis=1)
    d_block = half_of(w_down)
    q_col = grid.gather_z(q_block)
    x = own_slot(block_in)
    bits = [1 << at for at in range((grid.nz - 1).bit_length())]
    u_col, d_col = u_block[None], d_block[None]
    for bit in bits[:-1]:
        u_col = grid.gather_bit(u_col, bit)
        d_col = grid.gather_bit(d_col, bit)
    q_line = after(grid.gather_first(q_col, x), u_col, d_col)
    q_rest = grid.gather_second(q_line)
    u_col = grid.gather_bit(after(u_col, q_line), bits[-1])
    q_line_swap = grid.swap(q_line)
    q_rest_swap = [grid.swap(after(part, u_col)) for part in q_rest]
    q_group = finish_group(grid, q_seats, [q_line] + q_rest, [q_line_swap] + q_rest_swap)

    h1, qkv, qkv_held, vec = qkv_call(core_arr, q_seats, x, q_group)
    u_line = grid.gather_first(u_col, qkv)
    d_col = grid.gather_bit(after(d_col, u_col), bits[-1], qkv)
    og = own_slot(after(out_grad, qkv))
    att = attend_call(core_arr, lengths, after(qkv_held, u_line, d_col), 0, 4, ())
    u_line_swap = after(grid.swap(u_line), *att)
    u_rest = grid.gather_second(u_line, *att)
    d_col = after(d_col, *u_rest)
    a, lse = attend_call(core_arr, lengths, after(qkv_held, d_col), 4, 2, att)
    u_rest_swap = [after(grid.swap(part), a) for part in u_rest]
    d_line = grid.gather_first(d_col, a)
    u_group = finish_group(grid, seats, [u_line] + u_rest, [u_line_swap] + u_rest_swap)
    mid, h2, e, slope, dy, wo, wu = up_call(core_arr, lengths, seats, x, after(a, d_line), og, vec, u_group)
    d_line_swap = after(grid.swap(d_line), mid)
    d_rest = grid.gather_second(d_line, mid)
    d_own, d_other = weight_grad_call(core_arr, [(after(e, *d_rest), [dy])], 512, "grad_down", held=True)
    d_rest_swap = [after(grid.swap(part), d_own) for part in d_rest]
    d_group = finish_group(grid, seats, [d_line] + d_rest, [d_line_swap] + d_rest_swap)
    out_theirs, out_mine, dz, dmb, dm, da, acc_mid = down_call(
        core_arr, lengths, seats, mid, e, slope, dy, wo, wu, vec, d_group
    )

    d_pair = after(grid.swap(d_other), dz)
    u_own, u_other = weight_grad_call(
        core_arr, [(a, [dmb]), (h2, [after(dz, d_pair)])], 384, "grad_up", held=True
    )
    d_kept = grid.scatter_first(d_own, d_pair, u_own)

    def back_call(start, count, before, *needs):
        return attend_back_call(core_arr, lengths, qkv, a, after(da, *needs), lse, start, count, before)

    back = back_call(0, 2, (), u_own, *d_kept[1])
    d_sum, d_here = grid.scatter_second(d_kept, *back)
    u_pair = after(grid.swap(u_other), *back)
    back = back_call(2, 4, back, u_pair, *d_here)
    d_parts, _ = grid.scatter_bit(grid.order_z(d_sum), *back)
    u_kept = grid.scatter_first(u_own, u_pair, *back)
    dq, dk, dv = back
    block_out = both_slots(out_mine, after(grid.swap(after(out_theirs, back[0])), dq))
    q_own, q_other = weight_grad_call(
        core_arr, [(h1, [after(dq, *u_kept[1]), dk, dv])], 384, "grad_qkv", "turns"
    )
    u_sum, u_here = grid.scatter_second(u_kept, q_own)
    d_mine = grid.scatter_z(d_parts)
    in_theirs, in_mine, acc = last_call(
        core_arr, q_seats, x, dm, after(dq, q_own, *u_here), dk, dv, vec, acc_mid, q_group
    )
    q_pair = after(grid.swap(q_other), in_theirs)
    u_parts, u_got = grid.scatter_bit(grid.order_z(u_sum), in_theirs)
    d_other_mine = after(grid.swap(d_mine), in_theirs)
    q_kept = grid.scatter_first(q_own, after(q_pair, u_got))
    in_got = grid.swap(after(in_theirs, q_pair))
    down_new, = adam_call(
        core_arr,
        [(d_mine, d_other_mine)],
        [(after(w_down, in_theirs), first_down, second_down)],
        [(FF ** (-0.5), MATRIX_DECAY, [(0, 0, D // 2, 0, D // 2)])],
    )
    u_mine = grid.scatter_z(u_parts)
    q_sum, q_here = grid.scatter_second(q_kept)
    u_other_mine = grid.swap(u_mine)
    in_grad = both_slots(in_mine, in_got)
    vec_total = grid.total_small(acc, q_kept[1], q_here)
    q_mine = grid.scatter_z(grid.order_z(q_sum))
    q_other_mine = grid.swap(q_mine)

    half, wide = D // 2, FF // 2
    out_new, up_new = adam_call(
        core_arr,
        [(u_mine, u_other_mine)],
        [(w_out, first_out, second_out), (w_up, first_up, second_up)],
        [
            ((D // 64) ** (-0.5), MATRIX_DECAY, [(0, 0, half, 0, half)]),
            (D ** (-0.5), MATRIX_DECAY, [(0, half, wide, 0, wide)]),
        ],
    )
    moves = []
    for turn in range(3 * D // 256):
        moves.append((0, turn * 128, 128, turn * 256, turn * 256 + 128))
    qkv_new, = adam_call(
        core_arr,
        [(q_mine, q_other_mine)],
        [(w_qkv, first_qkv, second_qkv)],
        [(D ** (-0.5), MATRIX_DECAY, moves)],
    )
    vec_grad = lax.dynamic_slice(vec_total, (0, grid.chip * vec_here), (vec_count, vec_here))
    vec_new = adamw(vectors, vec_grad, first_vectors, second_vectors, VECTOR_RATE, 0.0)
    news = [qkv_new, out_new, up_new, down_new, vec_new]
    return (block_out, in_grad) + tuple(new[kind] for kind in range(3) for new in news)


def finish_group(grid, seats, own, other):
    rows, cols = own[0].shape[-2:]
    if rows % 16 == 0:
        return Pieces(own + other, rows)
    found = []
    for half, parts in enumerate((own, other)):
        here = seats[half * grid.chips : (half + 1) * grid.chips]
        order = jnp.zeros((grid.chips,), jnp.int32).at[here].set(jnp.arange(grid.chips, dtype=jnp.int32))
        blocks = jnp.concatenate(parts).reshape(grid.chips, rows, cols)
        found.append(jnp.take(blocks, order, axis=0).reshape(1, 1, grid.chips * rows, cols))
    return Pieces(found, grid.chips * rows, True)


def solution(mesh):
    weight = P("dp", None)
    vector = P(None, "dp")
    state = (weight, weight, weight, weight, vector)
    tokens = P("dp", "seq", None)
    return jax.shard_map(
        local,
        mesh=mesh,
        in_specs=(tokens, P("dp"), tokens) + state * 3,
        out_specs=(tokens, tokens) + state * 3,
        check_vma=False,
    )
```

```python
import functools

import jax
import jax.numpy as jnp
from jax import lax
from jax.experimental import pallas as pl
from jax.experimental.pallas import tpu as pltpu
from jax.sharding import PartitionSpec as P

D = 768
HEADS = 12
HEAD_DIM = 64
FF = 3072
STEP = 10

EPS_NORM = 1e-05
EPS_ADAM = 1e-08
BETA_ONE = 0.5
BETA_TWO = 0.5
MATRIX_DECAY = 0.1
VECTOR_RATE = 0.1
NEG_FILL = -1e30
GELU_ROOT = 0.7978845608028654
GELU_CUBE = 0.044715
QKV_HALF = 3 * D // 2

F32 = jnp.float32
BF16 = jnp.bfloat16

NN = (((1,), (0,)), ((), ()))
NT = (((1,), (1,)), ((), ()))
TN = (((0,), (0,)), ((), ()))


def mm(left, right, dims=NN):
    return lax.dot_general(left, right, dims, preferred_element_type=F32)


def cost(flops, nbytes, trans=0):
    return pl.CostEstimate(flops=int(4 * flops), bytes_accessed=int(4 * nbytes), transcendentals=int(trans))


def params(mib=60):
    return pltpu.CompilerParams(vmem_limit_bytes=mib * 1024 * 1024)


def held_spec():
    return pl.BlockSpec(memory_space=pltpu.VMEM)


def at_rows(block):
    return pl.ds(pl.multiple_of(pl.program_id(0) * block, block), block)


def whole_spec(shape):
    return pl.BlockSpec(shape, lambda *idx: (0,) * len(shape), pipeline_mode=pl.Buffered(1))


class Pieces:
    def __init__(self, arrays, rows, ordered=False):
        self.arrays = arrays
        self.rows = rows
        self.ordered = ordered
        self.halves = 2
        self.count = len(arrays) // self.halves
        self.lines, self.depth = arrays[0].shape[:2]

    def specs(self):
        return [pl.BlockSpec(memory_space=pltpu.HBM)] * len(self.arrays)

    def row(self, seat_ref, at):
        return 0 if self.ordered else pl.multiple_of(seat_ref[at] * self.rows, 16)

    def start(self, refs, core_ref, seat_ref, start_col, width, target, sem):
        core = core_ref[0]
        at = 0
        for half in range(self.halves):
            where = core if half == 0 else 1 - core
            for s2 in range(self.count):
                ref = refs[half * self.count + s2]
                for s1 in range(self.lines):
                    for sz in range(self.depth):
                        row = self.row(seat_ref, at)
                        at += 1
                        col = pl.multiple_of(where * width, 128)
                        pltpu.make_async_copy(
                            ref.at[s1, sz, :, pl.ds(start_col, width)],
                            target.at[pl.ds(row, self.rows), pl.ds(col, width)],
                            sem,
                        ).start()

    def start_once(self, refs, seat_ref, start_col, width, target, sem):
        at = 0
        for s2 in range(self.count):
            for s1 in range(self.lines):
                for sz in range(self.depth):
                    row = self.row(seat_ref, at)
                    at += 1
                    pltpu.make_async_copy(
                        refs[s2].at[s1, sz, :, pl.ds(start_col, width)],
                        target.at[pl.ds(row, self.rows), :],
                        sem,
                    ).start()


def wait_all(target, sem):
    pltpu.make_async_copy(target, target, sem).wait()


def norm_parts(rows):
    mean = jnp.mean(rows, axis=-1, keepdims=True)
    centred = rows - mean
    variance = jnp.mean(centred * centred, axis=-1, keepdims=True)
    scale = lax.rsqrt(variance + EPS_NORM)
    return centred * scale, scale


def norm_back(d_normed, normed, scale):
    first = jnp.mean(d_normed, axis=-1, keepdims=True)
    second = jnp.mean(d_normed * normed, axis=-1, keepdims=True)
    return scale * (d_normed - first - normed * second)


def qkv_kernel(group, core_ref, seat_ref, x_ref, *refs):
    refs, (h_ref, qkv_ref, vec_ref, back_ref, w_ref, turned_ref, sems) = refs[:-7], refs[-7:]

    @pl.when(pl.program_id(0) == 0)
    def _():
        group.start(refs, core_ref, seat_ref, 0, QKV_HALF, w_ref, sems.at[0])
        group.start_once(refs, seat_ref, QKV_HALF, 128, turned_ref, sems.at[1])
        wait_all(turned_ref, sems.at[1])
        vec_ref[...] = turned_ref[...].astype(F32).T[:16]
        wait_all(w_ref, sems.at[0])

    def norm(rows):
        normed, _ = norm_parts(x_ref[rows, :].astype(F32))
        h = (normed * vec_ref[0:1, :] + vec_ref[1:2, :]).astype(BF16)
        h_ref[rows, :] = h
        return h

    block = x_ref.shape[0]
    h = norm(slice(0, block))
    for part, bias in enumerate((2, None, 3)):
        cols = slice(part * D, (part + 1) * D)
        product = mm(h, w_ref[:, cols])
        if bias is not None:
            product = product + vec_ref[bias : bias + 1, :]
        qkv_ref[:, cols] = product.astype(BF16)

    @pl.when(pl.program_id(0) < 3)
    def _():
        back_ref[...] = w_ref[:, at_rows(D)].T


def sub_blocks(rows):
    return [slice(at, at + 256) for at in range(0, rows, 256)]


def qkv_call(core, seats, x, group, block=256):
    rows = x.shape[0]
    return pl.pallas_call(
        functools.partial(qkv_kernel, group),
        name="qkv",
        grid_spec=pltpu.PrefetchScalarGridSpec(
            num_scalar_prefetch=2,
            grid=(rows // block,),
            in_specs=[pl.BlockSpec((block, D), lambda i, *s: (i, 0))] + group.specs(),
            out_specs=[
                pl.BlockSpec((block, D), lambda i, *s: (i, 0)),
                pl.BlockSpec((block, 3 * D), lambda i, *s: (i, 0)),
                pl.BlockSpec((16, D), lambda i, *s: (0, 0)),
                pl.BlockSpec((D, D), lambda i, *s: (jnp.minimum(i, 2), 0)),
            ],
            scratch_shapes=[
                pltpu.VMEM((D, 3 * D), BF16),
                pltpu.VMEM((D, 128), BF16),
                pltpu.SemaphoreType.DMA((2,)),
            ],
        ),
        out_shape=[
            jax.ShapeDtypeStruct((rows, D), BF16),
            jax.ShapeDtypeStruct((rows, 3 * D), BF16),
            jax.ShapeDtypeStruct((16, D), F32),
            jax.ShapeDtypeStruct((3 * D, D), BF16),
        ],
        compiler_params=params(12),
        cost_estimate=cost(2 * rows * D * 3 * D, 10e6),
    )(core, seats, x, *group.arrays)


def head_parts(length, k_all, q_turned, head):
    full_len = k_all.shape[0]
    lane = lax.broadcasted_iota(jnp.int32, (1, 128), 1)
    row = lax.broadcasted_iota(jnp.int32, (128, 1), 0)
    zero, one = jnp.zeros((), BF16), jnp.ones((), BF16)
    mine = (lane // HEAD_DIM) == head
    spare = HEAD_DIM * (1 - head)
    pos = lax.broadcasted_iota(jnp.int32, (full_len, 128), 0)
    fill = jnp.where(pos < length, 0.0, NEG_FILL).astype(BF16)
    k_head = jnp.where(mine, k_all, jnp.where(lane == spare, fill, zero))
    q_head = jnp.where((row // HEAD_DIM) == head, q_turned, jnp.where(row == spare, one, zero))
    return mine, k_head, q_head


def causal_mask(scores, block):
    full = scores.shape[0]
    key_pos = lax.broadcasted_iota(jnp.int32, (block, block), 0)
    query_pos = lax.broadcasted_iota(jnp.int32, (block, block), 1)
    last = jnp.where(key_pos <= query_pos, scores[full - block :], NEG_FILL)
    if full == block:
        return last
    return jnp.concatenate([scores[: full - block], last], axis=0)


def attend_kernel(start, core_ref, len_ref, qkv_ref, *refs):
    a_ref, lse_ref, mixed_ref, scores_ref = refs[-4:]
    block = 256
    full_len = qkv_ref.shape[0]
    length = len_ref[core_ref[0]]
    q_all, k_all, v_all = [
        qkv_ref[:, pl.ds(pl.multiple_of((pl.program_id(0) + start) * 128 + part * D, 128), 128)] for part in range(3)
    ]
    q_all = q_all * jnp.asarray(HEAD_DIM ** (-0.5), BF16)
    v_turned = v_all.T
    q_turned = q_all.T
    ones = jnp.ones((16, full_len), BF16)
    parts = []
    for head in range(2):
        _, k_head, q_head = head_parts(length, k_all, q_turned, head)
        v_head = jnp.concatenate([v_turned[head * HEAD_DIM : (head + 1) * HEAD_DIM], ones], axis=0)
        parts.append((k_head, q_head, v_head))
    units = [(head, j) for j in reversed(range(full_len // block)) for head in range(2)]

    def score(at):
        head, j = units[at]
        k_head, q_head, _ = parts[head]
        top = None
        for i in range(j + 1):
            rows = slice(i * block, (i + 1) * block)
            tile = mm(k_head[rows], q_head[:, j * block : (j + 1) * block])
            if i == j:
                tile = causal_mask(tile, block)
            scores_ref[at % 2, rows, :] = tile
            part = jnp.max(tile.reshape(block // 8, 8, block), axis=0)
            top = part if top is None else jnp.maximum(top, part)
        return jnp.max(top, axis=0, keepdims=True)

    def finish(at, top):
        head, j = units[at]
        v_head = parts[head][2]
        cols = slice(j * block, (j + 1) * block)
        mixed = None
        for i in range(j + 1):
            rows = slice(i * block, (i + 1) * block)
            exped = jnp.exp(scores_ref[at % 2, rows, :] - top).astype(BF16)
            part = mm(v_head[:, rows], exped)
            mixed = part if mixed is None else mixed + part
        total = mixed[HEAD_DIM : HEAD_DIM + 1]
        mixed_ref[head * HEAD_DIM : (head + 1) * HEAD_DIM, cols] = mixed[:HEAD_DIM] / total
        lse_ref[0, head : head + 1, cols] = top + jnp.log(total)

    top = score(0)
    for at in range(len(units)):
        later = score(at + 1) if at + 1 < len(units) else None
        finish(at, top)
        top = later
    a_ref[...] = mixed_ref[...].T.astype(BF16)


def attend_call(core, lengths, qkv, first, count, before):
    rows = qkv.shape[0]
    pairs = HEADS // 2
    before = list(before)
    return pl.pallas_call(
        functools.partial(attend_kernel, first),
        name="attend",
        grid_spec=pltpu.PrefetchScalarGridSpec(
            num_scalar_prefetch=2,
            grid=(count,),
            in_specs=[held_spec()] + [pl.BlockSpec(memory_space=pl.ANY)] * len(before),
            out_specs=[
                pl.BlockSpec((rows, 128), lambda i, c, n: (0, i + first)),
                pl.BlockSpec((1, 8, rows), lambda i, c, n: (i + first, 0, 0)),
            ],
            scratch_shapes=[pltpu.VMEM((128, rows), F32), pltpu.VMEM((2, rows, 256), F32)],
        ),
        out_shape=[
            jax.ShapeDtypeStruct((rows, D), BF16),
            jax.ShapeDtypeStruct((pairs, 8, rows), F32),
        ],
        input_output_aliases={3 + i: i for i in range(len(before))},
        compiler_params=params(12),
        cost_estimate=cost(3e9 * count, 1.2e6 * count, 2 * rows * rows * 0.6 * count),
    )(core, lengths, qkv, *before)


def attend_back_kernel(core_ref, len_ref, q_ref, k_ref, v_ref, a_ref, da_ref, lse_ref, *refs):
    dq_ref, dk_ref, dv_ref, dqt_ref, dk_acc, dv_acc = refs[-6:]
    block = 256
    full_len = q_ref.shape[0]
    length = len_ref[core_ref[0]]
    scale = HEAD_DIM ** (-0.5)
    q_all = q_ref[...] * jnp.asarray(scale, BF16)
    k_all = k_ref[...]
    k_turned = k_all.T
    v_all = v_ref[...]
    da_all = da_ref[...]
    inner = (da_all.astype(F32) * a_ref[...].astype(F32)).T
    q_turned, da_turned = q_all.T, da_all.T
    parts = []
    for head in range(2):
        mine, k_head, q_head = head_parts(length, k_all, q_turned, head)
        zero = jnp.zeros((), BF16)
        q_plain = jnp.where(mine, q_all, zero)
        da_head = jnp.where(mine, da_all, zero)
        row = lax.broadcasted_iota(jnp.int32, (128, 1), 0)
        da_cols = jnp.where((row // HEAD_DIM) == head, da_turned, zero)
        lanes = slice(head * HEAD_DIM, (head + 1) * HEAD_DIM)
        centre = jnp.sum(inner[lanes], axis=0, keepdims=True)
        parts.append((k_head, q_plain, q_head, da_head, da_cols, lanes, centre))
    units = [
        (head, j, i)
        for j in reversed(range(full_len // block))
        for head in range(2)
        for i in range(j + 1)
    ]

    def score(at):
        head, j, i = units[at]
        k_head, _, q_head, _, da_cols, _, _ = parts[head]
        rows, cols = slice(i * block, (i + 1) * block), slice(j * block, (j + 1) * block)
        tile = mm(k_head[rows], q_head[:, cols])
        if i == j:
            tile = causal_mask(tile, block)
        return tile, mm(v_all[rows], da_cols[:, cols])

    seen = set()
    ready = score(0)
    dq_part = None
    for at, (head, j, i) in enumerate(units):
        later = score(at + 1) if at + 1 < len(units) else None
        scores, d_probs = ready
        _, q_plain, _, da_head, _, lanes, centre = parts[head]
        rows, cols = slice(i * block, (i + 1) * block), slice(j * block, (j + 1) * block)
        probs = jnp.exp(scores - lse_ref[0, head : head + 1, cols])
        d_scores = (probs * (d_probs - centre[:, cols])).astype(BF16)
        dv_part = mm(probs.astype(BF16), da_head[cols])
        dk_part = mm(d_scores, q_plain[cols])
        if i in seen:
            dv_acc[rows] += dv_part
            dk_acc[rows] += dk_part
        else:
            seen.add(i)
            dv_acc[rows] = dv_part
            dk_acc[rows] = dk_part
        part = mm(k_turned[lanes, rows], d_scores)
        dq_part = part if i == 0 else dq_part + part
        if i == j:
            dqt_ref[lanes, cols] = dq_part * scale
        ready = later
    dq_ref[...] = dqt_ref[...].T.astype(BF16)
    dk_ref[...] = dk_acc[...].astype(BF16)
    dv_ref[...] = dv_acc[...].astype(BF16)


def attend_back_call(core, lengths, qkv, a, da, lse, start, count, before):
    rows = qkv.shape[0]
    pairs = HEADS // 2
    before = list(before)
    pair_spec = pl.BlockSpec((rows, 128), lambda i, c, n: (0, i + start))
    return pl.pallas_call(
        attend_back_kernel,
        name="attend_back",
        grid_spec=pltpu.PrefetchScalarGridSpec(
            num_scalar_prefetch=2,
            grid=(count,),
            in_specs=[
                pair_spec,
                pl.BlockSpec((rows, 128), lambda i, c, n: (0, i + start + pairs)),
                pl.BlockSpec((rows, 128), lambda i, c, n: (0, i + start + 2 * pairs)),
                pair_spec,
                pair_spec,
                pl.BlockSpec((1, 8, rows), lambda i, c, n: (i + start, 0, 0)),
            ]
            + [pl.BlockSpec(memory_space=pl.ANY)] * len(before),
            out_specs=[pair_spec, pair_spec, pair_spec],
            scratch_shapes=[
                pltpu.VMEM((128, rows), F32),
                pltpu.VMEM((rows, 128), F32),
                pltpu.VMEM((rows, 128), F32),
            ],
        ),
        out_shape=[jax.ShapeDtypeStruct((rows, D), BF16)] * 3,
        input_output_aliases={8 + i: i for i in range(len(before))},
        compiler_params=params(16),
        cost_estimate=cost(6e9 * count, 2e6 * count, 2 * rows * rows * 0.6 * count),
    )(core, lengths, qkv, qkv, qkv, a, da, lse, *before)


def valid_rows(core_ref, len_ref, block):
    pos = pl.program_id(0) * block + lax.broadcasted_iota(jnp.int32, (block, 1), 0)
    return pos < len_ref[core_ref[0]]


def add_row(acc_ref, row, value):
    acc_ref[row : row + 1, :] += jnp.sum(value, axis=0, keepdims=True)


def row_block(core, i, steps):
    half = steps // 2
    return jnp.where(i < half, (1 - core) * half + i, core * half + i - half)


def up_kernel(group, core_ref, len_ref, seat_ref, x_ref, a_ref, og_ref, vec_ref, *refs):
    refs, (
        mid_ref, h_ref, e_ref, slope_ref, dy_ref, wo_back_ref, wu_back_ref, wo_ref, wu_ref, sems,
    ) = refs[:-10], refs[-10:]
    block = x_ref.shape[0]

    @pl.when(pl.program_id(0) == 0)
    def _():
        group.start(refs, core_ref, seat_ref, 0, D // 2, wo_ref, sems.at[0])
        group.start(refs, core_ref, seat_ref, D // 2, FF // 2, wu_ref, sems.at[1])
        wait_all(wo_ref, sems.at[0])
        wait_all(wu_ref, sems.at[1])

    valid = valid_rows(core_ref, len_ref, block)
    dy_ref[...] = jnp.where(valid, og_ref[...].astype(F32), 0.0).astype(BF16)
    mid = x_ref[...].astype(F32) + mm(a_ref[...], wo_ref[...]) + vec_ref[4:5, :]
    mid_ref[...] = mid
    normed, _ = norm_parts(mid)
    h = (normed * vec_ref[5:6, :] + vec_ref[6:7, :]).astype(BF16)
    h_ref[...] = h

    def act(j, z):
        cols = slice(j * D, (j + 1) * D)
        z = z + vec_ref[8 + j : 9 + j, :]
        squared = z * z
        turned = jnp.tanh(z * (GELU_ROOT + (GELU_ROOT * GELU_CUBE) * squared))
        half = 0.5 * turned + 0.5
        act = z * half
        e_ref[:, cols] = act.astype(BF16)
        slope = half + act * (1.0 - turned) * (GELU_ROOT + (3.0 * GELU_ROOT * GELU_CUBE) * squared)
        slope_ref[:, cols] = slope.astype(BF16)

    quarter = at_rows(D)
    wu_back_ref[...] = wu_ref[:, quarter].T

    @pl.when(pl.program_id(0) == 0)
    def _():
        wo_back_ref[...] = wo_ref[...].T

    waiting = None
    for j in range(FF // D):
        z = mm(h, wu_ref[:, j * D : (j + 1) * D])
        if waiting is not None:
            act(*waiting)
        waiting = (j, z)
    act(*waiting)


def up_call(core, lengths, seats, x, a, og, vec, group, block=256):
    rows = x.shape[0]
    assert rows // block == FF // D
    row_spec = pl.BlockSpec((block, D), lambda i, *s: (i, 0))
    wide_spec = pl.BlockSpec((block, FF), lambda i, *s: (i, 0))
    low, wide = [jax.ShapeDtypeStruct((rows, width), BF16) for width in (D, FF)]
    return pl.pallas_call(
        functools.partial(up_kernel, group),
        name="up",
        grid_spec=pltpu.PrefetchScalarGridSpec(
            num_scalar_prefetch=3,
            grid=(rows // block,),
            in_specs=[row_spec, row_spec, row_spec, whole_spec(vec.shape)] + group.specs(),
            out_specs=[
                row_spec, row_spec, wide_spec, wide_spec, row_spec,
                pl.BlockSpec((D, D), lambda i, *s: (0, 0)),
                pl.BlockSpec((D, D), lambda i, *s: (i, 0)),
            ],
            scratch_shapes=[
                pltpu.VMEM((D, D), BF16),
                pltpu.VMEM((D, FF), BF16),
                pltpu.SemaphoreType.DMA((2,)),
            ],
        ),
        out_shape=[
            jax.ShapeDtypeStruct((rows, D), F32),
            low,
            wide,
            wide,
            low,
            jax.ShapeDtypeStruct((D, D), BF16),
            jax.ShapeDtypeStruct((FF, D), BF16),
        ],
        compiler_params=params(48),
        cost_estimate=cost(6e9, 30e6, rows * FF),
    )(core, lengths, seats, x, a, og, vec, *group.arrays)


def down_kernel(
    group, core_ref, len_ref, seat_ref, mid_ref, e_ref, slope_ref, dy_ref, wo_back_ref, wu_back_ref, vec_ref, *refs
):
    refs, (
        theirs_ref, mine_ref, dz_ref, dmb_ref, dm_ref, da_ref, acc_ref, wd_ref, wd_back_ref, sems,
    ) = refs[:-10], refs[-10:]
    block = da_ref.shape[0]
    step, steps = pl.program_id(0), pl.num_programs(0)

    @pl.when(step == 0)
    def _():
        group.start(refs, core_ref, seat_ref, 0, D // 2, wd_ref, sems.at[0])
        acc_ref[...] = jnp.zeros_like(acc_ref)
        wait_all(wd_ref, sems.at[0])
        for j in range(FF // D):
            cols = slice(j * D, (j + 1) * D)
            wd_back_ref[:, cols] = wd_ref[cols, :].T

    mid = mid_ref[...]
    down = vec_ref[7:8, :] + mid + mm(e_ref[...], wd_ref[...])
    pos = row_block(core_ref[0], step, steps) * block + lax.broadcasted_iota(jnp.int32, (block, 1), 0)
    down = jnp.where(pos < len_ref[core_ref[0]], down, 0.0).astype(BF16)

    @pl.when(step < steps // 2)
    def _():
        theirs_ref[...] = down

    @pl.when(step >= steps // 2)
    def _():
        mine_ref[0] = down

    dy = dy_ref[...]
    add_row(acc_ref, 7, dy.astype(F32))
    dh = None
    waiting = None
    for j in range(FF // D + 1):
        later = None
        if j < FF // D:
            later = (j, mm(dy, wd_back_ref[:, j * D : (j + 1) * D]))
        if waiting is not None:
            at, de = waiting
            cols = slice(at * D, (at + 1) * D)
            dz = (de * slope_ref[:, cols].astype(F32)).astype(BF16)
            dz_ref[:, cols] = dz
            add_row(acc_ref, 8 + at, dz.astype(F32))
            part = mm(dz, wu_back_ref[cols, :])
            dh = part if dh is None else dh + part
        waiting = later
    normed, scale = norm_parts(mid)
    add_row(acc_ref, 5, dh * normed)
    add_row(acc_ref, 6, dh)
    dm = dy.astype(F32) + norm_back(dh * vec_ref[5:6, :], normed, scale)
    dm_ref[...] = dm
    dm_low = dm.astype(BF16)
    dmb_ref[...] = dm_low
    add_row(acc_ref, 4, dm_low.astype(F32))
    da_ref[...] = mm(dm_low, wo_back_ref[...]).astype(BF16)


def down_call(core, lengths, seats, mid, e, slope, dy, wo, wu, vec, group, block=256):
    rows = mid.shape[0]
    steps = rows // block
    half = steps // 2
    row_spec, wide_spec = [
        pl.BlockSpec((block, width), lambda i, c, *s: (row_block(c[0], i, steps), 0)) for width in (D, FF)
    ]
    return pl.pallas_call(
        functools.partial(down_kernel, group),
        name="down",
        grid_spec=pltpu.PrefetchScalarGridSpec(
            num_scalar_prefetch=3,
            grid=(steps,),
            in_specs=[row_spec, wide_spec, wide_spec, row_spec]
            + [whole_spec(part.shape) for part in (wo, wu, vec)]
            + group.specs(),
            out_specs=[
                pl.BlockSpec((block, D), lambda i, *s: (jnp.minimum(i, half - 1), 0)),
                pl.BlockSpec((1, block, D), lambda i, c, *s: (c[0], jnp.maximum(i - half, 0), 0)),
                wide_spec, row_spec, row_spec, row_spec,
                pl.BlockSpec((16, D), lambda i, *s: (0, 0)),
            ],
            scratch_shapes=[pltpu.VMEM((FF, D), BF16), pltpu.VMEM((D, FF), BF16), pltpu.SemaphoreType.DMA((1,))],
        ),
        out_shape=[
            jax.ShapeDtypeStruct((rows // 2, D), BF16),
            jax.ShapeDtypeStruct((2, rows // 2, D), BF16),
            jax.ShapeDtypeStruct((rows, FF), BF16),
            jax.ShapeDtypeStruct((rows, D), BF16),
            jax.ShapeDtypeStruct((rows, D), F32),
            jax.ShapeDtypeStruct((rows, D), BF16),
            jax.ShapeDtypeStruct((16, D), F32),
        ],
        compiler_params=params(48),
        cost_estimate=cost(1.6e10, 35e6),
    )(core, lengths, seats, mid, e, slope, dy, wo, wu, vec, *group.arrays)


def pick(values, half, mode):
    if mode == "split":
        width = values.shape[1] // 2
        return [values[:, half * width : (half + 1) * width]]
    return [values[:, at : at + 128] for at in range(half * 128, values.shape[1], 256)]


def weight_grad_kernel(lefts, rights, mode, core_ref, *refs):
    left_refs, right_refs = refs[:lefts], refs[lefts : lefts + sum(rights)]
    own_ref, other_ref = refs[-2:]
    halves = ([], [])
    at = 0
    for left_ref, count in zip(left_refs, rights):
        left = left_ref[...]
        for right_ref in right_refs[at : at + count]:
            whole = mm(left, right_ref[...], TN).astype(BF16)
            for half in range(2):
                halves[half].extend(pick(whole, half, mode))
        at += count
    low, high = [part[0] if len(part) == 1 else jnp.concatenate(part, axis=1) for part in halves]

    @pl.when(core_ref[0] == 0)
    def _():
        own_ref[...] = low
        other_ref[...] = high

    @pl.when(core_ref[0] != 0)
    def _():
        own_ref[...] = high
        other_ref[...] = low


def weight_grad_call(core, products, block, name, mode="split", cols=None):
    rows, height = products[0][0].shape
    lefts = [left for left, _ in products]
    rights = [right for _, group in products for right in group]
    widths = [right.shape[1] if cols is None else cols[0] for right in rights]
    width = sum(widths)
    seat = 0 if cols is None else cols[1]
    return pl.pallas_call(
        functools.partial(weight_grad_kernel, len(lefts), [len(group) for _, group in products], mode),
        name=name,
        grid_spec=pltpu.PrefetchScalarGridSpec(
            num_scalar_prefetch=1,
            grid=(height // block,),
            in_specs=[pl.BlockSpec((rows, block), lambda i, c: (0, i))] * len(lefts)
            + [
                pl.BlockSpec((rows, w), lambda i, c: (0, seat), pipeline_mode=pl.Buffered(1)) for w in widths
            ],
            out_specs=[pl.BlockSpec((block, width // 2), lambda i, c: (i, 0))] * 2,
        ),
        out_shape=[jax.ShapeDtypeStruct((height, width // 2), BF16)] * 2,
        compiler_params=params(16 if mode == "turns" else 48),
        cost_estimate=cost(2 * rows * height * width, rows * (height + width) * 2 + height * width * 2),
    )(core, *lefts, *rights)


def last_kernel(
    core_ref, x_ref, dm_ref, dq_ref, dk_ref, dv_ref, w_ref, vec_ref, before_ref, theirs_ref, mine_ref, acc_ref
):
    step, steps = pl.program_id(0), pl.num_programs(0)

    @pl.when(step == 0)
    def _():
        acc_ref[...] = before_ref[...]

    subs = sub_blocks(x_ref.shape[0])

    def product(rows):
        return (
            mm(dq_ref[rows, :], w_ref[:D])
            + mm(dk_ref[rows, :], w_ref[D : 2 * D])
            + mm(dv_ref[rows, :], w_ref[2 * D :])
        )

    grads = []
    dh = product(subs[0])
    add_row(acc_ref, 2, dq_ref[...].astype(F32))
    add_row(acc_ref, 3, dv_ref[...].astype(F32))
    for at, rows in enumerate(subs):
        later = product(subs[at + 1]) if at + 1 < len(subs) else None
        normed, scale = norm_parts(x_ref[rows, :].astype(F32))
        add_row(acc_ref, 0, dh * normed)
        add_row(acc_ref, 1, dh)
        grads.append(dm_ref[rows, :] + norm_back(dh * vec_ref[0:1, :], normed, scale))
        dh = later

    @pl.when(step < steps // 2)
    def _():
        for rows, grad in zip(subs, grads):
            theirs_ref[rows, :] = grad

    @pl.when(step >= steps // 2)
    def _():
        for rows, grad in zip(subs, grads):
            mine_ref[0, rows, :] = grad


def last_call(core, x, dm, dq, dk, dv, w, vec, before, block=256):
    rows = x.shape[0]
    steps = rows // block
    half = steps // 2
    row_spec = pl.BlockSpec((block, D), lambda i, c, *s: (row_block(c[0], i, steps), 0))
    return pl.pallas_call(
        last_kernel,
        name="last",
        grid_spec=pltpu.PrefetchScalarGridSpec(
            num_scalar_prefetch=1,
            grid=(steps,),
            in_specs=[row_spec] * 5 + [whole_spec(part.shape) for part in (w, vec, before)],
            out_specs=[
                pl.BlockSpec((block, D), lambda i, *s: (jnp.minimum(i, half - 1), 0)),
                pl.BlockSpec((1, block, D), lambda i, c, *s: (c[0], jnp.maximum(i - half, 0), 0)),
                pl.BlockSpec((16, D), lambda i, *s: (0, 0)),
            ],
        ),
        out_shape=[
            jax.ShapeDtypeStruct((rows // 2, D), F32),
            jax.ShapeDtypeStruct((2, rows // 2, D), F32),
            jax.ShapeDtypeStruct((16, D), F32),
        ],
        compiler_params=params(12),
        cost_estimate=cost(rows * 6 * D * D, 16e6),
    )(core, x, dm, dq, dk, dv, w, vec, before)


def adam_kernel(plans, sources, core_ref, *refs):
    halves = [refs[2 * i : 2 * i + 2] for i in range(sources)]
    count = len(plans)
    states = refs[2 * sources : 2 * sources + 3 * count]
    outs = refs[2 * sources + 3 * count : 2 * sources + 6 * count]
    grads = refs[2 * sources + 6 * count :]
    for core in range(2):

        @pl.when(core_ref[0] == core)
        def _():
            for (_, _, moves), grad_ref in zip(plans, grads):
                for source, start, width, place0, place1 in moves:
                    for half, place in ((0, place0), (1, place1)):
                        ref = halves[source][0 if half == core else 1]
                        grad_ref[:, place : place + width] = ref[:, start : start + width].astype(F32)

    for i, (rate, decay, _) in enumerate(plans):
        weight, first, second = states[3 * i : 3 * i + 3]
        new = adamw(weight[...], grads[i][...], first[...], second[...], rate, decay)
        for out, value in zip(outs[3 * i : 3 * i + 3], new):
            out[...] = value


def adam_call(core, halves, states, plans):
    flat = [part for pair in halves for part in pair]
    held = [part for state in states for part in state]
    spec = pl.BlockSpec(memory_space=pltpu.VMEM)
    news = pl.pallas_call(
        functools.partial(adam_kernel, plans, len(halves)),
        name="adam",
        in_specs=[pl.BlockSpec(memory_space=pltpu.SMEM)] + [spec] * (len(flat) + len(held)),
        out_specs=[spec] * len(held),
        out_shape=[jax.ShapeDtypeStruct(part.shape, F32) for part in held],
        scratch_shapes=[pltpu.VMEM(state[0].shape, F32) for state in states],
        compiler_params=params(12),
        cost_estimate=cost(1e6, 24 * sum(state[0].size for state in states)),
    )(core, *flat, *held)
    return [news[3 * i : 3 * i + 3] for i in range(len(states))]


def after(value, *others):
    if not others:
        return value
    return lax.optimization_barrier((value,) + others)[0]


def cut(array, axis, index, size=1):
    starts = [jnp.uint32(0)] * array.ndim
    sizes = list(array.shape)
    starts[axis], sizes[axis] = index, size
    return lax.dynamic_slice(array, starts, sizes)


class Grid:
    def __init__(self, chips):
        log = chips.bit_length() - 1
        side = 1 << (log // 3)
        if side * side * (chips // (side * side)) != chips:
            side = 1
        self.chips = chips
        self.n = side
        self.nz = chips // (side * side)
        self.core = lax.axis_index("seq")
        self.chip = lax.axis_index("dp")
        self.x = self.chip % side
        self.y = self.chip // side % side
        self.z = self.chip // (side * side)

    def pin(self, value):
        n, core = self.n, self.core
        first, second = self.coords(core)
        places = {
            "core": core,
            "other": 1 - core,
            "chip": self.chip,
            "seats": self.seats(True),
            "q_seats": self.seats(False),
        }
        for s in range(n):
            for t in range(n):
                places["plane", s, t] = self.plane((first + s) % n, (second + t) % n, core)
        for at in range(self.nz):
            places["z", at] = self.z ^ at
        names = list(places)
        held = lax.optimization_barrier((value, *[places[name].astype(jnp.uint32) for name in names]))
        self.places = dict(zip(names, held[1:]))
        return held[0]

    def plane(self, first, second, core):
        return jnp.where(core == 0, second * self.n + first, first * self.n + second)

    def coords(self, core):
        return jnp.where(core == 0, self.x, self.y), jnp.where(core == 0, self.y, self.x)

    def permute(self, value, axis, shift=0):
        pairs = []
        for chip in range(self.chips):
            for core in range(2):
                x, y, z = chip % self.n, chip // self.n % self.n, chip // (self.n * self.n)
                to_core = core
                if axis == "z":
                    z = (z + shift) % self.nz
                elif axis == "zx":
                    z = z ^ shift
                elif axis == "core":
                    to_core = 1 - core
                elif (axis == "first") == (core == 0):
                    x = (x + shift) % self.n
                else:
                    y = (y + shift) % self.n
                pairs.append((chip * 2 + core, ((z * self.n + y) * self.n + x) * 2 + to_core))
        return lax.ppermute(value, ("dp", "seq"), pairs)

    def swap(self, value):
        return self.permute(value, "core")

    def join(self, own, other, axis):
        return jnp.where(
            self.places["core"] == 0,
            jnp.concatenate([own, other], axis),
            jnp.concatenate([other, own], axis),
        )

    def seats(self, halving):
        found = []
        for half in range(2):
            core = self.core if half == 0 else 1 - self.core
            first, second = self.coords(core)
            for s2 in range(self.n):
                for s1 in range(self.n):
                    flat = self.plane((first - s1) % self.n, (second - s2) % self.n, core)
                    for sz in range(self.nz):
                        z = self.z ^ sz if halving else (self.z - sz) % self.nz
                        found.append(z * self.n * self.n + flat)
        return jnp.stack(found).astype(jnp.int32)

    def total_small(self, value, *untils):
        steps = [("core", 0), ("first", 1), ("second", 1)] if self.n == 2 else [("core", 0)]
        if self.n != 2:
            for axis in ("first", "second"):
                value = value + sum(self.permute(value, axis, s) for s in range(1, self.n))
        bit = 1
        while bit < self.nz:
            steps.append(("zx", bit))
            bit *= 2
        for at, (axis, shift) in enumerate(steps):
            until = untils[at] if at < len(untils) else ()
            value = value + after(self.permute(value, axis, shift), *until)
        return value

    def gather_z(self, block, *until):
        return jnp.stack([block] + [after(self.permute(block, "z", s), *until) for s in range(1, self.nz)])

    def gather_bit(self, held, bit, *until):
        return jnp.concatenate([held, after(self.permute(held, "zx", bit), *until)])

    def gather_first(self, column, *until):
        return jnp.stack([column] + [after(self.permute(column, "first", s), *until) for s in range(1, self.n)])

    def gather_second(self, line, *until):
        return [after(self.permute(line, "second", s), *until) for s in range(1, self.n)]

    def scatter_first(self, own, pair, *until):
        rows, cols = own.shape[0] // self.chips, own.shape[1]
        n = self.n

        def seat(s1, s2):
            own_part, pair_part = [
                cut(part.reshape(self.nz, n * n, rows, cols), 1, self.places["plane", s1, s2]).astype(F32)
                for part in (own, pair)
            ]
            return own_part + pair_part

        kept = [seat(0, t) for t in range(n)]
        for s in range(1, n):
            send = jnp.stack([seat(s, t).astype(BF16) for t in range(n)])
            got = after(self.permute(send, "first", s), *until)
            kept = [kept[t] + got[t].astype(F32) for t in range(n)]
        return kept[0], [part.astype(BF16) for part in kept[1:]]

    def scatter_second(self, kept, *until):
        mine, rest = kept
        got = [after(self.permute(rest[s - 1], "second", s), *until) for s in range(1, self.n)]
        for part in got:
            mine = mine + part.astype(F32)
        return mine.reshape((self.nz,) + mine.shape[2:]), got

    def order_z(self, mine):
        return [cut(mine, 0, self.places["z", at])[0] for at in range(self.nz)]

    def scatter_bit(self, parts, *until):
        half = len(parts) // 2
        send = parts[half] if half == 1 else jnp.stack([part.astype(BF16) for part in parts[half:]])
        got = after(self.permute(send.astype(BF16), "zx", half), *until)
        if half == 1:
            return [parts[0] + got.astype(F32)], got
        return [part + got[at].astype(F32) for at, part in enumerate(parts[:half])], got

    def scatter_z(self, parts):
        while len(parts) > 1:
            parts, _ = self.scatter_bit(parts)
        return parts[0]


def adamw(weight, gradient, first_moment, second_moment, step_rate, weight_decay):
    first_moment = BETA_ONE * first_moment + (1.0 - BETA_ONE) * gradient
    second_moment = BETA_TWO * second_moment + (1.0 - BETA_TWO) * gradient * gradient
    first_fix = 1.0 - BETA_ONE**STEP
    second_fix = 1.0 - BETA_TWO**STEP
    direction = first_moment / first_fix / (jnp.sqrt(second_moment / second_fix) + EPS_ADAM)
    return (weight - step_rate * (direction + weight_decay * weight), first_moment, second_moment)


def local(
    block_in, lengths, out_grad, w_qkv, w_out, w_up, w_down, vectors,
    first_qkv, first_out, first_up, first_down, first_vectors,
    second_qkv, second_out, second_up, second_down, second_vectors,
):
    grid = Grid(lax.axis_size("dp"))
    core = grid.core
    w_qkv_first = grid.pin(w_qkv)
    places = grid.places
    core_arr = places["core"].reshape(1).astype(jnp.int32)
    half_len = block_in.shape[1]
    vec_count, vec_here = vectors.shape

    def own_slot(halves):
        mine, theirs = [cut(halves, 0, places[name])[0] for name in ("core", "other")]
        return grid.join(mine, grid.swap(theirs), 0)

    def both_slots(mine, got):
        zero = jnp.uint32(0)
        return lax.dynamic_update_slice(mine, got[None], (places["other"], zero, zero))

    def half_of(shard):
        width = shard.shape[1] // 2
        return jnp.where(places["core"] == 0, shard[:, :width], shard[:, width:]).astype(BF16)

    seats, q_seats = [places[name].astype(jnp.int32) for name in ("seats", "q_seats")]

    turned = jnp.pad(vectors.T.astype(BF16), ((0, 0), (0, 128 - vec_count)))
    q_block = jnp.concatenate([half_of(w_qkv_first), turned], axis=1)
    u_block = jnp.concatenate([half_of(w_out), half_of(w_up)], axis=1)
    d_block = half_of(w_down)
    q_col = grid.gather_z(q_block)
    x = own_slot(block_in)
    bits = [1 << at for at in range((grid.nz - 1).bit_length())]
    u_col, d_col = u_block[None], d_block[None]
    for bit in bits[:-1]:
        u_col = grid.gather_bit(u_col, bit)
        d_col = grid.gather_bit(d_col, bit)
    q_line = after(grid.gather_first(q_col, x), u_col, d_col)
    q_rest = grid.gather_second(q_line)
    u_col = grid.gather_bit(after(u_col, q_line), bits[-1])
    q_line_swap = grid.swap(q_line)
    q_rest_swap = [grid.swap(after(part, u_col)) for part in q_rest]
    q_group = finish_group(grid, q_seats, [q_line] + q_rest, [q_line_swap] + q_rest_swap)

    h1, qkv, vec, w_back = qkv_call(core_arr, q_seats, x, q_group)
    u_line = grid.gather_first(u_col, qkv)
    d_col = grid.gather_bit(after(d_col, u_col), bits[-1], qkv)
    og = own_slot(after(out_grad, qkv))
    att = attend_call(core_arr, lengths, after(qkv, u_line, d_col), 0, 4, ())
    u_line_swap = after(grid.swap(u_line), *att)
    u_rest = grid.gather_second(u_line, *att)
    d_col = after(d_col, *u_rest)
    a, lse = attend_call(core_arr, lengths, after(qkv, d_col), 4, 2, att)
    u_rest_swap = [after(grid.swap(part), a) for part in u_rest]
    d_line = grid.gather_first(d_col, a)
    u_group = finish_group(grid, seats, [u_line] + u_rest, [u_line_swap] + u_rest_swap)
    mid, h2, e, slope, dy, wo, wu = up_call(core_arr, lengths, seats, x, after(a, d_line), og, vec, u_group)
    d_line_swap = after(grid.swap(d_line), mid)
    d_rest = grid.gather_second(d_line, mid)
    d_own, d_other = weight_grad_call(core_arr, [(after(e, *d_rest), [dy])], 512, "grad_down")
    d_rest_swap = [after(grid.swap(part), d_own) for part in d_rest]
    d_group = finish_group(grid, seats, [d_line] + d_rest, [d_line_swap] + d_rest_swap)
    out_theirs, out_mine, dz, dmb, dm, da, acc_mid = down_call(
        core_arr, lengths, seats, mid, e, slope, dy, wo, wu, vec, d_group
    )

    d_pair = after(grid.swap(d_other), dz)
    u_own, u_other = weight_grad_call(
        core_arr, [(a, [dmb]), (h2, [after(dz, d_pair)])], 384, "grad_up"
    )
    d_kept = grid.scatter_first(d_own, d_pair, u_own)

    def back_call(start, count, before, *needs):
        return attend_back_call(core_arr, lengths, qkv, a, after(da, *needs), lse, start, count, before)

    back = back_call(0, 2, (), u_own, *d_kept[1])
    d_sum, d_here = grid.scatter_second(d_kept, *back)
    u_pair = after(grid.swap(u_other), *back)
    back = back_call(2, 4, back, u_pair, *d_here)
    d_parts, _ = grid.scatter_bit(grid.order_z(d_sum), *back)
    u_kept = grid.scatter_first(u_own, u_pair, *back)
    dq, dk, dv = back
    block_out = both_slots(out_mine, after(grid.swap(after(out_theirs, back[0])), dq))
    q_own, q_other = weight_grad_call(
        core_arr, [(h1, [after(dq, *u_kept[1]), dk, dv])], 384, "grad_qkv", "turns"
    )
    u_sum, u_here = grid.scatter_second(u_kept, q_own)
    d_mine = grid.scatter_z(d_parts)
    in_theirs, in_mine, acc = last_call(
        core_arr, x, dm, after(dq, q_own, *u_here), dk, dv, w_back, vec, acc_mid
    )
    q_pair = after(grid.swap(q_other), in_theirs)
    u_parts, u_got = grid.scatter_bit(grid.order_z(u_sum), in_theirs)
    d_other_mine = after(grid.swap(d_mine), in_theirs)
    q_kept = grid.scatter_first(q_own, after(q_pair, u_got))
    in_got = grid.swap(after(in_theirs, q_pair))
    down_new, = adam_call(
        core_arr,
        [(d_mine, d_other_mine)],
        [(after(w_down, in_theirs), first_down, second_down)],
        [(FF ** (-0.5), MATRIX_DECAY, [(0, 0, D // 2, 0, D // 2)])],
    )
    u_mine = grid.scatter_z(u_parts)
    q_sum, q_here = grid.scatter_second(q_kept)
    u_other_mine = grid.swap(u_mine)
    in_grad = both_slots(in_mine, in_got)
    vec_total = grid.total_small(acc, q_kept[1], q_here)
    q_mine = grid.scatter_z(grid.order_z(q_sum))
    q_other_mine = grid.swap(q_mine)

    half, wide = D // 2, FF // 2
    out_new, up_new = adam_call(
        core_arr,
        [(u_mine, u_other_mine)],
        [(w_out, first_out, second_out), (w_up, first_up, second_up)],
        [
            ((D // 64) ** (-0.5), MATRIX_DECAY, [(0, 0, half, 0, half)]),
            (D ** (-0.5), MATRIX_DECAY, [(0, half, wide, 0, wide)]),
        ],
    )
    moves = []
    for turn in range(3 * D // 256):
        moves.append((0, turn * 128, 128, turn * 256, turn * 256 + 128))
    qkv_new, = adam_call(
        core_arr,
        [(q_mine, q_other_mine)],
        [(w_qkv, first_qkv, second_qkv)],
        [(D ** (-0.5), MATRIX_DECAY, moves)],
    )
    vec_grad = cut(vec_total[:vec_count].reshape(vec_count, -1, vec_here), 1, places["chip"])[:, 0]
    vec_new = adamw(vectors, vec_grad, first_vectors, second_vectors, VECTOR_RATE, 0.0)
    news = [qkv_new, out_new, up_new, down_new, vec_new]
    return (block_out, in_grad) + tuple(new[kind] for kind in range(3) for new in news)


def finish_group(grid, seats, own, other):
    rows, cols = own[0].shape[-2:]
    if rows % 16 == 0:
        return Pieces(own + other, rows)
    found = []
    for half, parts in enumerate((own, other)):
        here = seats[half * grid.chips : (half + 1) * grid.chips]
        order = jnp.zeros((grid.chips,), jnp.int32).at[here].set(jnp.arange(grid.chips, dtype=jnp.int32))
        blocks = jnp.concatenate(parts).reshape(grid.chips, rows, cols)
        found.append(jnp.take(blocks, order, axis=0).reshape(1, 1, grid.chips * rows, cols))
    return Pieces(found, grid.chips * rows, True)


def solution(mesh):
    weight = P("dp", None)
    vector = P(None, "dp")
    state = (weight, weight, weight, weight, vector)
    tokens = P("dp", "seq", None)
    return jax.shard_map(
        local,
        mesh=mesh,
        in_specs=(tokens, P("dp"), tokens) + state * 3,
        out_specs=(tokens, tokens) + state * 3,
        check_vma=False,
    )
```

```python
import functools

import jax
import jax.numpy as jnp
from jax import lax
from jax.experimental import pallas as pl
from jax.experimental.pallas import tpu as pltpu
from jax.sharding import PartitionSpec as P

D = 768
HEADS = 12
HEAD_DIM = 64
FF = 3072
STEP = 10

EPS_NORM = 1e-05
EPS_ADAM = 1e-08
BETA_ONE = 0.5
BETA_TWO = 0.5
MATRIX_DECAY = 0.1
VECTOR_RATE = 0.1
NEG_FILL = -1e30
GELU_ROOT = 0.7978845608028654
GELU_CUBE = 0.044715
QKV_HALF = 3 * D // 2

F32 = jnp.float32
BF16 = jnp.bfloat16

NN = (((1,), (0,)), ((), ()))
NT = (((1,), (1,)), ((), ()))
TN = (((0,), (0,)), ((), ()))


def mm(left, right, dims=NN):
    return lax.dot_general(left, right, dims, preferred_element_type=F32)


def cost(flops, nbytes, trans=0):
    return pl.CostEstimate(flops=int(4 * flops), bytes_accessed=int(4 * nbytes), transcendentals=int(trans))


def params(mib=60):
    return pltpu.CompilerParams(vmem_limit_bytes=mib * 1024 * 1024)


def held_spec():
    return pl.BlockSpec(memory_space=pltpu.VMEM)


def at_rows(block):
    return pl.ds(pl.multiple_of(pl.program_id(0) * block, block), block)


def whole_spec(shape):
    return pl.BlockSpec(shape, lambda *idx: (0,) * len(shape), pipeline_mode=pl.Buffered(1))


class Pieces:
    def __init__(self, arrays, rows, ordered=False):
        self.arrays = arrays
        self.rows = rows
        self.ordered = ordered
        self.halves = 2
        self.count = len(arrays) // self.halves
        self.lines, self.depth = arrays[0].shape[:2]

    def specs(self):
        return [pl.BlockSpec(memory_space=pltpu.HBM)] * len(self.arrays)

    def row(self, seat_ref, at):
        return 0 if self.ordered else pl.multiple_of(seat_ref[at] * self.rows, 16)

    def start(self, refs, core_ref, seat_ref, start_col, width, target, sem):
        core = core_ref[0]
        at = 0
        for half in range(self.halves):
            where = core if half == 0 else 1 - core
            for s2 in range(self.count):
                ref = refs[half * self.count + s2]
                for s1 in range(self.lines):
                    for sz in range(self.depth):
                        row = self.row(seat_ref, at)
                        at += 1
                        col = pl.multiple_of(where * width, 128)
                        pltpu.make_async_copy(
                            ref.at[s1, sz, :, pl.ds(start_col, width)],
                            target.at[pl.ds(row, self.rows), pl.ds(col, width)],
                            sem,
                        ).start()

    def start_once(self, refs, seat_ref, start_col, width, target, sem):
        at = 0
        for s2 in range(self.count):
            for s1 in range(self.lines):
                for sz in range(self.depth):
                    row = self.row(seat_ref, at)
                    at += 1
                    pltpu.make_async_copy(
                        refs[s2].at[s1, sz, :, pl.ds(start_col, width)],
                        target.at[pl.ds(row, self.rows), :],
                        sem,
                    ).start()


def wait_all(target, sem):
    pltpu.make_async_copy(target, target, sem).wait()


def norm_parts(rows):
    mean = jnp.mean(rows, axis=-1, keepdims=True)
    centred = rows - mean
    variance = jnp.mean(centred * centred, axis=-1, keepdims=True)
    scale = lax.rsqrt(variance + EPS_NORM)
    return centred * scale, scale


def norm_back(d_normed, normed, scale):
    first = jnp.mean(d_normed, axis=-1, keepdims=True)
    second = jnp.mean(d_normed * normed, axis=-1, keepdims=True)
    return scale * (d_normed - first - normed * second)


def qkv_kernel(group, core_ref, seat_ref, x_ref, *refs):
    refs, (h_ref, qkv_ref, vec_ref, back_ref, w_ref, turned_ref, sems) = refs[:-7], refs[-7:]

    @pl.when(pl.program_id(0) == 0)
    def _():
        group.start(refs, core_ref, seat_ref, 0, QKV_HALF, w_ref, sems.at[0])
        group.start_once(refs, seat_ref, QKV_HALF, 128, turned_ref, sems.at[1])
        wait_all(turned_ref, sems.at[1])
        vec_ref[...] = turned_ref[...].astype(F32).T[:16]
        wait_all(w_ref, sems.at[0])

    def norm(rows):
        normed, _ = norm_parts(x_ref[rows, :].astype(F32))
        h = (normed * vec_ref[0:1, :] + vec_ref[1:2, :]).astype(BF16)
        h_ref[rows, :] = h
        return h

    block = x_ref.shape[0]
    h = norm(slice(0, block))
    for part, bias in enumerate((2, None, 3)):
        cols = slice(part * D, (part + 1) * D)
        product = mm(h, w_ref[:, cols])
        if bias is not None:
            product = product + vec_ref[bias : bias + 1, :]
        qkv_ref[:, cols] = product.astype(BF16)

    @pl.when(pl.program_id(0) < 3)
    def _():
        back_ref[...] = w_ref[:, at_rows(D)].T


def sub_blocks(rows):
    return [slice(at, at + 256) for at in range(0, rows, 256)]


def qkv_call(core, seats, x, group, block=256):
    rows = x.shape[0]
    return pl.pallas_call(
        functools.partial(qkv_kernel, group),
        name="qkv",
        grid_spec=pltpu.PrefetchScalarGridSpec(
            num_scalar_prefetch=2,
            grid=(rows // block,),
            in_specs=[pl.BlockSpec((block, D), lambda i, *s: (i, 0))] + group.specs(),
            out_specs=[
                pl.BlockSpec((block, D), lambda i, *s: (i, 0)),
                pl.BlockSpec((block, 3 * D), lambda i, *s: (i, 0)),
                pl.BlockSpec((16, D), lambda i, *s: (0, 0)),
                pl.BlockSpec((D, D), lambda i, *s: (jnp.minimum(i, 2), 0)),
            ],
            scratch_shapes=[
                pltpu.VMEM((D, 3 * D), BF16),
                pltpu.VMEM((D, 128), BF16),
                pltpu.SemaphoreType.DMA((2,)),
            ],
        ),
        out_shape=[
            jax.ShapeDtypeStruct((rows, D), BF16),
            jax.ShapeDtypeStruct((rows, 3 * D), BF16),
            jax.ShapeDtypeStruct((16, D), F32),
            jax.ShapeDtypeStruct((3 * D, D), BF16),
        ],
        compiler_params=params(12),
        cost_estimate=cost(2 * rows * D * 3 * D, 10e6),
    )(core, seats, x, *group.arrays)


def head_parts(length, k_all, q_turned, head):
    full_len = k_all.shape[0]
    lane = lax.broadcasted_iota(jnp.int32, (1, 128), 1)
    row = lax.broadcasted_iota(jnp.int32, (128, 1), 0)
    zero, one = jnp.zeros((), BF16), jnp.ones((), BF16)
    mine = (lane // HEAD_DIM) == head
    spare = HEAD_DIM * (1 - head)
    pos = lax.broadcasted_iota(jnp.int32, (full_len, 128), 0)
    fill = jnp.where(pos < length, 0.0, NEG_FILL).astype(BF16)
    k_head = jnp.where(mine, k_all, jnp.where(lane == spare, fill, zero))
    q_head = jnp.where((row // HEAD_DIM) == head, q_turned, jnp.where(row == spare, one, zero))
    return mine, k_head, q_head


def causal_mask(scores, block):
    full = scores.shape[0]
    key_pos = lax.broadcasted_iota(jnp.int32, (block, block), 0)
    query_pos = lax.broadcasted_iota(jnp.int32, (block, block), 1)
    last = jnp.where(key_pos <= query_pos, scores[full - block :], NEG_FILL)
    if full == block:
        return last
    return jnp.concatenate([scores[: full - block], last], axis=0)


def attend_kernel(start, core_ref, len_ref, qkv_ref, *refs):
    a_ref, lse_ref, mixed_ref, scores_ref = refs[-4:]
    block = 256
    full_len = qkv_ref.shape[0]
    length = len_ref[core_ref[0]]
    q_all, k_all, v_all = [
        qkv_ref[:, pl.ds(pl.multiple_of((pl.program_id(0) + start) * 128 + part * D, 128), 128)] for part in range(3)
    ]
    q_all = q_all * jnp.asarray(HEAD_DIM ** (-0.5), BF16)
    v_turned = v_all.T
    q_turned = q_all.T
    ones = jnp.ones((16, full_len), BF16)
    parts = []
    for head in range(2):
        _, k_head, q_head = head_parts(length, k_all, q_turned, head)
        v_head = jnp.concatenate([v_turned[head * HEAD_DIM : (head + 1) * HEAD_DIM], ones], axis=0)
        parts.append((k_head, q_head, v_head))
    units = [(head, j) for j in reversed(range(full_len // block)) for head in range(2)]

    def score(at):
        head, j = units[at]
        k_head, q_head, _ = parts[head]
        top = None
        for i in range(j + 1):
            rows = slice(i * block, (i + 1) * block)
            tile = mm(k_head[rows], q_head[:, j * block : (j + 1) * block])
            if i == j:
                tile = causal_mask(tile, block)
            scores_ref[at % 2, rows, :] = tile
            part = jnp.max(tile.reshape(block // 8, 8, block), axis=0)
            top = part if top is None else jnp.maximum(top, part)
        return jnp.max(top, axis=0, keepdims=True)

    def finish(at, top):
        head, j = units[at]
        v_head = parts[head][2]
        cols = slice(j * block, (j + 1) * block)
        mixed = None
        for i in range(j + 1):
            rows = slice(i * block, (i + 1) * block)
            exped = jnp.exp(scores_ref[at % 2, rows, :] - top).astype(BF16)
            part = mm(v_head[:, rows], exped)
            mixed = part if mixed is None else mixed + part
        total = mixed[HEAD_DIM : HEAD_DIM + 1]
        mixed_ref[head * HEAD_DIM : (head + 1) * HEAD_DIM, cols] = mixed[:HEAD_DIM] / total
        lse_ref[0, head : head + 1, cols] = top + jnp.log(total)

    top = score(0)
    for at in range(len(units)):
        later = score(at + 1) if at + 1 < len(units) else None
        finish(at, top)
        top = later
    a_ref[...] = mixed_ref[...].T.astype(BF16)


def attend_call(core, lengths, qkv, first, count, before):
    rows = qkv.shape[0]
    pairs = HEADS // 2
    before = list(before)
    return pl.pallas_call(
        functools.partial(attend_kernel, first),
        name="attend",
        grid_spec=pltpu.PrefetchScalarGridSpec(
            num_scalar_prefetch=2,
            grid=(count,),
            in_specs=[held_spec()] + [pl.BlockSpec(memory_space=pl.ANY)] * len(before),
            out_specs=[
                pl.BlockSpec((rows, 128), lambda i, c, n: (0, i + first)),
                pl.BlockSpec((1, 8, rows), lambda i, c, n: (i + first, 0, 0)),
            ],
            scratch_shapes=[pltpu.VMEM((128, rows), F32), pltpu.VMEM((2, rows, 256), F32)],
        ),
        out_shape=[
            jax.ShapeDtypeStruct((rows, D), BF16),
            jax.ShapeDtypeStruct((pairs, 8, rows), F32),
        ],
        input_output_aliases={3 + i: i for i in range(len(before))},
        compiler_params=params(12),
        cost_estimate=cost(3e9 * count, 1.2e6 * count, 2 * rows * rows * 0.6 * count),
    )(core, lengths, qkv, *before)


def attend_back_kernel(core_ref, len_ref, q_ref, k_ref, v_ref, a_ref, da_ref, lse_ref, *refs):
    dq_ref, dk_ref, dv_ref, dqt_ref, dk_acc, dv_acc = refs[-6:]
    block = 256
    full_len = q_ref.shape[0]
    length = len_ref[core_ref[0]]
    scale = HEAD_DIM ** (-0.5)
    q_all = q_ref[...] * jnp.asarray(scale, BF16)
    k_all = k_ref[...]
    k_turned = k_all.T
    v_all = v_ref[...]
    da_all = da_ref[...]
    inner = (da_all.astype(F32) * a_ref[...].astype(F32)).T
    q_turned, da_turned = q_all.T, da_all.T
    parts = []
    for head in range(2):
        mine, k_head, q_head = head_parts(length, k_all, q_turned, head)
        zero = jnp.zeros((), BF16)
        q_plain = jnp.where(mine, q_all, zero)
        da_head = jnp.where(mine, da_all, zero)
        row = lax.broadcasted_iota(jnp.int32, (128, 1), 0)
        da_cols = jnp.where((row // HEAD_DIM) == head, da_turned, zero)
        lanes = slice(head * HEAD_DIM, (head + 1) * HEAD_DIM)
        centre = jnp.sum(inner[lanes], axis=0, keepdims=True)
        parts.append((k_head, q_plain, q_head, da_head, da_cols, lanes, centre))
    units = [
        (head, j, i)
        for j in reversed(range(full_len // block))
        for head in range(2)
        for i in range(j + 1)
    ]

    def score(at):
        head, j, i = units[at]
        k_head, _, q_head, _, da_cols, _, _ = parts[head]
        rows, cols = slice(i * block, (i + 1) * block), slice(j * block, (j + 1) * block)
        tile = mm(k_head[rows], q_head[:, cols])
        if i == j:
            tile = causal_mask(tile, block)
        return tile, mm(v_all[rows], da_cols[:, cols])

    seen = set()
    ready = score(0)
    dq_part = None
    for at, (head, j, i) in enumerate(units):
        later = score(at + 1) if at + 1 < len(units) else None
        scores, d_probs = ready
        _, q_plain, _, da_head, _, lanes, centre = parts[head]
        rows, cols = slice(i * block, (i + 1) * block), slice(j * block, (j + 1) * block)
        probs = jnp.exp(scores - lse_ref[0, head : head + 1, cols])
        d_scores = (probs * (d_probs - centre[:, cols])).astype(BF16)
        dv_part = mm(probs.astype(BF16), da_head[cols])
        dk_part = mm(d_scores, q_plain[cols])
        if i in seen:
            dv_acc[rows] += dv_part
            dk_acc[rows] += dk_part
        else:
            seen.add(i)
            dv_acc[rows] = dv_part
            dk_acc[rows] = dk_part
        part = mm(k_turned[lanes, rows], d_scores)
        dq_part = part if i == 0 else dq_part + part
        if i == j:
            dqt_ref[lanes, cols] = dq_part * scale
        ready = later
    dq_ref[...] = dqt_ref[...].T.astype(BF16)
    dk_ref[...] = dk_acc[...].astype(BF16)
    dv_ref[...] = dv_acc[...].astype(BF16)


def attend_back_call(core, lengths, qkv, a, da, lse, start, count, before):
    rows = qkv.shape[0]
    pairs = HEADS // 2
    before = list(before)
    pair_spec = pl.BlockSpec((rows, 128), lambda i, c, n: (0, i + start))
    return pl.pallas_call(
        attend_back_kernel,
        name="attend_back",
        grid_spec=pltpu.PrefetchScalarGridSpec(
            num_scalar_prefetch=2,
            grid=(count,),
            in_specs=[
                pair_spec,
                pl.BlockSpec((rows, 128), lambda i, c, n: (0, i + start + pairs)),
                pl.BlockSpec((rows, 128), lambda i, c, n: (0, i + start + 2 * pairs)),
                pair_spec,
                pair_spec,
                pl.BlockSpec((1, 8, rows), lambda i, c, n: (i + start, 0, 0)),
            ]
            + [pl.BlockSpec(memory_space=pl.ANY)] * len(before),
            out_specs=[pair_spec, pair_spec, pair_spec],
            scratch_shapes=[
                pltpu.VMEM((128, rows), F32),
                pltpu.VMEM((rows, 128), F32),
                pltpu.VMEM((rows, 128), F32),
            ],
        ),
        out_shape=[jax.ShapeDtypeStruct((rows, D), BF16)] * 3,
        input_output_aliases={8 + i: i for i in range(len(before))},
        compiler_params=params(16),
        cost_estimate=cost(6e9 * count, 2e6 * count, 2 * rows * rows * 0.6 * count),
    )(core, lengths, qkv, qkv, qkv, a, da, lse, *before)


def add_row(acc_ref, row, value):
    acc_ref[row : row + 1, :] += jnp.sum(value, axis=0, keepdims=True)


def row_block(core, i, steps):
    half = steps // 2
    return jnp.where(i < half, (1 - core) * half + i, core * half + i - half)


def middle_kernel(
    up_group, down_group, core_ref, len_ref, up_seat_ref, down_seat_ref, x_ref, a_ref, og_ref, vec_ref, *refs
):
    count = len(up_group.arrays)
    up_refs, down_refs = refs[:count], refs[count : count + len(down_group.arrays)]
    (
        theirs_ref, mine_ref, dy_ref, e_ref, dz_ref, h_ref, dmb_ref, dm_ref, da_ref, acc_ref,
        slope_ref, wo_ref, wu_ref, wd_ref, sems,
    ) = refs[-15:]
    block = x_ref.shape[0]
    step, steps = pl.program_id(0), pl.num_programs(0)
    starts = step == 0

    @pl.when(starts)
    def _():
        up_group.start(up_refs, core_ref, up_seat_ref, 0, D // 2, wo_ref, sems.at[0])
        up_group.start(up_refs, core_ref, up_seat_ref, D // 2, FF // 2, wu_ref, sems.at[1])
        down_group.start(down_refs, core_ref, down_seat_ref, 0, D // 2, wd_ref, sems.at[2])
        acc_ref[...] = jnp.zeros_like(acc_ref)
        wait_all(wo_ref, sems.at[0])

    pos = row_block(core_ref[0], step, steps) * block + lax.broadcasted_iota(jnp.int32, (block, 1), 0)
    valid = pos < len_ref[core_ref[0]]
    mid = x_ref[...].astype(F32) + mm(a_ref[...], wo_ref[...]) + vec_ref[4:5, :]
    normed, scale = norm_parts(mid)
    h = (normed * vec_ref[5:6, :] + vec_ref[6:7, :]).astype(BF16)
    h_ref[...] = h
    dy_low = jnp.where(valid, og_ref[...].astype(F32), 0.0).astype(BF16)
    dy_ref[...] = dy_low
    dy = dy_low.astype(F32)
    add_row(acc_ref, 7, dy)

    @pl.when(starts)
    def _():
        wait_all(wu_ref, sems.at[1])

    def act(j, z):
        cols = slice(j * D, (j + 1) * D)
        z = z + vec_ref[8 + j : 9 + j, :]
        squared = z * z
        turned = jnp.tanh(z * (GELU_ROOT + (GELU_ROOT * GELU_CUBE) * squared))
        half = 0.5 * turned + 0.5
        act = z * half
        e_ref[:, cols] = act.astype(BF16)
        slope_ref[:, cols] = half + act * (1.0 - turned) * (
            GELU_ROOT + (3.0 * GELU_ROOT * GELU_CUBE) * squared
        )

    waiting = None
    for j in range(FF // D):
        z = mm(h, wu_ref[:, j * D : (j + 1) * D])
        if waiting is not None:
            act(*waiting)
        waiting = (j, z)
    act(*waiting)

    @pl.when(starts)
    def _():
        wait_all(wd_ref, sems.at[2])

    down = vec_ref[7:8, :] + mid + mm(e_ref[...], wd_ref[...])
    down = jnp.where(valid, down, 0.0).astype(BF16)

    @pl.when(step < steps // 2)
    def _():
        theirs_ref[...] = down

    @pl.when(step >= steps // 2)
    def _():
        mine_ref[0] = down

    dh = None
    waiting = None
    for j in range(FF // D + 1):
        later = None
        if j < FF // D:
            later = (j, mm(dy_low, wd_ref[j * D : (j + 1) * D, :], NT))
        if waiting is not None:
            at, de = waiting
            cols = slice(at * D, (at + 1) * D)
            dz = (de * slope_ref[:, cols]).astype(BF16)
            dz_ref[:, cols] = dz
            add_row(acc_ref, 8 + at, dz.astype(F32))
            part = mm(dz, wu_ref[:, cols], NT)
            dh = part if dh is None else dh + part
        waiting = later
    add_row(acc_ref, 5, dh * normed)
    add_row(acc_ref, 6, dh)
    dm = dy + norm_back(dh * vec_ref[5:6, :], normed, scale)
    dm_ref[...] = dm
    dm_low = dm.astype(BF16)
    dmb_ref[...] = dm_low
    add_row(acc_ref, 4, dm_low.astype(F32))
    da_ref[...] = mm(dm_low, wo_ref[...], NT).astype(BF16)


def middle_call(core, lengths, up_seats, down_seats, x, a, og, vec, up_group, down_group, block=256):
    rows = x.shape[0]
    steps = rows // block
    half = steps // 2
    row_spec = pl.BlockSpec((block, D), lambda i, c, *s: (row_block(c[0], i, steps), 0))
    wide_spec = pl.BlockSpec((block, FF), lambda i, c, *s: (row_block(c[0], i, steps), 0))
    low = jax.ShapeDtypeStruct((rows, D), BF16)
    wide = jax.ShapeDtypeStruct((rows, FF), BF16)
    return pl.pallas_call(
        functools.partial(middle_kernel, up_group, down_group),
        name="middle",
        grid_spec=pltpu.PrefetchScalarGridSpec(
            num_scalar_prefetch=4,
            grid=(steps,),
            in_specs=[row_spec, row_spec, row_spec, whole_spec(vec.shape)]
            + up_group.specs()
            + down_group.specs(),
            out_specs=[
                pl.BlockSpec((block, D), lambda i, *s: (jnp.minimum(i, half - 1), 0)),
                pl.BlockSpec((1, block, D), lambda i, c, *s: (c[0], jnp.maximum(i - half, 0), 0)),
                row_spec, wide_spec, wide_spec, row_spec, row_spec, row_spec, row_spec,
                pl.BlockSpec((16, D), lambda i, *s: (0, 0)),
            ],
            scratch_shapes=[
                pltpu.VMEM((block, FF), F32),
                pltpu.VMEM((D, D), BF16),
                pltpu.VMEM((D, FF), BF16),
                pltpu.VMEM((FF, D), BF16),
                pltpu.SemaphoreType.DMA((3,)),
            ],
        ),
        out_shape=[
            jax.ShapeDtypeStruct((rows // 2, D), BF16),
            jax.ShapeDtypeStruct((2, rows // 2, D), BF16),
            low, wide, wide, low, low, jax.ShapeDtypeStruct((rows, D), F32), low,
            jax.ShapeDtypeStruct((16, D), F32),
        ],
        compiler_params=params(48),
        cost_estimate=cost(2.3e10, 40e6, rows * FF),
    )(core, lengths, up_seats, down_seats, x, a, og, vec, *up_group.arrays, *down_group.arrays)


def pick(values, half, mode):
    if mode == "split":
        width = values.shape[1] // 2
        return [values[:, half * width : (half + 1) * width]]
    return [values[:, at : at + 128] for at in range(half * 128, values.shape[1], 256)]


def weight_grad_kernel(lefts, rights, mode, core_ref, *refs):
    left_refs, right_refs = refs[:lefts], refs[lefts : lefts + sum(rights)]
    own_ref, other_ref = refs[-2:]
    halves = ([], [])
    at = 0
    for left_ref, count in zip(left_refs, rights):
        left = left_ref[...]
        for right_ref in right_refs[at : at + count]:
            whole = mm(left, right_ref[...], TN).astype(BF16)
            for half in range(2):
                halves[half].extend(pick(whole, half, mode))
        at += count
    low, high = [part[0] if len(part) == 1 else jnp.concatenate(part, axis=1) for part in halves]

    @pl.when(core_ref[0] == 0)
    def _():
        own_ref[...] = low
        other_ref[...] = high

    @pl.when(core_ref[0] != 0)
    def _():
        own_ref[...] = high
        other_ref[...] = low


def weight_grad_call(core, products, block, name, mode="split", cols=None):
    rows, height = products[0][0].shape
    lefts = [left for left, _ in products]
    rights = [right for _, group in products for right in group]
    widths = [right.shape[1] if cols is None else cols[0] for right in rights]
    width = sum(widths)
    seat = 0 if cols is None else cols[1]
    return pl.pallas_call(
        functools.partial(weight_grad_kernel, len(lefts), [len(group) for _, group in products], mode),
        name=name,
        grid_spec=pltpu.PrefetchScalarGridSpec(
            num_scalar_prefetch=1,
            grid=(height // block,),
            in_specs=[pl.BlockSpec((rows, block), lambda i, c: (0, i))] * len(lefts)
            + [
                pl.BlockSpec((rows, w), lambda i, c: (0, seat), pipeline_mode=pl.Buffered(1)) for w in widths
            ],
            out_specs=[pl.BlockSpec((block, width // 2), lambda i, c: (i, 0))] * 2,
        ),
        out_shape=[jax.ShapeDtypeStruct((height, width // 2), BF16)] * 2,
        compiler_params=params(16 if mode == "turns" else 48),
        cost_estimate=cost(2 * rows * height * width, rows * (height + width) * 2 + height * width * 2),
    )(core, *lefts, *rights)


def last_kernel(
    core_ref, x_ref, dm_ref, dq_ref, dk_ref, dv_ref, w_ref, vec_ref, before_ref, theirs_ref, mine_ref, acc_ref
):
    step, steps = pl.program_id(0), pl.num_programs(0)

    @pl.when(step == 0)
    def _():
        acc_ref[...] = before_ref[...]

    subs = sub_blocks(x_ref.shape[0])

    def product(rows):
        return (
            mm(dq_ref[rows, :], w_ref[:D])
            + mm(dk_ref[rows, :], w_ref[D : 2 * D])
            + mm(dv_ref[rows, :], w_ref[2 * D :])
        )

    grads = []
    dh = product(subs[0])
    add_row(acc_ref, 2, dq_ref[...].astype(F32))
    add_row(acc_ref, 3, dv_ref[...].astype(F32))
    for at, rows in enumerate(subs):
        later = product(subs[at + 1]) if at + 1 < len(subs) else None
        normed, scale = norm_parts(x_ref[rows, :].astype(F32))
        add_row(acc_ref, 0, dh * normed)
        add_row(acc_ref, 1, dh)
        grads.append(dm_ref[rows, :] + norm_back(dh * vec_ref[0:1, :], normed, scale))
        dh = later

    @pl.when(step < steps // 2)
    def _():
        for rows, grad in zip(subs, grads):
            theirs_ref[rows, :] = grad

    @pl.when(step >= steps // 2)
    def _():
        for rows, grad in zip(subs, grads):
            mine_ref[0, rows, :] = grad


def last_call(core, x, dm, dq, dk, dv, w, vec, before, block=256):
    rows = x.shape[0]
    steps = rows // block
    half = steps // 2
    row_spec = pl.BlockSpec((block, D), lambda i, c, *s: (row_block(c[0], i, steps), 0))
    return pl.pallas_call(
        last_kernel,
        name="last",
        grid_spec=pltpu.PrefetchScalarGridSpec(
            num_scalar_prefetch=1,
            grid=(steps,),
            in_specs=[row_spec] * 5 + [whole_spec(part.shape) for part in (w, vec, before)],
            out_specs=[
                pl.BlockSpec((block, D), lambda i, *s: (jnp.minimum(i, half - 1), 0)),
                pl.BlockSpec((1, block, D), lambda i, c, *s: (c[0], jnp.maximum(i - half, 0), 0)),
                pl.BlockSpec((16, D), lambda i, *s: (0, 0)),
            ],
        ),
        out_shape=[
            jax.ShapeDtypeStruct((rows // 2, D), F32),
            jax.ShapeDtypeStruct((2, rows // 2, D), F32),
            jax.ShapeDtypeStruct((16, D), F32),
        ],
        compiler_params=params(12),
        cost_estimate=cost(rows * 6 * D * D, 16e6),
    )(core, x, dm, dq, dk, dv, w, vec, before)


def adam_kernel(plans, sources, core_ref, *refs):
    halves = [refs[2 * i : 2 * i + 2] for i in range(sources)]
    count = len(plans)
    states = refs[2 * sources : 2 * sources + 3 * count]
    outs = refs[2 * sources + 3 * count : 2 * sources + 6 * count]
    grads = refs[2 * sources + 6 * count :]
    for core in range(2):

        @pl.when(core_ref[0] == core)
        def _():
            for (_, _, moves), grad_ref in zip(plans, grads):
                for source, start, width, place0, place1 in moves:
                    for half, place in ((0, place0), (1, place1)):
                        ref = halves[source][0 if half == core else 1]
                        grad_ref[:, place : place + width] = ref[:, start : start + width].astype(F32)

    for i, (rate, decay, _) in enumerate(plans):
        weight, first, second = states[3 * i : 3 * i + 3]
        new = adamw(weight[...], grads[i][...], first[...], second[...], rate, decay)
        for out, value in zip(outs[3 * i : 3 * i + 3], new):
            out[...] = value


def adam_call(core, halves, states, plans):
    flat = [part for pair in halves for part in pair]
    held = [part for state in states for part in state]
    spec = pl.BlockSpec(memory_space=pltpu.VMEM)
    news = pl.pallas_call(
        functools.partial(adam_kernel, plans, len(halves)),
        name="adam",
        in_specs=[pl.BlockSpec(memory_space=pltpu.SMEM)] + [spec] * (len(flat) + len(held)),
        out_specs=[spec] * len(held),
        out_shape=[jax.ShapeDtypeStruct(part.shape, F32) for part in held],
        scratch_shapes=[pltpu.VMEM(state[0].shape, F32) for state in states],
        compiler_params=params(12),
        cost_estimate=cost(1e6, 24 * sum(state[0].size for state in states)),
    )(core, *flat, *held)
    return [news[3 * i : 3 * i + 3] for i in range(len(states))]


def after(value, *others):
    if not others:
        return value
    return lax.optimization_barrier((value,) + others)[0]


def cut(array, axis, index, size=1):
    starts = [jnp.uint32(0)] * array.ndim
    sizes = list(array.shape)
    starts[axis], sizes[axis] = index, size
    return lax.dynamic_slice(array, starts, sizes)


class Grid:
    def __init__(self, chips):
        log = chips.bit_length() - 1
        side = 1 << (log // 3)
        if side * side * (chips // (side * side)) != chips:
            side = 1
        self.chips = chips
        self.n = side
        self.nz = chips // (side * side)
        self.core = lax.axis_index("seq")
        self.chip = lax.axis_index("dp")
        self.x = self.chip % side
        self.y = self.chip // side % side
        self.z = self.chip // (side * side)

    def pin(self, value):
        n, core = self.n, self.core
        first, second = self.coords(core)
        places = {
            "core": core,
            "other": 1 - core,
            "chip": self.chip,
            "seats": self.seats(True),
            "q_seats": self.seats(False),
            "d_seats": self.line_seats(),
            "line": self.z,
        }
        for s in range(n):
            for t in range(n):
                places["plane", s, t] = self.plane((first + s) % n, (second + t) % n, core)
        for at in range(self.nz):
            places["z", at] = self.z ^ at
        names = list(places)
        held = lax.optimization_barrier((value, *[places[name].astype(jnp.uint32) for name in names]))
        self.places = dict(zip(names, held[1:]))
        return held[0]

    def plane(self, first, second, core):
        return jnp.where(core == 0, second * self.n + first, first * self.n + second)

    def coords(self, core):
        return jnp.where(core == 0, self.x, self.y), jnp.where(core == 0, self.y, self.x)

    def permute(self, value, axis, shift=0):
        pairs = []
        for chip in range(self.chips):
            for core in range(2):
                x, y, z = chip % self.n, chip // self.n % self.n, chip // (self.n * self.n)
                to_core = core
                if axis == "z":
                    z = (z + shift) % self.nz
                elif axis == "zx":
                    z = z ^ shift
                elif axis == "line":
                    z = z + shift
                    if not 0 <= z < self.nz:
                        continue
                elif axis == "core":
                    to_core = 1 - core
                elif (axis == "first") == (core == 0):
                    x = (x + shift) % self.n
                else:
                    y = (y + shift) % self.n
                pairs.append((chip * 2 + core, ((z * self.n + y) * self.n + x) * 2 + to_core))
        return lax.ppermute(value, ("dp", "seq"), pairs)

    def swap(self, value):
        return self.permute(value, "core")

    def join(self, own, other, axis):
        return jnp.where(
            self.places["core"] == 0,
            jnp.concatenate([own, other], axis),
            jnp.concatenate([other, own], axis),
        )

    def line_seats(self):
        found = []
        for half in range(2):
            core = self.core if half == 0 else 1 - self.core
            first, second = self.coords(core)
            for sz in range(self.nz):
                for s2 in range(self.n):
                    for s1 in range(self.n):
                        flat = self.plane((first - s1) % self.n, (second - s2) % self.n, core)
                        found.append(((self.z - sz) % self.nz) * self.n * self.n + flat)
        return jnp.stack(found).astype(jnp.int32)

    def seats(self, halving):
        found = []
        for half in range(2):
            core = self.core if half == 0 else 1 - self.core
            first, second = self.coords(core)
            for s2 in range(self.n):
                for s1 in range(self.n):
                    flat = self.plane((first - s1) % self.n, (second - s2) % self.n, core)
                    for sz in range(self.nz):
                        z = self.z ^ sz if halving else (self.z - sz) % self.nz
                        found.append(z * self.n * self.n + flat)
        return jnp.stack(found).astype(jnp.int32)

    def total_small(self, value, *untils):
        steps = [("core", 0), ("first", 1), ("second", 1)] if self.n == 2 else [("core", 0)]
        if self.n != 2:
            for axis in ("first", "second"):
                value = value + sum(self.permute(value, axis, s) for s in range(1, self.n))
        bit = 1
        while bit < self.nz:
            steps.append(("zx", bit))
            bit *= 2
        for at, (axis, shift) in enumerate(steps):
            until = untils[at] if at < len(untils) else ()
            value = value + after(self.permute(value, axis, shift), *until)
        return value

    def gather_z(self, block, *until):
        return jnp.stack([block] + [after(self.permute(block, "z", s), *until) for s in range(1, self.nz)])

    def gather_bit(self, held, bit, *until):
        return jnp.concatenate([held, after(self.permute(held, "zx", bit), *until)])

    def ring(self, rising, falling, shift):
        return jnp.where(self.places["line"] >= shift, rising[shift - 1], falling[self.nz - shift - 1])

    def gather_first(self, column, *until):
        return jnp.stack([column] + [after(self.permute(column, "first", s), *until) for s in range(1, self.n)])

    def gather_second(self, line, *until):
        return [after(self.permute(line, "second", s), *until) for s in range(1, self.n)]

    def scatter_first(self, own, pair, *until):
        rows, cols = own.shape[0] // self.chips, own.shape[1]
        n = self.n

        def seat(s1, s2):
            own_part, pair_part = [
                cut(part.reshape(self.nz, n * n, rows, cols), 1, self.places["plane", s1, s2]).astype(F32)
                for part in (own, pair)
            ]
            return own_part + pair_part

        kept = [seat(0, t) for t in range(n)]
        for s in range(1, n):
            send = jnp.stack([seat(s, t).astype(BF16) for t in range(n)])
            got = after(self.permute(send, "first", s), *until)
            kept = [kept[t] + got[t].astype(F32) for t in range(n)]
        return kept[0], [part.astype(BF16) for part in kept[1:]]

    def scatter_second(self, kept, *until):
        mine, rest = kept
        got = [after(self.permute(rest[s - 1], "second", s), *until) for s in range(1, self.n)]
        for part in got:
            mine = mine + part.astype(F32)
        return mine.reshape((self.nz,) + mine.shape[2:]), got

    def order_z(self, mine):
        return [cut(mine, 0, self.places["z", at])[0] for at in range(self.nz)]

    def scatter_bit(self, parts, *until):
        half = len(parts) // 2
        send = parts[half] if half == 1 else jnp.stack([part.astype(BF16) for part in parts[half:]])
        got = after(self.permute(send.astype(BF16), "zx", half), *until)
        if half == 1:
            return [parts[0] + got.astype(F32)], got
        return [part + got[at].astype(F32) for at, part in enumerate(parts[:half])], got

    def scatter_z(self, parts):
        while len(parts) > 1:
            parts, _ = self.scatter_bit(parts)
        return parts[0]


def adamw(weight, gradient, first_moment, second_moment, step_rate, weight_decay):
    first_moment = BETA_ONE * first_moment + (1.0 - BETA_ONE) * gradient
    second_moment = BETA_TWO * second_moment + (1.0 - BETA_TWO) * gradient * gradient
    first_fix = 1.0 - BETA_ONE**STEP
    second_fix = 1.0 - BETA_TWO**STEP
    direction = first_moment / first_fix / (jnp.sqrt(second_moment / second_fix) + EPS_ADAM)
    return (weight - step_rate * (direction + weight_decay * weight), first_moment, second_moment)


def local(
    block_in, lengths, out_grad, w_qkv, w_out, w_up, w_down, vectors,
    first_qkv, first_out, first_up, first_down, first_vectors,
    second_qkv, second_out, second_up, second_down, second_vectors,
):
    grid = Grid(lax.axis_size("dp"))
    core = grid.core
    w_qkv_first = grid.pin(w_qkv)
    places = grid.places
    core_arr = places["core"].reshape(1).astype(jnp.int32)
    half_len = block_in.shape[1]
    vec_count, vec_here = vectors.shape

    def own_slot(halves):
        mine, theirs = [cut(halves, 0, places[name])[0] for name in ("core", "other")]
        return grid.join(mine, grid.swap(theirs), 0)

    def both_slots(mine, got):
        zero = jnp.uint32(0)
        return lax.dynamic_update_slice(mine, got[None], (places["other"], zero, zero))

    def half_of(shard):
        width = shard.shape[1] // 2
        return jnp.where(places["core"] == 0, shard[:, :width], shard[:, width:]).astype(BF16)

    seats, q_seats, d_seats = [places[name].astype(jnp.int32) for name in ("seats", "q_seats", "d_seats")]

    turned = jnp.pad(vectors.T.astype(BF16), ((0, 0), (0, 128 - vec_count)))
    q_block = jnp.concatenate([half_of(w_qkv_first), turned], axis=1)
    u_block = jnp.concatenate([half_of(w_out), half_of(w_up)], axis=1)
    d_block = half_of(w_down)
    q_col = grid.gather_z(q_block)
    x = own_slot(block_in)
    bits = [1 << at for at in range((grid.nz - 1).bit_length())]
    d_line = grid.gather_first(d_block)
    u_col = u_block[None]
    for bit in bits[:-1]:
        u_col = grid.gather_bit(u_col, bit)
    q_line = after(grid.gather_first(q_col, x), u_col, d_line)
    q_rest = grid.gather_second(q_line)
    d_plane = jnp.stack([d_line] + grid.gather_second(after(d_line, q_line)))
    u_col = grid.gather_bit(after(u_col, q_line), bits[-1])
    q_line_swap = grid.swap(q_line)
    q_rest_swap = [grid.swap(after(part, u_col, d_plane)) for part in q_rest]
    q_group = finish_group(grid, q_seats, [q_line] + q_rest, [q_line_swap] + q_rest_swap)

    h1, qkv, vec, w_back = qkv_call(core_arr, q_seats, x, q_group)
    u_line = grid.gather_first(u_col, qkv)
    rising, falling = [after(d_plane, u_col)], [after(d_plane, u_col)]

    def next_line(*until):
        for held, shift in ((rising, 1), (falling, -1)):
            held.append(after(grid.permute(held[-1], "line", shift), *until))

    steps = grid.nz - 1
    for _ in range(steps // 3):
        next_line(qkv)
    og = own_slot(after(out_grad, qkv))
    att = attend_call(core_arr, lengths, after(qkv, u_line, rising[-1], falling[-1]), 0, 4, ())
    u_line_swap = after(grid.swap(u_line), *att)
    d_plane_swap = after(grid.swap(d_plane), *att)
    u_rest = grid.gather_second(u_line, *att)
    for _ in range(steps // 3):
        next_line(*att)
    a, lse = attend_call(core_arr, lengths, after(qkv, rising[-1], falling[-1], *u_rest), 4, 2, att)
    for _ in range(steps - 2 * (steps // 3)):
        next_line(a)
    u_rest_swap = [after(grid.swap(part), a) for part in u_rest]
    u_group = finish_group(grid, seats, [u_line] + u_rest, [u_line_swap] + u_rest_swap)
    d_rings = [grid.ring(rising[1:], falling[1:], shift) for shift in range(1, grid.nz)]
    d_group = finish_group(
        grid, d_seats, [d_plane] + d_rings, [d_plane_swap] + [grid.swap(part) for part in d_rings]
    )
    out_theirs, out_mine, dy, e, dz, h2, dmb, dm, da, acc_mid = middle_call(
        core_arr, lengths, seats, d_seats, x, a, og, vec, u_group, d_group
    )
    d_own, d_other = weight_grad_call(core_arr, [(e, [dy])], 512, "grad_down")

    u_own, u_other = weight_grad_call(
        core_arr, [(a, [dmb]), (h2, [after(dz, d_own)])], 384, "grad_up"
    )
    d_pair = after(grid.swap(d_other), u_own)

    def back_call(start, count, before, *needs):
        return attend_back_call(core_arr, lengths, qkv, a, after(da, *needs), lse, start, count, before)

    back = back_call(0, 2, (), d_pair)
    d_kept = grid.scatter_first(d_own, d_pair, *back)
    u_pair = after(grid.swap(u_other), *back)
    back = back_call(2, 4, back, u_pair, *d_kept[1])
    d_sum, d_here = grid.scatter_second(d_kept, *back)
    u_kept = grid.scatter_first(u_own, u_pair, *back)
    dq, dk, dv = back
    block_out = both_slots(out_mine, after(grid.swap(after(out_theirs, back[0])), dq))
    q_own, q_other = weight_grad_call(
        core_arr, [(h1, [after(dq, *u_kept[1], *d_here), dk, dv])], 384, "grad_qkv", "turns"
    )
    d_parts, d_got = grid.scatter_bit(grid.order_z(d_sum), q_own)
    u_sum, u_here = grid.scatter_second(u_kept, q_own)
    d_mine = grid.scatter_z(d_parts)
    in_theirs, in_mine, acc = last_call(
        core_arr, x, dm, after(dq, q_own, d_got, *u_here), dk, dv, w_back, vec, acc_mid
    )
    q_pair = after(grid.swap(q_other), in_theirs)
    u_parts, u_got = grid.scatter_bit(grid.order_z(u_sum), in_theirs)
    d_other_mine = after(grid.swap(d_mine), in_theirs)
    q_kept = grid.scatter_first(q_own, after(q_pair, u_got))
    in_got = grid.swap(after(in_theirs, q_pair))
    down_new, = adam_call(
        core_arr,
        [(d_mine, d_other_mine)],
        [(after(w_down, in_theirs), first_down, second_down)],
        [(FF ** (-0.5), MATRIX_DECAY, [(0, 0, D // 2, 0, D // 2)])],
    )
    u_mine = grid.scatter_z(u_parts)
    q_sum, q_here = grid.scatter_second(q_kept)
    u_other_mine = grid.swap(u_mine)
    in_grad = both_slots(in_mine, in_got)
    vec_total = grid.total_small(acc, q_kept[1], q_here)
    q_mine = grid.scatter_z(grid.order_z(q_sum))
    q_other_mine = grid.swap(q_mine)

    half, wide = D // 2, FF // 2
    out_new, up_new = adam_call(
        core_arr,
        [(u_mine, u_other_mine)],
        [(w_out, first_out, second_out), (w_up, first_up, second_up)],
        [
            ((D // 64) ** (-0.5), MATRIX_DECAY, [(0, 0, half, 0, half)]),
            (D ** (-0.5), MATRIX_DECAY, [(0, half, wide, 0, wide)]),
        ],
    )
    moves = []
    for turn in range(3 * D // 256):
        moves.append((0, turn * 128, 128, turn * 256, turn * 256 + 128))
    qkv_new, = adam_call(
        core_arr,
        [(q_mine, q_other_mine)],
        [(w_qkv, first_qkv, second_qkv)],
        [(D ** (-0.5), MATRIX_DECAY, moves)],
    )
    vec_grad = cut(vec_total[:vec_count].reshape(vec_count, -1, vec_here), 1, places["chip"])[:, 0]
    vec_new = adamw(vectors, vec_grad, first_vectors, second_vectors, VECTOR_RATE, 0.0)
    news = [qkv_new, out_new, up_new, down_new, vec_new]
    return (block_out, in_grad) + tuple(new[kind] for kind in range(3) for new in news)


def finish_group(grid, seats, own, other):
    rows, cols = own[0].shape[-2:]
    if rows % 16 == 0:
        return Pieces(own + other, rows)
    found = []
    for half, parts in enumerate((own, other)):
        here = seats[half * grid.chips : (half + 1) * grid.chips]
        order = jnp.zeros((grid.chips,), jnp.int32).at[here].set(jnp.arange(grid.chips, dtype=jnp.int32))
        blocks = jnp.concatenate(parts).reshape(grid.chips, rows, cols)
        found.append(jnp.take(blocks, order, axis=0).reshape(1, 1, grid.chips * rows, cols))
    return Pieces(found, grid.chips * rows, True)


def solution(mesh):
    weight = P("dp", None)
    vector = P(None, "dp")
    state = (weight, weight, weight, weight, vector)
    tokens = P("dp", "seq", None)
    return jax.shard_map(
        local,
        mesh=mesh,
        in_specs=(tokens, P("dp"), tokens) + state * 3,
        out_specs=(tokens, tokens) + state * 3,
        check_vma=False,
    )
```

```python
import functools

import jax
import jax.numpy as jnp
from jax import lax
from jax.experimental import pallas as pl
from jax.experimental.pallas import tpu as pltpu
from jax.sharding import PartitionSpec as P

D = 768
HEADS = 12
HEAD_DIM = 64
FF = 3072
STEP = 10

EPS_NORM = 1e-05
EPS_ADAM = 1e-08
BETA_ONE = 0.5
BETA_TWO = 0.5
MATRIX_DECAY = 0.1
VECTOR_RATE = 0.1
NEG_FILL = -1e30
GELU_ROOT = 0.7978845608028654
GELU_CUBE = 0.044715
QKV_HALF = 3 * D // 2

F32 = jnp.float32
BF16 = jnp.bfloat16

NN = (((1,), (0,)), ((), ()))
NT = (((1,), (1,)), ((), ()))
TN = (((0,), (0,)), ((), ()))


def mm(left, right, dims=NN):
    return lax.dot_general(left, right, dims, preferred_element_type=F32)


def cost(flops, nbytes, trans=0):
    return pl.CostEstimate(flops=int(4 * flops), bytes_accessed=int(4 * nbytes), transcendentals=int(trans))


def params(mib=60):
    return pltpu.CompilerParams(vmem_limit_bytes=mib * 1024 * 1024)


def held_spec():
    return pl.BlockSpec(memory_space=pltpu.VMEM)


def at_rows(block):
    return pl.ds(pl.multiple_of(pl.program_id(0) * block, block), block)


def whole_spec(shape):
    return pl.BlockSpec(shape, lambda *idx: (0,) * len(shape), pipeline_mode=pl.Buffered(1))


class Pieces:
    def __init__(self, arrays, rows, ordered=False):
        self.arrays = arrays
        self.rows = rows
        self.ordered = ordered
        self.halves = 2
        self.count = len(arrays) // self.halves
        self.lines, self.depth = arrays[0].shape[:2]

    def specs(self):
        return [pl.BlockSpec(memory_space=pltpu.HBM)] * len(self.arrays)

    def row(self, seat_ref, at):
        return 0 if self.ordered else pl.multiple_of(seat_ref[at] * self.rows, 16)

    def start(self, refs, core_ref, seat_ref, start_col, width, target, sem):
        core = core_ref[0]
        at = 0
        for half in range(self.halves):
            where = core if half == 0 else 1 - core
            for s2 in range(self.count):
                ref = refs[half * self.count + s2]
                for s1 in range(self.lines):
                    for sz in range(self.depth):
                        row = self.row(seat_ref, at)
                        at += 1
                        col = pl.multiple_of(where * width, 128)
                        pltpu.make_async_copy(
                            ref.at[s1, sz, :, pl.ds(start_col, width)],
                            target.at[pl.ds(row, self.rows), pl.ds(col, width)],
                            sem,
                        ).start()

    def start_once(self, refs, seat_ref, start_col, width, target, sem):
        at = 0
        for s2 in range(self.count):
            for s1 in range(self.lines):
                for sz in range(self.depth):
                    row = self.row(seat_ref, at)
                    at += 1
                    pltpu.make_async_copy(
                        refs[s2].at[s1, sz, :, pl.ds(start_col, width)],
                        target.at[pl.ds(row, self.rows), :],
                        sem,
                    ).start()


def wait_all(target, sem):
    pltpu.make_async_copy(target, target, sem).wait()


def norm_parts(rows):
    mean = jnp.mean(rows, axis=-1, keepdims=True)
    centred = rows - mean
    variance = jnp.mean(centred * centred, axis=-1, keepdims=True)
    scale = lax.rsqrt(variance + EPS_NORM)
    return centred * scale, scale


def norm_back(d_normed, normed, scale):
    first = jnp.mean(d_normed, axis=-1, keepdims=True)
    second = jnp.mean(d_normed * normed, axis=-1, keepdims=True)
    return scale * (d_normed - first - normed * second)


def qkv_kernel(group, core_ref, seat_ref, x_ref, *refs):
    refs, (h_ref, qkv_ref, vec_ref, back_ref, w_ref, turned_ref, sems) = refs[:-7], refs[-7:]

    @pl.when(pl.program_id(0) == 0)
    def _():
        group.start(refs, core_ref, seat_ref, 0, QKV_HALF, w_ref, sems.at[0])
        group.start_once(refs, seat_ref, QKV_HALF, 128, turned_ref, sems.at[1])
        wait_all(turned_ref, sems.at[1])
        vec_ref[...] = turned_ref[...].astype(F32).T[:16]
        wait_all(w_ref, sems.at[0])

    def norm(rows):
        normed, _ = norm_parts(x_ref[rows, :].astype(F32))
        h = (normed * vec_ref[0:1, :] + vec_ref[1:2, :]).astype(BF16)
        h_ref[rows, :] = h
        return h

    block = x_ref.shape[0]
    h = norm(slice(0, block))
    for part, bias in enumerate((2, None, 3)):
        cols = slice(part * D, (part + 1) * D)
        product = mm(h, w_ref[:, cols])
        if bias is not None:
            product = product + vec_ref[bias : bias + 1, :]
        qkv_ref[:, cols] = product.astype(BF16)

    @pl.when(pl.program_id(0) < 3)
    def _():
        back_ref[...] = w_ref[:, at_rows(D)].T


def sub_blocks(rows):
    return [slice(at, at + 256) for at in range(0, rows, 256)]


def qkv_call(core, seats, x, group, block=256):
    rows = x.shape[0]
    return pl.pallas_call(
        functools.partial(qkv_kernel, group),
        name="qkv",
        grid_spec=pltpu.PrefetchScalarGridSpec(
            num_scalar_prefetch=2,
            grid=(rows // block,),
            in_specs=[pl.BlockSpec((block, D), lambda i, *s: (i, 0))] + group.specs(),
            out_specs=[
                pl.BlockSpec((block, D), lambda i, *s: (i, 0)),
                pl.BlockSpec((block, 3 * D), lambda i, *s: (i, 0)),
                pl.BlockSpec((16, D), lambda i, *s: (0, 0)),
                pl.BlockSpec((D, D), lambda i, *s: (jnp.minimum(i, 2), 0)),
            ],
            scratch_shapes=[
                pltpu.VMEM((D, 3 * D), BF16),
                pltpu.VMEM((D, 128), BF16),
                pltpu.SemaphoreType.DMA((2,)),
            ],
        ),
        out_shape=[
            jax.ShapeDtypeStruct((rows, D), BF16),
            jax.ShapeDtypeStruct((rows, 3 * D), BF16),
            jax.ShapeDtypeStruct((16, D), F32),
            jax.ShapeDtypeStruct((3 * D, D), BF16),
        ],
        compiler_params=params(12),
        cost_estimate=cost(2 * rows * D * 3 * D, 10e6),
    )(core, seats, x, *group.arrays)


def head_parts(length, k_all, q_turned, head):
    full_len = k_all.shape[0]
    lane = lax.broadcasted_iota(jnp.int32, (1, 128), 1)
    row = lax.broadcasted_iota(jnp.int32, (128, 1), 0)
    zero, one = jnp.zeros((), BF16), jnp.ones((), BF16)
    mine = (lane // HEAD_DIM) == head
    spare = HEAD_DIM * (1 - head)
    pos = lax.broadcasted_iota(jnp.int32, (full_len, 128), 0)
    fill = jnp.where(pos < length, 0.0, NEG_FILL).astype(BF16)
    k_head = jnp.where(mine, k_all, jnp.where(lane == spare, fill, zero))
    q_head = jnp.where((row // HEAD_DIM) == head, q_turned, jnp.where(row == spare, one, zero))
    return mine, k_head, q_head


def causal_mask(scores, block):
    full = scores.shape[0]
    key_pos = lax.broadcasted_iota(jnp.int32, (block, block), 0)
    query_pos = lax.broadcasted_iota(jnp.int32, (block, block), 1)
    last = jnp.where(key_pos <= query_pos, scores[full - block :], NEG_FILL)
    if full == block:
        return last
    return jnp.concatenate([scores[: full - block], last], axis=0)


def attend_kernel(start, core_ref, len_ref, qkv_ref, *refs):
    a_ref, lse_ref, mixed_ref, scores_ref = refs[-4:]
    block = 256
    full_len = qkv_ref.shape[0]
    length = len_ref[core_ref[0]]
    q_all, k_all, v_all = [
        qkv_ref[:, pl.ds(pl.multiple_of((pl.program_id(0) + start) * 128 + part * D, 128), 128)] for part in range(3)
    ]
    q_all = q_all * jnp.asarray(HEAD_DIM ** (-0.5), BF16)
    v_turned = v_all.T
    q_turned = q_all.T
    ones = jnp.ones((16, full_len), BF16)
    parts = []
    for head in range(2):
        _, k_head, q_head = head_parts(length, k_all, q_turned, head)
        v_head = jnp.concatenate([v_turned[head * HEAD_DIM : (head + 1) * HEAD_DIM], ones], axis=0)
        parts.append((k_head, q_head, v_head))
    units = [(head, j) for j in reversed(range(full_len // block)) for head in range(2)]

    def score(at):
        head, j = units[at]
        k_head, q_head, _ = parts[head]
        top = None
        for i in range(j + 1):
            rows = slice(i * block, (i + 1) * block)
            tile = mm(k_head[rows], q_head[:, j * block : (j + 1) * block])
            if i == j:
                tile = causal_mask(tile, block)
            scores_ref[at % 2, rows, :] = tile
            part = jnp.max(tile.reshape(block // 8, 8, block), axis=0)
            top = part if top is None else jnp.maximum(top, part)
        return jnp.max(top, axis=0, keepdims=True)

    def finish(at, top):
        head, j = units[at]
        v_head = parts[head][2]
        cols = slice(j * block, (j + 1) * block)
        mixed = None
        for i in range(j + 1):
            rows = slice(i * block, (i + 1) * block)
            exped = jnp.exp(scores_ref[at % 2, rows, :] - top).astype(BF16)
            part = mm(v_head[:, rows], exped)
            mixed = part if mixed is None else mixed + part
        total = mixed[HEAD_DIM : HEAD_DIM + 1]
        mixed_ref[head * HEAD_DIM : (head + 1) * HEAD_DIM, cols] = mixed[:HEAD_DIM] / total
        lse_ref[0, head : head + 1, cols] = top + jnp.log(total)

    top = score(0)
    for at in range(len(units)):
        later = score(at + 1) if at + 1 < len(units) else None
        finish(at, top)
        top = later
    a_ref[...] = mixed_ref[...].T.astype(BF16)


def attend_call(core, lengths, qkv, first, count, before):
    rows = qkv.shape[0]
    pairs = HEADS // 2
    before = list(before)
    return pl.pallas_call(
        functools.partial(attend_kernel, first),
        name="attend",
        grid_spec=pltpu.PrefetchScalarGridSpec(
            num_scalar_prefetch=2,
            grid=(count,),
            in_specs=[held_spec()] + [pl.BlockSpec(memory_space=pl.ANY)] * len(before),
            out_specs=[
                pl.BlockSpec((rows, 128), lambda i, c, n: (0, i + first)),
                pl.BlockSpec((1, 8, rows), lambda i, c, n: (i + first, 0, 0)),
            ],
            scratch_shapes=[pltpu.VMEM((128, rows), F32), pltpu.VMEM((2, rows, 256), F32)],
        ),
        out_shape=[
            jax.ShapeDtypeStruct((rows, D), BF16),
            jax.ShapeDtypeStruct((pairs, 8, rows), F32),
        ],
        input_output_aliases={3 + i: i for i in range(len(before))},
        compiler_params=params(12),
        cost_estimate=cost(3e9 * count, 1.2e6 * count, 2 * rows * rows * 0.6 * count),
    )(core, lengths, qkv, *before)


def attend_back_kernel(core_ref, len_ref, q_ref, k_ref, v_ref, a_ref, da_ref, lse_ref, *refs):
    dq_ref, dk_ref, dv_ref, dqt_ref, dk_acc, dv_acc = refs[-6:]
    block = 256
    full_len = q_ref.shape[0]
    length = len_ref[core_ref[0]]
    scale = HEAD_DIM ** (-0.5)
    q_all = q_ref[...] * jnp.asarray(scale, BF16)
    k_all = k_ref[...]
    k_turned = k_all.T
    v_all = v_ref[...]
    da_all = da_ref[...]
    inner = (da_all.astype(F32) * a_ref[...].astype(F32)).T
    q_turned, da_turned = q_all.T, da_all.T
    parts = []
    for head in range(2):
        mine, k_head, q_head = head_parts(length, k_all, q_turned, head)
        zero = jnp.zeros((), BF16)
        q_plain = jnp.where(mine, q_all, zero)
        da_head = jnp.where(mine, da_all, zero)
        row = lax.broadcasted_iota(jnp.int32, (128, 1), 0)
        da_cols = jnp.where((row // HEAD_DIM) == head, da_turned, zero)
        lanes = slice(head * HEAD_DIM, (head + 1) * HEAD_DIM)
        centre = jnp.sum(inner[lanes], axis=0, keepdims=True)
        parts.append((k_head, q_plain, q_head, da_head, da_cols, lanes, centre))
    units = [
        (head, j, i)
        for j in reversed(range(full_len // block))
        for head in range(2)
        for i in range(j + 1)
    ]

    def score(at):
        head, j, i = units[at]
        k_head, _, q_head, _, da_cols, _, _ = parts[head]
        rows, cols = slice(i * block, (i + 1) * block), slice(j * block, (j + 1) * block)
        tile = mm(k_head[rows], q_head[:, cols])
        if i == j:
            tile = causal_mask(tile, block)
        return tile, mm(v_all[rows], da_cols[:, cols])

    seen = set()
    ready = score(0)
    dq_part = None
    for at, (head, j, i) in enumerate(units):
        later = score(at + 1) if at + 1 < len(units) else None
        scores, d_probs = ready
        _, q_plain, _, da_head, _, lanes, centre = parts[head]
        rows, cols = slice(i * block, (i + 1) * block), slice(j * block, (j + 1) * block)
        probs = jnp.exp(scores - lse_ref[0, head : head + 1, cols])
        d_scores = (probs * (d_probs - centre[:, cols])).astype(BF16)
        dv_part = mm(probs.astype(BF16), da_head[cols])
        dk_part = mm(d_scores, q_plain[cols])
        if i in seen:
            dv_acc[rows] += dv_part
            dk_acc[rows] += dk_part
        else:
            seen.add(i)
            dv_acc[rows] = dv_part
            dk_acc[rows] = dk_part
        part = mm(k_turned[lanes, rows], d_scores)
        dq_part = part if i == 0 else dq_part + part
        if i == j:
            dqt_ref[lanes, cols] = dq_part * scale
        ready = later
    dq_ref[...] = dqt_ref[...].T.astype(BF16)
    dk_ref[...] = dk_acc[...].astype(BF16)
    dv_ref[...] = dv_acc[...].astype(BF16)


def attend_back_call(core, lengths, qkv, a, da, lse, start, count, before):
    rows = qkv.shape[0]
    pairs = HEADS // 2
    before = list(before)
    pair_spec = pl.BlockSpec((rows, 128), lambda i, c, n: (0, i + start))
    return pl.pallas_call(
        attend_back_kernel,
        name="attend_back",
        grid_spec=pltpu.PrefetchScalarGridSpec(
            num_scalar_prefetch=2,
            grid=(count,),
            in_specs=[
                pair_spec,
                pl.BlockSpec((rows, 128), lambda i, c, n: (0, i + start + pairs)),
                pl.BlockSpec((rows, 128), lambda i, c, n: (0, i + start + 2 * pairs)),
                pair_spec,
                pair_spec,
                pl.BlockSpec((1, 8, rows), lambda i, c, n: (i + start, 0, 0)),
            ]
            + [pl.BlockSpec(memory_space=pl.ANY)] * len(before),
            out_specs=[pair_spec, pair_spec, pair_spec],
            scratch_shapes=[
                pltpu.VMEM((128, rows), F32),
                pltpu.VMEM((rows, 128), F32),
                pltpu.VMEM((rows, 128), F32),
            ],
        ),
        out_shape=[jax.ShapeDtypeStruct((rows, D), BF16)] * 3,
        input_output_aliases={8 + i: i for i in range(len(before))},
        compiler_params=params(16),
        cost_estimate=cost(6e9 * count, 2e6 * count, 2 * rows * rows * 0.6 * count),
    )(core, lengths, qkv, qkv, qkv, a, da, lse, *before)


def valid_rows(core_ref, len_ref, block):
    pos = pl.program_id(0) * block + lax.broadcasted_iota(jnp.int32, (block, 1), 0)
    return pos < len_ref[core_ref[0]]


def add_row(acc_ref, row, value):
    acc_ref[row : row + 1, :] += jnp.sum(value, axis=0, keepdims=True)


def row_block(core, i, steps):
    half = steps // 2
    return jnp.where(i < half, (1 - core) * half + i, core * half + i - half)


def up_kernel(group, core_ref, len_ref, seat_ref, x_ref, a_ref, og_ref, vec_ref, *refs):
    refs, (
        mid_ref, h_ref, e_ref, slope_ref, dy_ref, wo_back_ref, wu_back_ref, wo_ref, wu_ref, sems,
    ) = refs[:-10], refs[-10:]
    block = x_ref.shape[0]

    @pl.when(pl.program_id(0) == 0)
    def _():
        group.start(refs, core_ref, seat_ref, 0, D // 2, wo_ref, sems.at[0])
        group.start(refs, core_ref, seat_ref, D // 2, FF // 2, wu_ref, sems.at[1])
        wait_all(wo_ref, sems.at[0])
        wait_all(wu_ref, sems.at[1])

    valid = valid_rows(core_ref, len_ref, block)
    dy_ref[...] = jnp.where(valid, og_ref[...].astype(F32), 0.0).astype(BF16)
    mid = x_ref[...].astype(F32) + mm(a_ref[...], wo_ref[...]) + vec_ref[4:5, :]
    mid_ref[...] = mid
    normed, _ = norm_parts(mid)
    h = (normed * vec_ref[5:6, :] + vec_ref[6:7, :]).astype(BF16)
    h_ref[...] = h

    def act(j, z):
        cols = slice(j * D, (j + 1) * D)
        z = z + vec_ref[8 + j : 9 + j, :]
        squared = z * z
        turned = jnp.tanh(z * (GELU_ROOT + (GELU_ROOT * GELU_CUBE) * squared))
        half = 0.5 * turned + 0.5
        act = z * half
        e_ref[:, cols] = act.astype(BF16)
        slope = half + act * (1.0 - turned) * (GELU_ROOT + (3.0 * GELU_ROOT * GELU_CUBE) * squared)
        slope_ref[:, cols] = slope.astype(BF16)

    quarter = at_rows(D)
    wu_back_ref[...] = wu_ref[:, quarter].T

    @pl.when(pl.program_id(0) == 0)
    def _():
        wo_back_ref[...] = wo_ref[...].T

    waiting = None
    for j in range(FF // D):
        z = mm(h, wu_ref[:, j * D : (j + 1) * D])
        if waiting is not None:
            act(*waiting)
        waiting = (j, z)
    act(*waiting)


def up_call(core, lengths, seats, x, a, og, vec, group, block=256):
    rows = x.shape[0]
    assert rows // block == FF // D
    row_spec = pl.BlockSpec((block, D), lambda i, *s: (i, 0))
    wide_spec = pl.BlockSpec((block, FF), lambda i, *s: (i, 0))
    low, wide = [jax.ShapeDtypeStruct((rows, width), BF16) for width in (D, FF)]
    return pl.pallas_call(
        functools.partial(up_kernel, group),
        name="up",
        grid_spec=pltpu.PrefetchScalarGridSpec(
            num_scalar_prefetch=3,
            grid=(rows // block,),
            in_specs=[row_spec, row_spec, row_spec, whole_spec(vec.shape)] + group.specs(),
            out_specs=[
                row_spec, row_spec, wide_spec, wide_spec, row_spec,
                pl.BlockSpec((D, D), lambda i, *s: (0, 0)),
                pl.BlockSpec((D, D), lambda i, *s: (i, 0)),
            ],
            scratch_shapes=[
                pltpu.VMEM((D, D), BF16),
                pltpu.VMEM((D, FF), BF16),
                pltpu.SemaphoreType.DMA((2,)),
            ],
        ),
        out_shape=[
            jax.ShapeDtypeStruct((rows, D), F32),
            low,
            wide,
            wide,
            low,
            jax.ShapeDtypeStruct((D, D), BF16),
            jax.ShapeDtypeStruct((FF, D), BF16),
        ],
        compiler_params=params(48),
        cost_estimate=cost(6e9, 30e6, rows * FF),
    )(core, lengths, seats, x, a, og, vec, *group.arrays)


def down_kernel(
    group, core_ref, len_ref, seat_ref, mid_ref, e_ref, slope_ref, dy_ref, wo_back_ref, wu_back_ref, vec_ref, *refs
):
    refs, (
        theirs_ref, mine_ref, dz_ref, dmb_ref, dm_ref, da_ref, acc_ref, wd_ref, wd_back_ref, sems,
    ) = refs[:-10], refs[-10:]
    block = da_ref.shape[0]
    step, steps = pl.program_id(0), pl.num_programs(0)

    @pl.when(step == 0)
    def _():
        group.start(refs, core_ref, seat_ref, 0, D // 2, wd_ref, sems.at[0])
        acc_ref[...] = jnp.zeros_like(acc_ref)
        wait_all(wd_ref, sems.at[0])
        for j in range(FF // D):
            cols = slice(j * D, (j + 1) * D)
            wd_back_ref[:, cols] = wd_ref[cols, :].T

    mid = mid_ref[...]
    down = vec_ref[7:8, :] + mid + mm(e_ref[...], wd_ref[...])
    pos = row_block(core_ref[0], step, steps) * block + lax.broadcasted_iota(jnp.int32, (block, 1), 0)
    down = jnp.where(pos < len_ref[core_ref[0]], down, 0.0).astype(BF16)

    @pl.when(step < steps // 2)
    def _():
        theirs_ref[...] = down

    @pl.when(step >= steps // 2)
    def _():
        mine_ref[0] = down

    dy = dy_ref[...]
    add_row(acc_ref, 7, dy.astype(F32))
    dh = None
    waiting = None
    for j in range(FF // D + 1):
        later = None
        if j < FF // D:
            later = (j, mm(dy, wd_back_ref[:, j * D : (j + 1) * D]))
        if waiting is not None:
            at, de = waiting
            cols = slice(at * D, (at + 1) * D)
            dz = (de * slope_ref[:, cols].astype(F32)).astype(BF16)
            dz_ref[:, cols] = dz
            add_row(acc_ref, 8 + at, dz.astype(F32))
            part = mm(dz, wu_back_ref[cols, :])
            dh = part if dh is None else dh + part
        waiting = later
    normed, scale = norm_parts(mid)
    add_row(acc_ref, 5, dh * normed)
    add_row(acc_ref, 6, dh)
    dm = dy.astype(F32) + norm_back(dh * vec_ref[5:6, :], normed, scale)
    dm_ref[...] = dm
    dm_low = dm.astype(BF16)
    dmb_ref[...] = dm_low
    add_row(acc_ref, 4, dm_low.astype(F32))
    da_ref[...] = mm(dm_low, wo_back_ref[...]).astype(BF16)


def down_call(core, lengths, seats, mid, e, slope, dy, wo, wu, vec, group, block=256):
    rows = mid.shape[0]
    steps = rows // block
    half = steps // 2
    row_spec, wide_spec = [
        pl.BlockSpec((block, width), lambda i, c, *s: (row_block(c[0], i, steps), 0)) for width in (D, FF)
    ]
    return pl.pallas_call(
        functools.partial(down_kernel, group),
        name="down",
        grid_spec=pltpu.PrefetchScalarGridSpec(
            num_scalar_prefetch=3,
            grid=(steps,),
            in_specs=[row_spec, wide_spec, wide_spec, row_spec]
            + [whole_spec(part.shape) for part in (wo, wu, vec)]
            + group.specs(),
            out_specs=[
                pl.BlockSpec((block, D), lambda i, *s: (jnp.minimum(i, half - 1), 0)),
                pl.BlockSpec((1, block, D), lambda i, c, *s: (c[0], jnp.maximum(i - half, 0), 0)),
                wide_spec, row_spec, row_spec, row_spec,
                pl.BlockSpec((16, D), lambda i, *s: (0, 0)),
            ],
            scratch_shapes=[pltpu.VMEM((FF, D), BF16), pltpu.VMEM((D, FF), BF16), pltpu.SemaphoreType.DMA((1,))],
        ),
        out_shape=[
            jax.ShapeDtypeStruct((rows // 2, D), BF16),
            jax.ShapeDtypeStruct((2, rows // 2, D), BF16),
            jax.ShapeDtypeStruct((rows, FF), BF16),
            jax.ShapeDtypeStruct((rows, D), BF16),
            jax.ShapeDtypeStruct((rows, D), F32),
            jax.ShapeDtypeStruct((rows, D), BF16),
            jax.ShapeDtypeStruct((16, D), F32),
        ],
        compiler_params=params(48),
        cost_estimate=cost(1.6e10, 35e6),
    )(core, lengths, seats, mid, e, slope, dy, wo, wu, vec, *group.arrays)


def pick(values, half, mode):
    if mode == "split":
        width = values.shape[1] // 2
        return [values[:, half * width : (half + 1) * width]]
    return [values[:, at : at + 128] for at in range(half * 128, values.shape[1], 256)]


def weight_grad_kernel(lefts, rights, mode, core_ref, *refs):
    left_refs, right_refs = refs[:lefts], refs[lefts : lefts + sum(rights)]
    own_ref, other_ref = refs[-2:]
    halves = ([], [])
    at = 0
    for left_ref, count in zip(left_refs, rights):
        left = left_ref[...]
        for right_ref in right_refs[at : at + count]:
            whole = mm(left, right_ref[...], TN).astype(BF16)
            for half in range(2):
                halves[half].extend(pick(whole, half, mode))
        at += count
    low, high = [part[0] if len(part) == 1 else jnp.concatenate(part, axis=1) for part in halves]

    @pl.when(core_ref[0] == 0)
    def _():
        own_ref[...] = low
        other_ref[...] = high

    @pl.when(core_ref[0] != 0)
    def _():
        own_ref[...] = high
        other_ref[...] = low


def weight_grad_call(core, products, block, name, mode="split", cols=None):
    rows, height = products[0][0].shape
    lefts = [left for left, _ in products]
    rights = [right for _, group in products for right in group]
    widths = [right.shape[1] if cols is None else cols[0] for right in rights]
    width = sum(widths)
    seat = 0 if cols is None else cols[1]
    return pl.pallas_call(
        functools.partial(weight_grad_kernel, len(lefts), [len(group) for _, group in products], mode),
        name=name,
        grid_spec=pltpu.PrefetchScalarGridSpec(
            num_scalar_prefetch=1,
            grid=(height // block,),
            in_specs=[pl.BlockSpec((rows, block), lambda i, c: (0, i))] * len(lefts)
            + [
                pl.BlockSpec((rows, w), lambda i, c: (0, seat), pipeline_mode=pl.Buffered(1)) for w in widths
            ],
            out_specs=[pl.BlockSpec((block, width // 2), lambda i, c: (i, 0))] * 2,
        ),
        out_shape=[jax.ShapeDtypeStruct((height, width // 2), BF16)] * 2,
        compiler_params=params(16 if mode == "turns" else 48),
        cost_estimate=cost(2 * rows * height * width, rows * (height + width) * 2 + height * width * 2),
    )(core, *lefts, *rights)


def last_kernel(
    core_ref, x_ref, dm_ref, dq_ref, dk_ref, dv_ref, w_ref, vec_ref, before_ref, theirs_ref, mine_ref, acc_ref
):
    step, steps = pl.program_id(0), pl.num_programs(0)

    @pl.when(step == 0)
    def _():
        acc_ref[...] = before_ref[...]

    subs = sub_blocks(x_ref.shape[0])

    def product(rows):
        return (
            mm(dq_ref[rows, :], w_ref[:D])
            + mm(dk_ref[rows, :], w_ref[D : 2 * D])
            + mm(dv_ref[rows, :], w_ref[2 * D :])
        )

    grads = []
    dh = product(subs[0])
    add_row(acc_ref, 2, dq_ref[...].astype(F32))
    add_row(acc_ref, 3, dv_ref[...].astype(F32))
    for at, rows in enumerate(subs):
        later = product(subs[at + 1]) if at + 1 < len(subs) else None
        normed, scale = norm_parts(x_ref[rows, :].astype(F32))
        add_row(acc_ref, 0, dh * normed)
        add_row(acc_ref, 1, dh)
        grads.append(dm_ref[rows, :] + norm_back(dh * vec_ref[0:1, :], normed, scale))
        dh = later

    @pl.when(step < steps // 2)
    def _():
        for rows, grad in zip(subs, grads):
            theirs_ref[rows, :] = grad

    @pl.when(step >= steps // 2)
    def _():
        for rows, grad in zip(subs, grads):
            mine_ref[0, rows, :] = grad


def last_call(core, x, dm, dq, dk, dv, w, vec, before, block=256):
    rows = x.shape[0]
    steps = rows // block
    half = steps // 2
    row_spec = pl.BlockSpec((block, D), lambda i, c, *s: (row_block(c[0], i, steps), 0))
    return pl.pallas_call(
        last_kernel,
        name="last",
        grid_spec=pltpu.PrefetchScalarGridSpec(
            num_scalar_prefetch=1,
            grid=(steps,),
            in_specs=[row_spec] * 5 + [whole_spec(part.shape) for part in (w, vec, before)],
            out_specs=[
                pl.BlockSpec((block, D), lambda i, *s: (jnp.minimum(i, half - 1), 0)),
                pl.BlockSpec((1, block, D), lambda i, c, *s: (c[0], jnp.maximum(i - half, 0), 0)),
                pl.BlockSpec((16, D), lambda i, *s: (0, 0)),
            ],
        ),
        out_shape=[
            jax.ShapeDtypeStruct((rows // 2, D), F32),
            jax.ShapeDtypeStruct((2, rows // 2, D), F32),
            jax.ShapeDtypeStruct((16, D), F32),
        ],
        compiler_params=params(12),
        cost_estimate=cost(rows * 6 * D * D, 16e6),
    )(core, x, dm, dq, dk, dv, w, vec, before)


def adam_kernel(plans, sources, core_ref, *refs):
    halves = [refs[2 * i : 2 * i + 2] for i in range(sources)]
    count = len(plans)
    states = refs[2 * sources : 2 * sources + 3 * count]
    outs = refs[2 * sources + 3 * count : 2 * sources + 6 * count]
    grads = refs[2 * sources + 6 * count :]
    for core in range(2):

        @pl.when(core_ref[0] == core)
        def _():
            for (_, _, moves), grad_ref in zip(plans, grads):
                for source, start, width, place0, place1 in moves:
                    for half, place in ((0, place0), (1, place1)):
                        ref = halves[source][0 if half == core else 1]
                        grad_ref[:, place : place + width] = ref[:, start : start + width].astype(F32)

    for i, (rate, decay, _) in enumerate(plans):
        weight, first, second = states[3 * i : 3 * i + 3]
        new = adamw(weight[...], grads[i][...], first[...], second[...], rate, decay)
        for out, value in zip(outs[3 * i : 3 * i + 3], new):
            out[...] = value


def adam_call(core, halves, states, plans):
    flat = [part for pair in halves for part in pair]
    held = [part for state in states for part in state]
    spec = pl.BlockSpec(memory_space=pltpu.VMEM)
    news = pl.pallas_call(
        functools.partial(adam_kernel, plans, len(halves)),
        name="adam",
        in_specs=[pl.BlockSpec(memory_space=pltpu.SMEM)] + [spec] * (len(flat) + len(held)),
        out_specs=[spec] * len(held),
        out_shape=[jax.ShapeDtypeStruct(part.shape, F32) for part in held],
        scratch_shapes=[pltpu.VMEM(state[0].shape, F32) for state in states],
        compiler_params=params(12),
        cost_estimate=cost(1e6, 24 * sum(state[0].size for state in states)),
    )(core, *flat, *held)
    return [news[3 * i : 3 * i + 3] for i in range(len(states))]


def after(value, *others):
    if not others:
        return value
    return lax.optimization_barrier((value,) + others)[0]


def cut(array, axis, index, size=1):
    starts = [jnp.uint32(0)] * array.ndim
    sizes = list(array.shape)
    starts[axis], sizes[axis] = index, size
    return lax.dynamic_slice(array, starts, sizes)


class Grid:
    def __init__(self, chips):
        log = chips.bit_length() - 1
        side = 1 << (log // 3)
        if side * side * (chips // (side * side)) != chips:
            side = 1
        self.chips = chips
        self.n = side
        self.nz = chips // (side * side)
        self.core = lax.axis_index("seq")
        self.chip = lax.axis_index("dp")
        self.x = self.chip % side
        self.y = self.chip // side % side
        self.z = self.chip // (side * side)

    def pin(self, value):
        n, core = self.n, self.core
        first, second = self.coords(core)
        places = {
            "core": core,
            "other": 1 - core,
            "chip": self.chip,
            "seats": self.seats(True),
            "q_seats": self.seats(False),
        }
        for s in range(n):
            for t in range(n):
                places["plane", s, t] = self.plane((first + s) % n, (second + t) % n, core)
        for at in range(self.nz):
            places["z", at] = self.z ^ at
        names = list(places)
        held = lax.optimization_barrier((value, *[places[name].astype(jnp.uint32) for name in names]))
        self.places = dict(zip(names, held[1:]))
        return held[0]

    def plane(self, first, second, core):
        return jnp.where(core == 0, second * self.n + first, first * self.n + second)

    def coords(self, core):
        return jnp.where(core == 0, self.x, self.y), jnp.where(core == 0, self.y, self.x)

    def permute(self, value, axis, shift=0):
        pairs = []
        for chip in range(self.chips):
            for core in range(2):
                x, y, z = chip % self.n, chip // self.n % self.n, chip // (self.n * self.n)
                to_core = core
                if axis == "z":
                    z = (z + shift) % self.nz
                elif axis == "zx":
                    z = z ^ shift
                elif axis == "core":
                    to_core = 1 - core
                elif (axis == "first") == (core == 0):
                    x = (x + shift) % self.n
                else:
                    y = (y + shift) % self.n
                pairs.append((chip * 2 + core, ((z * self.n + y) * self.n + x) * 2 + to_core))
        return lax.ppermute(value, ("dp", "seq"), pairs)

    def swap(self, value):
        return self.permute(value, "core")

    def join(self, own, other, axis):
        return jnp.where(
            self.places["core"] == 0,
            jnp.concatenate([own, other], axis),
            jnp.concatenate([other, own], axis),
        )

    def seats(self, halving):
        found = []
        for half in range(2):
            core = self.core if half == 0 else 1 - self.core
            first, second = self.coords(core)
            for s2 in range(self.n):
                for s1 in range(self.n):
                    flat = self.plane((first - s1) % self.n, (second - s2) % self.n, core)
                    for sz in range(self.nz):
                        z = self.z ^ sz if halving else (self.z - sz) % self.nz
                        found.append(z * self.n * self.n + flat)
        return jnp.stack(found).astype(jnp.int32)

    def total_small(self, value, *untils):
        steps = [("core", 0), ("first", 1), ("second", 1)] if self.n == 2 else [("core", 0)]
        if self.n != 2:
            for axis in ("first", "second"):
                value = value + sum(self.permute(value, axis, s) for s in range(1, self.n))
        bit = 1
        while bit < self.nz:
            steps.append(("zx", bit))
            bit *= 2
        for at, (axis, shift) in enumerate(steps):
            until = untils[at] if at < len(untils) else ()
            value = value + after(self.permute(value, axis, shift), *until)
        return value

    def gather_z(self, block, *until):
        return jnp.stack([block] + [after(self.permute(block, "z", s), *until) for s in range(1, self.nz)])

    def gather_bit(self, held, bit, *until):
        return jnp.concatenate([held, after(self.permute(held, "zx", bit), *until)])

    def gather_first(self, column, *until):
        return jnp.stack([column] + [after(self.permute(column, "first", s), *until) for s in range(1, self.n)])

    def gather_second(self, line, *until):
        return [after(self.permute(line, "second", s), *until) for s in range(1, self.n)]

    def scatter_first(self, own, pair, *until):
        rows, cols = own.shape[0] // self.chips, own.shape[1]
        n = self.n

        def seat(s1, s2):
            own_part, pair_part = [
                cut(part.reshape(self.nz, n * n, rows, cols), 1, self.places["plane", s1, s2]).astype(F32)
                for part in (own, pair)
            ]
            return own_part + pair_part

        kept = [seat(0, t) for t in range(n)]
        for s in range(1, n):
            send = jnp.stack([seat(s, t).astype(BF16) for t in range(n)])
            got = after(self.permute(send, "first", s), *until)
            kept = [kept[t] + got[t].astype(F32) for t in range(n)]
        return kept[0], [part.astype(BF16) for part in kept[1:]]

    def scatter_second(self, kept, *until):
        mine, rest = kept
        got = [after(self.permute(rest[s - 1], "second", s), *until) for s in range(1, self.n)]
        for part in got:
            mine = mine + part.astype(F32)
        return mine.reshape((self.nz,) + mine.shape[2:]), got

    def order_z(self, mine):
        return [cut(mine, 0, self.places["z", at])[0] for at in range(self.nz)]

    def scatter_bit(self, parts, *until):
        half = len(parts) // 2
        send = parts[half] if half == 1 else jnp.stack([part.astype(BF16) for part in parts[half:]])
        got = after(self.permute(send.astype(BF16), "zx", half), *until)
        if half == 1:
            return [parts[0] + got.astype(F32)], got
        return [part + got[at].astype(F32) for at, part in enumerate(parts[:half])], got

    def scatter_z(self, parts):
        while len(parts) > 1:
            parts, _ = self.scatter_bit(parts)
        return parts[0]


def adamw(weight, gradient, first_moment, second_moment, step_rate, weight_decay):
    first_moment = BETA_ONE * first_moment + (1.0 - BETA_ONE) * gradient
    second_moment = BETA_TWO * second_moment + (1.0 - BETA_TWO) * gradient * gradient
    first_fix = 1.0 - BETA_ONE**STEP
    second_fix = 1.0 - BETA_TWO**STEP
    direction = first_moment / first_fix / (jnp.sqrt(second_moment / second_fix) + EPS_ADAM)
    return (weight - step_rate * (direction + weight_decay * weight), first_moment, second_moment)


def local(
    block_in, lengths, out_grad, w_qkv, w_out, w_up, w_down, vectors,
    first_qkv, first_out, first_up, first_down, first_vectors,
    second_qkv, second_out, second_up, second_down, second_vectors,
):
    grid = Grid(lax.axis_size("dp"))
    core = grid.core
    w_qkv_first = grid.pin(w_qkv)
    places = grid.places
    core_arr = places["core"].reshape(1).astype(jnp.int32)
    half_len = block_in.shape[1]
    vec_count, vec_here = vectors.shape

    def own_slot(halves):
        mine, theirs = [cut(halves, 0, places[name])[0] for name in ("core", "other")]
        return grid.join(mine, grid.swap(theirs), 0)

    def both_slots(mine, got):
        zero = jnp.uint32(0)
        return lax.dynamic_update_slice(mine, got[None], (places["other"], zero, zero))

    def half_of(shard):
        width = shard.shape[1] // 2
        return jnp.where(places["core"] == 0, shard[:, :width], shard[:, width:]).astype(BF16)

    seats, q_seats = [places[name].astype(jnp.int32) for name in ("seats", "q_seats")]

    turned = jnp.pad(vectors.T.astype(BF16), ((0, 0), (0, 128 - vec_count)))
    q_block = jnp.concatenate([half_of(w_qkv_first), turned], axis=1)
    u_block = jnp.concatenate([half_of(w_out), half_of(w_up)], axis=1)
    d_block = half_of(w_down)
    q_col = grid.gather_z(q_block)
    x = own_slot(block_in)
    bits = [1 << at for at in range((grid.nz - 1).bit_length())]
    u_col, d_col = u_block[None], d_block[None]
    for bit in bits[:-1]:
        u_col = grid.gather_bit(u_col, bit)
        d_col = grid.gather_bit(d_col, bit)
    q_line = after(grid.gather_first(q_col, x), u_col, d_col)
    q_rest = grid.gather_second(q_line)
    u_col = grid.gather_bit(after(u_col, q_line), bits[-1])
    q_line_swap = grid.swap(q_line)
    q_rest_swap = [grid.swap(after(part, u_col)) for part in q_rest]
    q_group = finish_group(grid, q_seats, [q_line] + q_rest, [q_line_swap] + q_rest_swap)

    h1, qkv, vec, w_back = qkv_call(core_arr, q_seats, x, q_group)
    u_line = grid.gather_first(u_col, qkv)
    d_col = grid.gather_bit(after(d_col, u_col), bits[-1], qkv)
    og = own_slot(after(out_grad, qkv))
    att = attend_call(core_arr, lengths, after(qkv, u_line, d_col), 0, 4, ())
    u_line_swap = after(grid.swap(u_line), *att)
    u_rest = grid.gather_second(u_line, *att)
    d_col = after(d_col, *u_rest)
    a, lse = attend_call(core_arr, lengths, after(qkv, d_col), 4, 2, att)
    u_rest_swap = [after(grid.swap(part), a) for part in u_rest]
    d_line = grid.gather_first(d_col, a)
    u_group = finish_group(grid, seats, [u_line] + u_rest, [u_line_swap] + u_rest_swap)
    mid, h2, e, slope, dy, wo, wu = up_call(core_arr, lengths, seats, x, after(a, d_line), og, vec, u_group)
    d_line_swap = after(grid.swap(d_line), mid)
    d_rest = grid.gather_second(d_line, mid)
    d_own, d_other = weight_grad_call(core_arr, [(after(e, *d_rest), [dy])], 512, "grad_down")
    d_rest_swap = [after(grid.swap(part), d_own) for part in d_rest]
    d_group = finish_group(grid, seats, [d_line] + d_rest, [d_line_swap] + d_rest_swap)
    out_theirs, out_mine, dz, dmb, dm, da, acc_mid = down_call(
        core_arr, lengths, seats, mid, e, slope, dy, wo, wu, vec, d_group
    )

    d_pair = after(grid.swap(d_other), dz)
    u_own, u_other = weight_grad_call(
        core_arr, [(a, [dmb]), (h2, [after(dz, d_pair)])], 384, "grad_up"
    )
    d_kept = grid.scatter_first(d_own, d_pair, u_own)

    def back_call(start, count, before, *needs):
        return attend_back_call(core_arr, lengths, qkv, a, after(da, *needs), lse, start, count, before)

    back = back_call(0, 2, (), u_own, *d_kept[1])
    d_sum, d_here = grid.scatter_second(d_kept, *back)
    u_pair = after(grid.swap(u_other), *back)
    back = back_call(2, 4, back, u_pair, *d_here)
    d_parts, _ = grid.scatter_bit(grid.order_z(d_sum), *back)
    u_kept = grid.scatter_first(u_own, u_pair, *back)
    dq, dk, dv = back
    block_out = both_slots(out_mine, after(grid.swap(after(out_theirs, back[0])), dq))
    q_own, q_other = weight_grad_call(
        core_arr, [(h1, [after(dq, *u_kept[1]), dk, dv])], 384, "grad_qkv", "turns"
    )
    u_sum, u_here = grid.scatter_second(u_kept, q_own)
    d_mine = grid.scatter_z(d_parts)
    d_other_mine = grid.swap(d_mine)
    q_pair = after(grid.swap(q_other), *u_here)
    in_theirs, in_mine, acc = last_call(
        core_arr, x, dm, after(dq, q_own, q_pair), dk, dv, w_back, vec, acc_mid
    )
    q_kept = grid.scatter_first(q_own, q_pair, in_theirs)
    u_parts, u_got = grid.scatter_bit(grid.order_z(u_sum), *q_kept[1])
    q_sum, q_here = grid.scatter_second(q_kept, u_got)
    down_new, = adam_call(
        core_arr,
        [(d_mine, d_other_mine)],
        [(after(w_down, *q_kept[1]), first_down, second_down)],
        [(FF ** (-0.5), MATRIX_DECAY, [(0, 0, D // 2, 0, D // 2)])],
    )
    in_got = grid.swap(after(in_theirs, *q_kept[1]))
    u_mine = grid.scatter_z([after(part, *q_here) for part in u_parts])
    u_other_mine = grid.swap(u_mine)
    q_parts = grid.order_z(q_sum)
    q_gots = []
    while len(q_parts) > 1:
        q_parts, got = grid.scatter_bit(q_parts)
        q_gots.append((got,))
    q_mine = q_parts[0]
    q_other_mine = grid.swap(q_mine)
    in_grad = both_slots(in_mine, after(in_got, *q_here))
    w_qkv = after(w_qkv, in_grad)
    vec_total = grid.total_small(acc, q_kept[1], q_here, *q_gots)

    half, wide = D // 2, FF // 2
    out_new, up_new = adam_call(
        core_arr,
        [(u_mine, u_other_mine)],
        [(after(w_out, in_grad), first_out, second_out), (w_up, first_up, second_up)],
        [
            ((D // 64) ** (-0.5), MATRIX_DECAY, [(0, 0, half, 0, half)]),
            (D ** (-0.5), MATRIX_DECAY, [(0, half, wide, 0, wide)]),
        ],
    )
    moves = []
    for turn in range(3 * D // 256):
        moves.append((0, turn * 128, 128, turn * 256, turn * 256 + 128))
    qkv_new, = adam_call(
        core_arr,
        [(q_mine, q_other_mine)],
        [(w_qkv, first_qkv, second_qkv)],
        [(D ** (-0.5), MATRIX_DECAY, moves)],
    )
    vec_grad = cut(vec_total[:vec_count].reshape(vec_count, -1, vec_here), 1, places["chip"])[:, 0]
    vec_new = adamw(vectors, vec_grad, first_vectors, second_vectors, VECTOR_RATE, 0.0)
    news = [qkv_new, out_new, up_new, down_new, vec_new]
    return (block_out, in_grad) + tuple(new[kind] for kind in range(3) for new in news)


def finish_group(grid, seats, own, other):
    rows, cols = own[0].shape[-2:]
    if rows % 16 == 0:
        return Pieces(own + other, rows)
    found = []
    for half, parts in enumerate((own, other)):
        here = seats[half * grid.chips : (half + 1) * grid.chips]
        order = jnp.zeros((grid.chips,), jnp.int32).at[here].set(jnp.arange(grid.chips, dtype=jnp.int32))
        blocks = jnp.concatenate(parts).reshape(grid.chips, rows, cols)
        found.append(jnp.take(blocks, order, axis=0).reshape(1, 1, grid.chips * rows, cols))
    return Pieces(found, grid.chips * rows, True)


def solution(mesh):
    weight = P("dp", None)
    vector = P(None, "dp")
    state = (weight, weight, weight, weight, vector)
    tokens = P("dp", "seq", None)
    return jax.shard_map(
        local,
        mesh=mesh,
        in_specs=(tokens, P("dp"), tokens) + state * 3,
        out_specs=(tokens, tokens) + state * 3,
        check_vma=False,
    )
```

```python
import functools

import jax
import jax.numpy as jnp
from jax import lax
from jax.experimental import pallas as pl
from jax.experimental.pallas import tpu as pltpu
from jax.sharding import PartitionSpec as P

D = 768
HEADS = 12
HEAD_DIM = 64
FF = 3072
STEP = 10

EPS_NORM = 1e-05
EPS_ADAM = 1e-08
BETA_ONE = 0.5
BETA_TWO = 0.5
MATRIX_DECAY = 0.1
VECTOR_RATE = 0.1
NEG_FILL = -1e30
GELU_ROOT = 0.7978845608028654
GELU_CUBE = 0.044715
QKV_HALF = 3 * D // 2

F32 = jnp.float32
BF16 = jnp.bfloat16

NN = (((1,), (0,)), ((), ()))
NT = (((1,), (1,)), ((), ()))
TN = (((0,), (0,)), ((), ()))


def mm(left, right, dims=NN):
    return lax.dot_general(left, right, dims, preferred_element_type=F32)


def cost(flops, nbytes, trans=0):
    return pl.CostEstimate(flops=int(4 * flops), bytes_accessed=int(4 * nbytes), transcendentals=int(trans))


def params(mib=60):
    return pltpu.CompilerParams(vmem_limit_bytes=mib * 1024 * 1024)


def held_spec():
    return pl.BlockSpec(memory_space=pltpu.VMEM)


def at_rows(block):
    return pl.ds(pl.multiple_of(pl.program_id(0) * block, block), block)


def whole_spec(shape):
    return pl.BlockSpec(shape, lambda *idx: (0,) * len(shape), pipeline_mode=pl.Buffered(1))


class Pieces:
    def __init__(self, arrays, rows, ordered=False):
        self.arrays = arrays
        self.rows = rows
        self.ordered = ordered
        self.halves = 2
        self.count = len(arrays) // self.halves
        self.lines, self.depth = arrays[0].shape[:2]

    def specs(self):
        return [pl.BlockSpec(memory_space=pltpu.HBM)] * len(self.arrays)

    def row(self, seat_ref, at):
        return 0 if self.ordered else pl.multiple_of(seat_ref[at] * self.rows, 16)

    def start(self, refs, core_ref, seat_ref, start_col, width, target, sem):
        core = core_ref[0]
        at = 0
        for half in range(self.halves):
            where = core if half == 0 else 1 - core
            for s2 in range(self.count):
                ref = refs[half * self.count + s2]
                for s1 in range(self.lines):
                    for sz in range(self.depth):
                        row = self.row(seat_ref, at)
                        at += 1
                        col = pl.multiple_of(where * width, 128)
                        pltpu.make_async_copy(
                            ref.at[s1, sz, :, pl.ds(start_col, width)],
                            target.at[pl.ds(row, self.rows), pl.ds(col, width)],
                            sem,
                        ).start()

    def start_once(self, refs, seat_ref, start_col, width, target, sem):
        at = 0
        for s2 in range(self.count):
            for s1 in range(self.lines):
                for sz in range(self.depth):
                    row = self.row(seat_ref, at)
                    at += 1
                    pltpu.make_async_copy(
                        refs[s2].at[s1, sz, :, pl.ds(start_col, width)],
                        target.at[pl.ds(row, self.rows), :],
                        sem,
                    ).start()


def wait_all(target, sem):
    pltpu.make_async_copy(target, target, sem).wait()


def norm_parts(rows):
    mean = jnp.mean(rows, axis=-1, keepdims=True)
    centred = rows - mean
    variance = jnp.mean(centred * centred, axis=-1, keepdims=True)
    scale = lax.rsqrt(variance + EPS_NORM)
    return centred * scale, scale


def norm_back(d_normed, normed, scale):
    first = jnp.mean(d_normed, axis=-1, keepdims=True)
    second = jnp.mean(d_normed * normed, axis=-1, keepdims=True)
    return scale * (d_normed - first - normed * second)


def qkv_kernel(group, core_ref, seat_ref, x_ref, *refs):
    refs, (h_ref, qkv_ref, vec_ref, back_ref, w_ref, turned_ref, sems) = refs[:-7], refs[-7:]

    @pl.when(pl.program_id(0) == 0)
    def _():
        group.start(refs, core_ref, seat_ref, 0, QKV_HALF, w_ref, sems.at[0])
        group.start_once(refs, seat_ref, QKV_HALF, 128, turned_ref, sems.at[1])
        wait_all(turned_ref, sems.at[1])
        vec_ref[...] = turned_ref[...].astype(F32).T[:16]
        wait_all(w_ref, sems.at[0])

    def norm(rows):
        normed, _ = norm_parts(x_ref[rows, :].astype(F32))
        h = (normed * vec_ref[0:1, :] + vec_ref[1:2, :]).astype(BF16)
        h_ref[rows, :] = h
        return h

    block = x_ref.shape[0]
    h = norm(slice(0, block))
    for part, bias in enumerate((2, None, 3)):
        cols = slice(part * D, (part + 1) * D)
        product = mm(h, w_ref[:, cols])
        if bias is not None:
            product = product + vec_ref[bias : bias + 1, :]
        qkv_ref[:, cols] = product.astype(BF16)

    @pl.when(pl.program_id(0) < 3)
    def _():
        back_ref[...] = w_ref[:, at_rows(D)].T


def sub_blocks(rows):
    return [slice(at, at + 256) for at in range(0, rows, 256)]


def qkv_call(core, seats, x, group, block=256):
    rows = x.shape[0]
    return pl.pallas_call(
        functools.partial(qkv_kernel, group),
        name="qkv",
        grid_spec=pltpu.PrefetchScalarGridSpec(
            num_scalar_prefetch=2,
            grid=(rows // block,),
            in_specs=[pl.BlockSpec((block, D), lambda i, *s: (i, 0))] + group.specs(),
            out_specs=[
                pl.BlockSpec((block, D), lambda i, *s: (i, 0)),
                pl.BlockSpec((block, 3 * D), lambda i, *s: (i, 0)),
                pl.BlockSpec((16, D), lambda i, *s: (0, 0)),
                pl.BlockSpec((D, D), lambda i, *s: (jnp.minimum(i, 2), 0)),
            ],
            scratch_shapes=[
                pltpu.VMEM((D, 3 * D), BF16),
                pltpu.VMEM((D, 128), BF16),
                pltpu.SemaphoreType.DMA((2,)),
            ],
        ),
        out_shape=[
            jax.ShapeDtypeStruct((rows, D), BF16),
            jax.ShapeDtypeStruct((rows, 3 * D), BF16),
            jax.ShapeDtypeStruct((16, D), F32),
            jax.ShapeDtypeStruct((3 * D, D), BF16),
        ],
        compiler_params=params(12),
        cost_estimate=cost(2 * rows * D * 3 * D, 10e6),
    )(core, seats, x, *group.arrays)


def head_parts(length, k_all, q_turned, head):
    full_len = k_all.shape[0]
    lane = lax.broadcasted_iota(jnp.int32, (1, 128), 1)
    row = lax.broadcasted_iota(jnp.int32, (128, 1), 0)
    zero, one = jnp.zeros((), BF16), jnp.ones((), BF16)
    mine = (lane // HEAD_DIM) == head
    spare = HEAD_DIM * (1 - head)
    pos = lax.broadcasted_iota(jnp.int32, (full_len, 128), 0)
    fill = jnp.where(pos < length, 0.0, NEG_FILL).astype(BF16)
    k_head = jnp.where(mine, k_all, jnp.where(lane == spare, fill, zero))
    q_head = jnp.where((row // HEAD_DIM) == head, q_turned, jnp.where(row == spare, one, zero))
    return mine, k_head, q_head


def causal_mask(scores, block):
    full = scores.shape[0]
    key_pos = lax.broadcasted_iota(jnp.int32, (block, block), 0)
    query_pos = lax.broadcasted_iota(jnp.int32, (block, block), 1)
    last = jnp.where(key_pos <= query_pos, scores[full - block :], NEG_FILL)
    if full == block:
        return last
    return jnp.concatenate([scores[: full - block], last], axis=0)


def attend_kernel(start, core_ref, len_ref, qkv_ref, *refs):
    a_ref, lse_ref, mixed_ref, scores_ref = refs[-4:]
    block = 256
    full_len = qkv_ref.shape[0]
    length = len_ref[core_ref[0]]
    q_all, k_all, v_all = [
        qkv_ref[:, pl.ds(pl.multiple_of((pl.program_id(0) + start) * 128 + part * D, 128), 128)] for part in range(3)
    ]
    q_all = q_all * jnp.asarray(HEAD_DIM ** (-0.5), BF16)
    v_turned = v_all.T
    q_turned = q_all.T
    ones = jnp.ones((16, full_len), BF16)
    parts = []
    for head in range(2):
        _, k_head, q_head = head_parts(length, k_all, q_turned, head)
        v_head = jnp.concatenate([v_turned[head * HEAD_DIM : (head + 1) * HEAD_DIM], ones], axis=0)
        parts.append((k_head, q_head, v_head))
    units = [(head, j) for j in reversed(range(full_len // block)) for head in range(2)]

    def score(at):
        head, j = units[at]
        k_head, q_head, _ = parts[head]
        top = None
        for i in range(j + 1):
            rows = slice(i * block, (i + 1) * block)
            tile = mm(k_head[rows], q_head[:, j * block : (j + 1) * block])
            if i == j:
                tile = causal_mask(tile, block)
            scores_ref[at % 2, rows, :] = tile
            part = jnp.max(tile.reshape(block // 8, 8, block), axis=0)
            top = part if top is None else jnp.maximum(top, part)
        return jnp.max(top, axis=0, keepdims=True)

    def finish(at, top):
        head, j = units[at]
        v_head = parts[head][2]
        cols = slice(j * block, (j + 1) * block)
        mixed = None
        for i in range(j + 1):
            rows = slice(i * block, (i + 1) * block)
            exped = jnp.exp(scores_ref[at % 2, rows, :] - top).astype(BF16)
            part = mm(v_head[:, rows], exped)
            mixed = part if mixed is None else mixed + part
        total = mixed[HEAD_DIM : HEAD_DIM + 1]
        mixed_ref[head * HEAD_DIM : (head + 1) * HEAD_DIM, cols] = mixed[:HEAD_DIM] / total
        lse_ref[0, head : head + 1, cols] = top + jnp.log(total)

    top = score(0)
    for at in range(len(units)):
        later = score(at + 1) if at + 1 < len(units) else None
        finish(at, top)
        top = later
    a_ref[...] = mixed_ref[...].T.astype(BF16)


def attend_call(core, lengths, qkv, first, count, before):
    rows = qkv.shape[0]
    pairs = HEADS // 2
    before = list(before)
    return pl.pallas_call(
        functools.partial(attend_kernel, first),
        name="attend",
        grid_spec=pltpu.PrefetchScalarGridSpec(
            num_scalar_prefetch=2,
            grid=(count,),
            in_specs=[held_spec()] + [pl.BlockSpec(memory_space=pl.ANY)] * len(before),
            out_specs=[
                pl.BlockSpec((rows, 128), lambda i, c, n: (0, i + first)),
                pl.BlockSpec((1, 8, rows), lambda i, c, n: (i + first, 0, 0)),
            ],
            scratch_shapes=[pltpu.VMEM((128, rows), F32), pltpu.VMEM((2, rows, 256), F32)],
        ),
        out_shape=[
            jax.ShapeDtypeStruct((rows, D), BF16),
            jax.ShapeDtypeStruct((pairs, 8, rows), F32),
        ],
        input_output_aliases={3 + i: i for i in range(len(before))},
        compiler_params=params(12),
        cost_estimate=cost(3e9 * count, 1.2e6 * count, 2 * rows * rows * 0.6 * count),
    )(core, lengths, qkv, *before)


def attend_back_kernel(core_ref, len_ref, q_ref, k_ref, v_ref, a_ref, da_ref, lse_ref, *refs):
    dq_ref, dk_ref, dv_ref, dqt_ref, dk_acc, dv_acc = refs[-6:]
    block = 256
    full_len = q_ref.shape[0]
    length = len_ref[core_ref[0]]
    scale = HEAD_DIM ** (-0.5)
    q_all = q_ref[...] * jnp.asarray(scale, BF16)
    k_all = k_ref[...]
    k_turned = k_all.T
    v_all = v_ref[...]
    da_all = da_ref[...]
    inner = (da_all.astype(F32) * a_ref[...].astype(F32)).T
    q_turned, da_turned = q_all.T, da_all.T
    parts = []
    for head in range(2):
        mine, k_head, q_head = head_parts(length, k_all, q_turned, head)
        zero = jnp.zeros((), BF16)
        q_plain = jnp.where(mine, q_all, zero)
        da_head = jnp.where(mine, da_all, zero)
        row = lax.broadcasted_iota(jnp.int32, (128, 1), 0)
        da_cols = jnp.where((row // HEAD_DIM) == head, da_turned, zero)
        lanes = slice(head * HEAD_DIM, (head + 1) * HEAD_DIM)
        centre = jnp.sum(inner[lanes], axis=0, keepdims=True)
        parts.append((k_head, q_plain, q_head, da_head, da_cols, lanes, centre))
    units = [
        (head, j, i)
        for j in reversed(range(full_len // block))
        for head in range(2)
        for i in range(j + 1)
    ]

    def score(at):
        head, j, i = units[at]
        k_head, _, q_head, _, da_cols, _, _ = parts[head]
        rows, cols = slice(i * block, (i + 1) * block), slice(j * block, (j + 1) * block)
        tile = mm(k_head[rows], q_head[:, cols])
        if i == j:
            tile = causal_mask(tile, block)
        return tile, mm(v_all[rows], da_cols[:, cols])

    seen = set()
    ready = score(0)
    dq_part = None
    for at, (head, j, i) in enumerate(units):
        later = score(at + 1) if at + 1 < len(units) else None
        scores, d_probs = ready
        _, q_plain, _, da_head, _, lanes, centre = parts[head]
        rows, cols = slice(i * block, (i + 1) * block), slice(j * block, (j + 1) * block)
        probs = jnp.exp(scores - lse_ref[0, head : head + 1, cols])
        d_scores = (probs * (d_probs - centre[:, cols])).astype(BF16)
        dv_part = mm(probs.astype(BF16), da_head[cols])
        dk_part = mm(d_scores, q_plain[cols])
        if i in seen:
            dv_acc[rows] += dv_part
            dk_acc[rows] += dk_part
        else:
            seen.add(i)
            dv_acc[rows] = dv_part
            dk_acc[rows] = dk_part
        part = mm(k_turned[lanes, rows], d_scores)
        dq_part = part if i == 0 else dq_part + part
        if i == j:
            dqt_ref[lanes, cols] = dq_part * scale
        ready = later
    dq_ref[...] = dqt_ref[...].T.astype(BF16)
    dk_ref[...] = dk_acc[...].astype(BF16)
    dv_ref[...] = dv_acc[...].astype(BF16)


def attend_back_call(core, lengths, qkv, a, da, lse, start, count, before):
    rows = qkv.shape[0]
    pairs = HEADS // 2
    before = list(before)
    pair_spec = pl.BlockSpec((rows, 128), lambda i, c, n: (0, i + start))
    return pl.pallas_call(
        attend_back_kernel,
        name="attend_back",
        grid_spec=pltpu.PrefetchScalarGridSpec(
            num_scalar_prefetch=2,
            grid=(count,),
            in_specs=[
                pair_spec,
                pl.BlockSpec((rows, 128), lambda i, c, n: (0, i + start + pairs)),
                pl.BlockSpec((rows, 128), lambda i, c, n: (0, i + start + 2 * pairs)),
                pair_spec,
                pair_spec,
                pl.BlockSpec((1, 8, rows), lambda i, c, n: (i + start, 0, 0)),
            ]
            + [pl.BlockSpec(memory_space=pl.ANY)] * len(before),
            out_specs=[pair_spec, pair_spec, pair_spec],
            scratch_shapes=[
                pltpu.VMEM((128, rows), F32),
                pltpu.VMEM((rows, 128), F32),
                pltpu.VMEM((rows, 128), F32),
            ],
        ),
        out_shape=[jax.ShapeDtypeStruct((rows, D), BF16)] * 3,
        input_output_aliases={8 + i: i for i in range(len(before))},
        compiler_params=params(16),
        cost_estimate=cost(6e9 * count, 2e6 * count, 2 * rows * rows * 0.6 * count),
    )(core, lengths, qkv, qkv, qkv, a, da, lse, *before)


def valid_rows(core_ref, len_ref, block):
    pos = pl.program_id(0) * block + lax.broadcasted_iota(jnp.int32, (block, 1), 0)
    return pos < len_ref[core_ref[0]]


def add_row(acc_ref, row, value):
    acc_ref[row : row + 1, :] += jnp.sum(value, axis=0, keepdims=True)


def row_block(core, i, steps):
    half = steps // 2
    return jnp.where(i < half, (1 - core) * half + i, core * half + i - half)


def up_kernel(group, core_ref, len_ref, seat_ref, x_ref, a_ref, og_ref, vec_ref, *refs):
    refs, (mid_ref, h_ref, e_ref, slope_ref, dy_ref, wo_ref, wu_ref, sems) = refs[:-8], refs[-8:]
    block = x_ref.shape[0]

    @pl.when(pl.program_id(0) == 0)
    def _():
        group.start(refs, core_ref, seat_ref, 0, D // 2, wo_ref, sems.at[0])
        group.start(refs, core_ref, seat_ref, D // 2, FF // 2, wu_ref, sems.at[1])
        wait_all(wo_ref, sems.at[0])
        wait_all(wu_ref, sems.at[1])

    valid = valid_rows(core_ref, len_ref, block)
    dy_ref[...] = jnp.where(valid, og_ref[...].astype(F32), 0.0).astype(BF16)
    mid = x_ref[...].astype(F32) + mm(a_ref[...], wo_ref[...]) + vec_ref[4:5, :]
    mid_ref[...] = mid
    normed, _ = norm_parts(mid)
    h = (normed * vec_ref[5:6, :] + vec_ref[6:7, :]).astype(BF16)
    h_ref[...] = h

    def act(j, z):
        cols = slice(j * D, (j + 1) * D)
        z = z + vec_ref[8 + j : 9 + j, :]
        squared = z * z
        turned = jnp.tanh(z * (GELU_ROOT + (GELU_ROOT * GELU_CUBE) * squared))
        half = 0.5 * turned + 0.5
        act = z * half
        e_ref[:, cols] = act.astype(BF16)
        slope = half + act * (1.0 - turned) * (GELU_ROOT + (3.0 * GELU_ROOT * GELU_CUBE) * squared)
        slope_ref[:, cols] = slope.astype(BF16)

    waiting = None
    for j in range(FF // D):
        z = mm(h, wu_ref[:, j * D : (j + 1) * D])
        if waiting is not None:
            act(*waiting)
        waiting = (j, z)
    act(*waiting)


def up_call(core, lengths, seats, x, a, og, vec, group, block=256):
    rows = x.shape[0]
    row_spec = pl.BlockSpec((block, D), lambda i, *s: (i, 0))
    wide_spec = pl.BlockSpec((block, FF), lambda i, *s: (i, 0))
    low, wide = [jax.ShapeDtypeStruct((rows, width), BF16) for width in (D, FF)]
    return pl.pallas_call(
        functools.partial(up_kernel, group),
        name="up",
        grid_spec=pltpu.PrefetchScalarGridSpec(
            num_scalar_prefetch=3,
            grid=(rows // block,),
            in_specs=[row_spec, row_spec, row_spec, whole_spec(vec.shape)] + group.specs(),
            out_specs=[row_spec, row_spec, wide_spec, wide_spec, row_spec],
            scratch_shapes=[
                pltpu.VMEM((D, D), BF16),
                pltpu.VMEM((D, FF), BF16),
                pltpu.SemaphoreType.DMA((2,)),
            ],
        ),
        out_shape=[
            jax.ShapeDtypeStruct((rows, D), F32),
            low,
            wide,
            wide,
            low,
        ],
        compiler_params=params(48),
        cost_estimate=cost(6e9, 30e6, rows * FF),
    )(core, lengths, seats, x, a, og, vec, *group.arrays)


def down_kernel(up_group, down_group, core_ref, len_ref, seat_ref, mid_ref, e_ref, slope_ref, dy_ref, vec_ref, *refs):
    count = len(up_group.arrays)
    up_refs, down_refs = refs[:count], refs[count : count + len(down_group.arrays)]
    (
        theirs_ref, mine_ref, dz_ref, dmb_ref, dm_ref, da_ref, acc_ref, wo_ref, wu_ref, wd_ref, sems,
    ) = refs[-11:]
    block = da_ref.shape[0]
    step, steps = pl.program_id(0), pl.num_programs(0)

    @pl.when(step == 0)
    def _():
        down_group.start(down_refs, core_ref, seat_ref, 0, D // 2, wd_ref, sems.at[2])
        up_group.start(up_refs, core_ref, seat_ref, D // 2, FF // 2, wu_ref, sems.at[1])
        up_group.start(up_refs, core_ref, seat_ref, 0, D // 2, wo_ref, sems.at[0])
        acc_ref[...] = jnp.zeros_like(acc_ref)
        wait_all(wd_ref, sems.at[2])

    mid = mid_ref[...]
    down = vec_ref[7:8, :] + mid + mm(e_ref[...], wd_ref[...])
    pos = row_block(core_ref[0], step, steps) * block + lax.broadcasted_iota(jnp.int32, (block, 1), 0)
    down = jnp.where(pos < len_ref[core_ref[0]], down, 0.0).astype(BF16)

    @pl.when(step < steps // 2)
    def _():
        theirs_ref[...] = down

    @pl.when(step >= steps // 2)
    def _():
        mine_ref[0] = down

    @pl.when(step == 0)
    def _():
        wait_all(wu_ref, sems.at[1])
        wait_all(wo_ref, sems.at[0])

    dy = dy_ref[...]
    add_row(acc_ref, 7, dy.astype(F32))
    dh = None
    waiting = None
    for j in range(FF // D + 1):
        later = None
        if j < FF // D:
            later = (j, mm(dy, wd_ref[j * D : (j + 1) * D, :], NT))
        if waiting is not None:
            at, de = waiting
            cols = slice(at * D, (at + 1) * D)
            dz = (de * slope_ref[:, cols].astype(F32)).astype(BF16)
            dz_ref[:, cols] = dz
            add_row(acc_ref, 8 + at, dz.astype(F32))
            part = mm(dz, wu_ref[:, cols], NT)
            dh = part if dh is None else dh + part
        waiting = later
    normed, scale = norm_parts(mid)
    add_row(acc_ref, 5, dh * normed)
    add_row(acc_ref, 6, dh)
    dm = dy.astype(F32) + norm_back(dh * vec_ref[5:6, :], normed, scale)
    dm_ref[...] = dm
    dm_low = dm.astype(BF16)
    dmb_ref[...] = dm_low
    add_row(acc_ref, 4, dm_low.astype(F32))
    da_ref[...] = mm(dm_low, wo_ref[...], NT).astype(BF16)


def down_call(core, lengths, seats, mid, e, slope, dy, vec, up_group, down_group, block=256):
    rows = mid.shape[0]
    steps = rows // block
    half = steps // 2
    row_spec, wide_spec = [
        pl.BlockSpec((block, width), lambda i, c, *s: (row_block(c[0], i, steps), 0)) for width in (D, FF)
    ]
    return pl.pallas_call(
        functools.partial(down_kernel, up_group, down_group),
        name="down",
        grid_spec=pltpu.PrefetchScalarGridSpec(
            num_scalar_prefetch=3,
            grid=(steps,),
            in_specs=[row_spec, wide_spec, wide_spec, row_spec, whole_spec(vec.shape)]
            + up_group.specs()
            + down_group.specs(),
            out_specs=[
                pl.BlockSpec((block, D), lambda i, *s: (jnp.minimum(i, half - 1), 0)),
                pl.BlockSpec((1, block, D), lambda i, c, *s: (c[0], jnp.maximum(i - half, 0), 0)),
                wide_spec, row_spec, row_spec, row_spec,
                pl.BlockSpec((16, D), lambda i, *s: (0, 0)),
            ],
            scratch_shapes=[
                pltpu.VMEM((D, D), BF16),
                pltpu.VMEM((D, FF), BF16),
                pltpu.VMEM((FF, D), BF16),
                pltpu.SemaphoreType.DMA((3,)),
            ],
        ),
        out_shape=[
            jax.ShapeDtypeStruct((rows // 2, D), BF16),
            jax.ShapeDtypeStruct((2, rows // 2, D), BF16),
            jax.ShapeDtypeStruct((rows, FF), BF16),
            jax.ShapeDtypeStruct((rows, D), BF16),
            jax.ShapeDtypeStruct((rows, D), F32),
            jax.ShapeDtypeStruct((rows, D), BF16),
            jax.ShapeDtypeStruct((16, D), F32),
        ],
        compiler_params=params(48),
        cost_estimate=cost(1.6e10, 35e6),
    )(core, lengths, seats, mid, e, slope, dy, vec, *up_group.arrays, *down_group.arrays)


def pick(values, half, mode):
    if mode == "split":
        width = values.shape[1] // 2
        return [values[:, half * width : (half + 1) * width]]
    return [values[:, at : at + 128] for at in range(half * 128, values.shape[1], 256)]


def weight_grad_kernel(lefts, rights, mode, core_ref, *refs):
    left_refs, right_refs = refs[:lefts], refs[lefts : lefts + sum(rights)]
    own_ref, other_ref = refs[-2:]
    halves = ([], [])
    at = 0
    for left_ref, count in zip(left_refs, rights):
        left = left_ref[...]
        for right_ref in right_refs[at : at + count]:
            whole = mm(left, right_ref[...], TN).astype(BF16)
            for half in range(2):
                halves[half].extend(pick(whole, half, mode))
        at += count
    low, high = [part[0] if len(part) == 1 else jnp.concatenate(part, axis=1) for part in halves]

    @pl.when(core_ref[0] == 0)
    def _():
        own_ref[...] = low
        other_ref[...] = high

    @pl.when(core_ref[0] != 0)
    def _():
        own_ref[...] = high
        other_ref[...] = low


def weight_grad_call(core, products, block, name, mode="split", cols=None):
    rows, height = products[0][0].shape
    lefts = [left for left, _ in products]
    rights = [right for _, group in products for right in group]
    widths = [right.shape[1] if cols is None else cols[0] for right in rights]
    width = sum(widths)
    seat = 0 if cols is None else cols[1]
    return pl.pallas_call(
        functools.partial(weight_grad_kernel, len(lefts), [len(group) for _, group in products], mode),
        name=name,
        grid_spec=pltpu.PrefetchScalarGridSpec(
            num_scalar_prefetch=1,
            grid=(height // block,),
            in_specs=[pl.BlockSpec((rows, block), lambda i, c: (0, i))] * len(lefts)
            + [
                pl.BlockSpec((rows, w), lambda i, c: (0, seat), pipeline_mode=pl.Buffered(1)) for w in widths
            ],
            out_specs=[pl.BlockSpec((block, width // 2), lambda i, c: (i, 0))] * 2,
        ),
        out_shape=[jax.ShapeDtypeStruct((height, width // 2), BF16)] * 2,
        compiler_params=params(16 if mode == "turns" else 48),
        cost_estimate=cost(2 * rows * height * width, rows * (height + width) * 2 + height * width * 2),
    )(core, *lefts, *rights)


def last_kernel(
    core_ref, x_ref, dm_ref, dq_ref, dk_ref, dv_ref, w_ref, vec_ref, before_ref, theirs_ref, mine_ref, acc_ref
):
    step, steps = pl.program_id(0), pl.num_programs(0)

    @pl.when(step == 0)
    def _():
        acc_ref[...] = before_ref[...]

    subs = sub_blocks(x_ref.shape[0])

    def product(rows):
        return (
            mm(dq_ref[rows, :], w_ref[:D])
            + mm(dk_ref[rows, :], w_ref[D : 2 * D])
            + mm(dv_ref[rows, :], w_ref[2 * D :])
        )

    grads = []
    dh = product(subs[0])
    add_row(acc_ref, 2, dq_ref[...].astype(F32))
    add_row(acc_ref, 3, dv_ref[...].astype(F32))
    for at, rows in enumerate(subs):
        later = product(subs[at + 1]) if at + 1 < len(subs) else None
        normed, scale = norm_parts(x_ref[rows, :].astype(F32))
        add_row(acc_ref, 0, dh * normed)
        add_row(acc_ref, 1, dh)
        grads.append(dm_ref[rows, :] + norm_back(dh * vec_ref[0:1, :], normed, scale))
        dh = later

    @pl.when(step < steps // 2)
    def _():
        for rows, grad in zip(subs, grads):
            theirs_ref[rows, :] = grad

    @pl.when(step >= steps // 2)
    def _():
        for rows, grad in zip(subs, grads):
            mine_ref[0, rows, :] = grad


def last_call(core, x, dm, dq, dk, dv, w, vec, before, block=256):
    rows = x.shape[0]
    steps = rows // block
    half = steps // 2
    row_spec = pl.BlockSpec((block, D), lambda i, c, *s: (row_block(c[0], i, steps), 0))
    return pl.pallas_call(
        last_kernel,
        name="last",
        grid_spec=pltpu.PrefetchScalarGridSpec(
            num_scalar_prefetch=1,
            grid=(steps,),
            in_specs=[row_spec] * 5 + [whole_spec(part.shape) for part in (w, vec, before)],
            out_specs=[
                pl.BlockSpec((block, D), lambda i, *s: (jnp.minimum(i, half - 1), 0)),
                pl.BlockSpec((1, block, D), lambda i, c, *s: (c[0], jnp.maximum(i - half, 0), 0)),
                pl.BlockSpec((16, D), lambda i, *s: (0, 0)),
            ],
        ),
        out_shape=[
            jax.ShapeDtypeStruct((rows // 2, D), F32),
            jax.ShapeDtypeStruct((2, rows // 2, D), F32),
            jax.ShapeDtypeStruct((16, D), F32),
        ],
        compiler_params=params(12),
        cost_estimate=cost(rows * 6 * D * D, 16e6),
    )(core, x, dm, dq, dk, dv, w, vec, before)


def adam_kernel(plans, sources, core_ref, *refs):
    halves = [refs[2 * i : 2 * i + 2] for i in range(sources)]
    count = len(plans)
    states = refs[2 * sources : 2 * sources + 3 * count]
    outs = refs[2 * sources + 3 * count : 2 * sources + 6 * count]
    grads = refs[2 * sources + 6 * count :]
    for core in range(2):

        @pl.when(core_ref[0] == core)
        def _():
            for (_, _, moves), grad_ref in zip(plans, grads):
                for source, start, width, place0, place1 in moves:
                    for half, place in ((0, place0), (1, place1)):
                        ref = halves[source][0 if half == core else 1]
                        grad_ref[:, place : place + width] = ref[:, start : start + width].astype(F32)

    for i, (rate, decay, _) in enumerate(plans):
        weight, first, second = states[3 * i : 3 * i + 3]
        new = adamw(weight[...], grads[i][...], first[...], second[...], rate, decay)
        for out, value in zip(outs[3 * i : 3 * i + 3], new):
            out[...] = value


def adam_call(core, halves, states, plans):
    flat = [part for pair in halves for part in pair]
    held = [part for state in states for part in state]
    spec = pl.BlockSpec(memory_space=pltpu.VMEM)
    news = pl.pallas_call(
        functools.partial(adam_kernel, plans, len(halves)),
        name="adam",
        in_specs=[pl.BlockSpec(memory_space=pltpu.SMEM)] + [spec] * (len(flat) + len(held)),
        out_specs=[spec] * len(held),
        out_shape=[jax.ShapeDtypeStruct(part.shape, F32) for part in held],
        scratch_shapes=[pltpu.VMEM(state[0].shape, F32) for state in states],
        compiler_params=params(12),
        cost_estimate=cost(1e6, 24 * sum(state[0].size for state in states)),
    )(core, *flat, *held)
    return [news[3 * i : 3 * i + 3] for i in range(len(states))]


def after(value, *others):
    if not others:
        return value
    return lax.optimization_barrier((value,) + others)[0]


def cut(array, axis, index, size=1):
    starts = [jnp.uint32(0)] * array.ndim
    sizes = list(array.shape)
    starts[axis], sizes[axis] = index, size
    return lax.dynamic_slice(array, starts, sizes)


class Grid:
    def __init__(self, chips):
        log = chips.bit_length() - 1
        side = 1 << (log // 3)
        if side * side * (chips // (side * side)) != chips:
            side = 1
        self.chips = chips
        self.n = side
        self.nz = chips // (side * side)
        self.core = lax.axis_index("seq")
        self.chip = lax.axis_index("dp")
        self.x = self.chip % side
        self.y = self.chip // side % side
        self.z = self.chip // (side * side)

    def pin(self, value):
        n, core = self.n, self.core
        first, second = self.coords(core)
        places = {
            "core": core,
            "other": 1 - core,
            "chip": self.chip,
            "seats": self.seats(True),
            "q_seats": self.seats(False),
        }
        for s in range(n):
            for t in range(n):
                places["plane", s, t] = self.plane((first + s) % n, (second + t) % n, core)
        for at in range(self.nz):
            places["z", at] = self.z ^ at
        names = list(places)
        held = lax.optimization_barrier((value, *[places[name].astype(jnp.uint32) for name in names]))
        self.places = dict(zip(names, held[1:]))
        return held[0]

    def plane(self, first, second, core):
        return jnp.where(core == 0, second * self.n + first, first * self.n + second)

    def coords(self, core):
        return jnp.where(core == 0, self.x, self.y), jnp.where(core == 0, self.y, self.x)

    def permute(self, value, axis, shift=0):
        pairs = []
        for chip in range(self.chips):
            for core in range(2):
                x, y, z = chip % self.n, chip // self.n % self.n, chip // (self.n * self.n)
                to_core = core
                if axis == "z":
                    z = (z + shift) % self.nz
                elif axis == "zx":
                    z = z ^ shift
                elif axis == "core":
                    to_core = 1 - core
                elif (axis == "first") == (core == 0):
                    x = (x + shift) % self.n
                else:
                    y = (y + shift) % self.n
                pairs.append((chip * 2 + core, ((z * self.n + y) * self.n + x) * 2 + to_core))
        return lax.ppermute(value, ("dp", "seq"), pairs)

    def swap(self, value):
        return self.permute(value, "core")

    def join(self, own, other, axis):
        return jnp.where(
            self.places["core"] == 0,
            jnp.concatenate([own, other], axis),
            jnp.concatenate([other, own], axis),
        )

    def seats(self, halving):
        found = []
        for half in range(2):
            core = self.core if half == 0 else 1 - self.core
            first, second = self.coords(core)
            for s2 in range(self.n):
                for s1 in range(self.n):
                    flat = self.plane((first - s1) % self.n, (second - s2) % self.n, core)
                    for sz in range(self.nz):
                        z = self.z ^ sz if halving else (self.z - sz) % self.nz
                        found.append(z * self.n * self.n + flat)
        return jnp.stack(found).astype(jnp.int32)

    def total_small(self, value, *untils):
        steps = [("core", 0), ("first", 1), ("second", 1)] if self.n == 2 else [("core", 0)]
        if self.n != 2:
            for axis in ("first", "second"):
                value = value + sum(self.permute(value, axis, s) for s in range(1, self.n))
        bit = 1
        while bit < self.nz:
            steps.append(("zx", bit))
            bit *= 2
        for at, (axis, shift) in enumerate(steps):
            until = untils[at] if at < len(untils) else ()
            value = value + after(self.permute(value, axis, shift), *until)
        return value

    def gather_z(self, block, *until):
        return jnp.stack([block] + [after(self.permute(block, "z", s), *until) for s in range(1, self.nz)])

    def gather_bit(self, held, bit, *until):
        return jnp.concatenate([held, after(self.permute(held, "zx", bit), *until)])

    def gather_first(self, column, *until):
        return jnp.stack([column] + [after(self.permute(column, "first", s), *until) for s in range(1, self.n)])

    def gather_second(self, line, *until):
        return [after(self.permute(line, "second", s), *until) for s in range(1, self.n)]

    def scatter_first(self, own, pair, *until):
        rows, cols = own.shape[0] // self.chips, own.shape[1]
        n = self.n

        def seat(s1, s2):
            own_part, pair_part = [
                cut(part.reshape(self.nz, n * n, rows, cols), 1, self.places["plane", s1, s2]).astype(F32)
                for part in (own, pair)
            ]
            return own_part + pair_part

        kept = [seat(0, t) for t in range(n)]
        for s in range(1, n):
            send = jnp.stack([seat(s, t).astype(BF16) for t in range(n)])
            got = after(self.permute(send, "first", s), *until)
            kept = [kept[t] + got[t].astype(F32) for t in range(n)]
        return kept[0], [part.astype(BF16) for part in kept[1:]]

    def scatter_second(self, kept, *until):
        mine, rest = kept
        got = [after(self.permute(rest[s - 1], "second", s), *until) for s in range(1, self.n)]
        for part in got:
            mine = mine + part.astype(F32)
        return mine.reshape((self.nz,) + mine.shape[2:]), got

    def order_z(self, mine):
        return [cut(mine, 0, self.places["z", at])[0] for at in range(self.nz)]

    def scatter_bit(self, parts, *until):
        half = len(parts) // 2
        send = parts[half] if half == 1 else jnp.stack([part.astype(BF16) for part in parts[half:]])
        got = after(self.permute(send.astype(BF16), "zx", half), *until)
        if half == 1:
            return [parts[0] + got.astype(F32)], got
        return [part + got[at].astype(F32) for at, part in enumerate(parts[:half])], got

    def scatter_z(self, parts, *until):
        while len(parts) > 1:
            parts, _ = self.scatter_bit(parts, *until)
        return parts[0]


def adamw(weight, gradient, first_moment, second_moment, step_rate, weight_decay):
    first_moment = BETA_ONE * first_moment + (1.0 - BETA_ONE) * gradient
    second_moment = BETA_TWO * second_moment + (1.0 - BETA_TWO) * gradient * gradient
    first_fix = 1.0 - BETA_ONE**STEP
    second_fix = 1.0 - BETA_TWO**STEP
    direction = first_moment / first_fix / (jnp.sqrt(second_moment / second_fix) + EPS_ADAM)
    return (weight - step_rate * (direction + weight_decay * weight), first_moment, second_moment)


def local(
    block_in, lengths, out_grad, w_qkv, w_out, w_up, w_down, vectors,
    first_qkv, first_out, first_up, first_down, first_vectors,
    second_qkv, second_out, second_up, second_down, second_vectors,
):
    grid = Grid(lax.axis_size("dp"))
    core = grid.core
    w_qkv_first = grid.pin(w_qkv)
    places = grid.places
    core_arr = places["core"].reshape(1).astype(jnp.int32)
    half_len = block_in.shape[1]
    vec_count, vec_here = vectors.shape

    def own_slot(halves):
        mine, theirs = [cut(halves, 0, places[name])[0] for name in ("core", "other")]
        return grid.join(mine, grid.swap(theirs), 0)

    def both_slots(mine, got):
        zero = jnp.uint32(0)
        return lax.dynamic_update_slice(mine, got[None], (places["other"], zero, zero))

    def half_of(shard):
        width = shard.shape[1] // 2
        return jnp.where(places["core"] == 0, shard[:, :width], shard[:, width:]).astype(BF16)

    seats, q_seats = [places[name].astype(jnp.int32) for name in ("seats", "q_seats")]

    turned = jnp.pad(vectors.T.astype(BF16), ((0, 0), (0, 128 - vec_count)))
    q_block = jnp.concatenate([half_of(w_qkv_first), turned], axis=1)
    u_block = jnp.concatenate([half_of(w_out), half_of(w_up)], axis=1)
    d_block = half_of(w_down)
    q_col = grid.gather_z(q_block)
    x = own_slot(block_in)
    bits = [1 << at for at in range((grid.nz - 1).bit_length())]
    u_col, d_col = u_block[None], d_block[None]
    for bit in bits[:-1]:
        u_col = grid.gather_bit(u_col, bit)
        d_col = grid.gather_bit(d_col, bit)
    q_line = after(grid.gather_first(q_col, x), u_col, d_col)
    q_rest = grid.gather_second(q_line)
    u_col = grid.gather_bit(after(u_col, q_line), bits[-1])
    q_line_swap = grid.swap(q_line)
    q_rest_swap = [grid.swap(after(part, u_col)) for part in q_rest]
    q_group = finish_group(grid, q_seats, [q_line] + q_rest, [q_line_swap] + q_rest_swap)

    h1, qkv, vec, w_back = qkv_call(core_arr, q_seats, x, q_group)
    u_line = grid.gather_first(u_col, qkv)
    d_col = grid.gather_bit(after(d_col, u_col), bits[-1], qkv)
    og = own_slot(after(out_grad, qkv))
    att = attend_call(core_arr, lengths, after(qkv, u_line, d_col), 0, 4, ())
    u_line_swap = after(grid.swap(u_line), *att)
    u_rest = grid.gather_second(u_line, *att)
    d_col = after(d_col, *u_rest)
    a, lse = attend_call(core_arr, lengths, after(qkv, d_col), 4, 2, att)
    u_rest_swap = [after(grid.swap(part), a) for part in u_rest]
    d_line = grid.gather_first(d_col, a)
    u_group = finish_group(grid, seats, [u_line] + u_rest, [u_line_swap] + u_rest_swap)
    mid, h2, e, slope, dy = up_call(core_arr, lengths, seats, x, after(a, d_line), og, vec, u_group)
    d_line_swap = after(grid.swap(d_line), mid)
    d_rest = grid.gather_second(d_line, mid)
    d_own, d_other = weight_grad_call(core_arr, [(after(e, *d_rest), [dy])], 512, "grad_down")
    d_rest_swap = [after(grid.swap(part), d_own) for part in d_rest]
    d_group = finish_group(grid, seats, [d_line] + d_rest, [d_line_swap] + d_rest_swap)
    out_theirs, out_mine, dz, dmb, dm, da, acc_mid = down_call(
        core_arr, lengths, seats, mid, e, slope, dy, vec, u_group, d_group
    )

    d_pair = after(grid.swap(d_other), dz)
    u_own, u_other = weight_grad_call(
        core_arr, [(a, [dmb]), (h2, [after(dz, d_pair)])], 384, "grad_up"
    )
    d_kept = grid.scatter_first(d_own, d_pair, u_own)

    def back_call(start, count, before, *needs):
        return attend_back_call(core_arr, lengths, qkv, a, after(da, *needs), lse, start, count, before)

    back = back_call(0, 2, (), u_own, *d_kept[1])
    d_sum, d_here = grid.scatter_second(d_kept, *back)
    u_pair = after(grid.swap(u_other), *back)
    back = back_call(2, 4, back, u_pair, *d_here)
    d_parts, d_got = grid.scatter_bit(grid.order_z(d_sum), *back)
    u_kept = grid.scatter_first(u_own, u_pair, *back)
    dq, dk, dv = back
    block_out = both_slots(out_mine, after(grid.swap(after(out_theirs, back[0])), dq))
    q_own, q_other = weight_grad_call(
        core_arr, [(h1, [after(dq, d_got, *u_kept[1]), dk, dv])], 384, "grad_qkv", "turns"
    )
    u_sum, u_here = grid.scatter_second(u_kept, q_own)
    q_pair = grid.swap(after(q_other, *u_here))
    in_theirs, in_mine, acc = last_call(
        core_arr, x, dm, after(dq, q_own, q_pair), dk, dv, w_back, vec, acc_mid
    )
    d_mine = grid.scatter_z(d_parts, in_theirs)
    d_other_mine = grid.swap(d_mine)
    q_kept = grid.scatter_first(q_own, q_pair, in_theirs)
    u_parts, u_got = grid.scatter_bit(grid.order_z(u_sum), *q_kept[1])
    q_sum, q_here = grid.scatter_second(q_kept, u_got)
    down_new, = adam_call(
        core_arr,
        [(d_mine, d_other_mine)],
        [(after(w_down, *q_kept[1]), first_down, second_down)],
        [(FF ** (-0.5), MATRIX_DECAY, [(0, 0, D // 2, 0, D // 2)])],
    )
    in_got = grid.swap(after(in_theirs, *q_kept[1]))
    u_mine = grid.scatter_z([after(part, *q_here) for part in u_parts])
    u_other_mine = grid.swap(u_mine)
    in_grad = both_slots(in_mine, after(in_got, *q_here))
    q_parts, q_got = grid.scatter_bit(grid.order_z(q_sum), in_grad)
    q_gots = [(q_got,)]
    while len(q_parts) > 1:
        q_parts, q_got = grid.scatter_bit(q_parts)
        q_gots.append((q_got,))
    q_mine = q_parts[0]
    q_other_mine = grid.swap(q_mine)
    vec_total = grid.total_small(acc, (), q_kept[1], q_here, *q_gots)

    half, wide = D // 2, FF // 2
    out_new, up_new = adam_call(
        core_arr,
        [(u_mine, u_other_mine)],
        [(after(w_out, in_grad), first_out, second_out), (w_up, first_up, second_up)],
        [
            ((D // 64) ** (-0.5), MATRIX_DECAY, [(0, 0, half, 0, half)]),
            (D ** (-0.5), MATRIX_DECAY, [(0, half, wide, 0, wide)]),
        ],
    )
    moves = []
    for turn in range(3 * D // 256):
        moves.append((0, turn * 128, 128, turn * 256, turn * 256 + 128))
    qkv_new, = adam_call(
        core_arr,
        [(q_mine, q_other_mine)],
        [(w_qkv, first_qkv, second_qkv)],
        [(D ** (-0.5), MATRIX_DECAY, moves)],
    )
    vec_grad = cut(vec_total[:vec_count].reshape(vec_count, -1, vec_here), 1, places["chip"])[:, 0]
    vec_new = adamw(vectors, vec_grad, first_vectors, second_vectors, VECTOR_RATE, 0.0)
    news = [qkv_new, out_new, up_new, down_new, vec_new]
    return (block_out, in_grad) + tuple(new[kind] for kind in range(3) for new in news)


def finish_group(grid, seats, own, other):
    rows, cols = own[0].shape[-2:]
    if rows % 16 == 0:
        return Pieces(own + other, rows)
    found = []
    for half, parts in enumerate((own, other)):
        here = seats[half * grid.chips : (half + 1) * grid.chips]
        order = jnp.zeros((grid.chips,), jnp.int32).at[here].set(jnp.arange(grid.chips, dtype=jnp.int32))
        blocks = jnp.concatenate(parts).reshape(grid.chips, rows, cols)
        found.append(jnp.take(blocks, order, axis=0).reshape(1, 1, grid.chips * rows, cols))
    return Pieces(found, grid.chips * rows, True)


def solution(mesh):
    weight = P("dp", None)
    vector = P(None, "dp")
    state = (weight, weight, weight, weight, vector)
    tokens = P("dp", "seq", None)
    return jax.shard_map(
        local,
        mesh=mesh,
        in_specs=(tokens, P("dp"), tokens) + state * 3,
        out_specs=(tokens, tokens) + state * 3,
        check_vma=False,
    )
```

```python
import functools

import jax
import jax.numpy as jnp
from jax import lax
from jax.experimental import pallas as pl
from jax.experimental.pallas import tpu as pltpu
from jax.sharding import PartitionSpec as P

D = 768
HEADS = 12
HEAD_DIM = 64
FF = 3072
STEP = 10

EPS_NORM = 1e-05
EPS_ADAM = 1e-08
BETA_ONE = 0.5
BETA_TWO = 0.5
MATRIX_DECAY = 0.1
VECTOR_RATE = 0.1
NEG_FILL = -1e30
GELU_ROOT = 0.7978845608028654
GELU_CUBE = 0.044715
QKV_HALF = 3 * D // 2

F32 = jnp.float32
BF16 = jnp.bfloat16

NN = (((1,), (0,)), ((), ()))
NT = (((1,), (1,)), ((), ()))
TN = (((0,), (0,)), ((), ()))


def mm(left, right, dims=NN):
    return lax.dot_general(left, right, dims, preferred_element_type=F32)


def cost(flops, nbytes, trans=0):
    return pl.CostEstimate(flops=int(4 * flops), bytes_accessed=int(4 * nbytes), transcendentals=int(trans))


def params(mib=60):
    return pltpu.CompilerParams(vmem_limit_bytes=mib * 1024 * 1024)


def held_spec():
    return pl.BlockSpec(memory_space=pltpu.VMEM)


def at_rows(block):
    return pl.ds(pl.multiple_of(pl.program_id(0) * block, block), block)


def whole_spec(shape):
    return pl.BlockSpec(shape, lambda *idx: (0,) * len(shape), pipeline_mode=pl.Buffered(1))


class Pieces:
    def __init__(self, arrays, rows, ordered=False):
        self.arrays = arrays
        self.rows = rows
        self.ordered = ordered
        self.halves = 2
        self.count = len(arrays) // self.halves
        self.lines, self.depth = arrays[0].shape[:2]

    def specs(self):
        return [pl.BlockSpec(memory_space=pltpu.HBM)] * len(self.arrays)

    def row(self, seat_ref, at):
        return 0 if self.ordered else pl.multiple_of(seat_ref[at] * self.rows, 16)

    def start(self, refs, core_ref, seat_ref, start_col, width, target, sem):
        core = core_ref[0]
        at = 0
        for half in range(self.halves):
            where = core if half == 0 else 1 - core
            for s2 in range(self.count):
                ref = refs[half * self.count + s2]
                for s1 in range(self.lines):
                    for sz in range(self.depth):
                        row = self.row(seat_ref, at)
                        at += 1
                        col = pl.multiple_of(where * width, 128)
                        pltpu.make_async_copy(
                            ref.at[s1, sz, :, pl.ds(start_col, width)],
                            target.at[pl.ds(row, self.rows), pl.ds(col, width)],
                            sem,
                        ).start()

    def start_once(self, refs, seat_ref, start_col, width, target, sem):
        at = 0
        for s2 in range(self.count):
            for s1 in range(self.lines):
                for sz in range(self.depth):
                    row = self.row(seat_ref, at)
                    at += 1
                    pltpu.make_async_copy(
                        refs[s2].at[s1, sz, :, pl.ds(start_col, width)],
                        target.at[pl.ds(row, self.rows), :],
                        sem,
                    ).start()


def wait_all(target, sem):
    pltpu.make_async_copy(target, target, sem).wait()


def norm_parts(rows):
    mean = jnp.mean(rows, axis=-1, keepdims=True)
    centred = rows - mean
    variance = jnp.mean(centred * centred, axis=-1, keepdims=True)
    scale = lax.rsqrt(variance + EPS_NORM)
    return centred * scale, scale


def norm_back(d_normed, normed, scale):
    first = jnp.mean(d_normed, axis=-1, keepdims=True)
    second = jnp.mean(d_normed * normed, axis=-1, keepdims=True)
    return scale * (d_normed - first - normed * second)


def qkv_kernel(group, core_ref, seat_ref, x_ref, *refs):
    refs, (h_ref, qkv_ref, vec_ref, back_ref, w_ref, turned_ref, sems) = refs[:-7], refs[-7:]

    @pl.when(pl.program_id(0) == 0)
    def _():
        group.start(refs, core_ref, seat_ref, 0, QKV_HALF, w_ref, sems.at[0])
        group.start_once(refs, seat_ref, QKV_HALF, 128, turned_ref, sems.at[1])
        wait_all(turned_ref, sems.at[1])
        vec_ref[...] = turned_ref[...].astype(F32).T[:16]
        wait_all(w_ref, sems.at[0])

    def norm(rows):
        normed, _ = norm_parts(x_ref[rows, :].astype(F32))
        h = (normed * vec_ref[0:1, :] + vec_ref[1:2, :]).astype(BF16)
        h_ref[rows, :] = h
        return h

    block = x_ref.shape[0]
    h = norm(slice(0, block))
    for part, bias in enumerate((2, None, 3)):
        cols = slice(part * D, (part + 1) * D)
        product = mm(h, w_ref[:, cols])
        if bias is not None:
            product = product + vec_ref[bias : bias + 1, :]
        qkv_ref[:, cols] = product.astype(BF16)

    @pl.when(pl.program_id(0) < 3)
    def _():
        back_ref[...] = w_ref[:, at_rows(D)].T


def sub_blocks(rows):
    return [slice(at, at + 256) for at in range(0, rows, 256)]


def qkv_call(core, seats, x, group, block=256):
    rows = x.shape[0]
    return pl.pallas_call(
        functools.partial(qkv_kernel, group),
        name="qkv",
        grid_spec=pltpu.PrefetchScalarGridSpec(
            num_scalar_prefetch=2,
            grid=(rows // block,),
            in_specs=[pl.BlockSpec((block, D), lambda i, *s: (i, 0))] + group.specs(),
            out_specs=[
                pl.BlockSpec((block, D), lambda i, *s: (i, 0)),
                pl.BlockSpec((block, 3 * D), lambda i, *s: (i, 0)),
                pl.BlockSpec((16, D), lambda i, *s: (0, 0)),
                pl.BlockSpec((D, D), lambda i, *s: (jnp.minimum(i, 2), 0)),
            ],
            scratch_shapes=[
                pltpu.VMEM((D, 3 * D), BF16),
                pltpu.VMEM((D, 128), BF16),
                pltpu.SemaphoreType.DMA((2,)),
            ],
        ),
        out_shape=[
            jax.ShapeDtypeStruct((rows, D), BF16),
            jax.ShapeDtypeStruct((rows, 3 * D), BF16),
            jax.ShapeDtypeStruct((16, D), F32),
            jax.ShapeDtypeStruct((3 * D, D), BF16),
        ],
        compiler_params=params(12),
        cost_estimate=cost(2 * rows * D * 3 * D, 10e6),
    )(core, seats, x, *group.arrays)


def head_parts(length, k_all, q_turned, head):
    full_len = k_all.shape[0]
    lane = lax.broadcasted_iota(jnp.int32, (1, 128), 1)
    row = lax.broadcasted_iota(jnp.int32, (128, 1), 0)
    zero, one = jnp.zeros((), BF16), jnp.ones((), BF16)
    mine = (lane // HEAD_DIM) == head
    spare = HEAD_DIM * (1 - head)
    pos = lax.broadcasted_iota(jnp.int32, (full_len, 128), 0)
    fill = jnp.where(pos < length, 0.0, NEG_FILL).astype(BF16)
    k_head = jnp.where(mine, k_all, jnp.where(lane == spare, fill, zero))
    q_head = jnp.where((row // HEAD_DIM) == head, q_turned, jnp.where(row == spare, one, zero))
    return mine, k_head, q_head


def causal_mask(scores, block):
    full = scores.shape[0]
    key_pos = lax.broadcasted_iota(jnp.int32, (block, block), 0)
    query_pos = lax.broadcasted_iota(jnp.int32, (block, block), 1)
    last = jnp.where(key_pos <= query_pos, scores[full - block :], NEG_FILL)
    if full == block:
        return last
    return jnp.concatenate([scores[: full - block], last], axis=0)


def attend_kernel(start, core_ref, len_ref, qkv_ref, *refs):
    a_ref, lse_ref, mixed_ref, scores_ref = refs[-4:]
    block = 256
    full_len = qkv_ref.shape[0]
    length = len_ref[core_ref[0]]
    q_all, k_all, v_all = [
        qkv_ref[:, pl.ds(pl.multiple_of((pl.program_id(0) + start) * 128 + part * D, 128), 128)] for part in range(3)
    ]
    q_all = q_all * jnp.asarray(HEAD_DIM ** (-0.5), BF16)
    v_turned = v_all.T
    q_turned = q_all.T
    ones = jnp.ones((16, full_len), BF16)
    parts = []
    for head in range(2):
        _, k_head, q_head = head_parts(length, k_all, q_turned, head)
        v_head = jnp.concatenate([v_turned[head * HEAD_DIM : (head + 1) * HEAD_DIM], ones], axis=0)
        parts.append((k_head, q_head, v_head))
    units = [(head, j) for j in reversed(range(full_len // block)) for head in range(2)]

    def score(at):
        head, j = units[at]
        k_head, q_head, _ = parts[head]
        top = None
        for i in range(j + 1):
            rows = slice(i * block, (i + 1) * block)
            tile = mm(k_head[rows], q_head[:, j * block : (j + 1) * block])
            if i == j:
                tile = causal_mask(tile, block)
            scores_ref[at % 2, rows, :] = tile
            part = jnp.max(tile.reshape(block // 8, 8, block), axis=0)
            top = part if top is None else jnp.maximum(top, part)
        return jnp.max(top, axis=0, keepdims=True)

    def finish(at, top):
        head, j = units[at]
        v_head = parts[head][2]
        cols = slice(j * block, (j + 1) * block)
        mixed = None
        for i in range(j + 1):
            rows = slice(i * block, (i + 1) * block)
            exped = jnp.exp(scores_ref[at % 2, rows, :] - top).astype(BF16)
            part = mm(v_head[:, rows], exped)
            mixed = part if mixed is None else mixed + part
        total = mixed[HEAD_DIM : HEAD_DIM + 1]
        mixed_ref[head * HEAD_DIM : (head + 1) * HEAD_DIM, cols] = mixed[:HEAD_DIM] / total
        lse_ref[0, head : head + 1, cols] = top + jnp.log(total)

    top = score(0)
    for at in range(len(units)):
        later = score(at + 1) if at + 1 < len(units) else None
        finish(at, top)
        top = later
    a_ref[...] = mixed_ref[...].T.astype(BF16)


def attend_call(core, lengths, qkv, first, count, before):
    rows = qkv.shape[0]
    pairs = HEADS // 2
    before = list(before)
    return pl.pallas_call(
        functools.partial(attend_kernel, first),
        name="attend",
        grid_spec=pltpu.PrefetchScalarGridSpec(
            num_scalar_prefetch=2,
            grid=(count,),
            in_specs=[held_spec()] + [pl.BlockSpec(memory_space=pl.ANY)] * len(before),
            out_specs=[
                pl.BlockSpec((rows, 128), lambda i, c, n: (0, i + first)),
                pl.BlockSpec((1, 8, rows), lambda i, c, n: (i + first, 0, 0)),
            ],
            scratch_shapes=[pltpu.VMEM((128, rows), F32), pltpu.VMEM((2, rows, 256), F32)],
        ),
        out_shape=[
            jax.ShapeDtypeStruct((rows, D), BF16),
            jax.ShapeDtypeStruct((pairs, 8, rows), F32),
        ],
        input_output_aliases={3 + i: i for i in range(len(before))},
        compiler_params=params(12),
        cost_estimate=cost(3e9 * count, 1.2e6 * count, 2 * rows * rows * 0.6 * count),
    )(core, lengths, qkv, *before)


def attend_back_kernel(core_ref, len_ref, q_ref, k_ref, v_ref, a_ref, da_ref, lse_ref, *refs):
    dq_ref, dk_ref, dv_ref, dqt_ref, dk_acc, dv_acc = refs[-6:]
    block = 256
    full_len = q_ref.shape[0]
    length = len_ref[core_ref[0]]
    scale = HEAD_DIM ** (-0.5)
    q_all = q_ref[...] * jnp.asarray(scale, BF16)
    k_all = k_ref[...]
    k_turned = k_all.T
    v_all = v_ref[...]
    da_all = da_ref[...]
    inner = (da_all.astype(F32) * a_ref[...].astype(F32)).T
    q_turned, da_turned = q_all.T, da_all.T
    parts = []
    for head in range(2):
        mine, k_head, q_head = head_parts(length, k_all, q_turned, head)
        zero = jnp.zeros((), BF16)
        q_plain = jnp.where(mine, q_all, zero)
        da_head = jnp.where(mine, da_all, zero)
        row = lax.broadcasted_iota(jnp.int32, (128, 1), 0)
        da_cols = jnp.where((row // HEAD_DIM) == head, da_turned, zero)
        lanes = slice(head * HEAD_DIM, (head + 1) * HEAD_DIM)
        centre = jnp.sum(inner[lanes], axis=0, keepdims=True)
        parts.append((k_head, q_plain, q_head, da_head, da_cols, lanes, centre))
    units = [
        (head, j, i)
        for j in reversed(range(full_len // block))
        for head in range(2)
        for i in range(j + 1)
    ]

    def score(at):
        head, j, i = units[at]
        k_head, _, q_head, _, da_cols, _, _ = parts[head]
        rows, cols = slice(i * block, (i + 1) * block), slice(j * block, (j + 1) * block)
        tile = mm(k_head[rows], q_head[:, cols])
        if i == j:
            tile = causal_mask(tile, block)
        return tile, mm(v_all[rows], da_cols[:, cols])

    seen = set()
    ready = score(0)
    dq_part = None
    for at, (head, j, i) in enumerate(units):
        later = score(at + 1) if at + 1 < len(units) else None
        scores, d_probs = ready
        _, q_plain, _, da_head, _, lanes, centre = parts[head]
        rows, cols = slice(i * block, (i + 1) * block), slice(j * block, (j + 1) * block)
        probs = jnp.exp(scores - lse_ref[0, head : head + 1, cols])
        d_scores = (probs * (d_probs - centre[:, cols])).astype(BF16)
        dv_part = mm(probs.astype(BF16), da_head[cols])
        dk_part = mm(d_scores, q_plain[cols])
        if i in seen:
            dv_acc[rows] += dv_part
            dk_acc[rows] += dk_part
        else:
            seen.add(i)
            dv_acc[rows] = dv_part
            dk_acc[rows] = dk_part
        part = mm(k_turned[lanes, rows], d_scores)
        dq_part = part if i == 0 else dq_part + part
        if i == j:
            dqt_ref[lanes, cols] = dq_part * scale
        ready = later
    dq_ref[...] = dqt_ref[...].T.astype(BF16)
    dk_ref[...] = dk_acc[...].astype(BF16)
    dv_ref[...] = dv_acc[...].astype(BF16)


def attend_back_call(core, lengths, qkv, a, da, lse, start, count, before):
    rows = qkv.shape[0]
    pairs = HEADS // 2
    before = list(before)
    pair_spec = pl.BlockSpec((rows, 128), lambda i, c, n: (0, i + start))
    return pl.pallas_call(
        attend_back_kernel,
        name="attend_back",
        grid_spec=pltpu.PrefetchScalarGridSpec(
            num_scalar_prefetch=2,
            grid=(count,),
            in_specs=[
                pair_spec,
                pl.BlockSpec((rows, 128), lambda i, c, n: (0, i + start + pairs)),
                pl.BlockSpec((rows, 128), lambda i, c, n: (0, i + start + 2 * pairs)),
                pair_spec,
                pair_spec,
                pl.BlockSpec((1, 8, rows), lambda i, c, n: (i + start, 0, 0)),
            ]
            + [pl.BlockSpec(memory_space=pl.ANY)] * len(before),
            out_specs=[pair_spec, pair_spec, pair_spec],
            scratch_shapes=[
                pltpu.VMEM((128, rows), F32),
                pltpu.VMEM((rows, 128), F32),
                pltpu.VMEM((rows, 128), F32),
            ],
        ),
        out_shape=[jax.ShapeDtypeStruct((rows, D), BF16)] * 3,
        input_output_aliases={8 + i: i for i in range(len(before))},
        compiler_params=params(16),
        cost_estimate=cost(6e9 * count, 2e6 * count, 2 * rows * rows * 0.6 * count),
    )(core, lengths, qkv, qkv, qkv, a, da, lse, *before)


def valid_rows(core_ref, len_ref, block):
    pos = pl.program_id(0) * block + lax.broadcasted_iota(jnp.int32, (block, 1), 0)
    return pos < len_ref[core_ref[0]]


def add_row(acc_ref, row, value):
    acc_ref[row : row + 1, :] += jnp.sum(value, axis=0, keepdims=True)


def row_block(core, i, steps):
    half = steps // 2
    return jnp.where(i < half, (1 - core) * half + i, core * half + i - half)


def up_kernel(group, core_ref, len_ref, seat_ref, x_ref, a_ref, og_ref, vec_ref, *refs):
    refs, (mid_ref, h_ref, e_ref, slope_ref, dy_ref, wo_ref, wu_ref, sems) = refs[:-8], refs[-8:]
    block = x_ref.shape[0]

    @pl.when(pl.program_id(0) == 0)
    def _():
        group.start(refs, core_ref, seat_ref, 0, D // 2, wo_ref, sems.at[0])
        group.start(refs, core_ref, seat_ref, D // 2, FF // 2, wu_ref, sems.at[1])
        wait_all(wo_ref, sems.at[0])
        wait_all(wu_ref, sems.at[1])

    valid = valid_rows(core_ref, len_ref, block)
    dy_ref[...] = jnp.where(valid, og_ref[...].astype(F32), 0.0).astype(BF16)
    mid = x_ref[...].astype(F32) + mm(a_ref[...], wo_ref[...]) + vec_ref[4:5, :]
    mid_ref[...] = mid
    normed, _ = norm_parts(mid)
    h = (normed * vec_ref[5:6, :] + vec_ref[6:7, :]).astype(BF16)
    h_ref[...] = h

    def act(j, z):
        cols = slice(j * D, (j + 1) * D)
        z = z + vec_ref[8 + j : 9 + j, :]
        squared = z * z
        turned = jnp.tanh(z * (GELU_ROOT + (GELU_ROOT * GELU_CUBE) * squared))
        half = 0.5 * turned + 0.5
        act = z * half
        e_ref[:, cols] = act.astype(BF16)
        slope = half + act * (1.0 - turned) * (GELU_ROOT + (3.0 * GELU_ROOT * GELU_CUBE) * squared)
        slope_ref[:, cols] = slope.astype(BF16)

    waiting = None
    for j in range(FF // D):
        z = mm(h, wu_ref[:, j * D : (j + 1) * D])
        if waiting is not None:
            act(*waiting)
        waiting = (j, z)
    act(*waiting)


def up_call(core, lengths, seats, x, a, og, vec, group, block=256):
    rows = x.shape[0]
    row_spec = pl.BlockSpec((block, D), lambda i, *s: (i, 0))
    wide_spec = pl.BlockSpec((block, FF), lambda i, *s: (i, 0))
    low, wide = [jax.ShapeDtypeStruct((rows, width), BF16) for width in (D, FF)]
    return pl.pallas_call(
        functools.partial(up_kernel, group),
        name="up",
        grid_spec=pltpu.PrefetchScalarGridSpec(
            num_scalar_prefetch=3,
            grid=(rows // block,),
            in_specs=[row_spec, row_spec, row_spec, whole_spec(vec.shape)] + group.specs(),
            out_specs=[row_spec, row_spec, wide_spec, wide_spec, row_spec],
            scratch_shapes=[
                pltpu.VMEM((D, D), BF16),
                pltpu.VMEM((D, FF), BF16),
                pltpu.SemaphoreType.DMA((2,)),
            ],
        ),
        out_shape=[
            jax.ShapeDtypeStruct((rows, D), F32),
            low,
            wide,
            wide,
            low,
        ],
        compiler_params=params(40),
        cost_estimate=cost(6e9, 30e6, rows * FF),
    )(core, lengths, seats, x, a, og, vec, *group.arrays)


def down_kernel(up_group, down_group, core_ref, len_ref, seat_ref, mid_ref, e_ref, slope_ref, dy_ref, vec_ref, *refs):
    count = len(up_group.arrays)
    up_refs, down_refs = refs[:count], refs[count : count + len(down_group.arrays)]
    (
        theirs_ref, mine_ref, dz_ref, dmb_ref, dm_ref, da_ref, acc_ref, wo_ref, wu_ref, wd_ref, sems,
    ) = refs[-11:]
    block = da_ref.shape[0]
    step, steps = pl.program_id(0), pl.num_programs(0)

    @pl.when(step == 0)
    def _():
        down_group.start(down_refs, core_ref, seat_ref, 0, D // 2, wd_ref, sems.at[2])
        up_group.start(up_refs, core_ref, seat_ref, D // 2, FF // 2, wu_ref, sems.at[1])
        up_group.start(up_refs, core_ref, seat_ref, 0, D // 2, wo_ref, sems.at[0])
        acc_ref[...] = jnp.zeros_like(acc_ref)
        wait_all(wd_ref, sems.at[2])

    mid = mid_ref[...]
    down = vec_ref[7:8, :] + mid + mm(e_ref[...], wd_ref[...])
    pos = row_block(core_ref[0], step, steps) * block + lax.broadcasted_iota(jnp.int32, (block, 1), 0)
    down = jnp.where(pos < len_ref[core_ref[0]], down, 0.0).astype(BF16)

    @pl.when(step < steps // 2)
    def _():
        theirs_ref[...] = down

    @pl.when(step >= steps // 2)
    def _():
        mine_ref[0] = down

    @pl.when(step == 0)
    def _():
        wait_all(wu_ref, sems.at[1])
        wait_all(wo_ref, sems.at[0])

    dy = dy_ref[...]
    add_row(acc_ref, 7, dy.astype(F32))
    dh = None
    waiting = None
    for j in range(FF // D + 1):
        later = None
        if j < FF // D:
            later = (j, mm(dy, wd_ref[j * D : (j + 1) * D, :], NT))
        if waiting is not None:
            at, de = waiting
            cols = slice(at * D, (at + 1) * D)
            dz = (de * slope_ref[:, cols].astype(F32)).astype(BF16)
            dz_ref[:, cols] = dz
            add_row(acc_ref, 8 + at, dz.astype(F32))
            part = mm(dz, wu_ref[:, cols], NT)
            dh = part if dh is None else dh + part
        waiting = later
    normed, scale = norm_parts(mid)
    add_row(acc_ref, 5, dh * normed)
    add_row(acc_ref, 6, dh)
    dm = dy.astype(F32) + norm_back(dh * vec_ref[5:6, :], normed, scale)
    dm_ref[...] = dm
    dm_low = dm.astype(BF16)
    dmb_ref[...] = dm_low
    add_row(acc_ref, 4, dm_low.astype(F32))
    da_ref[...] = mm(dm_low, wo_ref[...], NT).astype(BF16)


def down_call(core, lengths, seats, mid, e, slope, dy, vec, up_group, down_group, block=256):
    rows = mid.shape[0]
    steps = rows // block
    half = steps // 2
    row_spec, wide_spec = [
        pl.BlockSpec((block, width), lambda i, c, *s: (row_block(c[0], i, steps), 0)) for width in (D, FF)
    ]
    return pl.pallas_call(
        functools.partial(down_kernel, up_group, down_group),
        name="down",
        grid_spec=pltpu.PrefetchScalarGridSpec(
            num_scalar_prefetch=3,
            grid=(steps,),
            in_specs=[row_spec, wide_spec, wide_spec, row_spec, whole_spec(vec.shape)]
            + up_group.specs()
            + down_group.specs(),
            out_specs=[
                pl.BlockSpec((block, D), lambda i, *s: (jnp.minimum(i, half - 1), 0)),
                pl.BlockSpec((1, block, D), lambda i, c, *s: (c[0], jnp.maximum(i - half, 0), 0)),
                wide_spec, row_spec, row_spec, row_spec,
                pl.BlockSpec((16, D), lambda i, *s: (0, 0)),
            ],
            scratch_shapes=[
                pltpu.VMEM((D, D), BF16),
                pltpu.VMEM((D, FF), BF16),
                pltpu.VMEM((FF, D), BF16),
                pltpu.SemaphoreType.DMA((3,)),
            ],
        ),
        out_shape=[
            jax.ShapeDtypeStruct((rows // 2, D), BF16),
            jax.ShapeDtypeStruct((2, rows // 2, D), BF16),
            jax.ShapeDtypeStruct((rows, FF), BF16),
            jax.ShapeDtypeStruct((rows, D), BF16),
            jax.ShapeDtypeStruct((rows, D), F32),
            jax.ShapeDtypeStruct((rows, D), BF16),
            jax.ShapeDtypeStruct((16, D), F32),
        ],
        compiler_params=params(40),
        cost_estimate=cost(1.6e10, 35e6),
    )(core, lengths, seats, mid, e, slope, dy, vec, *up_group.arrays, *down_group.arrays)


def pick(values, half, mode):
    if mode == "split":
        width = values.shape[1] // 2
        return [values[:, half * width : (half + 1) * width]]
    return [values[:, at : at + 128] for at in range(half * 128, values.shape[1], 256)]


def weight_grad_kernel(lefts, rights, mode, core_ref, *refs):
    left_refs, right_refs = refs[:lefts], refs[lefts : lefts + sum(rights)]
    own_ref, other_ref = refs[-2:]
    halves = ([], [])
    at = 0
    for left_ref, count in zip(left_refs, rights):
        left = left_ref[...]
        for right_ref in right_refs[at : at + count]:
            whole = mm(left, right_ref[...], TN).astype(BF16)
            for half in range(2):
                halves[half].extend(pick(whole, half, mode))
        at += count
    low, high = [part[0] if len(part) == 1 else jnp.concatenate(part, axis=1) for part in halves]

    @pl.when(core_ref[0] == 0)
    def _():
        own_ref[...] = low
        other_ref[...] = high

    @pl.when(core_ref[0] != 0)
    def _():
        own_ref[...] = high
        other_ref[...] = low


def weight_grad_call(core, products, block, name, mode="split", cols=None):
    rows, height = products[0][0].shape
    lefts = [left for left, _ in products]
    rights = [right for _, group in products for right in group]
    widths = [right.shape[1] if cols is None else cols[0] for right in rights]
    width = sum(widths)
    seat = 0 if cols is None else cols[1]
    return pl.pallas_call(
        functools.partial(weight_grad_kernel, len(lefts), [len(group) for _, group in products], mode),
        name=name,
        grid_spec=pltpu.PrefetchScalarGridSpec(
            num_scalar_prefetch=1,
            grid=(height // block,),
            in_specs=[pl.BlockSpec((rows, block), lambda i, c: (0, i))] * len(lefts)
            + [
                pl.BlockSpec((rows, w), lambda i, c: (0, seat), pipeline_mode=pl.Buffered(1)) for w in widths
            ],
            out_specs=[pl.BlockSpec((block, width // 2), lambda i, c: (i, 0))] * 2,
        ),
        out_shape=[jax.ShapeDtypeStruct((height, width // 2), BF16)] * 2,
        compiler_params=params(16 if mode == "turns" else 48),
        cost_estimate=cost(2 * rows * height * width, rows * (height + width) * 2 + height * width * 2),
    )(core, *lefts, *rights)


def last_kernel(
    core_ref, x_ref, dm_ref, dq_ref, dk_ref, dv_ref, w_ref, vec_ref, before_ref, theirs_ref, mine_ref, acc_ref
):
    step, steps = pl.program_id(0), pl.num_programs(0)

    @pl.when(step == 0)
    def _():
        acc_ref[...] = before_ref[...]

    subs = sub_blocks(x_ref.shape[0])

    def product(rows):
        return (
            mm(dq_ref[rows, :], w_ref[:D])
            + mm(dk_ref[rows, :], w_ref[D : 2 * D])
            + mm(dv_ref[rows, :], w_ref[2 * D :])
        )

    grads = []
    dh = product(subs[0])
    add_row(acc_ref, 2, dq_ref[...].astype(F32))
    add_row(acc_ref, 3, dv_ref[...].astype(F32))
    for at, rows in enumerate(subs):
        later = product(subs[at + 1]) if at + 1 < len(subs) else None
        normed, scale = norm_parts(x_ref[rows, :].astype(F32))
        add_row(acc_ref, 0, dh * normed)
        add_row(acc_ref, 1, dh)
        grads.append(dm_ref[rows, :] + norm_back(dh * vec_ref[0:1, :], normed, scale))
        dh = later

    @pl.when(step < steps // 2)
    def _():
        for rows, grad in zip(subs, grads):
            theirs_ref[rows, :] = grad

    @pl.when(step >= steps // 2)
    def _():
        for rows, grad in zip(subs, grads):
            mine_ref[0, rows, :] = grad


def last_call(core, x, dm, dq, dk, dv, w, vec, before, block=256):
    rows = x.shape[0]
    steps = rows // block
    half = steps // 2
    row_spec = pl.BlockSpec((block, D), lambda i, c, *s: (row_block(c[0], i, steps), 0))
    return pl.pallas_call(
        last_kernel,
        name="last",
        grid_spec=pltpu.PrefetchScalarGridSpec(
            num_scalar_prefetch=1,
            grid=(steps,),
            in_specs=[row_spec] * 5 + [whole_spec(part.shape) for part in (w, vec, before)],
            out_specs=[
                pl.BlockSpec((block, D), lambda i, *s: (jnp.minimum(i, half - 1), 0)),
                pl.BlockSpec((1, block, D), lambda i, c, *s: (c[0], jnp.maximum(i - half, 0), 0)),
                pl.BlockSpec((16, D), lambda i, *s: (0, 0)),
            ],
        ),
        out_shape=[
            jax.ShapeDtypeStruct((rows // 2, D), F32),
            jax.ShapeDtypeStruct((2, rows // 2, D), F32),
            jax.ShapeDtypeStruct((16, D), F32),
        ],
        compiler_params=params(12),
        cost_estimate=cost(rows * 6 * D * D, 16e6),
    )(core, x, dm, dq, dk, dv, w, vec, before)


def adam_kernel(plans, sources, core_ref, *refs):
    halves = [refs[2 * i : 2 * i + 2] for i in range(sources)]
    count = len(plans)
    states = refs[2 * sources : 2 * sources + 3 * count]
    outs = refs[2 * sources + 3 * count : 2 * sources + 6 * count]
    grads = refs[2 * sources + 6 * count :]
    for core in range(2):

        @pl.when(core_ref[0] == core)
        def _():
            for (_, _, moves), grad_ref in zip(plans, grads):
                for source, start, width, place0, place1 in moves:
                    for half, place in ((0, place0), (1, place1)):
                        ref = halves[source][0 if half == core else 1]
                        grad_ref[:, place : place + width] = ref[:, start : start + width].astype(F32)

    for i, (rate, decay, _) in enumerate(plans):
        weight, first, second = states[3 * i : 3 * i + 3]
        new = adamw(weight[...], grads[i][...], first[...], second[...], rate, decay)
        for out, value in zip(outs[3 * i : 3 * i + 3], new):
            out[...] = value


def adam_call(core, halves, states, plans):
    flat = [part for pair in halves for part in pair]
    held = [part for state in states for part in state]
    spec = pl.BlockSpec(memory_space=pltpu.VMEM)
    news = pl.pallas_call(
        functools.partial(adam_kernel, plans, len(halves)),
        name="adam",
        in_specs=[pl.BlockSpec(memory_space=pltpu.SMEM)] + [spec] * (len(flat) + len(held)),
        out_specs=[spec] * len(held),
        out_shape=[jax.ShapeDtypeStruct(part.shape, F32) for part in held],
        scratch_shapes=[pltpu.VMEM(state[0].shape, F32) for state in states],
        compiler_params=params(12),
        cost_estimate=cost(1e6, 24 * sum(state[0].size for state in states)),
    )(core, *flat, *held)
    return [news[3 * i : 3 * i + 3] for i in range(len(states))]


def after(value, *others):
    if not others:
        return value
    return lax.optimization_barrier((value,) + others)[0]


def cut(array, axis, index, size=1):
    starts = [jnp.uint32(0)] * array.ndim
    sizes = list(array.shape)
    starts[axis], sizes[axis] = index, size
    return lax.dynamic_slice(array, starts, sizes)


class Grid:
    def __init__(self, chips):
        log = chips.bit_length() - 1
        side = 1 << (log // 3)
        if side * side * (chips // (side * side)) != chips:
            side = 1
        self.chips = chips
        self.n = side
        self.nz = chips // (side * side)
        self.core = lax.axis_index("seq")
        self.chip = lax.axis_index("dp")
        self.x = self.chip % side
        self.y = self.chip // side % side
        self.z = self.chip // (side * side)

    def pin(self, value):
        n, core = self.n, self.core
        first, second = self.coords(core)
        places = {
            "core": core,
            "other": 1 - core,
            "chip": self.chip,
            "seats": self.seats(True),
            "q_seats": self.seats(False),
        }
        for s in range(n):
            for t in range(n):
                places["plane", s, t] = self.plane((first + s) % n, (second + t) % n, core)
        for at in range(self.nz):
            places["z", at] = self.z ^ at
        names = list(places)
        held = lax.optimization_barrier((value, *[places[name].astype(jnp.uint32) for name in names]))
        self.places = dict(zip(names, held[1:]))
        return held[0]

    def plane(self, first, second, core):
        return jnp.where(core == 0, second * self.n + first, first * self.n + second)

    def coords(self, core):
        return jnp.where(core == 0, self.x, self.y), jnp.where(core == 0, self.y, self.x)

    def permute(self, value, axis, shift=0):
        pairs = []
        for chip in range(self.chips):
            for core in range(2):
                x, y, z = chip % self.n, chip // self.n % self.n, chip // (self.n * self.n)
                to_core = core
                if axis == "z":
                    z = (z + shift) % self.nz
                elif axis == "zx":
                    z = z ^ shift
                elif axis == "core":
                    to_core = 1 - core
                elif (axis == "first") == (core == 0):
                    x = (x + shift) % self.n
                else:
                    y = (y + shift) % self.n
                pairs.append((chip * 2 + core, ((z * self.n + y) * self.n + x) * 2 + to_core))
        return lax.ppermute(value, ("dp", "seq"), pairs)

    def swap(self, value):
        return self.permute(value, "core")

    def join(self, own, other, axis):
        return jnp.where(
            self.places["core"] == 0,
            jnp.concatenate([own, other], axis),
            jnp.concatenate([other, own], axis),
        )

    def seats(self, halving):
        found = []
        for half in range(2):
            core = self.core if half == 0 else 1 - self.core
            first, second = self.coords(core)
            for s2 in range(self.n):
                for s1 in range(self.n):
                    flat = self.plane((first - s1) % self.n, (second - s2) % self.n, core)
                    for sz in range(self.nz):
                        z = self.z ^ sz if halving else (self.z - sz) % self.nz
                        found.append(z * self.n * self.n + flat)
        return jnp.stack(found).astype(jnp.int32)

    def total_small(self, value, *untils):
        steps = [("core", 0), ("first", 1), ("second", 1)] if self.n == 2 else [("core", 0)]
        if self.n != 2:
            for axis in ("first", "second"):
                value = value + sum(self.permute(value, axis, s) for s in range(1, self.n))
        bit = 1
        while bit < self.nz:
            steps.append(("zx", bit))
            bit *= 2
        for at, (axis, shift) in enumerate(steps):
            until = untils[at] if at < len(untils) else ()
            value = value + after(self.permute(value, axis, shift), *until)
        return value

    def gather_z(self, block, *until):
        return jnp.stack([block] + [after(self.permute(block, "z", s), *until) for s in range(1, self.nz)])

    def gather_bit(self, held, bit, *until):
        return jnp.concatenate([held, after(self.permute(held, "zx", bit), *until)])

    def along(self, axis, column, *until):
        return [after(self.permute(column, axis, s), *until) for s in range(1, self.n)]

    def plane_parts(self, column, firsts, seconds, passed):
        parts = [column] + firsts
        for s2 in range(1, self.n):
            parts += [seconds[s2 - 1]] + [passed[s1 - 1][s2 - 1] for s1 in range(1, self.n)]
        return [part[None] for part in parts]

    def gather_first(self, column, *until):
        return jnp.stack([column] + [after(self.permute(column, "first", s), *until) for s in range(1, self.n)])

    def gather_second(self, line, *until):
        return [after(self.permute(line, "second", s), *until) for s in range(1, self.n)]

    def scatter_first(self, own, pair, *until):
        rows, cols = own.shape[0] // self.chips, own.shape[1]
        n = self.n

        def seat(s1, s2):
            own_part, pair_part = [
                cut(part.reshape(self.nz, n * n, rows, cols), 1, self.places["plane", s1, s2]).astype(F32)
                for part in (own, pair)
            ]
            return own_part + pair_part

        kept = [seat(0, t) for t in range(n)]
        for s in range(1, n):
            send = jnp.stack([seat(s, t).astype(BF16) for t in range(n)])
            got = after(self.permute(send, "first", s), *until)
            kept = [kept[t] + got[t].astype(F32) for t in range(n)]
        return kept[0], [part.astype(BF16) for part in kept[1:]]

    def scatter_second(self, kept, *until):
        mine, rest = kept
        got = [after(self.permute(rest[s - 1], "second", s), *until) for s in range(1, self.n)]
        for part in got:
            mine = mine + part.astype(F32)
        return mine.reshape((self.nz,) + mine.shape[2:]), got

    def order_z(self, mine):
        return [cut(mine, 0, self.places["z", at])[0] for at in range(self.nz)]

    def scatter_bit(self, parts, *until):
        half = len(parts) // 2
        send = parts[half] if half == 1 else jnp.stack([part.astype(BF16) for part in parts[half:]])
        got = after(self.permute(send.astype(BF16), "zx", half), *until)
        if half == 1:
            return [parts[0] + got.astype(F32)], got
        return [part + got[at].astype(F32) for at, part in enumerate(parts[:half])], got

    def scatter_z(self, parts, *until):
        while len(parts) > 1:
            parts, _ = self.scatter_bit(parts, *until)
        return parts[0]


def adamw(weight, gradient, first_moment, second_moment, step_rate, weight_decay):
    first_moment = BETA_ONE * first_moment + (1.0 - BETA_ONE) * gradient
    second_moment = BETA_TWO * second_moment + (1.0 - BETA_TWO) * gradient * gradient
    first_fix = 1.0 - BETA_ONE**STEP
    second_fix = 1.0 - BETA_TWO**STEP
    direction = first_moment / first_fix / (jnp.sqrt(second_moment / second_fix) + EPS_ADAM)
    return (weight - step_rate * (direction + weight_decay * weight), first_moment, second_moment)


def local(
    block_in, lengths, out_grad, w_qkv, w_out, w_up, w_down, vectors,
    first_qkv, first_out, first_up, first_down, first_vectors,
    second_qkv, second_out, second_up, second_down, second_vectors,
):
    grid = Grid(lax.axis_size("dp"))
    core = grid.core
    w_qkv_first = grid.pin(w_qkv)
    places = grid.places
    core_arr = places["core"].reshape(1).astype(jnp.int32)
    half_len = block_in.shape[1]
    vec_count, vec_here = vectors.shape

    def own_slot(halves):
        mine, theirs = [cut(halves, 0, places[name])[0] for name in ("core", "other")]
        return grid.join(mine, grid.swap(theirs), 0)

    def both_slots(mine, got):
        zero = jnp.uint32(0)
        return lax.dynamic_update_slice(mine, got[None], (places["other"], zero, zero))

    def half_of(shard):
        width = shard.shape[1] // 2
        return jnp.where(places["core"] == 0, shard[:, :width], shard[:, width:]).astype(BF16)

    seats, q_seats = [places[name].astype(jnp.int32) for name in ("seats", "q_seats")]

    turned = jnp.pad(vectors.T.astype(BF16), ((0, 0), (0, 128 - vec_count)))
    q_block = jnp.concatenate([half_of(w_qkv_first), turned], axis=1)
    u_block = jnp.concatenate([half_of(w_out), half_of(w_up)], axis=1)
    d_block = half_of(w_down)
    q_col = grid.gather_z(q_block)
    x = own_slot(block_in)
    bits = [1 << at for at in range((grid.nz - 1).bit_length())]
    u_col, d_col = u_block[None], d_block[None]
    for bit in bits[:-1]:
        u_col = grid.gather_bit(u_col, bit)
        d_col = grid.gather_bit(d_col, bit)
    q_line = after(grid.gather_first(q_col, x), u_col, d_col)
    q_rest = grid.gather_second(q_line)
    u_col = grid.gather_bit(after(u_col, q_line), bits[-1])
    q_line_swap = grid.swap(q_line)
    q_rest_swap = [grid.swap(after(part, u_col)) for part in q_rest]
    q_group = finish_group(grid, q_seats, [q_line] + q_rest, [q_line_swap] + q_rest_swap)

    h1, qkv, vec, w_back = qkv_call(core_arr, q_seats, x, q_group)
    u_firsts = grid.along("first", u_col, qkv)
    d_col = grid.gather_bit(after(d_col, u_col), bits[-1], qkv)
    og = own_slot(after(out_grad, qkv))
    att = attend_call(core_arr, lengths, after(qkv, d_col, *u_firsts), 0, 4, ())
    u_seconds = grid.along("second", u_col, *att)
    u_passed = [grid.along("second", part, *att) for part in u_firsts]
    early = [after(grid.swap(part), *att) for part in [u_col] + u_firsts]
    d_col = after(d_col, *u_seconds, *[part for parts in u_passed for part in parts])
    a, lse = attend_call(core_arr, lengths, after(qkv, d_col), 4, 2, att)
    late_seconds = [after(grid.swap(part), a) for part in u_seconds]
    late_passed = [[after(grid.swap(part), a) for part in parts] for parts in u_passed]
    u_group = finish_group(
        grid,
        seats,
        grid.plane_parts(u_col, u_firsts, u_seconds, u_passed),
        grid.plane_parts(early[0], early[1:], late_seconds, late_passed),
    )
    mid, h2, e, slope, dy = up_call(core_arr, lengths, seats, x, a, og, vec, u_group)
    d_firsts = grid.along("first", d_col, mid)
    d_seconds = grid.along("second", d_col, mid)
    d_col_swap = after(grid.swap(d_col), mid)
    d_own, d_other = weight_grad_call(
        core_arr, [(after(e, *d_firsts, *d_seconds), [dy])], 512, "grad_down"
    )
    d_passed = [grid.along("second", part, d_own) for part in d_firsts]
    early = [[after(grid.swap(part), d_own) for part in parts] for parts in (d_firsts, d_seconds)]
    d_group = finish_group(
        grid,
        seats,
        grid.plane_parts(d_col, d_firsts, d_seconds, d_passed),
        grid.plane_parts(d_col_swap, *early, [[grid.swap(part) for part in parts] for parts in d_passed]),
    )
    out_theirs, out_mine, dz, dmb, dm, da, acc_mid = down_call(
        core_arr, lengths, seats, mid, e, slope, dy, vec, u_group, d_group
    )

    d_pair = after(grid.swap(d_other), dz)
    u_own, u_other = weight_grad_call(
        core_arr, [(a, [dmb]), (h2, [after(dz, d_pair)])], 384, "grad_up"
    )
    d_kept = grid.scatter_first(d_own, d_pair, u_own)

    def back_call(start, count, before, *needs):
        return attend_back_call(core_arr, lengths, qkv, a, after(da, *needs), lse, start, count, before)

    back = back_call(0, 2, (), u_own, *d_kept[1])
    d_sum, d_here = grid.scatter_second(d_kept, *back)
    u_pair = after(grid.swap(u_other), *back)
    back = back_call(2, 4, back, u_pair, *d_here)
    d_parts, d_got = grid.scatter_bit(grid.order_z(d_sum), *back)
    u_kept = grid.scatter_first(u_own, u_pair, *back)
    dq, dk, dv = back
    block_out = both_slots(out_mine, after(grid.swap(after(out_theirs, back[0])), dq))
    q_own, q_other = weight_grad_call(
        core_arr, [(h1, [after(dq, d_got, *u_kept[1]), dk, dv])], 384, "grad_qkv", "turns"
    )
    u_sum, u_here = grid.scatter_second(u_kept, q_own)
    q_pair = grid.swap(after(q_other, *u_here))
    in_theirs, in_mine, acc = last_call(
        core_arr, x, dm, after(dq, q_own, q_pair), dk, dv, w_back, vec, acc_mid
    )
    d_mine = grid.scatter_z(d_parts, in_theirs)
    d_other_mine = grid.swap(d_mine)
    q_kept = grid.scatter_first(q_own, q_pair, in_theirs)
    u_parts, u_got = grid.scatter_bit(grid.order_z(u_sum), *q_kept[1])
    q_sum, q_here = grid.scatter_second(q_kept, u_got)
    down_new, = adam_call(
        core_arr,
        [(d_mine, d_other_mine)],
        [(after(w_down, *q_kept[1]), first_down, second_down)],
        [(FF ** (-0.5), MATRIX_DECAY, [(0, 0, D // 2, 0, D // 2)])],
    )
    in_got = grid.swap(after(in_theirs, *q_kept[1]))
    u_mine = grid.scatter_z([after(part, *q_here) for part in u_parts])
    u_other_mine = grid.swap(u_mine)
    in_grad = both_slots(in_mine, after(in_got, *q_here))
    q_parts, q_got = grid.scatter_bit(grid.order_z(q_sum), in_grad)
    q_gots = [(q_got,)]
    while len(q_parts) > 1:
        q_parts, q_got = grid.scatter_bit(q_parts)
        q_gots.append((q_got,))
    q_mine = q_parts[0]
    q_other_mine = grid.swap(q_mine)
    vec_total = grid.total_small(acc, (), q_kept[1], q_here, *q_gots)

    half, wide = D // 2, FF // 2
    out_new, up_new = adam_call(
        core_arr,
        [(u_mine, u_other_mine)],
        [(after(w_out, in_grad), first_out, second_out), (w_up, first_up, second_up)],
        [
            ((D // 64) ** (-0.5), MATRIX_DECAY, [(0, 0, half, 0, half)]),
            (D ** (-0.5), MATRIX_DECAY, [(0, half, wide, 0, wide)]),
        ],
    )
    moves = []
    for turn in range(3 * D // 256):
        moves.append((0, turn * 128, 128, turn * 256, turn * 256 + 128))
    qkv_new, = adam_call(
        core_arr,
        [(q_mine, q_other_mine)],
        [(w_qkv, first_qkv, second_qkv)],
        [(D ** (-0.5), MATRIX_DECAY, moves)],
    )
    vec_grad = cut(vec_total[:vec_count].reshape(vec_count, -1, vec_here), 1, places["chip"])[:, 0]
    vec_new = adamw(vectors, vec_grad, first_vectors, second_vectors, VECTOR_RATE, 0.0)
    news = [qkv_new, out_new, up_new, down_new, vec_new]
    return (block_out, in_grad) + tuple(new[kind] for kind in range(3) for new in news)


def finish_group(grid, seats, own, other):
    rows, cols = own[0].shape[-2:]
    if rows % 16 == 0:
        return Pieces(own + other, rows)
    found = []
    for half, parts in enumerate((own, other)):
        here = seats[half * grid.chips : (half + 1) * grid.chips]
        order = jnp.zeros((grid.chips,), jnp.int32).at[here].set(jnp.arange(grid.chips, dtype=jnp.int32))
        blocks = jnp.concatenate(parts).reshape(grid.chips, rows, cols)
        found.append(jnp.take(blocks, order, axis=0).reshape(1, 1, grid.chips * rows, cols))
    return Pieces(found, grid.chips * rows, True)


def solution(mesh):
    weight = P("dp", None)
    vector = P(None, "dp")
    state = (weight, weight, weight, weight, vector)
    tokens = P("dp", "seq", None)
    return jax.shard_map(
        local,
        mesh=mesh,
        in_specs=(tokens, P("dp"), tokens) + state * 3,
        out_specs=(tokens, tokens) + state * 3,
        check_vma=False,
    )
```

```python
import functools

import jax
import jax.numpy as jnp
from jax import lax
from jax.experimental import pallas as pl
from jax.experimental.pallas import tpu as pltpu
from jax.sharding import PartitionSpec as P

D = 768
HEADS = 12
HEAD_DIM = 64
FF = 3072
STEP = 10

EPS_NORM = 1e-05
EPS_ADAM = 1e-08
BETA_ONE = 0.5
BETA_TWO = 0.5
MATRIX_DECAY = 0.1
VECTOR_RATE = 0.1
NEG_FILL = -1e30
GELU_ROOT = 0.7978845608028654
GELU_CUBE = 0.044715
QKV_HALF = 3 * D // 2

F32 = jnp.float32
BF16 = jnp.bfloat16

NN = (((1,), (0,)), ((), ()))
NT = (((1,), (1,)), ((), ()))
TN = (((0,), (0,)), ((), ()))


def mm(left, right, dims=NN):
    return lax.dot_general(left, right, dims, preferred_element_type=F32)


def cost(flops, nbytes, trans=0):
    return pl.CostEstimate(flops=int(4 * flops), bytes_accessed=int(4 * nbytes), transcendentals=int(trans))


def params(mib=60):
    return pltpu.CompilerParams(vmem_limit_bytes=mib * 1024 * 1024)


def held_spec():
    return pl.BlockSpec(memory_space=pltpu.VMEM)


def at_rows(block):
    return pl.ds(pl.multiple_of(pl.program_id(0) * block, block), block)


def whole_spec(shape):
    return pl.BlockSpec(shape, lambda *idx: (0,) * len(shape), pipeline_mode=pl.Buffered(1))


class Pieces:
    def __init__(self, arrays, rows, ordered=False):
        self.arrays = arrays
        self.rows = rows
        self.ordered = ordered
        self.halves = 2
        self.count = len(arrays) // self.halves
        self.lines, self.depth = arrays[0].shape[:2]

    def specs(self):
        return [pl.BlockSpec(memory_space=pltpu.HBM)] * len(self.arrays)

    def row(self, seat_ref, at):
        return 0 if self.ordered else pl.multiple_of(seat_ref[at] * self.rows, 16)

    def start(self, refs, core_ref, seat_ref, start_col, width, target, sem):
        core = core_ref[0]
        at = 0
        for half in range(self.halves):
            where = core if half == 0 else 1 - core
            for s2 in range(self.count):
                ref = refs[half * self.count + s2]
                for s1 in range(self.lines):
                    for sz in range(self.depth):
                        row = self.row(seat_ref, at)
                        at += 1
                        col = pl.multiple_of(where * width, 128)
                        pltpu.make_async_copy(
                            ref.at[s1, sz, :, pl.ds(start_col, width)],
                            target.at[pl.ds(row, self.rows), pl.ds(col, width)],
                            sem,
                        ).start()

    def start_once(self, refs, seat_ref, start_col, width, target, sem):
        at = 0
        for s2 in range(self.count):
            for s1 in range(self.lines):
                for sz in range(self.depth):
                    row = self.row(seat_ref, at)
                    at += 1
                    pltpu.make_async_copy(
                        refs[s2].at[s1, sz, :, pl.ds(start_col, width)],
                        target.at[pl.ds(row, self.rows), :],
                        sem,
                    ).start()


def wait_all(target, sem):
    pltpu.make_async_copy(target, target, sem).wait()


def norm_parts(rows):
    mean = jnp.mean(rows, axis=-1, keepdims=True)
    centred = rows - mean
    variance = jnp.mean(centred * centred, axis=-1, keepdims=True)
    scale = lax.rsqrt(variance + EPS_NORM)
    return centred * scale, scale


def norm_back(d_normed, normed, scale):
    first = jnp.mean(d_normed, axis=-1, keepdims=True)
    second = jnp.mean(d_normed * normed, axis=-1, keepdims=True)
    return scale * (d_normed - first - normed * second)


def qkv_kernel(group, core_ref, seat_ref, x_ref, *refs):
    refs, (h_ref, qkv_ref, vec_ref, back_ref, w_ref, turned_ref, sems) = refs[:-7], refs[-7:]

    @pl.when(pl.program_id(0) == 0)
    def _():
        group.start(refs, core_ref, seat_ref, 0, QKV_HALF, w_ref, sems.at[0])
        group.start_once(refs, seat_ref, QKV_HALF, 128, turned_ref, sems.at[1])
        wait_all(turned_ref, sems.at[1])
        vec_ref[...] = turned_ref[...].astype(F32).T[:16]
        wait_all(w_ref, sems.at[0])

    def norm(rows):
        normed, _ = norm_parts(x_ref[rows, :].astype(F32))
        h = (normed * vec_ref[0:1, :] + vec_ref[1:2, :]).astype(BF16)
        h_ref[rows, :] = h
        return h

    block = x_ref.shape[0]
    h = norm(slice(0, block))
    for part, bias in enumerate((2, None, 3)):
        cols = slice(part * D, (part + 1) * D)
        product = mm(h, w_ref[:, cols])
        if bias is not None:
            product = product + vec_ref[bias : bias + 1, :]
        qkv_ref[:, cols] = product.astype(BF16)

    @pl.when(pl.program_id(0) < 3)
    def _():
        back_ref[...] = w_ref[:, at_rows(D)].T


def sub_blocks(rows):
    return [slice(at, at + 256) for at in range(0, rows, 256)]


def qkv_call(core, seats, x, group, block=256):
    rows = x.shape[0]
    return pl.pallas_call(
        functools.partial(qkv_kernel, group),
        name="qkv",
        grid_spec=pltpu.PrefetchScalarGridSpec(
            num_scalar_prefetch=2,
            grid=(rows // block,),
            in_specs=[pl.BlockSpec((block, D), lambda i, *s: (i, 0))] + group.specs(),
            out_specs=[
                pl.BlockSpec((block, D), lambda i, *s: (i, 0)),
                pl.BlockSpec((block, 3 * D), lambda i, *s: (i, 0)),
                pl.BlockSpec((16, D), lambda i, *s: (0, 0)),
                pl.BlockSpec((D, D), lambda i, *s: (jnp.minimum(i, 2), 0)),
            ],
            scratch_shapes=[
                pltpu.VMEM((D, 3 * D), BF16),
                pltpu.VMEM((D, 128), BF16),
                pltpu.SemaphoreType.DMA((2,)),
            ],
        ),
        out_shape=[
            jax.ShapeDtypeStruct((rows, D), BF16),
            jax.ShapeDtypeStruct((rows, 3 * D), BF16),
            jax.ShapeDtypeStruct((16, D), F32),
            jax.ShapeDtypeStruct((3 * D, D), BF16),
        ],
        compiler_params=params(12),
        cost_estimate=cost(2 * rows * D * 3 * D, 10e6),
    )(core, seats, x, *group.arrays)


def head_parts(length, k_all, q_turned, head):
    full_len = k_all.shape[0]
    lane = lax.broadcasted_iota(jnp.int32, (1, 128), 1)
    row = lax.broadcasted_iota(jnp.int32, (128, 1), 0)
    zero, one = jnp.zeros((), BF16), jnp.ones((), BF16)
    mine = (lane // HEAD_DIM) == head
    spare = HEAD_DIM * (1 - head)
    pos = lax.broadcasted_iota(jnp.int32, (full_len, 128), 0)
    fill = jnp.where(pos < length, 0.0, NEG_FILL).astype(BF16)
    k_head = jnp.where(mine, k_all, jnp.where(lane == spare, fill, zero))
    q_head = jnp.where((row // HEAD_DIM) == head, q_turned, jnp.where(row == spare, one, zero))
    return mine, k_head, q_head


def causal_mask(scores, block):
    full = scores.shape[0]
    key_pos = lax.broadcasted_iota(jnp.int32, (block, block), 0)
    query_pos = lax.broadcasted_iota(jnp.int32, (block, block), 1)
    last = jnp.where(key_pos <= query_pos, scores[full - block :], NEG_FILL)
    if full == block:
        return last
    return jnp.concatenate([scores[: full - block], last], axis=0)


def attend_kernel(start, core_ref, len_ref, qkv_ref, *refs):
    a_ref, lse_ref, mixed_ref, scores_ref = refs[-4:]
    block = 256
    full_len = qkv_ref.shape[0]
    length = len_ref[core_ref[0]]
    q_all, k_all, v_all = [
        qkv_ref[:, pl.ds(pl.multiple_of((pl.program_id(0) + start) * 128 + part * D, 128), 128)] for part in range(3)
    ]
    q_all = q_all * jnp.asarray(HEAD_DIM ** (-0.5), BF16)
    v_turned = v_all.T
    q_turned = q_all.T
    ones = jnp.ones((16, full_len), BF16)
    parts = []
    for head in range(2):
        _, k_head, q_head = head_parts(length, k_all, q_turned, head)
        v_head = jnp.concatenate([v_turned[head * HEAD_DIM : (head + 1) * HEAD_DIM], ones], axis=0)
        parts.append((k_head, q_head, v_head))
    units = [(head, j) for j in reversed(range(full_len // block)) for head in range(2)]

    def score(at):
        head, j = units[at]
        k_head, q_head, _ = parts[head]
        top = None
        for i in range(j + 1):
            rows = slice(i * block, (i + 1) * block)
            tile = mm(k_head[rows], q_head[:, j * block : (j + 1) * block])
            if i == j:
                tile = causal_mask(tile, block)
            scores_ref[at % 2, rows, :] = tile
            part = jnp.max(tile.reshape(block // 8, 8, block), axis=0)
            top = part if top is None else jnp.maximum(top, part)
        return jnp.max(top, axis=0, keepdims=True)

    def finish(at, top):
        head, j = units[at]
        v_head = parts[head][2]
        cols = slice(j * block, (j + 1) * block)
        mixed = None
        for i in range(j + 1):
            rows = slice(i * block, (i + 1) * block)
            exped = jnp.exp(scores_ref[at % 2, rows, :] - top).astype(BF16)
            part = mm(v_head[:, rows], exped)
            mixed = part if mixed is None else mixed + part
        total = mixed[HEAD_DIM : HEAD_DIM + 1]
        mixed_ref[head * HEAD_DIM : (head + 1) * HEAD_DIM, cols] = mixed[:HEAD_DIM] / total
        lse_ref[0, head : head + 1, cols] = top + jnp.log(total)

    top = score(0)
    for at in range(len(units)):
        later = score(at + 1) if at + 1 < len(units) else None
        finish(at, top)
        top = later
    a_ref[...] = mixed_ref[...].T.astype(BF16)


def attend_call(core, lengths, qkv, first, count, before):
    rows = qkv.shape[0]
    pairs = HEADS // 2
    before = list(before)
    return pl.pallas_call(
        functools.partial(attend_kernel, first),
        name="attend",
        grid_spec=pltpu.PrefetchScalarGridSpec(
            num_scalar_prefetch=2,
            grid=(count,),
            in_specs=[held_spec()] + [pl.BlockSpec(memory_space=pl.ANY)] * len(before),
            out_specs=[
                pl.BlockSpec((rows, 128), lambda i, c, n: (0, i + first)),
                pl.BlockSpec((1, 8, rows), lambda i, c, n: (i + first, 0, 0)),
            ],
            scratch_shapes=[pltpu.VMEM((128, rows), F32), pltpu.VMEM((2, rows, 256), F32)],
        ),
        out_shape=[
            jax.ShapeDtypeStruct((rows, D), BF16),
            jax.ShapeDtypeStruct((pairs, 8, rows), F32),
        ],
        input_output_aliases={3 + i: i for i in range(len(before))},
        compiler_params=params(12),
        cost_estimate=cost(3e9 * count, 1.2e6 * count, 2 * rows * rows * 0.6 * count),
    )(core, lengths, qkv, *before)


def attend_back_kernel(core_ref, len_ref, q_ref, k_ref, v_ref, a_ref, da_ref, lse_ref, *refs):
    dq_ref, dk_ref, dv_ref, dqt_ref, dk_acc, dv_acc = refs[-6:]
    block = 256
    full_len = q_ref.shape[0]
    length = len_ref[core_ref[0]]
    scale = HEAD_DIM ** (-0.5)
    q_all = q_ref[...] * jnp.asarray(scale, BF16)
    k_all = k_ref[...]
    k_turned = k_all.T
    v_all = v_ref[...]
    da_all = da_ref[...]
    inner = (da_all.astype(F32) * a_ref[...].astype(F32)).T
    q_turned, da_turned = q_all.T, da_all.T
    parts = []
    for head in range(2):
        mine, k_head, q_head = head_parts(length, k_all, q_turned, head)
        zero = jnp.zeros((), BF16)
        q_plain = jnp.where(mine, q_all, zero)
        da_head = jnp.where(mine, da_all, zero)
        row = lax.broadcasted_iota(jnp.int32, (128, 1), 0)
        da_cols = jnp.where((row // HEAD_DIM) == head, da_turned, zero)
        lanes = slice(head * HEAD_DIM, (head + 1) * HEAD_DIM)
        centre = jnp.sum(inner[lanes], axis=0, keepdims=True)
        parts.append((k_head, q_plain, q_head, da_head, da_cols, lanes, centre))
    units = [
        (head, j, i)
        for j in reversed(range(full_len // block))
        for head in range(2)
        for i in range(j + 1)
    ]

    def score(at):
        head, j, i = units[at]
        k_head, _, q_head, _, da_cols, _, _ = parts[head]
        rows, cols = slice(i * block, (i + 1) * block), slice(j * block, (j + 1) * block)
        tile = mm(k_head[rows], q_head[:, cols])
        if i == j:
            tile = causal_mask(tile, block)
        return tile, mm(v_all[rows], da_cols[:, cols])

    seen = set()
    ready = score(0)
    dq_part = None
    for at, (head, j, i) in enumerate(units):
        later = score(at + 1) if at + 1 < len(units) else None
        scores, d_probs = ready
        _, q_plain, _, da_head, _, lanes, centre = parts[head]
        rows, cols = slice(i * block, (i + 1) * block), slice(j * block, (j + 1) * block)
        probs = jnp.exp(scores - lse_ref[0, head : head + 1, cols])
        d_scores = (probs * (d_probs - centre[:, cols])).astype(BF16)
        dv_part = mm(probs.astype(BF16), da_head[cols])
        dk_part = mm(d_scores, q_plain[cols])
        if i in seen:
            dv_acc[rows] += dv_part
            dk_acc[rows] += dk_part
        else:
            seen.add(i)
            dv_acc[rows] = dv_part
            dk_acc[rows] = dk_part
        part = mm(k_turned[lanes, rows], d_scores)
        dq_part = part if i == 0 else dq_part + part
        if i == j:
            dqt_ref[lanes, cols] = dq_part * scale
        ready = later
    dq_ref[...] = dqt_ref[...].T.astype(BF16)
    dk_ref[...] = dk_acc[...].astype(BF16)
    dv_ref[...] = dv_acc[...].astype(BF16)


def attend_back_call(core, lengths, qkv, a, da, lse, start, count, before):
    rows = qkv.shape[0]
    pairs = HEADS // 2
    before = list(before)
    pair_spec = pl.BlockSpec((rows, 128), lambda i, c, n: (0, i + start))
    return pl.pallas_call(
        attend_back_kernel,
        name="attend_back",
        grid_spec=pltpu.PrefetchScalarGridSpec(
            num_scalar_prefetch=2,
            grid=(count,),
            in_specs=[
                pair_spec,
                pl.BlockSpec((rows, 128), lambda i, c, n: (0, i + start + pairs)),
                pl.BlockSpec((rows, 128), lambda i, c, n: (0, i + start + 2 * pairs)),
                pair_spec,
                pair_spec,
                pl.BlockSpec((1, 8, rows), lambda i, c, n: (i + start, 0, 0)),
            ]
            + [pl.BlockSpec(memory_space=pl.ANY)] * len(before),
            out_specs=[pair_spec, pair_spec, pair_spec],
            scratch_shapes=[
                pltpu.VMEM((128, rows), F32),
                pltpu.VMEM((rows, 128), F32),
                pltpu.VMEM((rows, 128), F32),
            ],
        ),
        out_shape=[jax.ShapeDtypeStruct((rows, D), BF16)] * 3,
        input_output_aliases={8 + i: i for i in range(len(before))},
        compiler_params=params(16),
        cost_estimate=cost(6e9 * count, 2e6 * count, 2 * rows * rows * 0.6 * count),
    )(core, lengths, qkv, qkv, qkv, a, da, lse, *before)


def valid_rows(core_ref, len_ref, block):
    pos = pl.program_id(0) * block + lax.broadcasted_iota(jnp.int32, (block, 1), 0)
    return pos < len_ref[core_ref[0]]


def add_row(acc_ref, row, value):
    acc_ref[row : row + 1, :] += jnp.sum(value, axis=0, keepdims=True)


def row_block(core, i, steps):
    half = steps // 2
    return jnp.where(i < half, (1 - core) * half + i, core * half + i - half)


def up_kernel(group, core_ref, len_ref, seat_ref, x_ref, a_ref, og_ref, vec_ref, *refs):
    refs, (mid_ref, h_ref, e_ref, slope_ref, dy_ref, wo_ref, wu_ref, sems) = refs[:-8], refs[-8:]
    block = x_ref.shape[0]

    @pl.when(pl.program_id(0) == 0)
    def _():
        group.start(refs, core_ref, seat_ref, 0, D // 2, wo_ref, sems.at[0])
        group.start(refs, core_ref, seat_ref, D // 2, FF // 2, wu_ref, sems.at[1])
        wait_all(wo_ref, sems.at[0])
        wait_all(wu_ref, sems.at[1])

    valid = valid_rows(core_ref, len_ref, block)
    dy_ref[...] = jnp.where(valid, og_ref[...].astype(F32), 0.0).astype(BF16)
    mid = x_ref[...].astype(F32) + mm(a_ref[...], wo_ref[...]) + vec_ref[4:5, :]
    mid_ref[...] = mid
    normed, _ = norm_parts(mid)
    h = (normed * vec_ref[5:6, :] + vec_ref[6:7, :]).astype(BF16)
    h_ref[...] = h

    def act(j, z):
        cols = slice(j * D, (j + 1) * D)
        z = z + vec_ref[8 + j : 9 + j, :]
        squared = z * z
        turned = jnp.tanh(z * (GELU_ROOT + (GELU_ROOT * GELU_CUBE) * squared))
        half = 0.5 * turned + 0.5
        act = z * half
        e_ref[:, cols] = act.astype(BF16)
        slope = half + act * (1.0 - turned) * (GELU_ROOT + (3.0 * GELU_ROOT * GELU_CUBE) * squared)
        slope_ref[:, cols] = slope.astype(BF16)

    waiting = None
    for j in range(FF // D):
        z = mm(h, wu_ref[:, j * D : (j + 1) * D])
        if waiting is not None:
            act(*waiting)
        waiting = (j, z)
    act(*waiting)


def up_call(core, lengths, seats, x, a, og, vec, group, block=256):
    rows = x.shape[0]
    row_spec = pl.BlockSpec((block, D), lambda i, *s: (i, 0))
    wide_spec = pl.BlockSpec((block, FF), lambda i, *s: (i, 0))
    low, wide = [jax.ShapeDtypeStruct((rows, width), BF16) for width in (D, FF)]
    return pl.pallas_call(
        functools.partial(up_kernel, group),
        name="up",
        grid_spec=pltpu.PrefetchScalarGridSpec(
            num_scalar_prefetch=3,
            grid=(rows // block,),
            in_specs=[row_spec, row_spec, row_spec, whole_spec(vec.shape)] + group.specs(),
            out_specs=[row_spec, row_spec, wide_spec, wide_spec, row_spec],
            scratch_shapes=[
                pltpu.VMEM((D, D), BF16),
                pltpu.VMEM((D, FF), BF16),
                pltpu.SemaphoreType.DMA((2,)),
            ],
        ),
        out_shape=[
            jax.ShapeDtypeStruct((rows, D), F32),
            low,
            wide,
            wide,
            low,
        ],
        compiler_params=params(48),
        cost_estimate=cost(6e9, 30e6, rows * FF),
    )(core, lengths, seats, x, a, og, vec, *group.arrays)


def down_kernel(up_group, down_group, core_ref, len_ref, seat_ref, mid_ref, e_ref, slope_ref, dy_ref, vec_ref, *refs):
    count = len(up_group.arrays)
    up_refs, down_refs = refs[:count], refs[count : count + len(down_group.arrays)]
    (
        theirs_ref, mine_ref, dz_ref, dmb_ref, dm_ref, da_ref, acc_ref, wo_ref, wu_ref, wd_ref, sems,
    ) = refs[-11:]
    block = da_ref.shape[0]
    step, steps = pl.program_id(0), pl.num_programs(0)

    @pl.when(step == 0)
    def _():
        down_group.start(down_refs, core_ref, seat_ref, 0, D // 2, wd_ref, sems.at[2])
        up_group.start(up_refs, core_ref, seat_ref, D // 2, FF // 2, wu_ref, sems.at[1])
        up_group.start(up_refs, core_ref, seat_ref, 0, D // 2, wo_ref, sems.at[0])
        acc_ref[...] = jnp.zeros_like(acc_ref)
        wait_all(wd_ref, sems.at[2])

    mid = mid_ref[...]
    down = vec_ref[7:8, :] + mid + mm(e_ref[...], wd_ref[...])
    pos = row_block(core_ref[0], step, steps) * block + lax.broadcasted_iota(jnp.int32, (block, 1), 0)
    down = jnp.where(pos < len_ref[core_ref[0]], down, 0.0).astype(BF16)

    @pl.when(step < steps // 2)
    def _():
        theirs_ref[...] = down

    @pl.when(step >= steps // 2)
    def _():
        mine_ref[0] = down

    @pl.when(step == 0)
    def _():
        wait_all(wu_ref, sems.at[1])
        wait_all(wo_ref, sems.at[0])

    dy = dy_ref[...]
    add_row(acc_ref, 7, dy.astype(F32))
    dh = None
    waiting = None
    for j in range(FF // D + 1):
        later = None
        if j < FF // D:
            later = (j, mm(dy, wd_ref[j * D : (j + 1) * D, :], NT))
        if waiting is not None:
            at, de = waiting
            cols = slice(at * D, (at + 1) * D)
            dz = (de * slope_ref[:, cols].astype(F32)).astype(BF16)
            dz_ref[:, cols] = dz
            add_row(acc_ref, 8 + at, dz.astype(F32))
            part = mm(dz, wu_ref[:, cols], NT)
            dh = part if dh is None else dh + part
        waiting = later
    normed, scale = norm_parts(mid)
    add_row(acc_ref, 5, dh * normed)
    add_row(acc_ref, 6, dh)
    dm = dy.astype(F32) + norm_back(dh * vec_ref[5:6, :], normed, scale)
    dm_ref[...] = dm
    dm_low = dm.astype(BF16)
    dmb_ref[...] = dm_low
    add_row(acc_ref, 4, dm_low.astype(F32))
    da_ref[...] = mm(dm_low, wo_ref[...], NT).astype(BF16)


def down_call(core, lengths, seats, mid, e, slope, dy, vec, up_group, down_group, block=256):
    rows = mid.shape[0]
    steps = rows // block
    half = steps // 2
    row_spec, wide_spec = [
        pl.BlockSpec((block, width), lambda i, c, *s: (row_block(c[0], i, steps), 0)) for width in (D, FF)
    ]
    return pl.pallas_call(
        functools.partial(down_kernel, up_group, down_group),
        name="down",
        grid_spec=pltpu.PrefetchScalarGridSpec(
            num_scalar_prefetch=3,
            grid=(steps,),
            in_specs=[row_spec, wide_spec, wide_spec, row_spec, whole_spec(vec.shape)]
            + up_group.specs()
            + down_group.specs(),
            out_specs=[
                pl.BlockSpec((block, D), lambda i, *s: (jnp.minimum(i, half - 1), 0)),
                pl.BlockSpec((1, block, D), lambda i, c, *s: (c[0], jnp.maximum(i - half, 0), 0)),
                wide_spec, row_spec, row_spec, row_spec,
                pl.BlockSpec((16, D), lambda i, *s: (0, 0)),
            ],
            scratch_shapes=[
                pltpu.VMEM((D, D), BF16),
                pltpu.VMEM((D, FF), BF16),
                pltpu.VMEM((FF, D), BF16),
                pltpu.SemaphoreType.DMA((3,)),
            ],
        ),
        out_shape=[
            jax.ShapeDtypeStruct((rows // 2, D), BF16),
            jax.ShapeDtypeStruct((2, rows // 2, D), BF16),
            jax.ShapeDtypeStruct((rows, FF), BF16),
            jax.ShapeDtypeStruct((rows, D), BF16),
            jax.ShapeDtypeStruct((rows, D), F32),
            jax.ShapeDtypeStruct((rows, D), BF16),
            jax.ShapeDtypeStruct((16, D), F32),
        ],
        compiler_params=params(48),
        cost_estimate=cost(1.6e10, 35e6),
    )(core, lengths, seats, mid, e, slope, dy, vec, *up_group.arrays, *down_group.arrays)


def pick(values, half, mode):
    if mode == "split":
        width = values.shape[1] // 2
        return [values[:, half * width : (half + 1) * width]]
    return [values[:, at : at + 128] for at in range(half * 128, values.shape[1], 256)]


def weight_grad_kernel(lefts, rights, mode, core_ref, *refs):
    left_refs, right_refs = refs[:lefts], refs[lefts : lefts + sum(rights)]
    own_ref, other_ref = refs[-2:]
    halves = ([], [])
    at = 0
    for left_ref, count in zip(left_refs, rights):
        left = left_ref[...]
        for right_ref in right_refs[at : at + count]:
            whole = mm(left, right_ref[...], TN).astype(BF16)
            for half in range(2):
                halves[half].extend(pick(whole, half, mode))
        at += count
    low, high = [part[0] if len(part) == 1 else jnp.concatenate(part, axis=1) for part in halves]

    @pl.when(core_ref[0] == 0)
    def _():
        own_ref[...] = low
        other_ref[...] = high

    @pl.when(core_ref[0] != 0)
    def _():
        own_ref[...] = high
        other_ref[...] = low


def weight_grad_call(core, products, block, name, mode="split", cols=None):
    rows, height = products[0][0].shape
    lefts = [left for left, _ in products]
    rights = [right for _, group in products for right in group]
    widths = [right.shape[1] if cols is None else cols[0] for right in rights]
    width = sum(widths)
    seat = 0 if cols is None else cols[1]
    return pl.pallas_call(
        functools.partial(weight_grad_kernel, len(lefts), [len(group) for _, group in products], mode),
        name=name,
        grid_spec=pltpu.PrefetchScalarGridSpec(
            num_scalar_prefetch=1,
            grid=(height // block,),
            in_specs=[pl.BlockSpec((rows, block), lambda i, c: (0, i))] * len(lefts)
            + [
                pl.BlockSpec((rows, w), lambda i, c: (0, seat), pipeline_mode=pl.Buffered(1)) for w in widths
            ],
            out_specs=[pl.BlockSpec((block, width // 2), lambda i, c: (i, 0))] * 2,
        ),
        out_shape=[jax.ShapeDtypeStruct((height, width // 2), BF16)] * 2,
        compiler_params=params(16 if mode == "turns" else 48),
        cost_estimate=cost(2 * rows * height * width, rows * (height + width) * 2 + height * width * 2),
    )(core, *lefts, *rights)


def half_grad_kernel(lefts, core_ref, *refs):
    out_ref = refs[-1]
    parts = [mm(refs[at][...], refs[lefts + at][...], TN).astype(BF16) for at in range(lefts)]
    out_ref[...] = parts[0] if lefts == 1 else jnp.concatenate(parts, axis=1)


def half_grad_call(core, products, block, name, other):
    rows, height = products[0][0].shape
    widths = [right.shape[1] // 2 for _, right in products]

    def half(c):
        return 1 - c[0] if other else c[0]

    return pl.pallas_call(
        functools.partial(half_grad_kernel, len(products)),
        name=name,
        grid_spec=pltpu.PrefetchScalarGridSpec(
            num_scalar_prefetch=1,
            grid=(height // block,),
            in_specs=[pl.BlockSpec((rows, block), lambda i, c: (0, i))] * len(products)
            + [
                pl.BlockSpec((rows, width), lambda i, c: (0, half(c)), pipeline_mode=pl.Buffered(1))
                for width in widths
            ],
            out_specs=pl.BlockSpec((block, sum(widths)), lambda i, c: (i, 0)),
        ),
        out_shape=jax.ShapeDtypeStruct((height, sum(widths)), BF16),
        compiler_params=params(48),
        cost_estimate=cost(2 * rows * height * sum(widths), rows * (height + sum(widths)) * 2 + height * sum(widths) * 2),
    )(core, *[left for left, _ in products], *[right for _, right in products])


def last_kernel(
    core_ref, x_ref, dm_ref, dq_ref, dk_ref, dv_ref, w_ref, vec_ref, before_ref, theirs_ref, mine_ref, acc_ref
):
    step, steps = pl.program_id(0), pl.num_programs(0)

    @pl.when(step == 0)
    def _():
        acc_ref[...] = before_ref[...]

    subs = sub_blocks(x_ref.shape[0])

    def product(rows):
        return (
            mm(dq_ref[rows, :], w_ref[:D])
            + mm(dk_ref[rows, :], w_ref[D : 2 * D])
            + mm(dv_ref[rows, :], w_ref[2 * D :])
        )

    grads = []
    dh = product(subs[0])
    add_row(acc_ref, 2, dq_ref[...].astype(F32))
    add_row(acc_ref, 3, dv_ref[...].astype(F32))
    for at, rows in enumerate(subs):
        later = product(subs[at + 1]) if at + 1 < len(subs) else None
        normed, scale = norm_parts(x_ref[rows, :].astype(F32))
        add_row(acc_ref, 0, dh * normed)
        add_row(acc_ref, 1, dh)
        grads.append(dm_ref[rows, :] + norm_back(dh * vec_ref[0:1, :], normed, scale))
        dh = later

    @pl.when(step < steps // 2)
    def _():
        for rows, grad in zip(subs, grads):
            theirs_ref[rows, :] = grad

    @pl.when(step >= steps // 2)
    def _():
        for rows, grad in zip(subs, grads):
            mine_ref[0, rows, :] = grad


def last_call(core, x, dm, dq, dk, dv, w, vec, before, block=256):
    rows = x.shape[0]
    steps = rows // block
    half = steps // 2
    row_spec = pl.BlockSpec((block, D), lambda i, c, *s: (row_block(c[0], i, steps), 0))
    return pl.pallas_call(
        last_kernel,
        name="last",
        grid_spec=pltpu.PrefetchScalarGridSpec(
            num_scalar_prefetch=1,
            grid=(steps,),
            in_specs=[row_spec] * 5 + [whole_spec(part.shape) for part in (w, vec, before)],
            out_specs=[
                pl.BlockSpec((block, D), lambda i, *s: (jnp.minimum(i, half - 1), 0)),
                pl.BlockSpec((1, block, D), lambda i, c, *s: (c[0], jnp.maximum(i - half, 0), 0)),
                pl.BlockSpec((16, D), lambda i, *s: (0, 0)),
            ],
        ),
        out_shape=[
            jax.ShapeDtypeStruct((rows // 2, D), F32),
            jax.ShapeDtypeStruct((2, rows // 2, D), F32),
            jax.ShapeDtypeStruct((16, D), F32),
        ],
        compiler_params=params(12),
        cost_estimate=cost(rows * 6 * D * D, 16e6),
    )(core, x, dm, dq, dk, dv, w, vec, before)


def adam_kernel(plans, sources, core_ref, *refs):
    halves = [refs[2 * i : 2 * i + 2] for i in range(sources)]
    count = len(plans)
    states = refs[2 * sources : 2 * sources + 3 * count]
    outs = refs[2 * sources + 3 * count : 2 * sources + 6 * count]
    grads = refs[2 * sources + 6 * count :]
    for core in range(2):

        @pl.when(core_ref[0] == core)
        def _():
            for (_, _, moves), grad_ref in zip(plans, grads):
                for source, start, width, place0, place1 in moves:
                    for half, place in ((0, place0), (1, place1)):
                        ref = halves[source][0 if half == core else 1]
                        grad_ref[:, place : place + width] = ref[:, start : start + width].astype(F32)

    for i, (rate, decay, _) in enumerate(plans):
        weight, first, second = states[3 * i : 3 * i + 3]
        new = adamw(weight[...], grads[i][...], first[...], second[...], rate, decay)
        for out, value in zip(outs[3 * i : 3 * i + 3], new):
            out[...] = value


def adam_call(core, halves, states, plans):
    flat = [part for pair in halves for part in pair]
    held = [part for state in states for part in state]
    spec = pl.BlockSpec(memory_space=pltpu.VMEM)
    news = pl.pallas_call(
        functools.partial(adam_kernel, plans, len(halves)),
        name="adam",
        in_specs=[pl.BlockSpec(memory_space=pltpu.SMEM)] + [spec] * (len(flat) + len(held)),
        out_specs=[spec] * len(held),
        out_shape=[jax.ShapeDtypeStruct(part.shape, F32) for part in held],
        scratch_shapes=[pltpu.VMEM(state[0].shape, F32) for state in states],
        compiler_params=params(12),
        cost_estimate=cost(1e6, 24 * sum(state[0].size for state in states)),
    )(core, *flat, *held)
    return [news[3 * i : 3 * i + 3] for i in range(len(states))]


def after(value, *others):
    if not others:
        return value
    return lax.optimization_barrier((value,) + others)[0]


def cut(array, axis, index, size=1):
    starts = [jnp.uint32(0)] * array.ndim
    sizes = list(array.shape)
    starts[axis], sizes[axis] = index, size
    return lax.dynamic_slice(array, starts, sizes)


class Grid:
    def __init__(self, chips):
        log = chips.bit_length() - 1
        side = 1 << (log // 3)
        if side * side * (chips // (side * side)) != chips:
            side = 1
        self.chips = chips
        self.n = side
        self.nz = chips // (side * side)
        self.core = lax.axis_index("seq")
        self.chip = lax.axis_index("dp")
        self.x = self.chip % side
        self.y = self.chip // side % side
        self.z = self.chip // (side * side)

    def pin(self, value):
        n, core = self.n, self.core
        first, second = self.coords(core)
        places = {
            "core": core,
            "other": 1 - core,
            "chip": self.chip,
            "seats": self.seats(True),
            "q_seats": self.seats(False),
        }
        for s in range(n):
            for t in range(n):
                places["plane", s, t] = self.plane((first + s) % n, (second + t) % n, core)
        for at in range(self.nz):
            places["z", at] = self.z ^ at
        names = list(places)
        held = lax.optimization_barrier((value, *[places[name].astype(jnp.uint32) for name in names]))
        self.places = dict(zip(names, held[1:]))
        return held[0]

    def plane(self, first, second, core):
        return jnp.where(core == 0, second * self.n + first, first * self.n + second)

    def coords(self, core):
        return jnp.where(core == 0, self.x, self.y), jnp.where(core == 0, self.y, self.x)

    def permute(self, value, axis, shift=0):
        pairs = []
        for chip in range(self.chips):
            for core in range(2):
                x, y, z = chip % self.n, chip // self.n % self.n, chip // (self.n * self.n)
                to_core = core
                if axis == "z":
                    z = (z + shift) % self.nz
                elif axis == "zx":
                    z = z ^ shift
                elif axis == "core":
                    to_core = 1 - core
                elif (axis == "first") == (core == 0):
                    x = (x + shift) % self.n
                else:
                    y = (y + shift) % self.n
                pairs.append((chip * 2 + core, ((z * self.n + y) * self.n + x) * 2 + to_core))
        return lax.ppermute(value, ("dp", "seq"), pairs)

    def swap(self, value):
        return self.permute(value, "core")

    def join(self, own, other, axis):
        return jnp.where(
            self.places["core"] == 0,
            jnp.concatenate([own, other], axis),
            jnp.concatenate([other, own], axis),
        )

    def seats(self, halving):
        found = []
        for half in range(2):
            core = self.core if half == 0 else 1 - self.core
            first, second = self.coords(core)
            for s2 in range(self.n):
                for s1 in range(self.n):
                    flat = self.plane((first - s1) % self.n, (second - s2) % self.n, core)
                    for sz in range(self.nz):
                        z = self.z ^ sz if halving else (self.z - sz) % self.nz
                        found.append(z * self.n * self.n + flat)
        return jnp.stack(found).astype(jnp.int32)

    def total_small(self, value, *untils):
        steps = [("core", 0), ("first", 1), ("second", 1)] if self.n == 2 else [("core", 0)]
        if self.n != 2:
            for axis in ("first", "second"):
                value = value + sum(self.permute(value, axis, s) for s in range(1, self.n))
        bit = 1
        while bit < self.nz:
            steps.append(("zx", bit))
            bit *= 2
        for at, (axis, shift) in enumerate(steps):
            until = untils[at] if at < len(untils) else ()
            value = value + after(self.permute(value, axis, shift), *until)
        return value

    def gather_z(self, block, *until):
        return jnp.stack([block] + [after(self.permute(block, "z", s), *until) for s in range(1, self.nz)])

    def gather_bit(self, held, bit, *until):
        return jnp.concatenate([held, after(self.permute(held, "zx", bit), *until)])

    def along(self, axis, column, *until):
        return [after(self.permute(column, axis, s), *until) for s in range(1, self.n)]

    def plane_parts(self, column, firsts, seconds, passed):
        parts = [column] + firsts
        for s2 in range(1, self.n):
            parts += [seconds[s2 - 1]] + [passed[s1 - 1][s2 - 1] for s1 in range(1, self.n)]
        return [part[None] for part in parts]

    def gather_first(self, column, *until):
        return jnp.stack([column] + [after(self.permute(column, "first", s), *until) for s in range(1, self.n)])

    def gather_second(self, line, *until):
        return [after(self.permute(line, "second", s), *until) for s in range(1, self.n)]

    def scatter_first(self, own, pair, *until):
        rows, cols = own.shape[0] // self.chips, own.shape[1]
        n = self.n

        def seat(s1, s2):
            own_part, pair_part = [
                cut(part.reshape(self.nz, n * n, rows, cols), 1, self.places["plane", s1, s2]).astype(F32)
                for part in (own, pair)
            ]
            return own_part + pair_part

        kept = [seat(0, t) for t in range(n)]
        for s in range(1, n):
            send = jnp.stack([seat(s, t).astype(BF16) for t in range(n)])
            got = after(self.permute(send, "first", s), *until)
            kept = [kept[t] + got[t].astype(F32) for t in range(n)]
        return kept[0], [part.astype(BF16) for part in kept[1:]]

    def scatter_second(self, kept, *until):
        mine, rest = kept
        got = [after(self.permute(rest[s - 1], "second", s), *until) for s in range(1, self.n)]
        for part in got:
            mine = mine + part.astype(F32)
        return mine.reshape((self.nz,) + mine.shape[2:]), got

    def order_z(self, mine):
        return [cut(mine, 0, self.places["z", at])[0] for at in range(self.nz)]

    def scatter_bit(self, parts, *until):
        half = len(parts) // 2
        send = parts[half] if half == 1 else jnp.stack([part.astype(BF16) for part in parts[half:]])
        got = after(self.permute(send.astype(BF16), "zx", half), *until)
        if half == 1:
            return [parts[0] + got.astype(F32)], got
        return [part + got[at].astype(F32) for at, part in enumerate(parts[:half])], got

    def scatter_z(self, parts, *until):
        while len(parts) > 1:
            parts, _ = self.scatter_bit(parts, *until)
        return parts[0]


def adamw(weight, gradient, first_moment, second_moment, step_rate, weight_decay):
    first_moment = BETA_ONE * first_moment + (1.0 - BETA_ONE) * gradient
    second_moment = BETA_TWO * second_moment + (1.0 - BETA_TWO) * gradient * gradient
    first_fix = 1.0 - BETA_ONE**STEP
    second_fix = 1.0 - BETA_TWO**STEP
    direction = first_moment / first_fix / (jnp.sqrt(second_moment / second_fix) + EPS_ADAM)
    return (weight - step_rate * (direction + weight_decay * weight), first_moment, second_moment)


def local(
    block_in, lengths, out_grad, w_qkv, w_out, w_up, w_down, vectors,
    first_qkv, first_out, first_up, first_down, first_vectors,
    second_qkv, second_out, second_up, second_down, second_vectors,
):
    grid = Grid(lax.axis_size("dp"))
    core = grid.core
    w_qkv_first = grid.pin(w_qkv)
    places = grid.places
    core_arr = places["core"].reshape(1).astype(jnp.int32)
    half_len = block_in.shape[1]
    vec_count, vec_here = vectors.shape

    def own_slot(halves):
        mine, theirs = [cut(halves, 0, places[name])[0] for name in ("core", "other")]
        return grid.join(mine, grid.swap(theirs), 0)

    def both_slots(mine, got):
        zero = jnp.uint32(0)
        return lax.dynamic_update_slice(mine, got[None], (places["other"], zero, zero))

    def half_of(shard):
        width = shard.shape[1] // 2
        return jnp.where(places["core"] == 0, shard[:, :width], shard[:, width:]).astype(BF16)

    seats, q_seats = [places[name].astype(jnp.int32) for name in ("seats", "q_seats")]

    turned = jnp.pad(vectors.T.astype(BF16), ((0, 0), (0, 128 - vec_count)))
    q_block = jnp.concatenate([half_of(w_qkv_first), turned], axis=1)
    u_block = jnp.concatenate([half_of(w_out), half_of(w_up)], axis=1)
    d_block = half_of(w_down)
    q_col = grid.gather_z(q_block)
    x = own_slot(block_in)
    bits = [1 << at for at in range((grid.nz - 1).bit_length())]
    u_col, d_col = u_block[None], d_block[None]
    for bit in bits[:-1]:
        u_col = grid.gather_bit(u_col, bit)
        d_col = grid.gather_bit(d_col, bit)
    q_line = after(grid.gather_first(q_col, x), u_col, d_col)
    q_rest = grid.gather_second(q_line)
    u_col = grid.gather_bit(after(u_col, q_line), bits[-1])
    q_line_swap = grid.swap(q_line)
    q_rest_swap = [grid.swap(after(part, u_col)) for part in q_rest]
    q_group = finish_group(grid, q_seats, [q_line] + q_rest, [q_line_swap] + q_rest_swap)

    h1, qkv, vec, w_back = qkv_call(core_arr, q_seats, x, q_group)
    u_firsts = grid.along("first", u_col, qkv)
    d_col = grid.gather_bit(after(d_col, u_col), bits[-1], qkv)
    og = own_slot(after(out_grad, qkv))
    att = attend_call(core_arr, lengths, after(qkv, d_col, *u_firsts), 0, 4, ())
    u_seconds = grid.along("second", u_col, *att)
    u_passed = [grid.along("second", part, *att) for part in u_firsts]
    early = [after(grid.swap(part), *att) for part in [u_col] + u_firsts]
    d_col = after(d_col, *u_seconds, *[part for parts in u_passed for part in parts])
    a, lse = attend_call(core_arr, lengths, after(qkv, d_col), 4, 2, att)
    late_seconds = [after(grid.swap(part), a) for part in u_seconds]
    late_passed = [[after(grid.swap(part), a) for part in parts] for parts in u_passed]
    u_group = finish_group(
        grid,
        seats,
        grid.plane_parts(u_col, u_firsts, u_seconds, u_passed),
        grid.plane_parts(early[0], early[1:], late_seconds, late_passed),
    )
    mid, h2, e, slope, dy = up_call(core_arr, lengths, seats, x, a, og, vec, u_group)
    d_firsts = grid.along("first", d_col, mid)
    d_seconds = grid.along("second", d_col, mid)
    d_col_swap = after(grid.swap(d_col), mid)
    d_own, d_other = weight_grad_call(
        core_arr, [(after(e, *d_firsts, *d_seconds), [dy])], 512, "grad_down"
    )
    d_passed = [grid.along("second", part, d_own) for part in d_firsts]
    early = [[after(grid.swap(part), d_own) for part in parts] for parts in (d_firsts, d_seconds)]
    d_group = finish_group(
        grid,
        seats,
        grid.plane_parts(d_col, d_firsts, d_seconds, d_passed),
        grid.plane_parts(d_col_swap, *early, [[grid.swap(part) for part in parts] for parts in d_passed]),
    )
    out_theirs, out_mine, dz, dmb, dm, da, acc_mid = down_call(
        core_arr, lengths, seats, mid, e, slope, dy, vec, u_group, d_group
    )

    d_pair = after(grid.swap(d_other), dz)
    u_other = half_grad_call(core_arr, [(a, dmb), (h2, after(dz, d_pair))], 384, "grad_up", True)
    u_own = half_grad_call(core_arr, [(a, dmb), (h2, after(dz, u_other))], 384, "grad_up", False)
    d_kept = grid.scatter_first(d_own, d_pair, u_own)

    def back_call(start, count, before, *needs):
        return attend_back_call(core_arr, lengths, qkv, a, after(da, *needs), lse, start, count, before)

    back = back_call(0, 1, (), u_own, *d_kept[1])
    u_pair = after(grid.swap(u_other), *back)
    d_sum, d_here = grid.scatter_second(d_kept, *back)
    back = back_call(1, 3, back, u_pair, *d_here)
    u_kept = grid.scatter_first(u_own, u_pair, *back)
    d_parts, d_got = grid.scatter_bit(grid.order_z(d_sum), *back)
    back = back_call(4, 2, back, d_got, *u_kept[1])
    u_sum, u_here = grid.scatter_second(u_kept, *back)
    dq, dk, dv = back
    block_out = both_slots(out_mine, after(grid.swap(after(out_theirs, back[0])), dq))
    q_own, q_other = weight_grad_call(
        core_arr, [(h1, [after(dq, *u_here), dk, dv])], 384, "grad_qkv", "turns"
    )
    q_pair = grid.swap(q_other)
    in_theirs, in_mine, acc = last_call(
        core_arr, x, dm, after(dq, q_own, q_pair), dk, dv, w_back, vec, acc_mid
    )
    d_mine = grid.scatter_z(d_parts, in_theirs)
    d_other_mine = grid.swap(d_mine)
    q_kept = grid.scatter_first(q_own, q_pair, in_theirs)
    u_parts, u_got = grid.scatter_bit(grid.order_z(u_sum), *q_kept[1])
    q_sum, q_here = grid.scatter_second(q_kept, u_got)
    down_new, = adam_call(
        core_arr,
        [(d_mine, d_other_mine)],
        [(after(w_down, *q_kept[1]), first_down, second_down)],
        [(FF ** (-0.5), MATRIX_DECAY, [(0, 0, D // 2, 0, D // 2)])],
    )
    in_got = grid.swap(after(in_theirs, *q_kept[1]))
    u_mine = grid.scatter_z([after(part, *q_here) for part in u_parts])
    u_other_mine = grid.swap(u_mine)
    in_grad = both_slots(in_mine, after(in_got, *q_here))
    q_parts, q_got = grid.scatter_bit(grid.order_z(q_sum), in_grad)
    q_gots = [(q_got,)]
    while len(q_parts) > 1:
        q_parts, q_got = grid.scatter_bit(q_parts)
        q_gots.append((q_got,))
    q_mine = q_parts[0]
    q_other_mine = grid.swap(q_mine)
    vec_total = grid.total_small(acc, (), q_kept[1], q_here, *q_gots)

    half, wide = D // 2, FF // 2
    out_new, up_new = adam_call(
        core_arr,
        [(u_mine, u_other_mine)],
        [(after(w_out, in_grad), first_out, second_out), (w_up, first_up, second_up)],
        [
            ((D // 64) ** (-0.5), MATRIX_DECAY, [(0, 0, half, 0, half)]),
            (D ** (-0.5), MATRIX_DECAY, [(0, half, wide, 0, wide)]),
        ],
    )
    moves = []
    for turn in range(3 * D // 256):
        moves.append((0, turn * 128, 128, turn * 256, turn * 256 + 128))
    qkv_new, = adam_call(
        core_arr,
        [(q_mine, q_other_mine)],
        [(w_qkv, first_qkv, second_qkv)],
        [(D ** (-0.5), MATRIX_DECAY, moves)],
    )
    vec_grad = cut(vec_total[:vec_count].reshape(vec_count, -1, vec_here), 1, places["chip"])[:, 0]
    vec_new = adamw(vectors, vec_grad, first_vectors, second_vectors, VECTOR_RATE, 0.0)
    news = [qkv_new, out_new, up_new, down_new, vec_new]
    return (block_out, in_grad) + tuple(new[kind] for kind in range(3) for new in news)


def finish_group(grid, seats, own, other):
    rows, cols = own[0].shape[-2:]
    if rows % 16 == 0:
        return Pieces(own + other, rows)
    found = []
    for half, parts in enumerate((own, other)):
        here = seats[half * grid.chips : (half + 1) * grid.chips]
        order = jnp.zeros((grid.chips,), jnp.int32).at[here].set(jnp.arange(grid.chips, dtype=jnp.int32))
        blocks = jnp.concatenate(parts).reshape(grid.chips, rows, cols)
        found.append(jnp.take(blocks, order, axis=0).reshape(1, 1, grid.chips * rows, cols))
    return Pieces(found, grid.chips * rows, True)


def solution(mesh):
    weight = P("dp", None)
    vector = P(None, "dp")
    state = (weight, weight, weight, weight, vector)
    tokens = P("dp", "seq", None)
    return jax.shard_map(
        local,
        mesh=mesh,
        in_specs=(tokens, P("dp"), tokens) + state * 3,
        out_specs=(tokens, tokens) + state * 3,
        check_vma=False,
    )
```

```python
import functools

import jax
import jax.numpy as jnp
from jax import lax
from jax.experimental import pallas as pl
from jax.experimental.pallas import tpu as pltpu
from jax.sharding import PartitionSpec as P

D = 768
HEADS = 12
HEAD_DIM = 64
FF = 3072
STEP = 10

EPS_NORM = 1e-05
EPS_ADAM = 1e-08
BETA_ONE = 0.5
BETA_TWO = 0.5
MATRIX_DECAY = 0.1
VECTOR_RATE = 0.1
NEG_FILL = -1e30
GELU_ROOT = 0.7978845608028654
GELU_CUBE = 0.044715
QKV_HALF = 3 * D // 2

F32 = jnp.float32
BF16 = jnp.bfloat16

NN = (((1,), (0,)), ((), ()))
NT = (((1,), (1,)), ((), ()))
TN = (((0,), (0,)), ((), ()))


def mm(left, right, dims=NN):
    return lax.dot_general(left, right, dims, preferred_element_type=F32)


def cost(flops, nbytes, trans=0):
    return pl.CostEstimate(flops=int(4 * flops), bytes_accessed=int(4 * nbytes), transcendentals=int(trans))


def params(mib=60):
    return pltpu.CompilerParams(vmem_limit_bytes=mib * 1024 * 1024)


def held_spec():
    return pl.BlockSpec(memory_space=pltpu.VMEM)


def at_rows(block):
    return pl.ds(pl.multiple_of(pl.program_id(0) * block, block), block)


def whole_spec(shape):
    return pl.BlockSpec(shape, lambda *idx: (0,) * len(shape), pipeline_mode=pl.Buffered(1))


class Pieces:
    def __init__(self, arrays, rows, ordered=False):
        self.arrays = arrays
        self.rows = rows
        self.ordered = ordered
        self.halves = 2
        self.count = len(arrays) // self.halves
        self.lines, self.depth = arrays[0].shape[:2]

    def specs(self):
        return [pl.BlockSpec(memory_space=pltpu.HBM)] * len(self.arrays)

    def row(self, seat_ref, at):
        return 0 if self.ordered else pl.multiple_of(seat_ref[at] * self.rows, 16)

    def start(self, refs, core_ref, seat_ref, start_col, width, target, sem):
        core = core_ref[0]
        at = 0
        for half in range(self.halves):
            where = core if half == 0 else 1 - core
            for s2 in range(self.count):
                ref = refs[half * self.count + s2]
                for s1 in range(self.lines):
                    for sz in range(self.depth):
                        row = self.row(seat_ref, at)
                        at += 1
                        col = pl.multiple_of(where * width, 128)
                        pltpu.make_async_copy(
                            ref.at[s1, sz, :, pl.ds(start_col, width)],
                            target.at[pl.ds(row, self.rows), pl.ds(col, width)],
                            sem,
                        ).start()

    def start_once(self, refs, seat_ref, start_col, width, target, sem):
        at = 0
        for s2 in range(self.count):
            for s1 in range(self.lines):
                for sz in range(self.depth):
                    row = self.row(seat_ref, at)
                    at += 1
                    pltpu.make_async_copy(
                        refs[s2].at[s1, sz, :, pl.ds(start_col, width)],
                        target.at[pl.ds(row, self.rows), :],
                        sem,
                    ).start()


def wait_all(target, sem):
    pltpu.make_async_copy(target, target, sem).wait()


def norm_parts(rows):
    mean = jnp.mean(rows, axis=-1, keepdims=True)
    centred = rows - mean
    variance = jnp.mean(centred * centred, axis=-1, keepdims=True)
    scale = lax.rsqrt(variance + EPS_NORM)
    return centred * scale, scale


def norm_back(d_normed, normed, scale):
    first = jnp.mean(d_normed, axis=-1, keepdims=True)
    second = jnp.mean(d_normed * normed, axis=-1, keepdims=True)
    return scale * (d_normed - first - normed * second)


def qkv_kernel(group, core_ref, seat_ref, x_ref, *refs):
    refs, (h_ref, qkv_ref, vec_ref, back_ref, w_ref, turned_ref, sems) = refs[:-7], refs[-7:]

    @pl.when(pl.program_id(0) == 0)
    def _():
        group.start(refs, core_ref, seat_ref, 0, QKV_HALF, w_ref, sems.at[0])
        group.start_once(refs, seat_ref, QKV_HALF, 128, turned_ref, sems.at[1])
        wait_all(turned_ref, sems.at[1])
        vec_ref[...] = turned_ref[...].astype(F32).T[:16]
        wait_all(w_ref, sems.at[0])

    def norm(rows):
        normed, _ = norm_parts(x_ref[rows, :].astype(F32))
        h = (normed * vec_ref[0:1, :] + vec_ref[1:2, :]).astype(BF16)
        h_ref[rows, :] = h
        return h

    block = x_ref.shape[0]
    h = norm(slice(0, block))
    for part, bias in enumerate((2, None, 3)):
        cols = slice(part * D, (part + 1) * D)
        product = mm(h, w_ref[:, cols])
        if bias is not None:
            product = product + vec_ref[bias : bias + 1, :]
        qkv_ref[:, cols] = product.astype(BF16)

    @pl.when(pl.program_id(0) < 3)
    def _():
        back_ref[...] = w_ref[:, at_rows(D)].T


def sub_blocks(rows):
    return [slice(at, at + 256) for at in range(0, rows, 256)]


def qkv_call(core, seats, x, group, block=256):
    rows = x.shape[0]
    return pl.pallas_call(
        functools.partial(qkv_kernel, group),
        name="qkv",
        grid_spec=pltpu.PrefetchScalarGridSpec(
            num_scalar_prefetch=2,
            grid=(rows // block,),
            in_specs=[pl.BlockSpec((block, D), lambda i, *s: (i, 0))] + group.specs(),
            out_specs=[
                pl.BlockSpec((block, D), lambda i, *s: (i, 0)),
                pl.BlockSpec((block, 3 * D), lambda i, *s: (i, 0)),
                pl.BlockSpec((16, D), lambda i, *s: (0, 0)),
                pl.BlockSpec((D, D), lambda i, *s: (jnp.minimum(i, 2), 0)),
            ],
            scratch_shapes=[
                pltpu.VMEM((D, 3 * D), BF16),
                pltpu.VMEM((D, 128), BF16),
                pltpu.SemaphoreType.DMA((2,)),
            ],
        ),
        out_shape=[
            jax.ShapeDtypeStruct((rows, D), BF16),
            jax.ShapeDtypeStruct((rows, 3 * D), BF16),
            jax.ShapeDtypeStruct((16, D), F32),
            jax.ShapeDtypeStruct((3 * D, D), BF16),
        ],
        compiler_params=params(12),
        cost_estimate=cost(2 * rows * D * 3 * D, 10e6),
    )(core, seats, x, *group.arrays)


def head_parts(length, k_all, q_turned, head):
    full_len = k_all.shape[0]
    lane = lax.broadcasted_iota(jnp.int32, (1, 128), 1)
    row = lax.broadcasted_iota(jnp.int32, (128, 1), 0)
    zero, one = jnp.zeros((), BF16), jnp.ones((), BF16)
    mine = (lane // HEAD_DIM) == head
    spare = HEAD_DIM * (1 - head)
    pos = lax.broadcasted_iota(jnp.int32, (full_len, 128), 0)
    fill = jnp.where(pos < length, 0.0, NEG_FILL).astype(BF16)
    k_head = jnp.where(mine, k_all, jnp.where(lane == spare, fill, zero))
    q_head = jnp.where((row // HEAD_DIM) == head, q_turned, jnp.where(row == spare, one, zero))
    return mine, k_head, q_head


def causal_mask(scores, block):
    full = scores.shape[0]
    key_pos = lax.broadcasted_iota(jnp.int32, (block, block), 0)
    query_pos = lax.broadcasted_iota(jnp.int32, (block, block), 1)
    last = jnp.where(key_pos <= query_pos, scores[full - block :], NEG_FILL)
    if full == block:
        return last
    return jnp.concatenate([scores[: full - block], last], axis=0)


def attend_kernel(start, core_ref, len_ref, qkv_ref, *refs):
    a_ref, lse_ref, mixed_ref, scores_ref = refs[-4:]
    block = 256
    full_len = qkv_ref.shape[0]
    length = len_ref[core_ref[0]]
    q_all, k_all, v_all = [
        qkv_ref[:, pl.ds(pl.multiple_of((pl.program_id(0) + start) * 128 + part * D, 128), 128)] for part in range(3)
    ]
    q_all = q_all * jnp.asarray(HEAD_DIM ** (-0.5), BF16)
    v_turned = v_all.T
    q_turned = q_all.T
    ones = jnp.ones((16, full_len), BF16)
    parts = []
    for head in range(2):
        _, k_head, q_head = head_parts(length, k_all, q_turned, head)
        v_head = jnp.concatenate([v_turned[head * HEAD_DIM : (head + 1) * HEAD_DIM], ones], axis=0)
        parts.append((k_head, q_head, v_head))
    units = [(head, j) for j in reversed(range(full_len // block)) for head in range(2)]

    def score(at):
        head, j = units[at]
        k_head, q_head, _ = parts[head]
        top = None
        for i in range(j + 1):
            rows = slice(i * block, (i + 1) * block)
            tile = mm(k_head[rows], q_head[:, j * block : (j + 1) * block])
            if i == j:
                tile = causal_mask(tile, block)
            scores_ref[at % 2, rows, :] = tile
            part = jnp.max(tile.reshape(block // 8, 8, block), axis=0)
            top = part if top is None else jnp.maximum(top, part)
        return jnp.max(top, axis=0, keepdims=True)

    def finish(at, top):
        head, j = units[at]
        v_head = parts[head][2]
        cols = slice(j * block, (j + 1) * block)
        mixed = None
        for i in range(j + 1):
            rows = slice(i * block, (i + 1) * block)
            exped = jnp.exp(scores_ref[at % 2, rows, :] - top).astype(BF16)
            part = mm(v_head[:, rows], exped)
            mixed = part if mixed is None else mixed + part
        total = mixed[HEAD_DIM : HEAD_DIM + 1]
        mixed_ref[head * HEAD_DIM : (head + 1) * HEAD_DIM, cols] = mixed[:HEAD_DIM] / total
        lse_ref[0, head : head + 1, cols] = top + jnp.log(total)

    top = score(0)
    for at in range(len(units)):
        later = score(at + 1) if at + 1 < len(units) else None
        finish(at, top)
        top = later
    a_ref[...] = mixed_ref[...].T.astype(BF16)


def attend_call(core, lengths, qkv, first, count, before):
    rows = qkv.shape[0]
    pairs = HEADS // 2
    before = list(before)
    return pl.pallas_call(
        functools.partial(attend_kernel, first),
        name="attend",
        grid_spec=pltpu.PrefetchScalarGridSpec(
            num_scalar_prefetch=2,
            grid=(count,),
            in_specs=[held_spec()] + [pl.BlockSpec(memory_space=pl.ANY)] * len(before),
            out_specs=[
                pl.BlockSpec((rows, 128), lambda i, c, n: (0, i + first)),
                pl.BlockSpec((1, 8, rows), lambda i, c, n: (i + first, 0, 0)),
            ],
            scratch_shapes=[pltpu.VMEM((128, rows), F32), pltpu.VMEM((2, rows, 256), F32)],
        ),
        out_shape=[
            jax.ShapeDtypeStruct((rows, D), BF16),
            jax.ShapeDtypeStruct((pairs, 8, rows), F32),
        ],
        input_output_aliases={3 + i: i for i in range(len(before))},
        compiler_params=params(12),
        cost_estimate=cost(3e9 * count, 1.2e6 * count, 2 * rows * rows * 0.6 * count),
    )(core, lengths, qkv, *before)


def attend_back_kernel(core_ref, len_ref, q_ref, k_ref, v_ref, a_ref, da_ref, lse_ref, *refs):
    dq_ref, dk_ref, dv_ref, dqt_ref, dk_acc, dv_acc = refs[-6:]
    block = 256
    full_len = q_ref.shape[0]
    length = len_ref[core_ref[0]]
    scale = HEAD_DIM ** (-0.5)
    q_all = q_ref[...] * jnp.asarray(scale, BF16)
    k_all = k_ref[...]
    k_turned = k_all.T
    v_all = v_ref[...]
    da_all = da_ref[...]
    inner = (da_all.astype(F32) * a_ref[...].astype(F32)).T
    q_turned, da_turned = q_all.T, da_all.T
    parts = []
    for head in range(2):
        mine, k_head, q_head = head_parts(length, k_all, q_turned, head)
        zero = jnp.zeros((), BF16)
        q_plain = jnp.where(mine, q_all, zero)
        da_head = jnp.where(mine, da_all, zero)
        row = lax.broadcasted_iota(jnp.int32, (128, 1), 0)
        da_cols = jnp.where((row // HEAD_DIM) == head, da_turned, zero)
        lanes = slice(head * HEAD_DIM, (head + 1) * HEAD_DIM)
        centre = jnp.sum(inner[lanes], axis=0, keepdims=True)
        parts.append((k_head, q_plain, q_head, da_head, da_cols, lanes, centre))
    units = [
        (head, j, i)
        for j in reversed(range(full_len // block))
        for head in range(2)
        for i in range(j + 1)
    ]

    def score(at):
        head, j, i = units[at]
        k_head, _, q_head, _, da_cols, _, _ = parts[head]
        rows, cols = slice(i * block, (i + 1) * block), slice(j * block, (j + 1) * block)
        tile = mm(k_head[rows], q_head[:, cols])
        if i == j:
            tile = causal_mask(tile, block)
        return tile, mm(v_all[rows], da_cols[:, cols])

    seen = set()
    ready = score(0)
    dq_part = None
    for at, (head, j, i) in enumerate(units):
        later = score(at + 1) if at + 1 < len(units) else None
        scores, d_probs = ready
        _, q_plain, _, da_head, _, lanes, centre = parts[head]
        rows, cols = slice(i * block, (i + 1) * block), slice(j * block, (j + 1) * block)
        probs = jnp.exp(scores - lse_ref[0, head : head + 1, cols])
        d_scores = (probs * (d_probs - centre[:, cols])).astype(BF16)
        dv_part = mm(probs.astype(BF16), da_head[cols])
        dk_part = mm(d_scores, q_plain[cols])
        if i in seen:
            dv_acc[rows] += dv_part
            dk_acc[rows] += dk_part
        else:
            seen.add(i)
            dv_acc[rows] = dv_part
            dk_acc[rows] = dk_part
        part = mm(k_turned[lanes, rows], d_scores)
        dq_part = part if i == 0 else dq_part + part
        if i == j:
            dqt_ref[lanes, cols] = dq_part * scale
        ready = later
    dq_ref[...] = dqt_ref[...].T.astype(BF16)
    dk_ref[...] = dk_acc[...].astype(BF16)
    dv_ref[...] = dv_acc[...].astype(BF16)


def attend_back_call(core, lengths, qkv, a, da, lse, start, count, before):
    rows = qkv.shape[0]
    pairs = HEADS // 2
    before = list(before)
    pair_spec = pl.BlockSpec((rows, 128), lambda i, c, n: (0, i + start))
    return pl.pallas_call(
        attend_back_kernel,
        name="attend_back",
        grid_spec=pltpu.PrefetchScalarGridSpec(
            num_scalar_prefetch=2,
            grid=(count,),
            in_specs=[
                pair_spec,
                pl.BlockSpec((rows, 128), lambda i, c, n: (0, i + start + pairs)),
                pl.BlockSpec((rows, 128), lambda i, c, n: (0, i + start + 2 * pairs)),
                pair_spec,
                pair_spec,
                pl.BlockSpec((1, 8, rows), lambda i, c, n: (i + start, 0, 0)),
            ]
            + [pl.BlockSpec(memory_space=pl.ANY)] * len(before),
            out_specs=[pair_spec, pair_spec, pair_spec],
            scratch_shapes=[
                pltpu.VMEM((128, rows), F32),
                pltpu.VMEM((rows, 128), F32),
                pltpu.VMEM((rows, 128), F32),
            ],
        ),
        out_shape=[jax.ShapeDtypeStruct((rows, D), BF16)] * 3,
        input_output_aliases={8 + i: i for i in range(len(before))},
        compiler_params=params(16),
        cost_estimate=cost(6e9 * count, 2e6 * count, 2 * rows * rows * 0.6 * count),
    )(core, lengths, qkv, qkv, qkv, a, da, lse, *before)


def valid_rows(core_ref, len_ref, block):
    pos = pl.program_id(0) * block + lax.broadcasted_iota(jnp.int32, (block, 1), 0)
    return pos < len_ref[core_ref[0]]


def add_row(acc_ref, row, value):
    acc_ref[row : row + 1, :] += jnp.sum(value, axis=0, keepdims=True)


def row_block(core, i, steps):
    half = steps // 2
    return jnp.where(i < half, (1 - core) * half + i, core * half + i - half)


def up_kernel(group, core_ref, len_ref, seat_ref, x_ref, a_ref, og_ref, vec_ref, *refs):
    refs, (mid_ref, h_ref, e_ref, slope_ref, dy_ref, wo_ref, wu_ref, sems) = refs[:-8], refs[-8:]
    block = x_ref.shape[0]

    @pl.when(pl.program_id(0) == 0)
    def _():
        group.start(refs, core_ref, seat_ref, 0, D // 2, wo_ref, sems.at[0])
        group.start(refs, core_ref, seat_ref, D // 2, FF // 2, wu_ref, sems.at[1])
        wait_all(wo_ref, sems.at[0])
        wait_all(wu_ref, sems.at[1])

    valid = valid_rows(core_ref, len_ref, block)
    dy_ref[...] = jnp.where(valid, og_ref[...].astype(F32), 0.0).astype(BF16)
    mid = x_ref[...].astype(F32) + mm(a_ref[...], wo_ref[...]) + vec_ref[4:5, :]
    mid_ref[...] = mid
    normed, _ = norm_parts(mid)
    h = (normed * vec_ref[5:6, :] + vec_ref[6:7, :]).astype(BF16)
    h_ref[...] = h

    def act(j, z):
        cols = slice(j * D, (j + 1) * D)
        z = z + vec_ref[8 + j : 9 + j, :]
        squared = z * z
        turned = jnp.tanh(z * (GELU_ROOT + (GELU_ROOT * GELU_CUBE) * squared))
        half = 0.5 * turned + 0.5
        act = z * half
        e_ref[:, cols] = act.astype(BF16)
        slope = half + act * (1.0 - turned) * (GELU_ROOT + (3.0 * GELU_ROOT * GELU_CUBE) * squared)
        slope_ref[:, cols] = slope.astype(BF16)

    waiting = None
    for j in range(FF // D):
        z = mm(h, wu_ref[:, j * D : (j + 1) * D])
        if waiting is not None:
            act(*waiting)
        waiting = (j, z)
    act(*waiting)


def up_call(core, lengths, seats, x, a, og, vec, group, block=256):
    rows = x.shape[0]
    row_spec = pl.BlockSpec((block, D), lambda i, *s: (i, 0))
    wide_spec = pl.BlockSpec((block, FF), lambda i, *s: (i, 0))
    low, wide = [jax.ShapeDtypeStruct((rows, width), BF16) for width in (D, FF)]
    return pl.pallas_call(
        functools.partial(up_kernel, group),
        name="up",
        grid_spec=pltpu.PrefetchScalarGridSpec(
            num_scalar_prefetch=3,
            grid=(rows // block,),
            in_specs=[row_spec, row_spec, row_spec, whole_spec(vec.shape)] + group.specs(),
            out_specs=[row_spec, row_spec, wide_spec, wide_spec, row_spec],
            scratch_shapes=[
                pltpu.VMEM((D, D), BF16),
                pltpu.VMEM((D, FF), BF16),
                pltpu.SemaphoreType.DMA((2,)),
            ],
        ),
        out_shape=[
            jax.ShapeDtypeStruct((rows, D), F32),
            low,
            wide,
            wide,
            low,
        ],
        compiler_params=params(48),
        cost_estimate=cost(6e9, 30e6, rows * FF),
    )(core, lengths, seats, x, a, og, vec, *group.arrays)


def down_kernel(up_group, down_group, core_ref, seat_ref, mid_ref, slope_ref, dy_ref, vec_ref, *refs):
    count = len(up_group.arrays)
    up_refs, down_refs = refs[:count], refs[count : count + len(down_group.arrays)]
    dz_ref, dmb_ref, dm_ref, da_ref, acc_ref, wo_ref, wu_ref, wd_ref, sems = refs[-9:]
    step = pl.program_id(0)

    @pl.when(step == 0)
    def _():
        down_group.start(down_refs, core_ref, seat_ref, 0, D // 2, wd_ref, sems.at[2])
        up_group.start(up_refs, core_ref, seat_ref, D // 2, FF // 2, wu_ref, sems.at[1])
        up_group.start(up_refs, core_ref, seat_ref, 0, D // 2, wo_ref, sems.at[0])
        acc_ref[...] = jnp.zeros_like(acc_ref)
        wait_all(wd_ref, sems.at[2])

    mid = mid_ref[...]
    @pl.when(step == 0)
    def _():
        wait_all(wu_ref, sems.at[1])
        wait_all(wo_ref, sems.at[0])

    dy = dy_ref[...]
    add_row(acc_ref, 7, dy.astype(F32))
    dh = None
    waiting = None
    for j in range(FF // D + 1):
        later = None
        if j < FF // D:
            later = (j, mm(dy, wd_ref[j * D : (j + 1) * D, :], NT))
        if waiting is not None:
            at, de = waiting
            cols = slice(at * D, (at + 1) * D)
            dz = (de * slope_ref[:, cols].astype(F32)).astype(BF16)
            dz_ref[:, cols] = dz
            add_row(acc_ref, 8 + at, dz.astype(F32))
            part = mm(dz, wu_ref[:, cols], NT)
            dh = part if dh is None else dh + part
        waiting = later
    normed, scale = norm_parts(mid)
    add_row(acc_ref, 5, dh * normed)
    add_row(acc_ref, 6, dh)
    dm = dy.astype(F32) + norm_back(dh * vec_ref[5:6, :], normed, scale)
    dm_ref[...] = dm
    dm_low = dm.astype(BF16)
    dmb_ref[...] = dm_low
    add_row(acc_ref, 4, dm_low.astype(F32))
    da_ref[...] = mm(dm_low, wo_ref[...], NT).astype(BF16)


def down_call(core, seats, mid, slope, dy, vec, up_group, down_group, block=256):
    rows = mid.shape[0]
    row_spec, wide_spec = [
        pl.BlockSpec((block, width), lambda i, *s: (i, 0)) for width in (D, FF)
    ]
    return pl.pallas_call(
        functools.partial(down_kernel, up_group, down_group),
        name="down",
        grid_spec=pltpu.PrefetchScalarGridSpec(
            num_scalar_prefetch=2,
            grid=(rows // block,),
            in_specs=[row_spec, wide_spec, row_spec, whole_spec(vec.shape)]
            + up_group.specs()
            + down_group.specs(),
            out_specs=[
                wide_spec, row_spec, row_spec, row_spec,
                pl.BlockSpec((16, D), lambda i, *s: (0, 0)),
            ],
            scratch_shapes=[
                pltpu.VMEM((D, D), BF16),
                pltpu.VMEM((D, FF), BF16),
                pltpu.VMEM((FF, D), BF16),
                pltpu.SemaphoreType.DMA((3,)),
            ],
        ),
        out_shape=[
            jax.ShapeDtypeStruct((rows, FF), BF16),
            jax.ShapeDtypeStruct((rows, D), BF16),
            jax.ShapeDtypeStruct((rows, D), F32),
            jax.ShapeDtypeStruct((rows, D), BF16),
            jax.ShapeDtypeStruct((16, D), F32),
        ],
        compiler_params=params(48),
        cost_estimate=cost(1.1e10, 28e6),
    )(core, seats, mid, slope, dy, vec, *up_group.arrays, *down_group.arrays)


def out_kernel(group, core_ref, len_ref, seat_ref, mid_ref, e_ref, vec_ref, *refs):
    refs, (theirs_ref, mine_ref, wd_ref, sems) = refs[:-4], refs[-4:]
    block = mid_ref.shape[0]
    step, steps = pl.program_id(0), pl.num_programs(0)

    @pl.when(step == 0)
    def _():
        group.start(refs, core_ref, seat_ref, 0, D // 2, wd_ref, sems.at[0])
        wait_all(wd_ref, sems.at[0])

    down = vec_ref[7:8, :] + mid_ref[...] + mm(e_ref[...], wd_ref[...])
    pos = row_block(core_ref[0], step, steps) * block + lax.broadcasted_iota(jnp.int32, (block, 1), 0)
    down = jnp.where(pos < len_ref[core_ref[0]], down, 0.0).astype(BF16)

    @pl.when(step < steps // 2)
    def _():
        theirs_ref[...] = down

    @pl.when(step >= steps // 2)
    def _():
        mine_ref[0] = down


def out_call(core, lengths, seats, mid, e, vec, group, block=256):
    rows = mid.shape[0]
    steps = rows // block
    half = steps // 2
    row_spec, wide_spec = [
        pl.BlockSpec((block, width), lambda i, c, *s: (row_block(c[0], i, steps), 0)) for width in (D, FF)
    ]
    return pl.pallas_call(
        functools.partial(out_kernel, group),
        name="out",
        grid_spec=pltpu.PrefetchScalarGridSpec(
            num_scalar_prefetch=3,
            grid=(steps,),
            in_specs=[row_spec, wide_spec, whole_spec(vec.shape)] + group.specs(),
            out_specs=[
                pl.BlockSpec((block, D), lambda i, *s: (jnp.minimum(i, half - 1), 0)),
                pl.BlockSpec((1, block, D), lambda i, c, *s: (c[0], jnp.maximum(i - half, 0), 0)),
            ],
            scratch_shapes=[pltpu.VMEM((FF, D), BF16), pltpu.SemaphoreType.DMA((1,))],
        ),
        out_shape=[
            jax.ShapeDtypeStruct((rows // 2, D), BF16),
            jax.ShapeDtypeStruct((2, rows // 2, D), BF16),
        ],
        compiler_params=params(20),
        cost_estimate=cost(4.9e9, 16e6),
    )(core, lengths, seats, mid, e, vec, *group.arrays)


def pick(values, half, mode):
    if mode == "split":
        width = values.shape[1] // 2
        return [values[:, half * width : (half + 1) * width]]
    return [values[:, at : at + 128] for at in range(half * 128, values.shape[1], 256)]


def weight_grad_kernel(lefts, rights, mode, core_ref, *refs):
    left_refs, right_refs = refs[:lefts], refs[lefts : lefts + sum(rights)]
    own_ref, other_ref = refs[-2:]
    halves = ([], [])
    at = 0
    for left_ref, count in zip(left_refs, rights):
        left = left_ref[...]
        for right_ref in right_refs[at : at + count]:
            whole = mm(left, right_ref[...], TN).astype(BF16)
            for half in range(2):
                halves[half].extend(pick(whole, half, mode))
        at += count
    low, high = [part[0] if len(part) == 1 else jnp.concatenate(part, axis=1) for part in halves]

    @pl.when(core_ref[0] == 0)
    def _():
        own_ref[...] = low
        other_ref[...] = high

    @pl.when(core_ref[0] != 0)
    def _():
        own_ref[...] = high
        other_ref[...] = low


def weight_grad_call(core, products, block, name, mode="split", cols=None):
    rows, height = products[0][0].shape
    lefts = [left for left, _ in products]
    rights = [right for _, group in products for right in group]
    widths = [right.shape[1] if cols is None else cols[0] for right in rights]
    width = sum(widths)
    seat = 0 if cols is None else cols[1]
    return pl.pallas_call(
        functools.partial(weight_grad_kernel, len(lefts), [len(group) for _, group in products], mode),
        name=name,
        grid_spec=pltpu.PrefetchScalarGridSpec(
            num_scalar_prefetch=1,
            grid=(height // block,),
            in_specs=[pl.BlockSpec((rows, block), lambda i, c: (0, i))] * len(lefts)
            + [
                pl.BlockSpec((rows, w), lambda i, c: (0, seat), pipeline_mode=pl.Buffered(1)) for w in widths
            ],
            out_specs=[pl.BlockSpec((block, width // 2), lambda i, c: (i, 0))] * 2,
        ),
        out_shape=[jax.ShapeDtypeStruct((height, width // 2), BF16)] * 2,
        compiler_params=params(16 if mode == "turns" else 48),
        cost_estimate=cost(2 * rows * height * width, rows * (height + width) * 2 + height * width * 2),
    )(core, *lefts, *rights)


def last_kernel(
    core_ref, x_ref, dm_ref, dq_ref, dk_ref, dv_ref, w_ref, vec_ref, before_ref, theirs_ref, mine_ref, acc_ref
):
    step, steps = pl.program_id(0), pl.num_programs(0)

    @pl.when(step == 0)
    def _():
        acc_ref[...] = before_ref[...]

    subs = sub_blocks(x_ref.shape[0])

    def product(rows):
        return (
            mm(dq_ref[rows, :], w_ref[:D])
            + mm(dk_ref[rows, :], w_ref[D : 2 * D])
            + mm(dv_ref[rows, :], w_ref[2 * D :])
        )

    grads = []
    dh = product(subs[0])
    add_row(acc_ref, 2, dq_ref[...].astype(F32))
    add_row(acc_ref, 3, dv_ref[...].astype(F32))
    for at, rows in enumerate(subs):
        later = product(subs[at + 1]) if at + 1 < len(subs) else None
        normed, scale = norm_parts(x_ref[rows, :].astype(F32))
        add_row(acc_ref, 0, dh * normed)
        add_row(acc_ref, 1, dh)
        grads.append(dm_ref[rows, :] + norm_back(dh * vec_ref[0:1, :], normed, scale))
        dh = later

    @pl.when(step < steps // 2)
    def _():
        for rows, grad in zip(subs, grads):
            theirs_ref[rows, :] = grad

    @pl.when(step >= steps // 2)
    def _():
        for rows, grad in zip(subs, grads):
            mine_ref[0, rows, :] = grad


def last_call(core, x, dm, dq, dk, dv, w, vec, before, block=256):
    rows = x.shape[0]
    steps = rows // block
    half = steps // 2
    row_spec = pl.BlockSpec((block, D), lambda i, c, *s: (row_block(c[0], i, steps), 0))
    return pl.pallas_call(
        last_kernel,
        name="last",
        grid_spec=pltpu.PrefetchScalarGridSpec(
            num_scalar_prefetch=1,
            grid=(steps,),
            in_specs=[row_spec] * 5 + [whole_spec(part.shape) for part in (w, vec, before)],
            out_specs=[
                pl.BlockSpec((block, D), lambda i, *s: (jnp.minimum(i, half - 1), 0)),
                pl.BlockSpec((1, block, D), lambda i, c, *s: (c[0], jnp.maximum(i - half, 0), 0)),
                pl.BlockSpec((16, D), lambda i, *s: (0, 0)),
            ],
        ),
        out_shape=[
            jax.ShapeDtypeStruct((rows // 2, D), F32),
            jax.ShapeDtypeStruct((2, rows // 2, D), F32),
            jax.ShapeDtypeStruct((16, D), F32),
        ],
        compiler_params=params(12),
        cost_estimate=cost(rows * 6 * D * D, 16e6),
    )(core, x, dm, dq, dk, dv, w, vec, before)


def adam_kernel(plans, sources, core_ref, *refs):
    halves = [refs[2 * i : 2 * i + 2] for i in range(sources)]
    count = len(plans)
    states = refs[2 * sources : 2 * sources + 3 * count]
    outs = refs[2 * sources + 3 * count : 2 * sources + 6 * count]
    grads = refs[2 * sources + 6 * count :]
    for core in range(2):

        @pl.when(core_ref[0] == core)
        def _():
            for (_, _, moves), grad_ref in zip(plans, grads):
                for source, start, width, place0, place1 in moves:
                    for half, place in ((0, place0), (1, place1)):
                        ref = halves[source][0 if half == core else 1]
                        grad_ref[:, place : place + width] = ref[:, start : start + width].astype(F32)

    for i, (rate, decay, _) in enumerate(plans):
        weight, first, second = states[3 * i : 3 * i + 3]
        new = adamw(weight[...], grads[i][...], first[...], second[...], rate, decay)
        for out, value in zip(outs[3 * i : 3 * i + 3], new):
            out[...] = value


def adam_call(core, halves, states, plans):
    flat = [part for pair in halves for part in pair]
    held = [part for state in states for part in state]
    spec = pl.BlockSpec(memory_space=pltpu.VMEM)
    news = pl.pallas_call(
        functools.partial(adam_kernel, plans, len(halves)),
        name="adam",
        in_specs=[pl.BlockSpec(memory_space=pltpu.SMEM)] + [spec] * (len(flat) + len(held)),
        out_specs=[spec] * len(held),
        out_shape=[jax.ShapeDtypeStruct(part.shape, F32) for part in held],
        scratch_shapes=[pltpu.VMEM(state[0].shape, F32) for state in states],
        compiler_params=params(12),
        cost_estimate=cost(1e6, 24 * sum(state[0].size for state in states)),
    )(core, *flat, *held)
    return [news[3 * i : 3 * i + 3] for i in range(len(states))]


def after(value, *others):
    if not others:
        return value
    return lax.optimization_barrier((value,) + others)[0]


def cut(array, axis, index, size=1):
    starts = [jnp.uint32(0)] * array.ndim
    sizes = list(array.shape)
    starts[axis], sizes[axis] = index, size
    return lax.dynamic_slice(array, starts, sizes)


class Grid:
    def __init__(self, chips):
        log = chips.bit_length() - 1
        side = 1 << (log // 3)
        if side * side * (chips // (side * side)) != chips:
            side = 1
        self.chips = chips
        self.n = side
        self.nz = chips // (side * side)
        self.core = lax.axis_index("seq")
        self.chip = lax.axis_index("dp")
        self.x = self.chip % side
        self.y = self.chip // side % side
        self.z = self.chip // (side * side)

    def pin(self, value):
        n, core = self.n, self.core
        first, second = self.coords(core)
        places = {
            "core": core,
            "other": 1 - core,
            "chip": self.chip,
            "seats": self.seats(True),
            "q_seats": self.seats(False),
        }
        for s in range(n):
            for t in range(n):
                places["plane", s, t] = self.plane((first + s) % n, (second + t) % n, core)
        for at in range(self.nz):
            places["z", at] = self.z ^ at
        names = list(places)
        held = lax.optimization_barrier((value, *[places[name].astype(jnp.uint32) for name in names]))
        self.places = dict(zip(names, held[1:]))
        return held[0]

    def plane(self, first, second, core):
        return jnp.where(core == 0, second * self.n + first, first * self.n + second)

    def coords(self, core):
        return jnp.where(core == 0, self.x, self.y), jnp.where(core == 0, self.y, self.x)

    def permute(self, value, axis, shift=0):
        pairs = []
        for chip in range(self.chips):
            for core in range(2):
                x, y, z = chip % self.n, chip // self.n % self.n, chip // (self.n * self.n)
                to_core = core
                if axis == "z":
                    z = (z + shift) % self.nz
                elif axis == "zx":
                    z = z ^ shift
                elif axis == "core":
                    to_core = 1 - core
                elif (axis == "first") == (core == 0):
                    x = (x + shift) % self.n
                else:
                    y = (y + shift) % self.n
                pairs.append((chip * 2 + core, ((z * self.n + y) * self.n + x) * 2 + to_core))
        return lax.ppermute(value, ("dp", "seq"), pairs)

    def swap(self, value):
        return self.permute(value, "core")

    def join(self, own, other, axis):
        return jnp.where(
            self.places["core"] == 0,
            jnp.concatenate([own, other], axis),
            jnp.concatenate([other, own], axis),
        )

    def seats(self, halving):
        found = []
        for half in range(2):
            core = self.core if half == 0 else 1 - self.core
            first, second = self.coords(core)
            for s2 in range(self.n):
                for s1 in range(self.n):
                    flat = self.plane((first - s1) % self.n, (second - s2) % self.n, core)
                    for sz in range(self.nz):
                        z = self.z ^ sz if halving else (self.z - sz) % self.nz
                        found.append(z * self.n * self.n + flat)
        return jnp.stack(found).astype(jnp.int32)

    def total_small(self, value, *untils):
        steps = [("core", 0), ("first", 1), ("second", 1)] if self.n == 2 else [("core", 0)]
        if self.n != 2:
            for axis in ("first", "second"):
                value = value + sum(self.permute(value, axis, s) for s in range(1, self.n))
        bit = 1
        while bit < self.nz:
            steps.append(("zx", bit))
            bit *= 2
        for at, (axis, shift) in enumerate(steps):
            until = untils[at] if at < len(untils) else ()
            value = value + after(self.permute(value, axis, shift), *until)
        return value

    def gather_z(self, block, *until):
        return jnp.stack([block] + [after(self.permute(block, "z", s), *until) for s in range(1, self.nz)])

    def gather_bit(self, held, bit, *until):
        return jnp.concatenate([held, after(self.permute(held, "zx", bit), *until)])

    def along(self, axis, column, *until):
        return [after(self.permute(column, axis, s), *until) for s in range(1, self.n)]

    def plane_parts(self, column, firsts, seconds, passed):
        parts = [column] + firsts
        for s2 in range(1, self.n):
            parts += [seconds[s2 - 1]] + [passed[s1 - 1][s2 - 1] for s1 in range(1, self.n)]
        return [part[None] for part in parts]

    def gather_first(self, column, *until):
        return jnp.stack([column] + [after(self.permute(column, "first", s), *until) for s in range(1, self.n)])

    def gather_second(self, line, *until):
        return [after(self.permute(line, "second", s), *until) for s in range(1, self.n)]

    def scatter_first(self, own, pair, *until):
        rows, cols = own.shape[0] // self.chips, own.shape[1]
        n = self.n

        def seat(s1, s2):
            own_part, pair_part = [
                cut(part.reshape(self.nz, n * n, rows, cols), 1, self.places["plane", s1, s2]).astype(F32)
                for part in (own, pair)
            ]
            return own_part + pair_part

        kept = [seat(0, t) for t in range(n)]
        for s in range(1, n):
            send = jnp.stack([seat(s, t).astype(BF16) for t in range(n)])
            got = after(self.permute(send, "first", s), *until)
            kept = [kept[t] + got[t].astype(F32) for t in range(n)]
        return kept[0], [part.astype(BF16) for part in kept[1:]]

    def scatter_second(self, kept, *until):
        mine, rest = kept
        got = [after(self.permute(rest[s - 1], "second", s), *until) for s in range(1, self.n)]
        for part in got:
            mine = mine + part.astype(F32)
        return mine.reshape((self.nz,) + mine.shape[2:]), got

    def order_z(self, mine):
        return [cut(mine, 0, self.places["z", at])[0] for at in range(self.nz)]

    def scatter_bit(self, parts, *until):
        half = len(parts) // 2
        send = parts[half] if half == 1 else jnp.stack([part.astype(BF16) for part in parts[half:]])
        got = after(self.permute(send.astype(BF16), "zx", half), *until)
        if half == 1:
            return [parts[0] + got.astype(F32)], got
        return [part + got[at].astype(F32) for at, part in enumerate(parts[:half])], got

    def scatter_z(self, parts, *until):
        while len(parts) > 1:
            parts, _ = self.scatter_bit(parts, *until)
        return parts[0]


def adamw(weight, gradient, first_moment, second_moment, step_rate, weight_decay):
    first_moment = BETA_ONE * first_moment + (1.0 - BETA_ONE) * gradient
    second_moment = BETA_TWO * second_moment + (1.0 - BETA_TWO) * gradient * gradient
    first_fix = 1.0 - BETA_ONE**STEP
    second_fix = 1.0 - BETA_TWO**STEP
    direction = first_moment / first_fix / (jnp.sqrt(second_moment / second_fix) + EPS_ADAM)
    return (weight - step_rate * (direction + weight_decay * weight), first_moment, second_moment)


def local(
    block_in, lengths, out_grad, w_qkv, w_out, w_up, w_down, vectors,
    first_qkv, first_out, first_up, first_down, first_vectors,
    second_qkv, second_out, second_up, second_down, second_vectors,
):
    grid = Grid(lax.axis_size("dp"))
    core = grid.core
    w_qkv_first = grid.pin(w_qkv)
    places = grid.places
    core_arr = places["core"].reshape(1).astype(jnp.int32)
    half_len = block_in.shape[1]
    vec_count, vec_here = vectors.shape

    def own_slot(halves):
        mine, theirs = [cut(halves, 0, places[name])[0] for name in ("core", "other")]
        return grid.join(mine, grid.swap(theirs), 0)

    def both_slots(mine, got):
        zero = jnp.uint32(0)
        return lax.dynamic_update_slice(mine, got[None], (places["other"], zero, zero))

    def half_of(shard):
        width = shard.shape[1] // 2
        return jnp.where(places["core"] == 0, shard[:, :width], shard[:, width:]).astype(BF16)

    seats, q_seats = [places[name].astype(jnp.int32) for name in ("seats", "q_seats")]

    turned = jnp.pad(vectors.T.astype(BF16), ((0, 0), (0, 128 - vec_count)))
    q_block = jnp.concatenate([half_of(w_qkv_first), turned], axis=1)
    u_block = jnp.concatenate([half_of(w_out), half_of(w_up)], axis=1)
    d_block = half_of(w_down)
    q_col = grid.gather_z(q_block)
    x = own_slot(block_in)
    bits = [1 << at for at in range((grid.nz - 1).bit_length())]
    u_col, d_col = u_block[None], d_block[None]
    for bit in bits[:-1]:
        u_col = grid.gather_bit(u_col, bit)
        d_col = grid.gather_bit(d_col, bit)
    q_line = after(grid.gather_first(q_col, x), u_col, d_col)
    q_rest = grid.gather_second(q_line)
    u_col = grid.gather_bit(after(u_col, q_line), bits[-1])
    q_line_swap = grid.swap(q_line)
    q_rest_swap = [grid.swap(after(part, u_col)) for part in q_rest]
    q_group = finish_group(grid, q_seats, [q_line] + q_rest, [q_line_swap] + q_rest_swap)

    h1, qkv, vec, w_back = qkv_call(core_arr, q_seats, x, q_group)
    u_firsts = grid.along("first", u_col, qkv)
    d_col = grid.gather_bit(after(d_col, u_col), bits[-1], qkv)
    og = own_slot(after(out_grad, qkv))
    att = attend_call(core_arr, lengths, after(qkv, d_col, *u_firsts), 0, 4, ())
    u_seconds = grid.along("second", u_col, *att)
    u_passed = [grid.along("second", part, *att) for part in u_firsts]
    early = [after(grid.swap(part), *att) for part in [u_col] + u_firsts]
    d_col = after(d_col, *u_seconds, *[part for parts in u_passed for part in parts])
    a, lse = attend_call(core_arr, lengths, after(qkv, d_col), 4, 2, att)
    late_seconds = [after(grid.swap(part), a) for part in u_seconds]
    late_passed = [[after(grid.swap(part), a) for part in parts] for parts in u_passed]
    u_group = finish_group(
        grid,
        seats,
        grid.plane_parts(u_col, u_firsts, u_seconds, u_passed),
        grid.plane_parts(early[0], early[1:], late_seconds, late_passed),
    )
    mid, h2, e, slope, dy = up_call(core_arr, lengths, seats, x, a, og, vec, u_group)
    d_firsts = grid.along("first", d_col, mid)
    d_seconds = grid.along("second", d_col, mid)
    d_col_swap = after(grid.swap(d_col), mid)
    d_own, d_other = weight_grad_call(
        core_arr, [(after(e, *d_firsts, *d_seconds), [dy])], 512, "grad_down"
    )
    d_passed = [grid.along("second", part, d_own) for part in d_firsts]
    early = [[after(grid.swap(part), d_own) for part in parts] for parts in (d_firsts, d_seconds)]
    d_group = finish_group(
        grid,
        seats,
        grid.plane_parts(d_col, d_firsts, d_seconds, d_passed),
        grid.plane_parts(d_col_swap, *early, [[grid.swap(part) for part in parts] for parts in d_passed]),
    )
    dz, dmb, dm, da, acc_mid = down_call(core_arr, seats, mid, slope, dy, vec, u_group, d_group)

    d_pair = after(grid.swap(d_other), dz)
    u_own, u_other = weight_grad_call(
        core_arr, [(a, [dmb]), (h2, [after(dz, d_pair)])], 384, "grad_up"
    )
    d_kept = grid.scatter_first(d_own, d_pair, u_own)

    def back_call(start, count, before, *needs):
        return attend_back_call(core_arr, lengths, qkv, a, after(da, *needs), lse, start, count, before)

    back = back_call(0, 2, (), u_own, *d_kept[1])
    d_sum, d_here = grid.scatter_second(d_kept, *back)
    u_pair = after(grid.swap(u_other), *back)
    back = back_call(2, 4, back, u_pair, *d_here)
    d_parts, d_got = grid.scatter_bit(grid.order_z(d_sum), *back)
    u_kept = grid.scatter_first(u_own, u_pair, *back)
    dq, dk, dv = back
    q_own, q_other = weight_grad_call(
        core_arr, [(h1, [after(dq, d_got, *u_kept[1]), dk, dv])], 384, "grad_qkv", "turns"
    )
    u_sum, u_here = grid.scatter_second(u_kept, q_own)
    q_pair = grid.swap(after(q_other, *u_here))
    in_theirs, in_mine, acc = last_call(
        core_arr, x, dm, after(dq, q_own, q_pair), dk, dv, w_back, vec, acc_mid
    )
    d_mine = grid.scatter_z(d_parts, in_theirs)
    d_other_mine = grid.swap(d_mine)
    q_kept = grid.scatter_first(q_own, q_pair, in_theirs)
    u_parts, u_got = grid.scatter_bit(grid.order_z(u_sum), *q_kept[1])
    q_sum, q_here = grid.scatter_second(q_kept, u_got)
    down_new, = adam_call(
        core_arr,
        [(d_mine, d_other_mine)],
        [(after(w_down, *q_kept[1]), first_down, second_down)],
        [(FF ** (-0.5), MATRIX_DECAY, [(0, 0, D // 2, 0, D // 2)])],
    )
    in_got = grid.swap(after(in_theirs, *q_kept[1]))
    u_mine = grid.scatter_z([after(part, *q_here) for part in u_parts])
    u_other_mine = grid.swap(u_mine)
    in_grad = both_slots(in_mine, after(in_got, *q_here))
    out_theirs, out_mine = out_call(core_arr, lengths, seats, after(mid, in_grad, *q_here), e, vec, d_group)
    q_parts, q_got = grid.scatter_bit(grid.order_z(q_sum), out_theirs)
    block_out = both_slots(out_mine, grid.swap(out_theirs))
    q_gots = [(q_got,)]
    while len(q_parts) > 1:
        q_parts, q_got = grid.scatter_bit(q_parts)
        q_gots.append((q_got,))
    q_mine = q_parts[0]
    q_other_mine = grid.swap(q_mine)
    vec_total = grid.total_small(acc, (), q_kept[1], q_here, *q_gots)

    half, wide = D // 2, FF // 2
    out_new, up_new = adam_call(
        core_arr,
        [(u_mine, u_other_mine)],
        [(after(w_out, in_grad), first_out, second_out), (w_up, first_up, second_up)],
        [
            ((D // 64) ** (-0.5), MATRIX_DECAY, [(0, 0, half, 0, half)]),
            (D ** (-0.5), MATRIX_DECAY, [(0, half, wide, 0, wide)]),
        ],
    )
    moves = []
    for turn in range(3 * D // 256):
        moves.append((0, turn * 128, 128, turn * 256, turn * 256 + 128))
    qkv_new, = adam_call(
        core_arr,
        [(q_mine, q_other_mine)],
        [(w_qkv, first_qkv, second_qkv)],
        [(D ** (-0.5), MATRIX_DECAY, moves)],
    )
    vec_grad = cut(vec_total[:vec_count].reshape(vec_count, -1, vec_here), 1, places["chip"])[:, 0]
    vec_new = adamw(vectors, vec_grad, first_vectors, second_vectors, VECTOR_RATE, 0.0)
    news = [qkv_new, out_new, up_new, down_new, vec_new]
    return (block_out, in_grad) + tuple(new[kind] for kind in range(3) for new in news)


def finish_group(grid, seats, own, other):
    rows, cols = own[0].shape[-2:]
    if rows % 16 == 0:
        return Pieces(own + other, rows)
    found = []
    for half, parts in enumerate((own, other)):
        here = seats[half * grid.chips : (half + 1) * grid.chips]
        order = jnp.zeros((grid.chips,), jnp.int32).at[here].set(jnp.arange(grid.chips, dtype=jnp.int32))
        blocks = jnp.concatenate(parts).reshape(grid.chips, rows, cols)
        found.append(jnp.take(blocks, order, axis=0).reshape(1, 1, grid.chips * rows, cols))
    return Pieces(found, grid.chips * rows, True)


def solution(mesh):
    weight = P("dp", None)
    vector = P(None, "dp")
    state = (weight, weight, weight, weight, vector)
    tokens = P("dp", "seq", None)
    return jax.shard_map(
        local,
        mesh=mesh,
        in_specs=(tokens, P("dp"), tokens) + state * 3,
        out_specs=(tokens, tokens) + state * 3,
        check_vma=False,
    )
```

```python
import functools

import jax
import jax.numpy as jnp
from jax import lax
from jax.experimental import pallas as pl
from jax.experimental.pallas import tpu as pltpu
from jax.sharding import PartitionSpec as P

D = 768
HEADS = 12
HEAD_DIM = 64
FF = 3072
STEP = 10

EPS_NORM = 1e-05
EPS_ADAM = 1e-08
BETA_ONE = 0.5
BETA_TWO = 0.5
MATRIX_DECAY = 0.1
VECTOR_RATE = 0.1
NEG_FILL = -1e30
GELU_ROOT = 0.7978845608028654
GELU_CUBE = 0.044715
QKV_HALF = 3 * D // 2

F32 = jnp.float32
BF16 = jnp.bfloat16

NN = (((1,), (0,)), ((), ()))
NT = (((1,), (1,)), ((), ()))
TN = (((0,), (0,)), ((), ()))


def mm(left, right, dims=NN):
    return lax.dot_general(left, right, dims, preferred_element_type=F32)


def cost(flops, nbytes, trans=0):
    return pl.CostEstimate(flops=int(4 * flops), bytes_accessed=int(4 * nbytes), transcendentals=int(trans))


def params(mib=60):
    return pltpu.CompilerParams(vmem_limit_bytes=mib * 1024 * 1024)


def held_spec():
    return pl.BlockSpec(memory_space=pltpu.VMEM)


def at_rows(block):
    return pl.ds(pl.multiple_of(pl.program_id(0) * block, block), block)


def whole_spec(shape):
    return pl.BlockSpec(shape, lambda *idx: (0,) * len(shape), pipeline_mode=pl.Buffered(1))


class Pieces:
    def __init__(self, arrays, rows, ordered=False):
        self.arrays = arrays
        self.rows = rows
        self.ordered = ordered
        self.halves = 2
        self.count = len(arrays) // self.halves
        self.lines, self.depth = arrays[0].shape[:2]

    def specs(self):
        return [pl.BlockSpec(memory_space=pltpu.HBM)] * len(self.arrays)

    def row(self, seat_ref, at):
        return 0 if self.ordered else pl.multiple_of(seat_ref[at] * self.rows, 16)

    def start(self, refs, core_ref, seat_ref, start_col, width, target, sem):
        core = core_ref[0]
        at = 0
        for half in range(self.halves):
            where = core if half == 0 else 1 - core
            for s2 in range(self.count):
                ref = refs[half * self.count + s2]
                for s1 in range(self.lines):
                    for sz in range(self.depth):
                        row = self.row(seat_ref, at)
                        at += 1
                        col = pl.multiple_of(where * width, 128)
                        pltpu.make_async_copy(
                            ref.at[s1, sz, :, pl.ds(start_col, width)],
                            target.at[pl.ds(row, self.rows), pl.ds(col, width)],
                            sem,
                        ).start()

    def start_once(self, refs, seat_ref, start_col, width, target, sem):
        at = 0
        for s2 in range(self.count):
            for s1 in range(self.lines):
                for sz in range(self.depth):
                    row = self.row(seat_ref, at)
                    at += 1
                    pltpu.make_async_copy(
                        refs[s2].at[s1, sz, :, pl.ds(start_col, width)],
                        target.at[pl.ds(row, self.rows), :],
                        sem,
                    ).start()


def wait_all(target, sem):
    pltpu.make_async_copy(target, target, sem).wait()


def norm_parts(rows):
    mean = jnp.mean(rows, axis=-1, keepdims=True)
    centred = rows - mean
    variance = jnp.mean(centred * centred, axis=-1, keepdims=True)
    scale = lax.rsqrt(variance + EPS_NORM)
    return centred * scale, scale


def norm_back(d_normed, normed, scale):
    first = jnp.mean(d_normed, axis=-1, keepdims=True)
    second = jnp.mean(d_normed * normed, axis=-1, keepdims=True)
    return scale * (d_normed - first - normed * second)


def qkv_kernel(group, core_ref, seat_ref, x_ref, *refs):
    refs, (h_ref, qkv_ref, vec_ref, back_ref, w_ref, turned_ref, sems) = refs[:-7], refs[-7:]

    @pl.when(pl.program_id(0) == 0)
    def _():
        group.start(refs, core_ref, seat_ref, 0, QKV_HALF, w_ref, sems.at[0])
        group.start_once(refs, seat_ref, QKV_HALF, 128, turned_ref, sems.at[1])
        wait_all(turned_ref, sems.at[1])
        vec_ref[...] = turned_ref[...].astype(F32).T[:16]
        wait_all(w_ref, sems.at[0])

    def norm(rows):
        normed, _ = norm_parts(x_ref[rows, :].astype(F32))
        h = (normed * vec_ref[0:1, :] + vec_ref[1:2, :]).astype(BF16)
        h_ref[rows, :] = h
        return h

    block = x_ref.shape[0]
    h = norm(slice(0, block))
    for part, bias in enumerate((2, None, 3)):
        cols = slice(part * D, (part + 1) * D)
        product = mm(h, w_ref[:, cols])
        if bias is not None:
            product = product + vec_ref[bias : bias + 1, :]
        qkv_ref[:, cols] = product.astype(BF16)

    @pl.when(pl.program_id(0) < 3)
    def _():
        back_ref[...] = w_ref[:, at_rows(D)].T


def sub_blocks(rows):
    return [slice(at, at + 256) for at in range(0, rows, 256)]


def qkv_call(core, seats, x, group, block=256):
    rows = x.shape[0]
    return pl.pallas_call(
        functools.partial(qkv_kernel, group),
        name="qkv",
        grid_spec=pltpu.PrefetchScalarGridSpec(
            num_scalar_prefetch=2,
            grid=(rows // block,),
            in_specs=[pl.BlockSpec((block, D), lambda i, *s: (i, 0))] + group.specs(),
            out_specs=[
                pl.BlockSpec((block, D), lambda i, *s: (i, 0)),
                pl.BlockSpec((block, 3 * D), lambda i, *s: (i, 0)),
                pl.BlockSpec((16, D), lambda i, *s: (0, 0)),
                pl.BlockSpec((D, D), lambda i, *s: (jnp.minimum(i, 2), 0)),
            ],
            scratch_shapes=[
                pltpu.VMEM((D, 3 * D), BF16),
                pltpu.VMEM((D, 128), BF16),
                pltpu.SemaphoreType.DMA((2,)),
            ],
        ),
        out_shape=[
            jax.ShapeDtypeStruct((rows, D), BF16),
            jax.ShapeDtypeStruct((rows, 3 * D), BF16),
            jax.ShapeDtypeStruct((16, D), F32),
            jax.ShapeDtypeStruct((3 * D, D), BF16),
        ],
        compiler_params=params(12),
        cost_estimate=cost(2 * rows * D * 3 * D, 10e6),
    )(core, seats, x, *group.arrays)


def head_parts(length, k_all, q_turned, head):
    full_len = k_all.shape[0]
    lane = lax.broadcasted_iota(jnp.int32, (1, 128), 1)
    row = lax.broadcasted_iota(jnp.int32, (128, 1), 0)
    zero, one = jnp.zeros((), BF16), jnp.ones((), BF16)
    mine = (lane // HEAD_DIM) == head
    spare = HEAD_DIM * (1 - head)
    pos = lax.broadcasted_iota(jnp.int32, (full_len, 128), 0)
    fill = jnp.where(pos < length, 0.0, NEG_FILL).astype(BF16)
    k_head = jnp.where(mine, k_all, jnp.where(lane == spare, fill, zero))
    q_head = jnp.where((row // HEAD_DIM) == head, q_turned, jnp.where(row == spare, one, zero))
    return mine, k_head, q_head


def causal_mask(scores, block):
    full = scores.shape[0]
    key_pos = lax.broadcasted_iota(jnp.int32, (block, block), 0)
    query_pos = lax.broadcasted_iota(jnp.int32, (block, block), 1)
    last = jnp.where(key_pos <= query_pos, scores[full - block :], NEG_FILL)
    if full == block:
        return last
    return jnp.concatenate([scores[: full - block], last], axis=0)


def attend_kernel(start, core_ref, len_ref, qkv_ref, *refs):
    a_ref, lse_ref, mixed_ref, scores_ref = refs[-4:]
    block = 256
    full_len = qkv_ref.shape[0]
    length = len_ref[core_ref[0]]
    q_all, k_all, v_all = [
        qkv_ref[:, pl.ds(pl.multiple_of((pl.program_id(0) + start) * 128 + part * D, 128), 128)] for part in range(3)
    ]
    q_all = q_all * jnp.asarray(HEAD_DIM ** (-0.5), BF16)
    v_turned = v_all.T
    q_turned = q_all.T
    ones = jnp.ones((16, full_len), BF16)
    parts = []
    for head in range(2):
        _, k_head, q_head = head_parts(length, k_all, q_turned, head)
        v_head = jnp.concatenate([v_turned[head * HEAD_DIM : (head + 1) * HEAD_DIM], ones], axis=0)
        parts.append((k_head, q_head, v_head))
    units = [(head, j) for j in reversed(range(full_len // block)) for head in range(2)]

    def score(at):
        head, j = units[at]
        k_head, q_head, _ = parts[head]
        top = None
        for i in range(j + 1):
            rows = slice(i * block, (i + 1) * block)
            tile = mm(k_head[rows], q_head[:, j * block : (j + 1) * block])
            if i == j:
                tile = causal_mask(tile, block)
            scores_ref[at % 2, rows, :] = tile
            part = jnp.max(tile.reshape(block // 8, 8, block), axis=0)
            top = part if top is None else jnp.maximum(top, part)
        return jnp.max(top, axis=0, keepdims=True)

    def finish(at, top):
        head, j = units[at]
        v_head = parts[head][2]
        cols = slice(j * block, (j + 1) * block)
        mixed = None
        for i in range(j + 1):
            rows = slice(i * block, (i + 1) * block)
            exped = jnp.exp(scores_ref[at % 2, rows, :] - top).astype(BF16)
            part = mm(v_head[:, rows], exped)
            mixed = part if mixed is None else mixed + part
        total = mixed[HEAD_DIM : HEAD_DIM + 1]
        mixed_ref[head * HEAD_DIM : (head + 1) * HEAD_DIM, cols] = mixed[:HEAD_DIM] / total
        lse_ref[0, head : head + 1, cols] = top + jnp.log(total)

    top = score(0)
    for at in range(len(units)):
        later = score(at + 1) if at + 1 < len(units) else None
        finish(at, top)
        top = later
    a_ref[...] = mixed_ref[...].T.astype(BF16)


def attend_call(core, lengths, qkv, first, count, before):
    rows = qkv.shape[0]
    pairs = HEADS // 2
    before = list(before)
    return pl.pallas_call(
        functools.partial(attend_kernel, first),
        name="attend",
        grid_spec=pltpu.PrefetchScalarGridSpec(
            num_scalar_prefetch=2,
            grid=(count,),
            in_specs=[held_spec()] + [pl.BlockSpec(memory_space=pl.ANY)] * len(before),
            out_specs=[
                pl.BlockSpec((rows, 128), lambda i, c, n: (0, i + first)),
                pl.BlockSpec((1, 8, rows), lambda i, c, n: (i + first, 0, 0)),
            ],
            scratch_shapes=[pltpu.VMEM((128, rows), F32), pltpu.VMEM((2, rows, 256), F32)],
        ),
        out_shape=[
            jax.ShapeDtypeStruct((rows, D), BF16),
            jax.ShapeDtypeStruct((pairs, 8, rows), F32),
        ],
        input_output_aliases={3 + i: i for i in range(len(before))},
        compiler_params=params(12),
        cost_estimate=cost(3e9 * count, 1.2e6 * count, 2 * rows * rows * 0.6 * count),
    )(core, lengths, qkv, *before)


def attend_back_kernel(core_ref, len_ref, q_ref, k_ref, v_ref, a_ref, da_ref, lse_ref, *refs):
    dq_ref, dk_ref, dv_ref, dqt_ref, dk_acc, dv_acc = refs[-6:]
    block = 256
    full_len = q_ref.shape[0]
    length = len_ref[core_ref[0]]
    scale = HEAD_DIM ** (-0.5)
    q_all = q_ref[...] * jnp.asarray(scale, BF16)
    k_all = k_ref[...]
    k_turned = k_all.T
    v_all = v_ref[...]
    da_all = da_ref[...]
    inner = (da_all.astype(F32) * a_ref[...].astype(F32)).T
    q_turned, da_turned = q_all.T, da_all.T
    parts = []
    for head in range(2):
        mine, k_head, q_head = head_parts(length, k_all, q_turned, head)
        zero = jnp.zeros((), BF16)
        q_plain = jnp.where(mine, q_all, zero)
        da_head = jnp.where(mine, da_all, zero)
        row = lax.broadcasted_iota(jnp.int32, (128, 1), 0)
        da_cols = jnp.where((row // HEAD_DIM) == head, da_turned, zero)
        lanes = slice(head * HEAD_DIM, (head + 1) * HEAD_DIM)
        centre = jnp.sum(inner[lanes], axis=0, keepdims=True)
        parts.append((k_head, q_plain, q_head, da_head, da_cols, lanes, centre))
    units = [
        (head, j, i)
        for j in reversed(range(full_len // block))
        for head in range(2)
        for i in range(j + 1)
    ]

    def score(at):
        head, j, i = units[at]
        k_head, _, q_head, _, da_cols, _, _ = parts[head]
        rows, cols = slice(i * block, (i + 1) * block), slice(j * block, (j + 1) * block)
        tile = mm(k_head[rows], q_head[:, cols])
        if i == j:
            tile = causal_mask(tile, block)
        return tile, mm(v_all[rows], da_cols[:, cols])

    seen = set()
    ready = score(0)
    dq_part = None
    for at, (head, j, i) in enumerate(units):
        later = score(at + 1) if at + 1 < len(units) else None
        scores, d_probs = ready
        _, q_plain, _, da_head, _, lanes, centre = parts[head]
        rows, cols = slice(i * block, (i + 1) * block), slice(j * block, (j + 1) * block)
        probs = jnp.exp(scores - lse_ref[0, head : head + 1, cols])
        d_scores = (probs * (d_probs - centre[:, cols])).astype(BF16)
        dv_part = mm(probs.astype(BF16), da_head[cols])
        dk_part = mm(d_scores, q_plain[cols])
        if i in seen:
            dv_acc[rows] += dv_part
            dk_acc[rows] += dk_part
        else:
            seen.add(i)
            dv_acc[rows] = dv_part
            dk_acc[rows] = dk_part
        part = mm(k_turned[lanes, rows], d_scores)
        dq_part = part if i == 0 else dq_part + part
        if i == j:
            dqt_ref[lanes, cols] = dq_part * scale
        ready = later
    dq_ref[...] = dqt_ref[...].T.astype(BF16)
    dk_ref[...] = dk_acc[...].astype(BF16)
    dv_ref[...] = dv_acc[...].astype(BF16)


def attend_back_call(core, lengths, qkv, a, da, lse, start, count, before):
    rows = qkv.shape[0]
    pairs = HEADS // 2
    before = list(before)
    pair_spec = pl.BlockSpec((rows, 128), lambda i, c, n: (0, i + start))
    return pl.pallas_call(
        attend_back_kernel,
        name="attend_back",
        grid_spec=pltpu.PrefetchScalarGridSpec(
            num_scalar_prefetch=2,
            grid=(count,),
            in_specs=[
                pair_spec,
                pl.BlockSpec((rows, 128), lambda i, c, n: (0, i + start + pairs)),
                pl.BlockSpec((rows, 128), lambda i, c, n: (0, i + start + 2 * pairs)),
                pair_spec,
                pair_spec,
                pl.BlockSpec((1, 8, rows), lambda i, c, n: (i + start, 0, 0)),
            ]
            + [pl.BlockSpec(memory_space=pl.ANY)] * len(before),
            out_specs=[pair_spec, pair_spec, pair_spec],
            scratch_shapes=[
                pltpu.VMEM((128, rows), F32),
                pltpu.VMEM((rows, 128), F32),
                pltpu.VMEM((rows, 128), F32),
            ],
        ),
        out_shape=[jax.ShapeDtypeStruct((rows, D), BF16)] * 3,
        input_output_aliases={8 + i: i for i in range(len(before))},
        compiler_params=params(16),
        cost_estimate=cost(6e9 * count, 2e6 * count, 2 * rows * rows * 0.6 * count),
    )(core, lengths, qkv, qkv, qkv, a, da, lse, *before)


def valid_rows(core_ref, len_ref, block):
    pos = pl.program_id(0) * block + lax.broadcasted_iota(jnp.int32, (block, 1), 0)
    return pos < len_ref[core_ref[0]]


def add_row(acc_ref, row, value):
    acc_ref[row : row + 1, :] += jnp.sum(value, axis=0, keepdims=True)


def row_block(core, i, steps):
    half = steps // 2
    return jnp.where(i < half, (1 - core) * half + i, core * half + i - half)


def up_kernel(group, core_ref, len_ref, seat_ref, x_ref, a_ref, og_ref, vec_ref, *refs):
    refs, (mid_ref, h_ref, e_ref, slope_ref, dy_ref, wo_ref, wu_ref, sems) = refs[:-8], refs[-8:]
    block = x_ref.shape[0]

    @pl.when(pl.program_id(0) == 0)
    def _():
        group.start(refs, core_ref, seat_ref, 0, D // 2, wo_ref, sems.at[0])
        group.start(refs, core_ref, seat_ref, D // 2, FF // 2, wu_ref, sems.at[1])
        wait_all(wo_ref, sems.at[0])
        wait_all(wu_ref, sems.at[1])

    valid = valid_rows(core_ref, len_ref, block)
    dy_ref[...] = jnp.where(valid, og_ref[...].astype(F32), 0.0).astype(BF16)
    mid = x_ref[...].astype(F32) + mm(a_ref[...], wo_ref[...]) + vec_ref[4:5, :]
    mid_ref[...] = mid
    normed, _ = norm_parts(mid)
    h = (normed * vec_ref[5:6, :] + vec_ref[6:7, :]).astype(BF16)
    h_ref[...] = h

    def act(j, z):
        cols = slice(j * D, (j + 1) * D)
        z = z + vec_ref[8 + j : 9 + j, :]
        squared = z * z
        turned = jnp.tanh(z * (GELU_ROOT + (GELU_ROOT * GELU_CUBE) * squared))
        half = 0.5 * turned + 0.5
        act = z * half
        e_ref[:, cols] = act.astype(BF16)
        slope = half + act * (1.0 - turned) * (GELU_ROOT + (3.0 * GELU_ROOT * GELU_CUBE) * squared)
        slope_ref[:, cols] = slope.astype(BF16)

    waiting = None
    for j in range(FF // D):
        z = mm(h, wu_ref[:, j * D : (j + 1) * D])
        if waiting is not None:
            act(*waiting)
        waiting = (j, z)
    act(*waiting)


def up_call(core, lengths, seats, x, a, og, vec, group, block=256):
    rows = x.shape[0]
    row_spec = pl.BlockSpec((block, D), lambda i, *s: (i, 0))
    wide_spec = pl.BlockSpec((block, FF), lambda i, *s: (i, 0))
    low, wide = [jax.ShapeDtypeStruct((rows, width), BF16) for width in (D, FF)]
    return pl.pallas_call(
        functools.partial(up_kernel, group),
        name="up",
        grid_spec=pltpu.PrefetchScalarGridSpec(
            num_scalar_prefetch=3,
            grid=(rows // block,),
            in_specs=[row_spec, row_spec, row_spec, whole_spec(vec.shape)] + group.specs(),
            out_specs=[row_spec, row_spec, wide_spec, wide_spec, row_spec],
            scratch_shapes=[
                pltpu.VMEM((D, D), BF16),
                pltpu.VMEM((D, FF), BF16),
                pltpu.SemaphoreType.DMA((2,)),
            ],
        ),
        out_shape=[
            jax.ShapeDtypeStruct((rows, D), F32),
            low,
            wide,
            wide,
            low,
        ],
        compiler_params=params(48),
        cost_estimate=cost(6e9, 30e6, rows * FF),
    )(core, lengths, seats, x, a, og, vec, *group.arrays)


def down_kernel(up_group, down_group, core_ref, seat_ref, mid_ref, slope_ref, dy_ref, vec_ref, *refs):
    count = len(up_group.arrays)
    up_refs, down_refs = refs[:count], refs[count : count + len(down_group.arrays)]
    dz_ref, dmb_ref, dm_ref, da_ref, acc_ref, wo_ref, wu_ref, wd_ref, sems = refs[-9:]
    step = pl.program_id(0)

    @pl.when(step == 0)
    def _():
        down_group.start(down_refs, core_ref, seat_ref, 0, D // 2, wd_ref, sems.at[2])
        up_group.start(up_refs, core_ref, seat_ref, D // 2, FF // 2, wu_ref, sems.at[1])
        up_group.start(up_refs, core_ref, seat_ref, 0, D // 2, wo_ref, sems.at[0])
        acc_ref[...] = jnp.zeros_like(acc_ref)
        wait_all(wd_ref, sems.at[2])

    mid = mid_ref[...]
    @pl.when(step == 0)
    def _():
        wait_all(wu_ref, sems.at[1])
        wait_all(wo_ref, sems.at[0])

    dy = dy_ref[...]
    add_row(acc_ref, 7, dy.astype(F32))
    dh = None
    waiting = None
    for j in range(FF // D + 1):
        later = None
        if j < FF // D:
            later = (j, mm(dy, wd_ref[j * D : (j + 1) * D, :], NT))
        if waiting is not None:
            at, de = waiting
            cols = slice(at * D, (at + 1) * D)
            dz = (de * slope_ref[:, cols].astype(F32)).astype(BF16)
            dz_ref[:, cols] = dz
            add_row(acc_ref, 8 + at, dz.astype(F32))
            part = mm(dz, wu_ref[:, cols], NT)
            dh = part if dh is None else dh + part
        waiting = later
    normed, scale = norm_parts(mid)
    add_row(acc_ref, 5, dh * normed)
    add_row(acc_ref, 6, dh)
    dm = dy.astype(F32) + norm_back(dh * vec_ref[5:6, :], normed, scale)
    dm_ref[...] = dm
    dm_low = dm.astype(BF16)
    dmb_ref[...] = dm_low
    add_row(acc_ref, 4, dm_low.astype(F32))
    da_ref[...] = mm(dm_low, wo_ref[...], NT).astype(BF16)


def down_call(core, seats, mid, slope, dy, vec, up_group, down_group, block=256):
    rows = mid.shape[0]
    row_spec, wide_spec = [
        pl.BlockSpec((block, width), lambda i, *s: (i, 0)) for width in (D, FF)
    ]
    return pl.pallas_call(
        functools.partial(down_kernel, up_group, down_group),
        name="down",
        grid_spec=pltpu.PrefetchScalarGridSpec(
            num_scalar_prefetch=2,
            grid=(rows // block,),
            in_specs=[row_spec, wide_spec, row_spec, whole_spec(vec.shape)]
            + up_group.specs()
            + down_group.specs(),
            out_specs=[
                wide_spec, row_spec, row_spec, row_spec,
                pl.BlockSpec((16, D), lambda i, *s: (0, 0)),
            ],
            scratch_shapes=[
                pltpu.VMEM((D, D), BF16),
                pltpu.VMEM((D, FF), BF16),
                pltpu.VMEM((FF, D), BF16),
                pltpu.SemaphoreType.DMA((3,)),
            ],
        ),
        out_shape=[
            jax.ShapeDtypeStruct((rows, FF), BF16),
            jax.ShapeDtypeStruct((rows, D), BF16),
            jax.ShapeDtypeStruct((rows, D), F32),
            jax.ShapeDtypeStruct((rows, D), BF16),
            jax.ShapeDtypeStruct((16, D), F32),
        ],
        compiler_params=params(48),
        cost_estimate=cost(1.1e10, 28e6),
    )(core, seats, mid, slope, dy, vec, *up_group.arrays, *down_group.arrays)


def out_kernel(group, core_ref, len_ref, seat_ref, mid_ref, e_ref, vec_ref, *refs):
    refs, (theirs_ref, mine_ref, wd_ref, sems) = refs[:-4], refs[-4:]
    block = mid_ref.shape[0]
    step, steps = pl.program_id(0), pl.num_programs(0)

    @pl.when(step == 0)
    def _():
        group.start(refs, core_ref, seat_ref, 0, D // 2, wd_ref, sems.at[0])
        wait_all(wd_ref, sems.at[0])

    down = vec_ref[7:8, :] + mid_ref[...] + mm(e_ref[...], wd_ref[...])
    pos = row_block(core_ref[0], step, steps) * block + lax.broadcasted_iota(jnp.int32, (block, 1), 0)
    down = jnp.where(pos < len_ref[core_ref[0]], down, 0.0).astype(BF16)

    @pl.when(step < steps // 2)
    def _():
        theirs_ref[...] = down

    @pl.when(step >= steps // 2)
    def _():
        mine_ref[0] = down


def out_call(core, lengths, seats, mid, e, vec, group, block=256):
    rows = mid.shape[0]
    steps = rows // block
    half = steps // 2
    row_spec, wide_spec = [
        pl.BlockSpec((block, width), lambda i, c, *s: (row_block(c[0], i, steps), 0)) for width in (D, FF)
    ]
    return pl.pallas_call(
        functools.partial(out_kernel, group),
        name="out",
        grid_spec=pltpu.PrefetchScalarGridSpec(
            num_scalar_prefetch=3,
            grid=(steps,),
            in_specs=[row_spec, wide_spec, whole_spec(vec.shape)] + group.specs(),
            out_specs=[
                pl.BlockSpec((block, D), lambda i, *s: (jnp.minimum(i, half - 1), 0)),
                pl.BlockSpec((1, block, D), lambda i, c, *s: (c[0], jnp.maximum(i - half, 0), 0)),
            ],
            scratch_shapes=[pltpu.VMEM((FF, D), BF16), pltpu.SemaphoreType.DMA((1,))],
        ),
        out_shape=[
            jax.ShapeDtypeStruct((rows // 2, D), BF16),
            jax.ShapeDtypeStruct((2, rows // 2, D), BF16),
        ],
        compiler_params=params(20),
        cost_estimate=cost(4.9e9, 16e6),
    )(core, lengths, seats, mid, e, vec, *group.arrays)


def pick(values, half, mode):
    if mode == "split":
        width = values.shape[1] // 2
        return [values[:, half * width : (half + 1) * width]]
    return [values[:, at : at + 128] for at in range(half * 128, values.shape[1], 256)]


def weight_grad_kernel(lefts, rights, mode, core_ref, *refs):
    left_refs, right_refs = refs[:lefts], refs[lefts : lefts + sum(rights)]
    own_ref, other_ref = refs[-2:]
    halves = ([], [])
    at = 0
    for left_ref, count in zip(left_refs, rights):
        left = left_ref[...]
        for right_ref in right_refs[at : at + count]:
            whole = mm(left, right_ref[...], TN).astype(BF16)
            for half in range(2):
                halves[half].extend(pick(whole, half, mode))
        at += count
    low, high = [part[0] if len(part) == 1 else jnp.concatenate(part, axis=1) for part in halves]

    @pl.when(core_ref[0] == 0)
    def _():
        own_ref[...] = low
        other_ref[...] = high

    @pl.when(core_ref[0] != 0)
    def _():
        own_ref[...] = high
        other_ref[...] = low


def weight_grad_call(core, products, block, name, mode="split", cols=None):
    rows, height = products[0][0].shape
    lefts = [left for left, _ in products]
    rights = [right for _, group in products for right in group]
    widths = [right.shape[1] if cols is None else cols[0] for right in rights]
    width = sum(widths)
    seat = 0 if cols is None else cols[1]
    return pl.pallas_call(
        functools.partial(weight_grad_kernel, len(lefts), [len(group) for _, group in products], mode),
        name=name,
        grid_spec=pltpu.PrefetchScalarGridSpec(
            num_scalar_prefetch=1,
            grid=(height // block,),
            in_specs=[pl.BlockSpec((rows, block), lambda i, c: (0, i))] * len(lefts)
            + [
                pl.BlockSpec((rows, w), lambda i, c: (0, seat), pipeline_mode=pl.Buffered(1)) for w in widths
            ],
            out_specs=[pl.BlockSpec((block, width // 2), lambda i, c: (i, 0))] * 2,
        ),
        out_shape=[jax.ShapeDtypeStruct((height, width // 2), BF16)] * 2,
        compiler_params=params(16 if mode == "turns" else 48),
        cost_estimate=cost(2 * rows * height * width, rows * (height + width) * 2 + height * width * 2),
    )(core, *lefts, *rights)


def last_kernel(
    core_ref, x_ref, dm_ref, dq_ref, dk_ref, dv_ref, w_ref, vec_ref, before_ref, theirs_ref, mine_ref, acc_ref
):
    step, steps = pl.program_id(0), pl.num_programs(0)

    @pl.when(step == 0)
    def _():
        acc_ref[...] = before_ref[...]

    subs = sub_blocks(x_ref.shape[0])

    def product(rows):
        return (
            mm(dq_ref[rows, :], w_ref[:D])
            + mm(dk_ref[rows, :], w_ref[D : 2 * D])
            + mm(dv_ref[rows, :], w_ref[2 * D :])
        )

    grads = []
    dh = product(subs[0])
    add_row(acc_ref, 2, dq_ref[...].astype(F32))
    add_row(acc_ref, 3, dv_ref[...].astype(F32))
    for at, rows in enumerate(subs):
        later = product(subs[at + 1]) if at + 1 < len(subs) else None
        normed, scale = norm_parts(x_ref[rows, :].astype(F32))
        add_row(acc_ref, 0, dh * normed)
        add_row(acc_ref, 1, dh)
        grads.append(dm_ref[rows, :] + norm_back(dh * vec_ref[0:1, :], normed, scale))
        dh = later

    @pl.when(step < steps // 2)
    def _():
        for rows, grad in zip(subs, grads):
            theirs_ref[rows, :] = grad

    @pl.when(step >= steps // 2)
    def _():
        for rows, grad in zip(subs, grads):
            mine_ref[0, rows, :] = grad


def last_call(core, x, dm, dq, dk, dv, w, vec, before, block=256):
    rows = x.shape[0]
    steps = rows // block
    half = steps // 2
    row_spec = pl.BlockSpec((block, D), lambda i, c, *s: (row_block(c[0], i, steps), 0))
    return pl.pallas_call(
        last_kernel,
        name="last",
        grid_spec=pltpu.PrefetchScalarGridSpec(
            num_scalar_prefetch=1,
            grid=(steps,),
            in_specs=[row_spec] * 5 + [whole_spec(part.shape) for part in (w, vec, before)],
            out_specs=[
                pl.BlockSpec((block, D), lambda i, *s: (jnp.minimum(i, half - 1), 0)),
                pl.BlockSpec((1, block, D), lambda i, c, *s: (c[0], jnp.maximum(i - half, 0), 0)),
                pl.BlockSpec((16, D), lambda i, *s: (0, 0)),
            ],
        ),
        out_shape=[
            jax.ShapeDtypeStruct((rows // 2, D), F32),
            jax.ShapeDtypeStruct((2, rows // 2, D), F32),
            jax.ShapeDtypeStruct((16, D), F32),
        ],
        compiler_params=params(12),
        cost_estimate=cost(rows * 6 * D * D, 16e6),
    )(core, x, dm, dq, dk, dv, w, vec, before)


def adam_kernel(plans, sources, core_ref, *refs):
    halves = [refs[2 * i : 2 * i + 2] for i in range(sources)]
    count = len(plans)
    states = refs[2 * sources : 2 * sources + 3 * count]
    outs = refs[2 * sources + 3 * count : 2 * sources + 6 * count]
    grads = refs[2 * sources + 6 * count :]
    for core in range(2):

        @pl.when(core_ref[0] == core)
        def _():
            for (_, _, moves), grad_ref in zip(plans, grads):
                for source, start, width, place0, place1 in moves:
                    for half, place in ((0, place0), (1, place1)):
                        ref = halves[source][0 if half == core else 1]
                        grad_ref[:, place : place + width] = ref[:, start : start + width].astype(F32)

    for i, (rate, decay, _) in enumerate(plans):
        weight, first, second = states[3 * i : 3 * i + 3]
        new = adamw(weight[...], grads[i][...], first[...], second[...], rate, decay)
        for out, value in zip(outs[3 * i : 3 * i + 3], new):
            out[...] = value


def adam_call(core, halves, states, plans):
    flat = [part for pair in halves for part in pair]
    held = [part for state in states for part in state]
    spec = pl.BlockSpec(memory_space=pltpu.VMEM)
    news = pl.pallas_call(
        functools.partial(adam_kernel, plans, len(halves)),
        name="adam",
        in_specs=[pl.BlockSpec(memory_space=pltpu.SMEM)] + [spec] * (len(flat) + len(held)),
        out_specs=[spec] * len(held),
        out_shape=[jax.ShapeDtypeStruct(part.shape, F32) for part in held],
        scratch_shapes=[pltpu.VMEM(state[0].shape, F32) for state in states],
        compiler_params=params(12),
        cost_estimate=cost(1e6, 24 * sum(state[0].size for state in states)),
    )(core, *flat, *held)
    return [news[3 * i : 3 * i + 3] for i in range(len(states))]


def after(value, *others):
    if not others:
        return value
    return lax.optimization_barrier((value,) + others)[0]


def cut(array, axis, index, size=1):
    starts = [jnp.uint32(0)] * array.ndim
    sizes = list(array.shape)
    starts[axis], sizes[axis] = index, size
    return lax.dynamic_slice(array, starts, sizes)


class Grid:
    def __init__(self, chips):
        log = chips.bit_length() - 1
        side = 1 << (log // 3)
        if side * side * (chips // (side * side)) != chips:
            side = 1
        self.chips = chips
        self.n = side
        self.nz = chips // (side * side)
        self.core = lax.axis_index("seq")
        self.chip = lax.axis_index("dp")
        self.x = self.chip % side
        self.y = self.chip // side % side
        self.z = self.chip // (side * side)

    def pin(self, value):
        n, core = self.n, self.core
        first, second = self.coords(core)
        places = {
            "core": core,
            "other": 1 - core,
            "chip": self.chip,
            "seats": self.seats(True),
            "q_seats": self.seats(False),
        }
        for s in range(n):
            for t in range(n):
                places["plane", s, t] = self.plane((first + s) % n, (second + t) % n, core)
        for at in range(self.nz):
            places["z", at] = self.z ^ at
        names = list(places)
        held = lax.optimization_barrier((value, *[places[name].astype(jnp.uint32) for name in names]))
        self.places = dict(zip(names, held[1:]))
        return held[0]

    def plane(self, first, second, core):
        return jnp.where(core == 0, second * self.n + first, first * self.n + second)

    def coords(self, core):
        return jnp.where(core == 0, self.x, self.y), jnp.where(core == 0, self.y, self.x)

    def permute(self, value, axis, shift=0):
        pairs = []
        for chip in range(self.chips):
            for core in range(2):
                x, y, z = chip % self.n, chip // self.n % self.n, chip // (self.n * self.n)
                to_core = core
                if axis == "z":
                    z = (z + shift) % self.nz
                elif axis == "zx":
                    z = z ^ shift
                elif axis == "core":
                    to_core = 1 - core
                elif (axis == "first") == (core == 0):
                    x = (x + shift) % self.n
                else:
                    y = (y + shift) % self.n
                pairs.append((chip * 2 + core, ((z * self.n + y) * self.n + x) * 2 + to_core))
        return lax.ppermute(value, ("dp", "seq"), pairs)

    def swap(self, value):
        return self.permute(value, "core")

    def join(self, own, other, axis):
        return jnp.where(
            self.places["core"] == 0,
            jnp.concatenate([own, other], axis),
            jnp.concatenate([other, own], axis),
        )

    def seats(self, halving):
        found = []
        for half in range(2):
            core = self.core if half == 0 else 1 - self.core
            first, second = self.coords(core)
            for s2 in range(self.n):
                for s1 in range(self.n):
                    flat = self.plane((first - s1) % self.n, (second - s2) % self.n, core)
                    for sz in range(self.nz):
                        z = self.z ^ sz if halving else (self.z - sz) % self.nz
                        found.append(z * self.n * self.n + flat)
        return jnp.stack(found).astype(jnp.int32)

    def small(self, value, axis, shifts, *until):
        got = [after(self.permute(value, axis, s), *until) for s in shifts]
        return value + sum(got), got

    def gather_z(self, block, *until):
        return jnp.stack([block] + [after(self.permute(block, "z", s), *until) for s in range(1, self.nz)])

    def gather_bit(self, held, bit, *until):
        return jnp.concatenate([held, after(self.permute(held, "zx", bit), *until)])

    def along(self, axis, column, *until):
        return [after(self.permute(column, axis, s), *until) for s in range(1, self.n)]

    def plane_parts(self, column, firsts, seconds, passed):
        parts = [column] + firsts
        for s2 in range(1, self.n):
            parts += [seconds[s2 - 1]] + [passed[s1 - 1][s2 - 1] for s1 in range(1, self.n)]
        return [part[None] for part in parts]

    def gather_first(self, column, *until):
        return jnp.stack([column] + [after(self.permute(column, "first", s), *until) for s in range(1, self.n)])

    def gather_second(self, line, *until):
        return [after(self.permute(line, "second", s), *until) for s in range(1, self.n)]

    def scatter_first(self, own, pair, *until):
        rows, cols = own.shape[0] // self.chips, own.shape[1]
        n = self.n

        def seat(s1, s2):
            own_part, pair_part = [
                cut(part.reshape(self.nz, n * n, rows, cols), 1, self.places["plane", s1, s2]).astype(F32)
                for part in (own, pair)
            ]
            return own_part + pair_part

        kept = [seat(0, t) for t in range(n)]
        for s in range(1, n):
            send = jnp.stack([seat(s, t).astype(BF16) for t in range(n)])
            got = after(self.permute(send, "first", s), *until)
            kept = [kept[t] + got[t].astype(F32) for t in range(n)]
        return kept[0], [part.astype(BF16) for part in kept[1:]]

    def scatter_second(self, kept, *until):
        mine, rest = kept
        got = [after(self.permute(rest[s - 1], "second", s), *until) for s in range(1, self.n)]
        for part in got:
            mine = mine + part.astype(F32)
        return mine.reshape((self.nz,) + mine.shape[2:]), got

    def order_z(self, mine):
        return [cut(mine, 0, self.places["z", at])[0] for at in range(self.nz)]

    def scatter_bit(self, parts, *until):
        half = len(parts) // 2
        send = parts[half] if half == 1 else jnp.stack([part.astype(BF16) for part in parts[half:]])
        got = after(self.permute(send.astype(BF16), "zx", half), *until)
        if half == 1:
            return [parts[0] + got.astype(F32)], got
        return [part + got[at].astype(F32) for at, part in enumerate(parts[:half])], got

    def scatter_z(self, parts, *until):
        while len(parts) > 1:
            parts, _ = self.scatter_bit(parts, *until)
        return parts[0]


def adamw(weight, gradient, first_moment, second_moment, step_rate, weight_decay):
    first_moment = BETA_ONE * first_moment + (1.0 - BETA_ONE) * gradient
    second_moment = BETA_TWO * second_moment + (1.0 - BETA_TWO) * gradient * gradient
    first_fix = 1.0 - BETA_ONE**STEP
    second_fix = 1.0 - BETA_TWO**STEP
    direction = first_moment / first_fix / (jnp.sqrt(second_moment / second_fix) + EPS_ADAM)
    return (weight - step_rate * (direction + weight_decay * weight), first_moment, second_moment)


def local(
    block_in, lengths, out_grad, w_qkv, w_out, w_up, w_down, vectors,
    first_qkv, first_out, first_up, first_down, first_vectors,
    second_qkv, second_out, second_up, second_down, second_vectors,
):
    grid = Grid(lax.axis_size("dp"))
    core = grid.core
    w_qkv_first = grid.pin(w_qkv)
    places = grid.places
    core_arr = places["core"].reshape(1).astype(jnp.int32)
    half_len = block_in.shape[1]
    vec_count, vec_here = vectors.shape

    def own_slot(halves):
        mine, theirs = [cut(halves, 0, places[name])[0] for name in ("core", "other")]
        return grid.join(mine, grid.swap(theirs), 0)

    def both_slots(mine, got):
        zero = jnp.uint32(0)
        return lax.dynamic_update_slice(mine, got[None], (places["other"], zero, zero))

    def half_of(shard):
        width = shard.shape[1] // 2
        return jnp.where(places["core"] == 0, shard[:, :width], shard[:, width:]).astype(BF16)

    seats, q_seats = [places[name].astype(jnp.int32) for name in ("seats", "q_seats")]

    turned = jnp.pad(vectors.T.astype(BF16), ((0, 0), (0, 128 - vec_count)))
    q_block = jnp.concatenate([half_of(w_qkv_first), turned], axis=1)
    u_block = jnp.concatenate([half_of(w_out), half_of(w_up)], axis=1)
    d_block = half_of(w_down)
    q_col = grid.gather_z(q_block)
    x = own_slot(block_in)
    bits = [1 << at for at in range((grid.nz - 1).bit_length())]
    u_col, d_col = u_block[None], d_block[None]
    for bit in bits[:-1]:
        u_col = grid.gather_bit(u_col, bit)
        d_col = grid.gather_bit(d_col, bit)
    q_line = after(grid.gather_first(q_col, x), u_col, d_col)
    q_rest = grid.gather_second(q_line)
    u_col = grid.gather_bit(after(u_col, q_line), bits[-1])
    q_line_swap = grid.swap(q_line)
    q_rest_swap = [grid.swap(after(part, u_col)) for part in q_rest]
    q_group = finish_group(grid, q_seats, [q_line] + q_rest, [q_line_swap] + q_rest_swap)

    h1, qkv, vec, w_back = qkv_call(core_arr, q_seats, x, q_group)
    u_firsts = grid.along("first", u_col, qkv)
    d_col = grid.gather_bit(after(d_col, u_col), bits[-1], qkv)
    og = own_slot(after(out_grad, qkv))
    att = attend_call(core_arr, lengths, after(qkv, d_col, *u_firsts), 0, 4, ())
    u_seconds = grid.along("second", u_col, *att)
    u_passed = [grid.along("second", part, *att) for part in u_firsts]
    early = [after(grid.swap(part), *att) for part in [u_col] + u_firsts]
    d_col = after(d_col, *u_seconds, *[part for parts in u_passed for part in parts])
    a, lse = attend_call(core_arr, lengths, after(qkv, d_col), 4, 2, att)
    late_seconds = [after(grid.swap(part), a) for part in u_seconds]
    late_passed = [[after(grid.swap(part), a) for part in parts] for parts in u_passed]
    u_group = finish_group(
        grid,
        seats,
        grid.plane_parts(u_col, u_firsts, u_seconds, u_passed),
        grid.plane_parts(early[0], early[1:], late_seconds, late_passed),
    )
    mid, h2, e, slope, dy = up_call(core_arr, lengths, seats, x, a, og, vec, u_group)
    d_firsts = grid.along("first", d_col, mid)
    d_seconds = grid.along("second", d_col, mid)
    d_col_swap = after(grid.swap(d_col), mid)
    d_own, d_other = weight_grad_call(
        core_arr, [(after(e, *d_firsts, *d_seconds), [dy])], 512, "grad_down"
    )
    d_passed = [grid.along("second", part, d_own) for part in d_firsts]
    early = [[after(grid.swap(part), d_own) for part in parts] for parts in (d_firsts, d_seconds)]
    d_group = finish_group(
        grid,
        seats,
        grid.plane_parts(d_col, d_firsts, d_seconds, d_passed),
        grid.plane_parts(d_col_swap, *early, [[grid.swap(part) for part in parts] for parts in d_passed]),
    )
    dz, dmb, dm, da, acc_mid = down_call(core_arr, seats, mid, slope, dy, vec, u_group, d_group)

    d_pair = after(grid.swap(d_other), dz)
    u_own, u_other = weight_grad_call(
        core_arr, [(a, [dmb]), (h2, [after(dz, d_pair)])], 384, "grad_up"
    )
    d_kept = grid.scatter_first(d_own, d_pair, u_own)

    def back_call(start, count, before, *needs):
        return attend_back_call(core_arr, lengths, qkv, a, after(da, *needs), lse, start, count, before)

    back = back_call(0, 2, (), u_own, *d_kept[1])
    d_sum, d_here = grid.scatter_second(d_kept, *back)
    u_pair = after(grid.swap(u_other), *back)
    back = back_call(2, 4, back, u_pair, *d_here)
    d_parts, d_got = grid.scatter_bit(grid.order_z(d_sum), *back)
    u_kept = grid.scatter_first(u_own, u_pair, *back)
    dq, dk, dv = back
    q_own, q_other = weight_grad_call(
        core_arr, [(h1, [after(dq, d_got, *u_kept[1]), dk, dv])], 384, "grad_qkv", "turns"
    )
    u_sum, u_here = grid.scatter_second(u_kept, q_own)
    q_pair = grid.swap(after(q_other, *u_here))
    in_theirs, in_mine, acc = last_call(
        core_arr, x, dm, after(dq, q_own, q_pair), dk, dv, w_back, vec, acc_mid
    )
    d_mine = grid.scatter_z(d_parts, in_theirs)
    d_other_mine = grid.swap(d_mine)
    q_kept = grid.scatter_first(q_own, q_pair, in_theirs)
    u_parts, u_got = grid.scatter_bit(grid.order_z(u_sum), *q_kept[1])
    q_sum, q_here = grid.scatter_second(q_kept, u_got)
    down_new, = adam_call(
        core_arr,
        [(d_mine, d_other_mine)],
        [(after(w_down, *q_kept[1]), first_down, second_down)],
        [(FF ** (-0.5), MATRIX_DECAY, [(0, 0, D // 2, 0, D // 2)])],
    )
    in_got = grid.swap(after(in_theirs, *q_kept[1]))
    in_grad = both_slots(in_mine, after(in_got, *q_here))
    w_qkv = after(w_qkv, in_grad)
    shifts = range(1, grid.n)
    vec_total, _ = grid.small(acc, "core", [0])
    vec_total, _ = grid.small(vec_total, "first", shifts, *q_kept[1])
    vec_total, vec_here_got = grid.small(vec_total, "second", shifts, *q_here)
    out_theirs, out_mine = out_call(
        core_arr, lengths, seats, after(mid, *q_here, *vec_here_got), e, vec, d_group
    )
    u_mine = grid.scatter_z([after(part, *q_here) for part in u_parts], out_theirs)
    u_other_mine = grid.swap(u_mine)
    q_parts, q_got = grid.scatter_bit(grid.order_z(q_sum), out_theirs)
    block_out = both_slots(out_mine, grid.swap(out_theirs))
    until = (out_theirs,)
    for bit in bits[:-1]:
        vec_total, _ = grid.small(vec_total, "zx", [bit], *until)
    while len(q_parts) > 1:
        q_parts, q_got = grid.scatter_bit(q_parts)
    vec_total, _ = grid.small(vec_total, "zx", [bits[-1]], q_got)
    q_mine = q_parts[0]
    q_other_mine = grid.swap(q_mine)

    half, wide = D // 2, FF // 2
    out_new, up_new = adam_call(
        core_arr,
        [(u_mine, u_other_mine)],
        [(after(w_out, in_grad), first_out, second_out), (w_up, first_up, second_up)],
        [
            ((D // 64) ** (-0.5), MATRIX_DECAY, [(0, 0, half, 0, half)]),
            (D ** (-0.5), MATRIX_DECAY, [(0, half, wide, 0, wide)]),
        ],
    )
    moves = []
    for turn in range(3 * D // 256):
        moves.append((0, turn * 128, 128, turn * 256, turn * 256 + 128))
    qkv_new, = adam_call(
        core_arr,
        [(q_mine, q_other_mine)],
        [(w_qkv, first_qkv, second_qkv)],
        [(D ** (-0.5), MATRIX_DECAY, moves)],
    )
    vec_grad = cut(vec_total[:vec_count].reshape(vec_count, -1, vec_here), 1, places["chip"])[:, 0]
    vec_new = adamw(vectors, vec_grad, first_vectors, second_vectors, VECTOR_RATE, 0.0)
    news = [qkv_new, out_new, up_new, down_new, vec_new]
    return (block_out, in_grad) + tuple(new[kind] for kind in range(3) for new in news)


def finish_group(grid, seats, own, other):
    rows, cols = own[0].shape[-2:]
    if rows % 16 == 0:
        return Pieces(own + other, rows)
    found = []
    for half, parts in enumerate((own, other)):
        here = seats[half * grid.chips : (half + 1) * grid.chips]
        order = jnp.zeros((grid.chips,), jnp.int32).at[here].set(jnp.arange(grid.chips, dtype=jnp.int32))
        blocks = jnp.concatenate(parts).reshape(grid.chips, rows, cols)
        found.append(jnp.take(blocks, order, axis=0).reshape(1, 1, grid.chips * rows, cols))
    return Pieces(found, grid.chips * rows, True)


def solution(mesh):
    weight = P("dp", None)
    vector = P(None, "dp")
    state = (weight, weight, weight, weight, vector)
    tokens = P("dp", "seq", None)
    return jax.shard_map(
        local,
        mesh=mesh,
        in_specs=(tokens, P("dp"), tokens) + state * 3,
        out_specs=(tokens, tokens) + state * 3,
        check_vma=False,
    )
```

```python
import functools

import jax
import jax.numpy as jnp
from jax import lax
from jax.experimental import pallas as pl
from jax.experimental.pallas import tpu as pltpu
from jax.sharding import PartitionSpec as P

D = 768
HEADS = 12
HEAD_DIM = 64
FF = 3072
STEP = 10

EPS_NORM = 1e-05
EPS_ADAM = 1e-08
BETA_ONE = 0.5
BETA_TWO = 0.5
MATRIX_DECAY = 0.1
VECTOR_RATE = 0.1
NEG_FILL = -1e30
GELU_ROOT = 0.7978845608028654
GELU_CUBE = 0.044715
QKV_HALF = 3 * D // 2

F32 = jnp.float32
BF16 = jnp.bfloat16

NN = (((1,), (0,)), ((), ()))
NT = (((1,), (1,)), ((), ()))
TN = (((0,), (0,)), ((), ()))


def mm(left, right, dims=NN):
    return lax.dot_general(left, right, dims, preferred_element_type=F32)


def cost(flops, nbytes, trans=0):
    return pl.CostEstimate(flops=int(4 * flops), bytes_accessed=int(4 * nbytes), transcendentals=int(trans))


def params(mib=60):
    return pltpu.CompilerParams(vmem_limit_bytes=mib * 1024 * 1024)


def held_spec():
    return pl.BlockSpec(memory_space=pltpu.VMEM)


def at_rows(block):
    return pl.ds(pl.multiple_of(pl.program_id(0) * block, block), block)


def whole_spec(shape):
    return pl.BlockSpec(shape, lambda *idx: (0,) * len(shape), pipeline_mode=pl.Buffered(1))


class Pieces:
    def __init__(self, arrays, rows, ordered=False):
        self.arrays = arrays
        self.rows = rows
        self.ordered = ordered
        self.halves = 2
        self.count = len(arrays) // self.halves
        self.lines, self.depth = arrays[0].shape[:2]

    def specs(self):
        return [pl.BlockSpec(memory_space=pltpu.HBM)] * len(self.arrays)

    def row(self, seat_ref, at):
        return 0 if self.ordered else pl.multiple_of(seat_ref[at] * self.rows, 16)

    def start(self, refs, core_ref, seat_ref, start_col, width, target, sem):
        core = core_ref[0]
        at = 0
        for half in range(self.halves):
            where = core if half == 0 else 1 - core
            for s2 in range(self.count):
                ref = refs[half * self.count + s2]
                for s1 in range(self.lines):
                    for sz in range(self.depth):
                        row = self.row(seat_ref, at)
                        at += 1
                        col = pl.multiple_of(where * width, 128)
                        pltpu.make_async_copy(
                            ref.at[s1, sz, :, pl.ds(start_col, width)],
                            target.at[pl.ds(row, self.rows), pl.ds(col, width)],
                            sem,
                        ).start()

    def start_once(self, refs, seat_ref, start_col, width, target, sem):
        at = 0
        for s2 in range(self.count):
            for s1 in range(self.lines):
                for sz in range(self.depth):
                    row = self.row(seat_ref, at)
                    at += 1
                    pltpu.make_async_copy(
                        refs[s2].at[s1, sz, :, pl.ds(start_col, width)],
                        target.at[pl.ds(row, self.rows), :],
                        sem,
                    ).start()


def wait_all(target, sem):
    pltpu.make_async_copy(target, target, sem).wait()


def norm_parts(rows):
    mean = jnp.mean(rows, axis=-1, keepdims=True)
    centred = rows - mean
    variance = jnp.mean(centred * centred, axis=-1, keepdims=True)
    scale = lax.rsqrt(variance + EPS_NORM)
    return centred * scale, scale


def norm_back(d_normed, normed, scale):
    first = jnp.mean(d_normed, axis=-1, keepdims=True)
    second = jnp.mean(d_normed * normed, axis=-1, keepdims=True)
    return scale * (d_normed - first - normed * second)


def qkv_kernel(group, core_ref, seat_ref, x_ref, *refs):
    refs, (h_ref, qkv_ref, vec_ref, back_ref, w_ref, turned_ref, sems) = refs[:-7], refs[-7:]

    @pl.when(pl.program_id(0) == 0)
    def _():
        group.start(refs, core_ref, seat_ref, 0, QKV_HALF, w_ref, sems.at[0])
        group.start_once(refs, seat_ref, QKV_HALF, 128, turned_ref, sems.at[1])
        wait_all(turned_ref, sems.at[1])
        vec_ref[...] = turned_ref[...].astype(F32).T[:16]
        wait_all(w_ref, sems.at[0])

    def norm(rows):
        normed, _ = norm_parts(x_ref[rows, :].astype(F32))
        h = (normed * vec_ref[0:1, :] + vec_ref[1:2, :]).astype(BF16)
        h_ref[rows, :] = h
        return h

    block = x_ref.shape[0]
    h = norm(slice(0, block))
    for part, bias in enumerate((2, None, 3)):
        cols = slice(part * D, (part + 1) * D)
        product = mm(h, w_ref[:, cols])
        if bias is not None:
            product = product + vec_ref[bias : bias + 1, :]
        qkv_ref[:, cols] = product.astype(BF16)

    @pl.when(pl.program_id(0) < 3)
    def _():
        back_ref[...] = w_ref[:, at_rows(D)].T


def sub_blocks(rows):
    return [slice(at, at + 256) for at in range(0, rows, 256)]


def qkv_call(core, seats, x, group, block=256):
    rows = x.shape[0]
    return pl.pallas_call(
        functools.partial(qkv_kernel, group),
        name="qkv",
        grid_spec=pltpu.PrefetchScalarGridSpec(
            num_scalar_prefetch=2,
            grid=(rows // block,),
            in_specs=[pl.BlockSpec((block, D), lambda i, *s: (i, 0))] + group.specs(),
            out_specs=[
                pl.BlockSpec((block, D), lambda i, *s: (i, 0)),
                pl.BlockSpec((block, 3 * D), lambda i, *s: (i, 0)),
                pl.BlockSpec((16, D), lambda i, *s: (0, 0)),
                pl.BlockSpec((D, D), lambda i, *s: (jnp.minimum(i, 2), 0)),
            ],
            scratch_shapes=[
                pltpu.VMEM((D, 3 * D), BF16),
                pltpu.VMEM((D, 128), BF16),
                pltpu.SemaphoreType.DMA((2,)),
            ],
        ),
        out_shape=[
            jax.ShapeDtypeStruct((rows, D), BF16),
            jax.ShapeDtypeStruct((rows, 3 * D), BF16),
            jax.ShapeDtypeStruct((16, D), F32),
            jax.ShapeDtypeStruct((3 * D, D), BF16),
        ],
        compiler_params=params(12),
        cost_estimate=cost(2 * rows * D * 3 * D, 10e6),
    )(core, seats, x, *group.arrays)


def head_parts(length, k_all, q_turned, head):
    full_len = k_all.shape[0]
    lane = lax.broadcasted_iota(jnp.int32, (1, 128), 1)
    row = lax.broadcasted_iota(jnp.int32, (128, 1), 0)
    zero, one = jnp.zeros((), BF16), jnp.ones((), BF16)
    mine = (lane // HEAD_DIM) == head
    spare = HEAD_DIM * (1 - head)
    pos = lax.broadcasted_iota(jnp.int32, (full_len, 128), 0)
    fill = jnp.where(pos < length, 0.0, NEG_FILL).astype(BF16)
    k_head = jnp.where(mine, k_all, jnp.where(lane == spare, fill, zero))
    q_head = jnp.where((row // HEAD_DIM) == head, q_turned, jnp.where(row == spare, one, zero))
    return mine, k_head, q_head


def causal_mask(scores, block):
    full = scores.shape[0]
    key_pos = lax.broadcasted_iota(jnp.int32, (block, block), 0)
    query_pos = lax.broadcasted_iota(jnp.int32, (block, block), 1)
    last = jnp.where(key_pos <= query_pos, scores[full - block :], NEG_FILL)
    if full == block:
        return last
    return jnp.concatenate([scores[: full - block], last], axis=0)


def attend_kernel(start, core_ref, len_ref, qkv_ref, *refs):
    a_ref, lse_ref, mixed_ref, scores_ref = refs[-4:]
    block = 256
    full_len = qkv_ref.shape[0]
    length = len_ref[core_ref[0]]
    q_all, k_all, v_all = [
        qkv_ref[:, pl.ds(pl.multiple_of((pl.program_id(0) + start) * 128 + part * D, 128), 128)] for part in range(3)
    ]
    q_all = q_all * jnp.asarray(HEAD_DIM ** (-0.5), BF16)
    v_turned = v_all.T
    q_turned = q_all.T
    ones = jnp.ones((16, full_len), BF16)
    parts = []
    for head in range(2):
        _, k_head, q_head = head_parts(length, k_all, q_turned, head)
        v_head = jnp.concatenate([v_turned[head * HEAD_DIM : (head + 1) * HEAD_DIM], ones], axis=0)
        parts.append((k_head, q_head, v_head))
    units = [(head, j) for j in reversed(range(full_len // block)) for head in range(2)]

    def score(at):
        head, j = units[at]
        k_head, q_head, _ = parts[head]
        top = None
        for i in range(j + 1):
            rows = slice(i * block, (i + 1) * block)
            tile = mm(k_head[rows], q_head[:, j * block : (j + 1) * block])
            if i == j:
                tile = causal_mask(tile, block)
            scores_ref[at % 2, rows, :] = tile
            part = jnp.max(tile.reshape(block // 8, 8, block), axis=0)
            top = part if top is None else jnp.maximum(top, part)
        return jnp.max(top, axis=0, keepdims=True)

    def finish(at, top):
        head, j = units[at]
        v_head = parts[head][2]
        cols = slice(j * block, (j + 1) * block)
        mixed = None
        for i in range(j + 1):
            rows = slice(i * block, (i + 1) * block)
            exped = jnp.exp(scores_ref[at % 2, rows, :] - top).astype(BF16)
            part = mm(v_head[:, rows], exped)
            mixed = part if mixed is None else mixed + part
        total = mixed[HEAD_DIM : HEAD_DIM + 1]
        mixed_ref[head * HEAD_DIM : (head + 1) * HEAD_DIM, cols] = mixed[:HEAD_DIM] / total
        lse_ref[0, head : head + 1, cols] = top + jnp.log(total)

    top = score(0)
    for at in range(len(units)):
        later = score(at + 1) if at + 1 < len(units) else None
        finish(at, top)
        top = later
    a_ref[...] = mixed_ref[...].T.astype(BF16)


def attend_call(core, lengths, qkv, first, count, before):
    rows = qkv.shape[0]
    pairs = HEADS // 2
    before = list(before)
    return pl.pallas_call(
        functools.partial(attend_kernel, first),
        name="attend",
        grid_spec=pltpu.PrefetchScalarGridSpec(
            num_scalar_prefetch=2,
            grid=(count,),
            in_specs=[held_spec()] + [pl.BlockSpec(memory_space=pl.ANY)] * len(before),
            out_specs=[
                pl.BlockSpec((rows, 128), lambda i, c, n: (0, i + first)),
                pl.BlockSpec((1, 8, rows), lambda i, c, n: (i + first, 0, 0)),
            ],
            scratch_shapes=[pltpu.VMEM((128, rows), F32), pltpu.VMEM((2, rows, 256), F32)],
        ),
        out_shape=[
            jax.ShapeDtypeStruct((rows, D), BF16),
            jax.ShapeDtypeStruct((pairs, 8, rows), F32),
        ],
        input_output_aliases={3 + i: i for i in range(len(before))},
        compiler_params=params(12),
        cost_estimate=cost(3e9 * count, 1.2e6 * count, 2 * rows * rows * 0.6 * count),
    )(core, lengths, qkv, *before)


def attend_back_kernel(core_ref, len_ref, q_ref, k_ref, v_ref, a_ref, da_ref, lse_ref, *refs):
    dq_ref, dk_ref, dv_ref, dqt_ref, dk_acc, dv_acc = refs[-6:]
    block = 256
    full_len = q_ref.shape[0]
    length = len_ref[core_ref[0]]
    scale = HEAD_DIM ** (-0.5)
    q_all = q_ref[...] * jnp.asarray(scale, BF16)
    k_all = k_ref[...]
    k_turned = k_all.T
    v_all = v_ref[...]
    da_all = da_ref[...]
    inner = (da_all.astype(F32) * a_ref[...].astype(F32)).T
    q_turned, da_turned = q_all.T, da_all.T
    parts = []
    for head in range(2):
        mine, k_head, q_head = head_parts(length, k_all, q_turned, head)
        zero = jnp.zeros((), BF16)
        q_plain = jnp.where(mine, q_all, zero)
        da_head = jnp.where(mine, da_all, zero)
        row = lax.broadcasted_iota(jnp.int32, (128, 1), 0)
        da_cols = jnp.where((row // HEAD_DIM) == head, da_turned, zero)
        lanes = slice(head * HEAD_DIM, (head + 1) * HEAD_DIM)
        centre = jnp.sum(inner[lanes], axis=0, keepdims=True)
        parts.append((k_head, q_plain, q_head, da_head, da_cols, lanes, centre))
    units = [
        (head, j, i)
        for j in reversed(range(full_len // block))
        for head in range(2)
        for i in range(j + 1)
    ]

    def score(at):
        head, j, i = units[at]
        k_head, _, q_head, _, da_cols, _, _ = parts[head]
        rows, cols = slice(i * block, (i + 1) * block), slice(j * block, (j + 1) * block)
        tile = mm(k_head[rows], q_head[:, cols])
        if i == j:
            tile = causal_mask(tile, block)
        return tile, mm(v_all[rows], da_cols[:, cols])

    seen = set()
    ready = score(0)
    dq_part = None
    for at, (head, j, i) in enumerate(units):
        later = score(at + 1) if at + 1 < len(units) else None
        scores, d_probs = ready
        _, q_plain, _, da_head, _, lanes, centre = parts[head]
        rows, cols = slice(i * block, (i + 1) * block), slice(j * block, (j + 1) * block)
        probs = jnp.exp(scores - lse_ref[0, head : head + 1, cols])
        d_scores = (probs * (d_probs - centre[:, cols])).astype(BF16)
        dv_part = mm(probs.astype(BF16), da_head[cols])
        dk_part = mm(d_scores, q_plain[cols])
        if i in seen:
            dv_acc[rows] += dv_part
            dk_acc[rows] += dk_part
        else:
            seen.add(i)
            dv_acc[rows] = dv_part
            dk_acc[rows] = dk_part
        part = mm(k_turned[lanes, rows], d_scores)
        dq_part = part if i == 0 else dq_part + part
        if i == j:
            dqt_ref[lanes, cols] = dq_part * scale
        ready = later
    dq_ref[...] = dqt_ref[...].T.astype(BF16)
    dk_ref[...] = dk_acc[...].astype(BF16)
    dv_ref[...] = dv_acc[...].astype(BF16)


def attend_back_call(core, lengths, qkv, a, da, lse, start, count, before):
    rows = qkv.shape[0]
    pairs = HEADS // 2
    before = list(before)
    pair_spec = pl.BlockSpec((rows, 128), lambda i, c, n: (0, i + start))
    return pl.pallas_call(
        attend_back_kernel,
        name="attend_back",
        grid_spec=pltpu.PrefetchScalarGridSpec(
            num_scalar_prefetch=2,
            grid=(count,),
            in_specs=[
                pair_spec,
                pl.BlockSpec((rows, 128), lambda i, c, n: (0, i + start + pairs)),
                pl.BlockSpec((rows, 128), lambda i, c, n: (0, i + start + 2 * pairs)),
                pair_spec,
                pair_spec,
                pl.BlockSpec((1, 8, rows), lambda i, c, n: (i + start, 0, 0)),
            ]
            + [pl.BlockSpec(memory_space=pl.ANY)] * len(before),
            out_specs=[pair_spec, pair_spec, pair_spec],
            scratch_shapes=[
                pltpu.VMEM((128, rows), F32),
                pltpu.VMEM((rows, 128), F32),
                pltpu.VMEM((rows, 128), F32),
            ],
        ),
        out_shape=[jax.ShapeDtypeStruct((rows, D), BF16)] * 3,
        input_output_aliases={8 + i: i for i in range(len(before))},
        compiler_params=params(16),
        cost_estimate=cost(6e9 * count, 2e6 * count, 2 * rows * rows * 0.6 * count),
    )(core, lengths, qkv, qkv, qkv, a, da, lse, *before)


def valid_rows(core_ref, len_ref, block):
    pos = pl.program_id(0) * block + lax.broadcasted_iota(jnp.int32, (block, 1), 0)
    return pos < len_ref[core_ref[0]]


def add_row(acc_ref, row, value):
    acc_ref[row : row + 1, :] += jnp.sum(value, axis=0, keepdims=True)


def row_block(core, i, steps):
    half = steps // 2
    return jnp.where(i < half, (1 - core) * half + i, core * half + i - half)


def up_kernel(group, core_ref, len_ref, seat_ref, x_ref, a_ref, og_ref, vec_ref, *refs):
    refs, (mid_ref, h_ref, e_ref, slope_ref, dy_ref, wo_ref, wu_ref, sems) = refs[:-8], refs[-8:]
    block = x_ref.shape[0]

    @pl.when(pl.program_id(0) == 0)
    def _():
        group.start(refs, core_ref, seat_ref, 0, D // 2, wo_ref, sems.at[0])
        group.start(refs, core_ref, seat_ref, D // 2, FF // 2, wu_ref, sems.at[1])
        wait_all(wo_ref, sems.at[0])
        wait_all(wu_ref, sems.at[1])

    valid = valid_rows(core_ref, len_ref, block)
    dy_ref[...] = jnp.where(valid, og_ref[...].astype(F32), 0.0).astype(BF16)
    mid = x_ref[...].astype(F32) + mm(a_ref[...], wo_ref[...]) + vec_ref[4:5, :]
    mid_ref[...] = mid
    normed, _ = norm_parts(mid)
    h = (normed * vec_ref[5:6, :] + vec_ref[6:7, :]).astype(BF16)
    h_ref[...] = h

    def act(j, z):
        cols = slice(j * D, (j + 1) * D)
        z = z + vec_ref[8 + j : 9 + j, :]
        squared = z * z
        turned = jnp.tanh(z * (GELU_ROOT + (GELU_ROOT * GELU_CUBE) * squared))
        half = 0.5 * turned + 0.5
        act = z * half
        e_ref[:, cols] = act.astype(BF16)
        slope = half + act * (1.0 - turned) * (GELU_ROOT + (3.0 * GELU_ROOT * GELU_CUBE) * squared)
        slope_ref[:, cols] = slope.astype(BF16)

    waiting = None
    for j in range(FF // D):
        z = mm(h, wu_ref[:, j * D : (j + 1) * D])
        if waiting is not None:
            act(*waiting)
        waiting = (j, z)
    act(*waiting)


def up_call(core, lengths, seats, x, a, og, vec, group, block=256):
    rows = x.shape[0]
    row_spec = pl.BlockSpec((block, D), lambda i, *s: (i, 0))
    wide_spec = pl.BlockSpec((block, FF), lambda i, *s: (i, 0))
    low, wide = [jax.ShapeDtypeStruct((rows, width), BF16) for width in (D, FF)]
    return pl.pallas_call(
        functools.partial(up_kernel, group),
        name="up",
        grid_spec=pltpu.PrefetchScalarGridSpec(
            num_scalar_prefetch=3,
            grid=(rows // block,),
            in_specs=[row_spec, row_spec, row_spec, whole_spec(vec.shape)] + group.specs(),
            out_specs=[row_spec, row_spec, wide_spec, wide_spec, row_spec],
            scratch_shapes=[
                pltpu.VMEM((D, D), BF16),
                pltpu.VMEM((D, FF), BF16),
                pltpu.SemaphoreType.DMA((2,)),
            ],
        ),
        out_shape=[
            jax.ShapeDtypeStruct((rows, D), F32),
            low,
            wide,
            wide,
            low,
        ],
        compiler_params=params(48),
        cost_estimate=cost(6e9, 30e6, rows * FF),
    )(core, lengths, seats, x, a, og, vec, *group.arrays)


def down_kernel(up_group, down_group, core_ref, seat_ref, mid_ref, slope_ref, dy_ref, vec_ref, *refs):
    count = len(up_group.arrays)
    up_refs, down_refs = refs[:count], refs[count : count + len(down_group.arrays)]
    dz_ref, dmb_ref, dm_ref, da_ref, acc_ref, wo_ref, wu_ref, wd_ref, sems = refs[-9:]
    step = pl.program_id(0)

    @pl.when(step == 0)
    def _():
        down_group.start(down_refs, core_ref, seat_ref, 0, D // 2, wd_ref, sems.at[2])
        up_group.start(up_refs, core_ref, seat_ref, D // 2, FF // 2, wu_ref, sems.at[1])
        up_group.start(up_refs, core_ref, seat_ref, 0, D // 2, wo_ref, sems.at[0])
        acc_ref[...] = jnp.zeros_like(acc_ref)
        wait_all(wd_ref, sems.at[2])

    mid = mid_ref[...]
    @pl.when(step == 0)
    def _():
        wait_all(wu_ref, sems.at[1])
        wait_all(wo_ref, sems.at[0])

    dy = dy_ref[...]
    add_row(acc_ref, 7, dy.astype(F32))
    dh = None
    waiting = None
    for j in range(FF // D + 1):
        later = None
        if j < FF // D:
            later = (j, mm(dy, wd_ref[j * D : (j + 1) * D, :], NT))
        if waiting is not None:
            at, de = waiting
            cols = slice(at * D, (at + 1) * D)
            dz = (de * slope_ref[:, cols].astype(F32)).astype(BF16)
            dz_ref[:, cols] = dz
            add_row(acc_ref, 8 + at, dz.astype(F32))
            part = mm(dz, wu_ref[:, cols], NT)
            dh = part if dh is None else dh + part
        waiting = later
    normed, scale = norm_parts(mid)
    add_row(acc_ref, 5, dh * normed)
    add_row(acc_ref, 6, dh)
    dm = dy.astype(F32) + norm_back(dh * vec_ref[5:6, :], normed, scale)
    dm_ref[...] = dm
    dm_low = dm.astype(BF16)
    dmb_ref[...] = dm_low
    add_row(acc_ref, 4, dm_low.astype(F32))
    da_ref[...] = mm(dm_low, wo_ref[...], NT).astype(BF16)


def down_call(core, seats, mid, slope, dy, vec, up_group, down_group, block=256):
    rows = mid.shape[0]
    row_spec, wide_spec = [
        pl.BlockSpec((block, width), lambda i, *s: (i, 0)) for width in (D, FF)
    ]
    return pl.pallas_call(
        functools.partial(down_kernel, up_group, down_group),
        name="down",
        grid_spec=pltpu.PrefetchScalarGridSpec(
            num_scalar_prefetch=2,
            grid=(rows // block,),
            in_specs=[row_spec, wide_spec, row_spec, whole_spec(vec.shape)]
            + up_group.specs()
            + down_group.specs(),
            out_specs=[
                wide_spec, row_spec, row_spec, row_spec,
                pl.BlockSpec((16, D), lambda i, *s: (0, 0)),
            ],
            scratch_shapes=[
                pltpu.VMEM((D, D), BF16),
                pltpu.VMEM((D, FF), BF16),
                pltpu.VMEM((FF, D), BF16),
                pltpu.SemaphoreType.DMA((3,)),
            ],
        ),
        out_shape=[
            jax.ShapeDtypeStruct((rows, FF), BF16),
            jax.ShapeDtypeStruct((rows, D), BF16),
            jax.ShapeDtypeStruct((rows, D), F32),
            jax.ShapeDtypeStruct((rows, D), BF16),
            jax.ShapeDtypeStruct((16, D), F32),
        ],
        compiler_params=params(48),
        cost_estimate=cost(1.1e10, 28e6),
    )(core, seats, mid, slope, dy, vec, *up_group.arrays, *down_group.arrays)


def out_kernel(group, core_ref, len_ref, seat_ref, mid_ref, e_ref, vec_ref, *refs):
    refs, (theirs_ref, mine_ref, wd_ref, sems) = refs[:-4], refs[-4:]
    block = mid_ref.shape[0]
    step, steps = pl.program_id(0), pl.num_programs(0)

    @pl.when(step == 0)
    def _():
        group.start(refs, core_ref, seat_ref, 0, D // 2, wd_ref, sems.at[0])
        wait_all(wd_ref, sems.at[0])

    down = vec_ref[7:8, :] + mid_ref[...] + mm(e_ref[...], wd_ref[...])
    pos = row_block(core_ref[0], step, steps) * block + lax.broadcasted_iota(jnp.int32, (block, 1), 0)
    down = jnp.where(pos < len_ref[core_ref[0]], down, 0.0).astype(BF16)

    @pl.when(step < steps // 2)
    def _():
        theirs_ref[...] = down

    @pl.when(step >= steps // 2)
    def _():
        mine_ref[0] = down


def out_call(core, lengths, seats, mid, e, vec, group, block=256):
    rows = mid.shape[0]
    steps = rows // block
    half = steps // 2
    row_spec, wide_spec = [
        pl.BlockSpec((block, width), lambda i, c, *s: (row_block(c[0], i, steps), 0)) for width in (D, FF)
    ]
    return pl.pallas_call(
        functools.partial(out_kernel, group),
        name="out",
        grid_spec=pltpu.PrefetchScalarGridSpec(
            num_scalar_prefetch=3,
            grid=(steps,),
            in_specs=[row_spec, wide_spec, whole_spec(vec.shape)] + group.specs(),
            out_specs=[
                pl.BlockSpec((block, D), lambda i, *s: (jnp.minimum(i, half - 1), 0)),
                pl.BlockSpec((1, block, D), lambda i, c, *s: (c[0], jnp.maximum(i - half, 0), 0)),
            ],
            scratch_shapes=[pltpu.VMEM((FF, D), BF16), pltpu.SemaphoreType.DMA((1,))],
        ),
        out_shape=[
            jax.ShapeDtypeStruct((rows // 2, D), BF16),
            jax.ShapeDtypeStruct((2, rows // 2, D), BF16),
        ],
        compiler_params=params(20),
        cost_estimate=cost(4.9e9, 16e6),
    )(core, lengths, seats, mid, e, vec, *group.arrays)


def pick(values, half, mode):
    if mode == "split":
        width = values.shape[1] // 2
        return [values[:, half * width : (half + 1) * width]]
    return [values[:, at : at + 128] for at in range(half * 128, values.shape[1], 256)]


def weight_grad_kernel(lefts, rights, mode, core_ref, *refs):
    left_refs, right_refs = refs[:lefts], refs[lefts : lefts + sum(rights)]
    own_ref, other_ref = refs[-2:]
    halves = ([], [])
    at = 0
    for left_ref, count in zip(left_refs, rights):
        left = left_ref[...]
        for right_ref in right_refs[at : at + count]:
            whole = mm(left, right_ref[...], TN).astype(BF16)
            for half in range(2):
                halves[half].extend(pick(whole, half, mode))
        at += count
    low, high = [part[0] if len(part) == 1 else jnp.concatenate(part, axis=1) for part in halves]

    @pl.when(core_ref[0] == 0)
    def _():
        own_ref[...] = low
        other_ref[...] = high

    @pl.when(core_ref[0] != 0)
    def _():
        own_ref[...] = high
        other_ref[...] = low


def weight_grad_call(core, products, block, name, mode="split", cols=None):
    rows, height = products[0][0].shape
    lefts = [left for left, _ in products]
    rights = [right for _, group in products for right in group]
    widths = [right.shape[1] if cols is None else cols[0] for right in rights]
    width = sum(widths)
    seat = 0 if cols is None else cols[1]
    return pl.pallas_call(
        functools.partial(weight_grad_kernel, len(lefts), [len(group) for _, group in products], mode),
        name=name,
        grid_spec=pltpu.PrefetchScalarGridSpec(
            num_scalar_prefetch=1,
            grid=(height // block,),
            in_specs=[pl.BlockSpec((rows, block), lambda i, c: (0, i))] * len(lefts)
            + [
                pl.BlockSpec((rows, w), lambda i, c: (0, seat), pipeline_mode=pl.Buffered(1)) for w in widths
            ],
            out_specs=[pl.BlockSpec((block, width // 2), lambda i, c: (i, 0))] * 2,
        ),
        out_shape=[jax.ShapeDtypeStruct((height, width // 2), BF16)] * 2,
        compiler_params=params(16 if mode == "turns" else 48),
        cost_estimate=cost(2 * rows * height * width, rows * (height + width) * 2 + height * width * 2),
    )(core, *lefts, *rights)


def last_kernel(
    core_ref, x_ref, dm_ref, dq_ref, dk_ref, dv_ref, w_ref, vec_ref, before_ref, theirs_ref, mine_ref, acc_ref
):
    step, steps = pl.program_id(0), pl.num_programs(0)

    @pl.when(step == 0)
    def _():
        acc_ref[...] = before_ref[...]

    subs = sub_blocks(x_ref.shape[0])

    def product(rows):
        return (
            mm(dq_ref[rows, :], w_ref[:D])
            + mm(dk_ref[rows, :], w_ref[D : 2 * D])
            + mm(dv_ref[rows, :], w_ref[2 * D :])
        )

    grads = []
    dh = product(subs[0])
    add_row(acc_ref, 2, dq_ref[...].astype(F32))
    add_row(acc_ref, 3, dv_ref[...].astype(F32))
    for at, rows in enumerate(subs):
        later = product(subs[at + 1]) if at + 1 < len(subs) else None
        normed, scale = norm_parts(x_ref[rows, :].astype(F32))
        add_row(acc_ref, 0, dh * normed)
        add_row(acc_ref, 1, dh)
        grads.append(dm_ref[rows, :] + norm_back(dh * vec_ref[0:1, :], normed, scale))
        dh = later

    @pl.when(step < steps // 2)
    def _():
        for rows, grad in zip(subs, grads):
            theirs_ref[rows, :] = grad

    @pl.when(step >= steps // 2)
    def _():
        for rows, grad in zip(subs, grads):
            mine_ref[0, rows, :] = grad


def last_call(core, x, dm, dq, dk, dv, w, vec, before, block=256):
    rows = x.shape[0]
    steps = rows // block
    half = steps // 2
    row_spec = pl.BlockSpec((block, D), lambda i, c, *s: (row_block(c[0], i, steps), 0))
    return pl.pallas_call(
        last_kernel,
        name="last",
        grid_spec=pltpu.PrefetchScalarGridSpec(
            num_scalar_prefetch=1,
            grid=(steps,),
            in_specs=[row_spec] * 5 + [whole_spec(part.shape) for part in (w, vec, before)],
            out_specs=[
                pl.BlockSpec((block, D), lambda i, *s: (jnp.minimum(i, half - 1), 0)),
                pl.BlockSpec((1, block, D), lambda i, c, *s: (c[0], jnp.maximum(i - half, 0), 0)),
                pl.BlockSpec((16, D), lambda i, *s: (0, 0)),
            ],
        ),
        out_shape=[
            jax.ShapeDtypeStruct((rows // 2, D), F32),
            jax.ShapeDtypeStruct((2, rows // 2, D), F32),
            jax.ShapeDtypeStruct((16, D), F32),
        ],
        compiler_params=params(12),
        cost_estimate=cost(rows * 6 * D * D, 16e6),
    )(core, x, dm, dq, dk, dv, w, vec, before)


def adam_kernel(plans, sources, core_ref, *refs):
    halves = [refs[2 * i : 2 * i + 2] for i in range(sources)]
    count = len(plans)
    states = refs[2 * sources : 2 * sources + 3 * count]
    outs = refs[2 * sources + 3 * count : 2 * sources + 6 * count]
    grads = refs[2 * sources + 6 * count :]
    for core in range(2):

        @pl.when(core_ref[0] == core)
        def _():
            for (_, _, moves), grad_ref in zip(plans, grads):
                for source, start, width, place0, place1 in moves:
                    for half, place in ((0, place0), (1, place1)):
                        ref = halves[source][0 if half == core else 1]
                        grad_ref[:, place : place + width] = ref[:, start : start + width].astype(F32)

    for i, (rate, decay, _) in enumerate(plans):
        weight, first, second = states[3 * i : 3 * i + 3]
        new = adamw(weight[...], grads[i][...], first[...], second[...], rate, decay)
        for out, value in zip(outs[3 * i : 3 * i + 3], new):
            out[...] = value


def adam_call(core, halves, states, plans):
    flat = [part for pair in halves for part in pair]
    held = [part for state in states for part in state]
    spec = pl.BlockSpec(memory_space=pltpu.VMEM)
    news = pl.pallas_call(
        functools.partial(adam_kernel, plans, len(halves)),
        name="adam",
        in_specs=[pl.BlockSpec(memory_space=pltpu.SMEM)] + [spec] * (len(flat) + len(held)),
        out_specs=[spec] * len(held),
        out_shape=[jax.ShapeDtypeStruct(part.shape, F32) for part in held],
        scratch_shapes=[pltpu.VMEM(state[0].shape, F32) for state in states],
        compiler_params=params(12),
        cost_estimate=cost(1e6, 24 * sum(state[0].size for state in states)),
    )(core, *flat, *held)
    return [news[3 * i : 3 * i + 3] for i in range(len(states))]


def after(value, *others):
    if not others:
        return value
    return lax.optimization_barrier((value,) + others)[0]


def cut(array, axis, index, size=1):
    starts = [jnp.uint32(0)] * array.ndim
    sizes = list(array.shape)
    starts[axis], sizes[axis] = index, size
    return lax.dynamic_slice(array, starts, sizes)


class Grid:
    def __init__(self, chips):
        log = chips.bit_length() - 1
        side = 1 << (log // 3)
        if side * side * (chips // (side * side)) != chips:
            side = 1
        self.chips = chips
        self.n = side
        self.nz = chips // (side * side)
        self.core = lax.axis_index("seq")
        self.chip = lax.axis_index("dp")
        self.x = self.chip % side
        self.y = self.chip // side % side
        self.z = self.chip // (side * side)

    def pin(self, value):
        n, core = self.n, self.core
        first, second = self.coords(core)
        places = {
            "core": core,
            "other": 1 - core,
            "chip": self.chip,
            "seats": self.seats(True),
            "q_seats": self.seats(False),
        }
        for s in range(n):
            for t in range(n):
                places["plane", s, t] = self.plane((first + s) % n, (second + t) % n, core)
        for at in range(self.nz):
            places["z", at] = self.z ^ at
        names = list(places)
        held = lax.optimization_barrier((value, *[places[name].astype(jnp.uint32) for name in names]))
        self.places = dict(zip(names, held[1:]))
        return held[0]

    def plane(self, first, second, core):
        return jnp.where(core == 0, second * self.n + first, first * self.n + second)

    def coords(self, core):
        return jnp.where(core == 0, self.x, self.y), jnp.where(core == 0, self.y, self.x)

    def permute(self, value, axis, shift=0):
        pairs = []
        for chip in range(self.chips):
            for core in range(2):
                x, y, z = chip % self.n, chip // self.n % self.n, chip // (self.n * self.n)
                to_core = core
                if axis == "z":
                    z = (z + shift) % self.nz
                elif axis == "zx":
                    z = z ^ shift
                elif axis == "core":
                    to_core = 1 - core
                elif (axis == "first") == (core == 0):
                    x = (x + shift) % self.n
                else:
                    y = (y + shift) % self.n
                pairs.append((chip * 2 + core, ((z * self.n + y) * self.n + x) * 2 + to_core))
        return lax.ppermute(value, ("dp", "seq"), pairs)

    def swap(self, value):
        return self.permute(value, "core")

    def join(self, own, other, axis):
        return jnp.where(
            self.places["core"] == 0,
            jnp.concatenate([own, other], axis),
            jnp.concatenate([other, own], axis),
        )

    def seats(self, halving):
        found = []
        for half in range(2):
            core = self.core if half == 0 else 1 - self.core
            first, second = self.coords(core)
            for s2 in range(self.n):
                for s1 in range(self.n):
                    flat = self.plane((first - s1) % self.n, (second - s2) % self.n, core)
                    for sz in range(self.nz):
                        z = self.z ^ sz if halving else (self.z - sz) % self.nz
                        found.append(z * self.n * self.n + flat)
        return jnp.stack(found).astype(jnp.int32)

    def small(self, value, axis, shifts, *until):
        got = [after(self.permute(value, axis, s), *until) for s in shifts]
        return value + sum(got), got

    def gather_z(self, block, *until):
        return jnp.stack([block] + [after(self.permute(block, "z", s), *until) for s in range(1, self.nz)])

    def gather_bit(self, held, bit, *until):
        return jnp.concatenate([held, after(self.permute(held, "zx", bit), *until)])

    def along(self, axis, column, *until):
        return [after(self.permute(column, axis, s), *until) for s in range(1, self.n)]

    def plane_parts(self, column, firsts, seconds, passed):
        parts = [column] + firsts
        for s2 in range(1, self.n):
            parts += [seconds[s2 - 1]] + [passed[s1 - 1][s2 - 1] for s1 in range(1, self.n)]
        return [part[None] for part in parts]

    def gather_first(self, column, *until):
        return jnp.stack([column] + [after(self.permute(column, "first", s), *until) for s in range(1, self.n)])

    def gather_second(self, line, *until):
        return [after(self.permute(line, "second", s), *until) for s in range(1, self.n)]

    def scatter_first(self, own, pair, *until):
        rows, cols = own.shape[0] // self.chips, own.shape[1]
        n = self.n

        def seat(s1, s2):
            own_part, pair_part = [
                cut(part.reshape(self.nz, n * n, rows, cols), 1, self.places["plane", s1, s2]).astype(F32)
                for part in (own, pair)
            ]
            return own_part + pair_part

        kept = [seat(0, t) for t in range(n)]
        for s in range(1, n):
            send = jnp.stack([seat(s, t).astype(BF16) for t in range(n)])
            got = after(self.permute(send, "first", s), *until)
            kept = [kept[t] + got[t].astype(F32) for t in range(n)]
        return kept[0], [part.astype(BF16) for part in kept[1:]]

    def scatter_second(self, kept, *until):
        mine, rest = kept
        got = [after(self.permute(rest[s - 1], "second", s), *until) for s in range(1, self.n)]
        for part in got:
            mine = mine + part.astype(F32)
        return mine.reshape((self.nz,) + mine.shape[2:]), got

    def order_z(self, mine):
        return [cut(mine, 0, self.places["z", at])[0] for at in range(self.nz)]

    def scatter_bit(self, parts, *until):
        half = len(parts) // 2
        send = parts[half] if half == 1 else jnp.stack([part.astype(BF16) for part in parts[half:]])
        got = after(self.permute(send.astype(BF16), "zx", half), *until)
        if half == 1:
            return [parts[0] + got.astype(F32)], got
        return [part + got[at].astype(F32) for at, part in enumerate(parts[:half])], got

    def scatter_z(self, parts, *until):
        while len(parts) > 1:
            parts, _ = self.scatter_bit(parts, *until)
        return parts[0]


def adamw(weight, gradient, first_moment, second_moment, step_rate, weight_decay):
    first_moment = BETA_ONE * first_moment + (1.0 - BETA_ONE) * gradient
    second_moment = BETA_TWO * second_moment + (1.0 - BETA_TWO) * gradient * gradient
    first_fix = 1.0 - BETA_ONE**STEP
    second_fix = 1.0 - BETA_TWO**STEP
    direction = first_moment / first_fix / (jnp.sqrt(second_moment / second_fix) + EPS_ADAM)
    return (weight - step_rate * (direction + weight_decay * weight), first_moment, second_moment)


def local(
    block_in, lengths, out_grad, w_qkv, w_out, w_up, w_down, vectors,
    first_qkv, first_out, first_up, first_down, first_vectors,
    second_qkv, second_out, second_up, second_down, second_vectors,
):
    grid = Grid(lax.axis_size("dp"))
    core = grid.core
    w_qkv_first = grid.pin(w_qkv)
    places = grid.places
    core_arr = places["core"].reshape(1).astype(jnp.int32)
    half_len = block_in.shape[1]
    vec_count, vec_here = vectors.shape

    def own_slot(halves):
        mine, theirs = [cut(halves, 0, places[name])[0] for name in ("core", "other")]
        return grid.join(mine, grid.swap(theirs), 0)

    def both_slots(mine, got):
        zero = jnp.uint32(0)
        return lax.dynamic_update_slice(mine, got[None], (places["other"], zero, zero))

    def half_of(shard):
        width = shard.shape[1] // 2
        return jnp.where(places["core"] == 0, shard[:, :width], shard[:, width:]).astype(BF16)

    seats, q_seats = [places[name].astype(jnp.int32) for name in ("seats", "q_seats")]

    turned = jnp.pad(vectors.T.astype(BF16), ((0, 0), (0, 128 - vec_count)))
    q_block = jnp.concatenate([half_of(w_qkv_first), turned], axis=1)
    u_block = jnp.concatenate([half_of(w_out), half_of(w_up)], axis=1)
    d_block = half_of(w_down)
    q_col = grid.gather_z(q_block)
    x = own_slot(block_in)
    bits = [1 << at for at in range((grid.nz - 1).bit_length())]
    u_col, d_col = u_block[None], d_block[None]
    for bit in bits[:-1]:
        u_col = grid.gather_bit(u_col, bit)
        d_col = grid.gather_bit(d_col, bit)
    q_line = after(grid.gather_first(q_col, x), u_col, d_col)
    q_rest = grid.gather_second(q_line)
    u_col = grid.gather_bit(after(u_col, q_line), bits[-1])
    q_line_swap = grid.swap(q_line)
    q_rest_swap = [grid.swap(after(part, u_col)) for part in q_rest]
    q_group = finish_group(grid, q_seats, [q_line] + q_rest, [q_line_swap] + q_rest_swap)

    h1, qkv, vec, w_back = qkv_call(core_arr, q_seats, x, q_group)
    u_firsts = grid.along("first", u_col, qkv)
    d_col = grid.gather_bit(after(d_col, u_col), bits[-1], qkv)
    og = own_slot(after(out_grad, qkv))
    att = attend_call(core_arr, lengths, after(qkv, d_col, *u_firsts), 0, 4, ())
    u_seconds = grid.along("second", u_col, *att)
    u_passed = [grid.along("second", part, *att) for part in u_firsts]
    early = [after(grid.swap(part), *att) for part in [u_col] + u_firsts]
    d_col = after(d_col, *u_seconds, *[part for parts in u_passed for part in parts])
    a, lse = attend_call(core_arr, lengths, after(qkv, d_col), 4, 2, att)
    late_seconds = [after(grid.swap(part), a) for part in u_seconds]
    late_passed = [[after(grid.swap(part), a) for part in parts] for parts in u_passed]
    u_group = finish_group(
        grid,
        seats,
        grid.plane_parts(u_col, u_firsts, u_seconds, u_passed),
        grid.plane_parts(early[0], early[1:], late_seconds, late_passed),
    )
    mid, h2, e, slope, dy = up_call(core_arr, lengths, seats, x, a, og, vec, u_group)
    d_firsts = grid.along("first", d_col, mid)
    d_seconds = grid.along("second", d_col, mid)
    d_col_swap = after(grid.swap(d_col), mid)
    d_own, d_other = weight_grad_call(
        core_arr, [(after(e, *d_firsts, *d_seconds), [dy])], 512, "grad_down"
    )
    d_passed = [grid.along("second", part, d_own) for part in d_firsts]
    early = [[after(grid.swap(part), d_own) for part in parts] for parts in (d_firsts, d_seconds)]
    d_group = finish_group(
        grid,
        seats,
        grid.plane_parts(d_col, d_firsts, d_seconds, d_passed),
        grid.plane_parts(d_col_swap, *early, [[grid.swap(part) for part in parts] for parts in d_passed]),
    )
    dz, dmb, dm, da, acc_mid = down_call(core_arr, seats, mid, slope, dy, vec, u_group, d_group)

    d_pair = after(grid.swap(d_other), dz)
    u_own, u_other = weight_grad_call(
        core_arr, [(a, [dmb]), (h2, [after(dz, d_pair)])], 384, "grad_up"
    )
    d_kept = grid.scatter_first(d_own, d_pair, u_own)

    def back_call(start, count, before, *needs):
        return attend_back_call(core_arr, lengths, qkv, a, after(da, *needs), lse, start, count, before)

    back = back_call(0, 2, (), u_own, *d_kept[1])
    d_sum, d_here = grid.scatter_second(d_kept, *back)
    u_pair = after(grid.swap(u_other), *back)
    back = back_call(2, 4, back, u_pair, *d_here)
    d_parts, d_got = grid.scatter_bit(grid.order_z(d_sum), *back)
    u_kept = grid.scatter_first(u_own, u_pair, *back)
    dq, dk, dv = back
    q_own, q_other = weight_grad_call(
        core_arr, [(h1, [after(dq, d_got, *u_kept[1]), dk, dv])], 384, "grad_qkv", "turns"
    )
    u_sum, u_here = grid.scatter_second(u_kept, q_own)
    q_pair = grid.swap(after(q_other, *u_here))
    in_theirs, in_mine, acc = last_call(
        core_arr, x, dm, after(dq, q_own, q_pair), dk, dv, w_back, vec, acc_mid
    )
    d_mine = grid.scatter_z(d_parts, in_theirs)
    d_other_mine = grid.swap(d_mine)
    q_kept = grid.scatter_first(q_own, q_pair, in_theirs)
    u_parts, u_got = grid.scatter_bit(grid.order_z(u_sum), *q_kept[1])
    q_sum, q_here = grid.scatter_second(q_kept, u_got)
    down_new, = adam_call(
        core_arr,
        [(d_mine, d_other_mine)],
        [(after(w_down, *q_kept[1]), first_down, second_down)],
        [(FF ** (-0.5), MATRIX_DECAY, [(0, 0, D // 2, 0, D // 2)])],
    )
    in_got = grid.swap(after(in_theirs, *q_kept[1]))
    in_grad = both_slots(in_mine, after(in_got, *q_here))
    w_qkv = after(w_qkv, in_grad)
    shifts = range(1, grid.n)
    vec_total, _ = grid.small(acc, "core", [0])
    vec_total, _ = grid.small(vec_total, "first", shifts, *q_kept[1])
    vec_total, vec_here_got = grid.small(vec_total, "second", shifts, *q_here)
    out_theirs, out_mine = out_call(
        core_arr, lengths, seats, after(mid, in_grad, *q_here, *vec_here_got), e, vec, d_group
    )
    u_mine = grid.scatter_z([after(part, *q_here) for part in u_parts], out_theirs)
    u_other_mine = grid.swap(u_mine)
    q_parts, q_got = grid.scatter_bit(grid.order_z(q_sum), out_theirs)
    block_out = both_slots(out_mine, grid.swap(out_theirs))
    until = (out_theirs,)
    for bit in bits[:-1]:
        vec_total, _ = grid.small(vec_total, "zx", [bit], *until)
    while len(q_parts) > 1:
        q_parts, q_got = grid.scatter_bit(q_parts)
    vec_total, _ = grid.small(vec_total, "zx", [bits[-1]], q_got)
    q_mine = q_parts[0]
    q_other_mine = grid.swap(q_mine)

    half, wide = D // 2, FF // 2
    out_new, up_new = adam_call(
        core_arr,
        [(u_mine, u_other_mine)],
        [(after(w_out, in_grad), first_out, second_out), (w_up, first_up, second_up)],
        [
            ((D // 64) ** (-0.5), MATRIX_DECAY, [(0, 0, half, 0, half)]),
            (D ** (-0.5), MATRIX_DECAY, [(0, half, wide, 0, wide)]),
        ],
    )
    moves = []
    for turn in range(3 * D // 256):
        moves.append((0, turn * 128, 128, turn * 256, turn * 256 + 128))
    qkv_new, = adam_call(
        core_arr,
        [(q_mine, q_other_mine)],
        [(w_qkv, first_qkv, second_qkv)],
        [(D ** (-0.5), MATRIX_DECAY, moves)],
    )
    vec_grad = cut(vec_total[:vec_count].reshape(vec_count, -1, vec_here), 1, places["chip"])[:, 0]
    vec_new = adamw(vectors, vec_grad, first_vectors, second_vectors, VECTOR_RATE, 0.0)
    news = [qkv_new, out_new, up_new, down_new, vec_new]
    return (block_out, in_grad) + tuple(new[kind] for kind in range(3) for new in news)


def finish_group(grid, seats, own, other):
    rows, cols = own[0].shape[-2:]
    if rows % 16 == 0:
        return Pieces(own + other, rows)
    found = []
    for half, parts in enumerate((own, other)):
        here = seats[half * grid.chips : (half + 1) * grid.chips]
        order = jnp.zeros((grid.chips,), jnp.int32).at[here].set(jnp.arange(grid.chips, dtype=jnp.int32))
        blocks = jnp.concatenate(parts).reshape(grid.chips, rows, cols)
        found.append(jnp.take(blocks, order, axis=0).reshape(1, 1, grid.chips * rows, cols))
    return Pieces(found, grid.chips * rows, True)


def solution(mesh):
    weight = P("dp", None)
    vector = P(None, "dp")
    state = (weight, weight, weight, weight, vector)
    tokens = P("dp", "seq", None)
    return jax.shard_map(
        local,
        mesh=mesh,
        in_specs=(tokens, P("dp"), tokens) + state * 3,
        out_specs=(tokens, tokens) + state * 3,
        check_vma=False,
    )
```
